32 devices in a mesh: wide: 8 (over y, x, core), narrow: 4 (over z).
Axes of the slice: x: 2, y: 2, z: 4, core: 2. Of those that a mesh axis runs over, the one named last changes fastest.
Arguments:
- covariates: bfloat16 [65536, 128], P(('wide', 'narrow')), may hold values from -6 to 6
- level_codes: int32 [65536], P(('wide', 'narrow')), may hold values from 0 to 3
- sign_bits: int32 [65536], P(('wide', 'narrow')), may hold values from 0 to 1
- sample_rows: int32 [1024], P(('wide', 'narrow')), may hold values from 0 to 2047, as said below
- effects: float32 [512], replicated, may hold values from -6 to 6
- noise: float32 [65536], P(('wide', 'narrow')), may hold values from -8 to 8
Outputs:
- coefficients: float32 [512], replicated
- residual: float32 [65536], P(('wide', 'narrow'))
- factor: float32 [512, 512], replicated
The draws below stay inside these ranges and needn't reach their ends.
Inputs may be any that keep to these rules, and one draw needn't show every extreme that they name: `sample_rows`: a local row offset on the device that owns the entry.
All inputs are finite; a program needn't handle non-finite values.
Results may differ from the reference program's by a relative error of at most 0.0006.
The reference program's roundings to bfloat16 on the way count: a program that leaves them out, or rounds other values in their place, can miss the bound.
Values may be sent and summed in bfloat16 or wider, within the bound.
No kernel may reach another device: no remote copies, remote signals or barrier semaphores. Data moves between devices by JAX's collectives and lax.ppermute only.
A program may use at most 64 MiB of HBM per device.

```python
import math
import jax
import jax.numpy as jnp
from jax import lax

COV = 128
LEVELS = 4
COLS = 512
ROWS_DEV = 2048
HB = 256
SKETCH = 1024
SAMP = 32
ITERS = 4
ROWS = 65536
N_WIDE = 8
N_NARROW = 4


def draw_sample_rows(key, part):
    key_values = jax.random.fold_in(key, 11)
    key_place = jax.random.fold_in(key, 12)
    key_other = jax.random.fold_in(key, 13)
    offsets = jax.random.randint(key_values, (SKETCH,), 0, ROWS_DEV, dtype=jnp.int32)
    top_place = jax.random.randint(key_place, (), 0, SKETCH, dtype=jnp.int32)
    step_other = jax.random.randint(key_other, (), 1, SKETCH, dtype=jnp.int32)
    low_place = (top_place + step_other) % SKETCH
    offsets = offsets.at[top_place].set(ROWS_DEV - 1)
    offsets = offsets.at[low_place].set(0)
    return offsets


def place_ends(array, own_key, smallest, high):
    dims = array.shape
    spot = [jax.random.randint(jax.random.fold_in(own_key, axis), (), 0, dims[axis]) for axis in range(len(dims))]
    array = array.at[tuple(spot)].set(smallest)
    longest = dims.index(max(dims))
    spot[longest] = (spot[longest] + 1) % dims[longest]
    return array.at[tuple(spot)].set(high)


def block_scale(rng, dims, split, least, largest):
    level, own = 1.0, jax.random.fold_in(rng, 6)
    for position, blocks in split:
        steps = jnp.exp(jax.random.uniform(jax.random.fold_in(own, position), (blocks,), jnp.float32, least / len(split), largest / len(split)))
        level = level * jnp.repeat(steps, dims[position] // blocks).reshape([-1 if axis == position else 1 for axis in range(len(dims))])
    return level


def bell_draw(own_key, shape, spread, most, pieces=(), kind=jnp.bfloat16):
    level = block_scale(own_key, shape, pieces, -0.22, 0.18) if pieces else 1.0
    array = jax.random.normal(own_key, shape, jnp.float32) * spread * level
    return jnp.minimum(jnp.maximum(array, -most), most).astype(kind)


def setup_inputs(seed: int = 0) -> dict:
    arg_keys = jax.random.split(jax.random.key(seed), 7)
    covariates = bell_draw(arg_keys[0], (ROWS, COV), 1.0, 6.0, ((0, 32),))
    level_codes = place_ends(jax.random.randint(arg_keys[1], (ROWS,), 0, LEVELS), jax.random.fold_in(arg_keys[1], 1), 0, LEVELS - 1).astype(jnp.int32)
    sign_bits = place_ends(jax.random.randint(arg_keys[2], (ROWS,), 0, 2), jax.random.fold_in(arg_keys[2], 1), 0, 1).astype(jnp.int32)
    sample_rows = draw_sample_rows(jax.random.fold_in(arg_keys[6], 71), 0)
    effects = bell_draw(arg_keys[4], (COLS,), 1.0, 6.0, (), jnp.float32)
    noise = bell_draw(arg_keys[5], (ROWS,), 3.0, 8.0, ((0, 32),), jnp.float32)
    return {"covariates": covariates, "level_codes": level_codes, "sign_bits": sign_bits, "sample_rows": sample_rows, "effects": effects, "noise": noise}


half_root = math.sqrt(0.5)

def hadamard(size):
    left = jnp.arange(size, dtype=jnp.int32)[:, None]
    right = jnp.arange(size, dtype=jnp.int32)[None, :]
    common = jnp.bitwise_and(left, right)
    parity = jnp.zeros((size, size), jnp.int32)
    for place in range(size.bit_length()):
        parity = parity + jnp.bitwise_and(jnp.right_shift(common, place), 1)
    return (1 - 2 * (parity % 2)).astype(jnp.float32)

def tri_solve(lower, vector, transpose):
    return lax.linalg.triangular_solve(lower, vector[:, None], left_side=True, lower=True, transpose_a=transpose)[:, 0]

def reference(covariates, level_codes, sign_bits, sample_rows, effects, noise):
    cols = LEVELS * COV
    table = hadamard(HB)
    cov_four = covariates.reshape(N_WIDE, N_NARROW, ROWS_DEV, COV).transpose(1, 0, 2, 3)
    code_three = level_codes.reshape(N_WIDE, N_NARROW, ROWS_DEV).transpose(1, 0, 2)
    sign_three = sign_bits.reshape(N_WIDE, N_NARROW, ROWS_DEV).transpose(1, 0, 2)
    samp_three = sample_rows.reshape(N_WIDE, N_NARROW, SAMP).transpose(1, 0, 2)

    def one_group(pack):
        cov_part, code_part, sign_part, samp_part = pack
        onehot = (code_part[..., None] == jnp.arange(LEVELS, dtype=jnp.int32)).astype(jnp.bfloat16)
        flipped = cov_part * (1 - 2 * sign_part).astype(jnp.bfloat16)[..., None]
        design = (onehot[..., None] * flipped[..., None, :]).reshape(N_WIDE, ROWS_DEV // HB, HB, cols)
        mixed = jnp.einsum('ij,wgjc->wgic', table, design.astype(jnp.float32), precision=lax.Precision.HIGHEST)
        mixed = (mixed * (1.0 / math.sqrt(HB))).astype(jnp.bfloat16).reshape(N_WIDE, ROWS_DEV, cols)
        for place in range(3):
            span = 2 ** place
            shaped = mixed.astype(jnp.float32).reshape(N_WIDE // (2 * span), 2, span, ROWS_DEV, cols)
            low = shaped[:, 0]
            high = shaped[:, 1]
            mixed = (jnp.stack([low + high, low - high], axis=1) * half_root).astype(jnp.bfloat16)
            mixed = mixed.reshape(N_WIDE, ROWS_DEV, cols)
        return jnp.take_along_axis(mixed, samp_part[:, :, None], axis=1)
    sketch = lax.map(one_group, (cov_four, code_three, sign_three, samp_three))
    sketch = sketch.transpose(1, 0, 2, 3).reshape(SKETCH, cols)
    gram = jnp.dot(sketch.T.astype(jnp.float32), sketch.astype(jnp.float32), preferred_element_type=jnp.float32)
    lower = jnp.linalg.cholesky(gram)
    factor = lower.T * math.sqrt(LEVELS / SKETCH)
    onehot = (level_codes[:, None] == jnp.arange(LEVELS, dtype=jnp.int32)[None, :]).astype(jnp.float32)
    wide_cov = covariates.astype(jnp.float32)

    def apply_design(vector):
        values = jnp.dot(wide_cov, vector.reshape(LEVELS, COV).T, precision=lax.Precision.HIGHEST)
        return lax.optimization_barrier(jnp.sum(values * onehot, axis=1))

    def adjoint(vector):
        return jnp.dot((onehot * vector[:, None]).T, wide_cov, precision=lax.Precision.HIGHEST).reshape(cols)
    timings = apply_design(effects) + noise
    resid = timings
    steer = tri_solve(lower, adjoint(resid), False)
    direction = steer
    gamma = jnp.sum(steer * steer)
    solved = jnp.zeros((cols,), jnp.float32)
    for step in range(ITERS):
        image = apply_design(tri_solve(lower, direction, True))
        alpha = gamma / jnp.sum(image * image)
        solved = solved + alpha * direction
        resid = resid - alpha * image
        steer = tri_solve(lower, adjoint(resid), False)
        gamma_new = jnp.sum(steer * steer)
        direction = steer + gamma_new / gamma * direction
        gamma = gamma_new
    return (tri_solve(lower, solved, True), resid, factor)
```

```python
import math

import jax
import jax.numpy as jnp
from jax import lax
from jax.sharding import PartitionSpec as P

COV = 128
LEVELS = 4
HB = 256
SKETCH = 1024
ITERS = 4
MIX_BITS = 3

half_root = math.sqrt(0.5)
HIGHEST = lax.Precision.HIGHEST


def partner(value, axis, mask):
    pairs = [(source, source ^ mask) for source in range(lax.axis_size(axis))]
    return lax.ppermute(value, axis, pairs)


def rounded(value):
    return lax.reduce_precision(value, 8, 7).astype(jnp.bfloat16)


def hadamard_rows(rows, size):
    common = jnp.bitwise_and(rows[:, None], jnp.arange(size, dtype=jnp.int32)[None, :])
    for shift in (4, 2, 1):
        common = jnp.bitwise_xor(common, jnp.right_shift(common, shift))
    return 1 - 2 * jnp.bitwise_and(common, 1)


def mix(pieces):
    wide_index = lax.axis_index("wide")
    for place in range(MIX_BITS):
        bit = jnp.bitwise_and(jnp.right_shift(wide_index, place), 1)
        sign = (1 - 2 * bit).astype(jnp.float32)
        pieces = [
            rounded((sign * own.astype(jnp.float32) + other.astype(jnp.float32)) * half_root)
            for own, other in zip(pieces[0::2], pieces[1::2])
        ]
    return pieces[0]


def gather_rows(rows):
    wide, narrow = lax.axis_size("wide"), lax.axis_size("narrow")
    samp, cols = rows.shape
    rows = jnp.concatenate([rows] + [partner(rows, "narrow", m) for m in range(1, narrow)])
    rows = jnp.concatenate([rows] + [partner(rows, "wide", m) for m in range(2, wide, 2)])
    rows = jnp.concatenate([rows, partner(rows, "wide", 1)])
    apart_wide = jnp.bitwise_xor(jnp.arange(wide), lax.axis_index("wide"))
    apart_narrow = jnp.bitwise_xor(jnp.arange(narrow), lax.axis_index("narrow"))
    place = jnp.bitwise_and(apart_wide, 1) * (wide // 2) + jnp.right_shift(apart_wide, 1)
    order = (place[:, None] * narrow + apart_narrow[None, :]).reshape(-1)
    return rows.reshape(wide * narrow, samp, cols)[order].reshape(-1, cols)


def body(covariates, level_codes, sign_bits, sample_rows, effects, noise):
    rows_dev = covariates.shape[0]
    samp = sample_rows.shape[0]
    cols = LEVELS * COV
    wide_cov = covariates.astype(jnp.float32)
    onehot = level_codes[:, None] == jnp.arange(LEVELS, dtype=jnp.int32)[None, :]
    design = (onehot.astype(jnp.bfloat16)[:, :, None] * covariates[:, None, :]).reshape(rows_dev, cols)

    wanted = [sample_rows] + [partner(sample_rows, "wide", m) for m in range(1, 2**MIX_BITS)]

    normal = jnp.dot(design.T, covariates, preferred_element_type=jnp.float32)
    back = jnp.dot((onehot.astype(jnp.float32) * noise[:, None]).T, wide_cov, precision=HIGHEST)
    sums = lax.psum(jnp.concatenate([normal, back]), ("wide", "narrow"))

    want = jnp.concatenate(wanted)
    signs = 1 - 2 * sign_bits
    table = hadamard_rows(jnp.bitwise_and(want, HB - 1), HB)
    table = jnp.tile(table, (1, rows_dev // HB)) * signs[None, :]
    block = jnp.arange(rows_dev, dtype=jnp.int32) // HB
    table = jnp.where((want // HB)[:, None] == block[None, :], table, 0).astype(jnp.bfloat16)
    local = jnp.dot(table, design, preferred_element_type=jnp.float32)
    local = rounded(local * (1.0 / math.sqrt(HB)))
    local = [local[m * samp : (m + 1) * samp] for m in range(2**MIX_BITS)]
    pieces = [local[0]] + [partner(local[m], "wide", m) for m in range(1, 2**MIX_BITS)]
    sketch = gather_rows(mix(pieces))

    gram = jnp.dot(sketch.T, sketch, preferred_element_type=jnp.float32)
    lower = jnp.linalg.cholesky(gram)
    factor = lower.T * math.sqrt(LEVELS / SKETCH)
    inverse = lax.linalg.triangular_solve(lower, jnp.eye(cols, dtype=jnp.float32), left_side=True, lower=True)

    normal = sums[:cols].reshape(LEVELS, COV, COV)
    back = sums[cols:]

    def normal_times(vector):
        return jnp.einsum("lij,lj->li", normal, vector.reshape(LEVELS, COV), precision=HIGHEST).reshape(cols)

    def precondition(vector):
        steer = jnp.dot(inverse, vector, precision=HIGHEST)
        return jnp.dot(steer, inverse, precision=HIGHEST), jnp.sum(steer * steer)

    gradient = normal_times(effects) + back.reshape(cols)
    step_to, gamma = precondition(gradient)
    solved = jnp.zeros((cols,), jnp.float32)
    for step in range(ITERS):
        image = normal_times(step_to)
        alpha = gamma / jnp.sum(step_to * image)
        solved = solved + alpha * step_to
        if step == ITERS - 1:
            break
        gradient = gradient - alpha * image
        steer, gamma_new = precondition(gradient)
        step_to = steer + gamma_new / gamma * step_to
        gamma = gamma_new
    left = (effects - solved).reshape(LEVELS, COV)
    values = jnp.dot(wide_cov, left.T, precision=HIGHEST)
    resid = noise + jnp.sum(jnp.where(onehot, values, 0.0), axis=1)
    return (solved, resid, factor)


def solution(mesh):
    return jax.shard_map(
        body,
        mesh=mesh,
        in_specs=(
            P(("wide", "narrow"), None),
            P(("wide", "narrow")),
            P(("wide", "narrow")),
            P(("wide", "narrow")),
            P(),
            P(("wide", "narrow")),
        ),
        out_specs=(P(), P(("wide", "narrow")), P()),
        check_vma=False,
    )
```

```python
import functools
import math

import jax
import jax.numpy as jnp
from jax import lax
from jax.experimental import pallas as pl
from jax.experimental.pallas import tpu as pltpu
from jax.sharding import PartitionSpec as P

COV = 128
LEVELS = 4
HB = 256
SKETCH = 1024
ITERS = 4
MIX_BITS = 3

half_root = math.sqrt(0.5)
HIGHEST = lax.Precision.HIGHEST
f32 = jnp.float32
SUB, LANE = 8, 128
COUNT = 4


def partner(value, axis, mask):
    pairs = [(source, source ^ mask) for source in range(lax.axis_size(axis))]
    return lax.ppermute(value, axis, pairs)


def rounded(value):
    return lax.reduce_precision(value, 8, 7).astype(jnp.bfloat16)


def hadamard_rows(rows, size):
    common = jnp.bitwise_and(rows[:, None], jnp.arange(size, dtype=jnp.int32)[None, :])
    for shift in (4, 2, 1):
        common = jnp.bitwise_xor(common, jnp.right_shift(common, shift))
    return 1 - 2 * jnp.bitwise_and(common, 1)


def mix(pieces):
    wide_index = lax.axis_index("wide")
    for place in range(MIX_BITS):
        bit = jnp.bitwise_and(jnp.right_shift(wide_index, place), 1)
        sign = (1 - 2 * bit).astype(jnp.float32)
        pieces = [
            rounded((sign * own.astype(jnp.float32) + other.astype(jnp.float32)) * half_root)
            for own, other in zip(pieces[0::2], pieces[1::2])
        ]
    return pieces[0]


def spread(value):
    return jnp.broadcast_to(value, (SUB, LANE))


def eliminate(tiles, count):
    lane = lax.broadcasted_iota(jnp.int32, (SUB, LANE), 1)
    sub = lax.broadcasted_iota(jnp.int32, (SUB, LANE), 0)
    tiles = list(tiles)
    scales = [None] * len(tiles)
    for first in range(0, LANE, count):
        tile, offset = divmod(first, SUB)
        window = (lane >= first) & (lane < first + count)
        columns = [
            [spread(tiles[i][:, first + k : first + k + 1]) for k in range(count)] for i in range(tile, len(tiles))
        ]
        pivot = [
            [spread(columns[0][m][offset + k : offset + k + 1, :]) if m >= k else None for m in range(count)]
            for k in range(count)
        ]
        rows = []
        for k in range(count):
            row = spread(tiles[tile][offset + k : offset + k + 1, :])
            row = jnp.where(window, 0.0, row)
            rows.append(jnp.where(lane == first + k, 1.0, row))
        inverse, ratio = [], [[None] * count for _ in range(count)]
        for k in range(count):
            inverse.append(1.0 / pivot[k][k])
            for m in range(k + 1, count):
                ratio[k][m] = pivot[k][m] * inverse[k]
                for n in range(m, count):
                    pivot[m][n] = pivot[m][n] - ratio[k][m] * pivot[k][n]
                rows[m] = rows[m] - ratio[k][m] * rows[k]
        steps = [None] * count
        for k in reversed(range(count)):
            steps[k] = rows[k] * inverse[k]
            for m in range(k + 1, count):
                steps[k] = steps[k] - ratio[k][m] * steps[m]
        old = tiles[tile]
        scale = scales[tile]
        for i in range(tile, len(tiles)):
            new = jnp.where(window, 0.0, tiles[i])
            for k in range(count):
                new = new - columns[i - tile][k] * steps[k]
            tiles[i] = new
        fixed = old
        if offset + count < SUB:
            fixed = jnp.where(sub >= offset + count, tiles[tile], old)
        for k in range(count):
            kept = rows[k]
            for m in range(k, count):
                kept = jnp.where(lane == first + m, pivot[k][m], kept)
            root = lax.rsqrt(pivot[k][k])
            fixed = jnp.where(sub == offset + k, kept, fixed)
            scale = root if scale is None else jnp.where(sub == offset + k, root, scale)
        tiles[tile] = fixed
        scales[tile] = scale
    return tiles, scales


def factor_kernel(samp, ratio, place_ref, *refs):
    piece_refs, (factor_ref, inverse_ref, sketch, work, line) = refs[:-5], refs[-5:]
    cols = work.shape[0]
    at = 0
    for piece in piece_refs:
        for start in range(0, piece.shape[0], samp):
            put = pl.multiple_of(place_ref[at] * samp, samp)
            sketch[pl.ds(put, samp), :] = piece[start : start + samp, :]
            at += 1
    rows = sketch[...]
    work[...] = lax.dot_general(rows, rows, (((0,), (0,)), ((), ())), preferred_element_type=f32)

    row_in = lax.broadcasted_iota(jnp.int32, (LANE, LANE), 0)
    lane_in = lax.broadcasted_iota(jnp.int32, (LANE, LANE), 1)
    lane_all = lax.broadcasted_iota(jnp.int32, (LANE, cols), 1)
    row_all = lax.broadcasted_iota(jnp.int32, (cols, LANE), 0)

    def block_step(block, _):
        base = pl.multiple_of(block * LANE, LANE)
        here = pl.ds(base, LANE)
        tiles = [work[pl.ds(base + SUB * i, SUB), here] for i in range(LANE // SUB)]
        tiles, scales = eliminate(tiles, COUNT)
        scale = jnp.concatenate(scales)
        inner = jnp.concatenate(tiles) * scale
        upper = jnp.where(lane_in >= row_in, inner, 0.0)
        lower = jnp.where(lane_in < row_in, inner, jnp.where(lane_in == row_in, scale, 0.0))
        line[...] = jnp.dot(lower, work[here, :], precision=HIGHEST, preferred_element_type=f32)
        whole = line[...]
        factor_ref[here, :] = jnp.where(lane_all >= base, whole, 0.0) * ratio
        factor_ref[here, here] = upper * ratio
        inverse_ref[here, :] = jnp.where(lane_all < base, whole, 0.0)
        inverse_ref[here, here] = lower

        @pl.when(block < cols // LANE - 1)
        def _():
            line[:, here] = lower
            steps = jnp.dot(lower.T, line[...], precision=HIGHEST, preferred_element_type=f32)
            panel = jnp.where(row_all >= base + LANE, work[:, here], 0.0)
            work[:, here] = jnp.where(row_all >= base + LANE, 0.0, work[:, here])
            work[...] -= jnp.dot(panel, steps, precision=HIGHEST, preferred_element_type=f32)

        return 0

    lax.fori_loop(0, cols // LANE, block_step, 0)


def factorize(pieces, place, samp, ratio):
    cols = pieces[0].shape[1]
    total = sum(piece.shape[0] for piece in pieces)
    if samp % (2 * SUB):
        rows = jnp.concatenate(pieces).reshape(total // samp, samp, cols)
        pieces = [jnp.zeros_like(rows).at[place].set(rows).reshape(total, cols)]
        place, samp = jnp.zeros((1,), jnp.int32), total
    vmem = pl.BlockSpec(memory_space=pltpu.VMEM)
    return pl.pallas_call(
        functools.partial(factor_kernel, samp, ratio),
        out_shape=[jax.ShapeDtypeStruct((cols, cols), f32)] * 2,
        in_specs=[pl.BlockSpec(memory_space=pltpu.SMEM)] + [vmem] * len(pieces),
        out_specs=[vmem] * 2,
        scratch_shapes=[
            pltpu.VMEM((total, cols), jnp.bfloat16),
            pltpu.VMEM((cols, cols), f32),
            pltpu.VMEM((LANE, cols), f32),
        ],
        compiler_params=pltpu.CompilerParams(vmem_limit_bytes=32 * 2**20),
        name="factor",
    )(place, *pieces)


def gather_rows(rows):
    wide, narrow = lax.axis_size("wide"), lax.axis_size("narrow")
    rows = jnp.concatenate([rows] + [partner(rows, "narrow", m) for m in range(1, narrow)])
    pieces = [rows] + [partner(rows, "wide", m) for m in range(2, wide, 2)]
    pieces += [partner(piece, "wide", 1) for piece in pieces]
    apart = jnp.concatenate([jnp.arange(0, wide, 2), jnp.arange(1, wide, 2)])
    wide_place = jnp.bitwise_xor(apart, lax.axis_index("wide"))
    narrow_place = jnp.bitwise_xor(jnp.arange(narrow), lax.axis_index("narrow"))
    return pieces, (wide_place[:, None] * narrow + narrow_place[None, :]).reshape(-1)


def sum_everywhere(value):
    wide, narrow = lax.axis_size("wide"), lax.axis_size("narrow")
    wide_index = lax.axis_index("wide")
    core, chip = jnp.bitwise_and(wide_index, 1), jnp.right_shift(wide_index, 1)
    rows, lanes = value.shape
    share = -(-rows // (SUB * wide)) * SUB
    value = jnp.pad(value, ((0, share * wide - rows), (0, 0))).reshape(2, wide // 2, share, lanes)
    value = value[core] + partner(value[1 - core], "wide", 1)
    total = value[chip]
    for m in range(1, wide // 2):
        total = total + partner(value[jnp.bitwise_xor(chip, m)], "wide", 2 * m)
    parts = [total] + [partner(total, "narrow", m) for m in range(1, narrow)]
    while len(parts) > 1:
        parts = [left + right for left, right in zip(parts[0::2], parts[1::2])]
    shares = [parts[0]] + [partner(parts[0], "wide", m) for m in range(2, wide, 2)]
    shares += [partner(piece, "wide", 1) for piece in shares]
    order = jnp.concatenate([jnp.arange(0, wide, 2), jnp.arange(1, wide, 2)])
    source = jnp.bitwise_xor(order, wide_index)
    source = jnp.bitwise_and(source, 1) * (wide // 2) + jnp.right_shift(source, 1)
    return jnp.stack(shares)[source].reshape(wide * share, lanes)[:rows]


def body(covariates, level_codes, sign_bits, sample_rows, effects, noise):
    rows_dev = covariates.shape[0]
    samp = sample_rows.shape[0]
    cols = LEVELS * COV
    wide_cov = covariates.astype(jnp.float32)
    onehot = level_codes[:, None] == jnp.arange(LEVELS, dtype=jnp.int32)[None, :]
    design = (onehot.astype(jnp.bfloat16)[:, :, None] * covariates[:, None, :]).reshape(rows_dev, cols)

    wanted = [sample_rows] + [partner(sample_rows, "wide", m) for m in range(1, 2**MIX_BITS)]

    normal = jnp.dot(design.T, covariates, preferred_element_type=jnp.float32)
    back = jnp.dot((onehot.astype(jnp.float32) * noise[:, None]).T, wide_cov, precision=HIGHEST)
    sums = sum_everywhere(jnp.concatenate([normal, back]))

    want = jnp.concatenate(wanted)
    signs = 1 - 2 * sign_bits
    table = hadamard_rows(jnp.bitwise_and(want, HB - 1), HB)
    table = jnp.tile(table, (1, rows_dev // HB)) * signs[None, :]
    block = jnp.arange(rows_dev, dtype=jnp.int32) // HB
    table = jnp.where((want // HB)[:, None] == block[None, :], table, 0).astype(jnp.bfloat16)
    local = jnp.dot(table, design, preferred_element_type=jnp.float32)
    local = rounded(local * (1.0 / math.sqrt(HB)))
    local = [local[m * samp : (m + 1) * samp] for m in range(2**MIX_BITS)]
    pieces = [local[0]] + [partner(local[m], "wide", m) for m in range(1, 2**MIX_BITS)]
    rows, place = gather_rows(mix(pieces))
    factor, inverse = factorize(rows, place, samp, math.sqrt(LEVELS / SKETCH))

    normal = sums[:cols].reshape(LEVELS, COV, COV)
    back = sums[cols:]

    def normal_times(vector):
        return jnp.einsum("lij,lj->li", normal, vector.reshape(LEVELS, COV), precision=HIGHEST).reshape(cols)

    def precondition(vector):
        steer = jnp.dot(inverse, vector, precision=HIGHEST)
        return jnp.dot(steer, inverse, precision=HIGHEST), jnp.sum(steer * steer)

    gradient = normal_times(effects) + back.reshape(cols)
    step_to, gamma = precondition(gradient)
    solved = jnp.zeros((cols,), jnp.float32)
    for step in range(ITERS):
        image = normal_times(step_to)
        alpha = gamma / jnp.sum(step_to * image)
        solved = solved + alpha * step_to
        if step == ITERS - 1:
            break
        gradient = gradient - alpha * image
        steer, gamma_new = precondition(gradient)
        step_to = steer + gamma_new / gamma * step_to
        gamma = gamma_new
    left = (effects - solved).reshape(LEVELS, COV)
    values = jnp.dot(wide_cov, left.T, precision=HIGHEST)
    resid = noise + jnp.sum(jnp.where(onehot, values, 0.0), axis=1)
    return (solved, resid, factor)


def solution(mesh):
    return jax.shard_map(
        body,
        mesh=mesh,
        in_specs=(
            P(("wide", "narrow"), None),
            P(("wide", "narrow")),
            P(("wide", "narrow")),
            P(("wide", "narrow")),
            P(),
            P(("wide", "narrow")),
        ),
        out_specs=(P(), P(("wide", "narrow")), P()),
        check_vma=False,
    )
```

```python
import functools
import math

import jax
import jax.numpy as jnp
from jax import lax
from jax.experimental import pallas as pl
from jax.experimental.pallas import tpu as pltpu
from jax.sharding import PartitionSpec as P

COV = 128
LEVELS = 4
HB = 256
SKETCH = 1024
ITERS = 4
MIX_BITS = 3

half_root = math.sqrt(0.5)
HIGHEST = lax.Precision.HIGHEST
f32 = jnp.float32
SUB, LANE = 8, 128
COUNT = 4


def swap(value, axis, groups=None):
    return lax.all_to_all(value, axis, 0, 0, axis_index_groups=groups)


def share_all(value, axis, groups=None):
    count = len(groups[0]) if groups else lax.axis_size(axis)
    return swap(jnp.broadcast_to(value, (count,) + value.shape), axis, groups)


def rounded(value):
    return lax.reduce_precision(value, 8, 7).astype(jnp.bfloat16)


def hadamard_rows(rows, size):
    common = jnp.bitwise_and(rows[:, None], jnp.arange(size, dtype=jnp.int32)[None, :])
    for shift in (4, 2, 1):
        common = jnp.bitwise_xor(common, jnp.right_shift(common, shift))
    return 1 - 2 * jnp.bitwise_and(common, 1)


def mix(pieces):
    wide_index = lax.axis_index("wide")
    for place in range(MIX_BITS):
        bit = jnp.bitwise_and(jnp.right_shift(wide_index, place), 1)
        sign = (1 - 2 * bit).astype(jnp.float32)
        pieces = [
            rounded((low.astype(jnp.float32) + sign * high.astype(jnp.float32)) * half_root)
            for low, high in zip(pieces[0::2], pieces[1::2])
        ]
    return pieces[0]


def spread(value):
    return jnp.broadcast_to(value, (SUB, LANE))


def eliminate(tiles, count):
    lane = lax.broadcasted_iota(jnp.int32, (SUB, LANE), 1)
    sub = lax.broadcasted_iota(jnp.int32, (SUB, LANE), 0)
    tiles = list(tiles)
    scales = [None] * len(tiles)
    for first in range(0, LANE, count):
        tile, offset = divmod(first, SUB)
        window = (lane >= first) & (lane < first + count)
        columns = [
            [spread(tiles[i][:, first + k : first + k + 1]) for k in range(count)] for i in range(tile, len(tiles))
        ]
        pivot = [
            [spread(columns[0][m][offset + k : offset + k + 1, :]) if m >= k else None for m in range(count)]
            for k in range(count)
        ]
        rows = []
        for k in range(count):
            row = spread(tiles[tile][offset + k : offset + k + 1, :])
            row = jnp.where(window, 0.0, row)
            rows.append(jnp.where(lane == first + k, 1.0, row))
        inverse, ratio = [], [[None] * count for _ in range(count)]
        for k in range(count):
            inverse.append(1.0 / pivot[k][k])
            for m in range(k + 1, count):
                ratio[k][m] = pivot[k][m] * inverse[k]
                for n in range(m, count):
                    pivot[m][n] = pivot[m][n] - ratio[k][m] * pivot[k][n]
                rows[m] = rows[m] - ratio[k][m] * rows[k]
        steps = [None] * count
        for k in reversed(range(count)):
            steps[k] = rows[k] * inverse[k]
            for m in range(k + 1, count):
                steps[k] = steps[k] - ratio[k][m] * steps[m]
        old = tiles[tile]
        scale = scales[tile]
        for i in range(tile, len(tiles)):
            new = jnp.where(window, 0.0, tiles[i])
            for k in range(count):
                new = new - columns[i - tile][k] * steps[k]
            tiles[i] = new
        fixed = old
        if offset + count < SUB:
            fixed = jnp.where(sub >= offset + count, tiles[tile], old)
        for k in range(count):
            kept = rows[k]
            for m in range(k, count):
                kept = jnp.where(lane == first + m, pivot[k][m], kept)
            root = lax.rsqrt(pivot[k][k])
            fixed = jnp.where(sub == offset + k, kept, fixed)
            scale = root if scale is None else jnp.where(sub == offset + k, root, scale)
        tiles[tile] = fixed
        scales[tile] = scale
    return tiles, scales


def factor_kernel(ratio, sketch_ref, factor_ref, inverse_ref, work, line):
    cols = work.shape[0]
    rows = sketch_ref[...]
    work[...] = lax.dot_general(rows, rows, (((0,), (0,)), ((), ())), preferred_element_type=f32)

    row_in = lax.broadcasted_iota(jnp.int32, (LANE, LANE), 0)
    lane_in = lax.broadcasted_iota(jnp.int32, (LANE, LANE), 1)
    lane_all = lax.broadcasted_iota(jnp.int32, (LANE, cols), 1)
    row_all = lax.broadcasted_iota(jnp.int32, (cols, LANE), 0)

    def block_step(block, _):
        base = pl.multiple_of(block * LANE, LANE)
        here = pl.ds(base, LANE)
        tiles = [work[pl.ds(base + SUB * i, SUB), here] for i in range(LANE // SUB)]
        tiles, scales = eliminate(tiles, COUNT)
        scale = jnp.concatenate(scales)
        inner = jnp.concatenate(tiles) * scale
        upper = jnp.where(lane_in >= row_in, inner, 0.0)
        lower = jnp.where(lane_in < row_in, inner, jnp.where(lane_in == row_in, scale, 0.0))
        line[...] = jnp.dot(lower, work[here, :], precision=HIGHEST, preferred_element_type=f32)
        whole = line[...]
        factor_ref[here, :] = jnp.where(lane_all >= base, whole, 0.0) * ratio
        factor_ref[here, here] = upper * ratio
        inverse_ref[here, :] = jnp.where(lane_all < base, whole, 0.0)
        inverse_ref[here, here] = lower

        @pl.when(block < cols // LANE - 1)
        def _():
            line[:, here] = lower
            steps = jnp.dot(lower.T, line[...], precision=HIGHEST, preferred_element_type=f32)
            panel = jnp.where(row_all >= base + LANE, work[:, here], 0.0)
            work[:, here] = jnp.where(row_all >= base + LANE, 0.0, work[:, here])
            work[...] -= jnp.dot(panel, steps, precision=HIGHEST, preferred_element_type=f32)

        return 0

    lax.fori_loop(0, cols // LANE, block_step, 0)


def factorize(sketch, ratio):
    cols = sketch.shape[1]
    vmem = pl.BlockSpec(memory_space=pltpu.VMEM)
    return pl.pallas_call(
        functools.partial(factor_kernel, ratio),
        out_shape=[jax.ShapeDtypeStruct((cols, cols), f32)] * 2,
        in_specs=[vmem],
        out_specs=[vmem] * 2,
        scratch_shapes=[pltpu.VMEM((cols, cols), f32), pltpu.VMEM((LANE, cols), f32)],
        compiler_params=pltpu.CompilerParams(vmem_limit_bytes=32 * 2**20),
        name="factor",
    )(sketch)


def sum_everywhere(value):
    wide = lax.axis_size("wide")
    rows, lanes = value.shape
    share = -(-rows // (SUB * wide)) * SUB
    value = jnp.pad(value, ((0, share * wide - rows), (0, 0))).reshape(wide, share, lanes)
    value = jnp.sum(swap(value, "wide"), axis=0)
    value = jnp.sum(share_all(value, "narrow"), axis=0)
    return share_all(value, "wide").reshape(wide * share, lanes)[:rows]


def body(covariates, level_codes, sign_bits, sample_rows, effects, noise):
    rows_dev = covariates.shape[0]
    samp = sample_rows.shape[0]
    cols = LEVELS * COV
    wide_cov = covariates.astype(jnp.float32)
    onehot = level_codes[:, None] == jnp.arange(LEVELS, dtype=jnp.int32)[None, :]
    design = (onehot.astype(jnp.bfloat16)[:, :, None] * covariates[:, None, :]).reshape(rows_dev, cols)

    mates = 2**MIX_BITS
    groups = [[first + e for e in range(mates)] for first in range(0, lax.axis_size("wide"), mates)]
    want = share_all(sample_rows, "wide", groups).reshape(-1)

    normal = jnp.dot(design.T, covariates, preferred_element_type=jnp.float32)
    back = jnp.dot((onehot.astype(jnp.float32) * noise[:, None]).T, wide_cov, precision=HIGHEST)
    sums = sum_everywhere(jnp.concatenate([normal, back]))

    signs = 1 - 2 * sign_bits
    table = hadamard_rows(jnp.bitwise_and(want, HB - 1), HB)
    table = jnp.tile(table, (1, rows_dev // HB)) * signs[None, :]
    block = jnp.arange(rows_dev, dtype=jnp.int32) // HB
    table = jnp.where((want // HB)[:, None] == block[None, :], table, 0).astype(jnp.bfloat16)
    local = jnp.dot(table, design, preferred_element_type=jnp.float32)
    local = rounded(local * (1.0 / math.sqrt(HB)))
    sketch = mix(list(swap(local.reshape(mates, samp, cols), "wide", groups)))
    sketch = share_all(share_all(sketch, "narrow"), "wide").reshape(-1, cols)
    factor, inverse = factorize(sketch, math.sqrt(LEVELS / SKETCH))

    normal = sums[:cols].reshape(LEVELS, COV, COV)
    back = sums[cols:]

    def normal_times(vector):
        return jnp.einsum("lij,lj->li", normal, vector.reshape(LEVELS, COV), precision=HIGHEST).reshape(cols)

    def precondition(vector):
        steer = jnp.dot(inverse, vector, precision=HIGHEST)
        return jnp.dot(steer, inverse, precision=HIGHEST), jnp.sum(steer * steer)

    gradient = normal_times(effects) + back.reshape(cols)
    step_to, gamma = precondition(gradient)
    solved = jnp.zeros((cols,), jnp.float32)
    for step in range(ITERS):
        image = normal_times(step_to)
        alpha = gamma / jnp.sum(step_to * image)
        solved = solved + alpha * step_to
        if step == ITERS - 1:
            break
        gradient = gradient - alpha * image
        steer, gamma_new = precondition(gradient)
        step_to = steer + gamma_new / gamma * step_to
        gamma = gamma_new
    left = (effects - solved).reshape(LEVELS, COV)
    values = jnp.dot(wide_cov, left.T, precision=HIGHEST)
    resid = noise + jnp.sum(jnp.where(onehot, values, 0.0), axis=1)
    return (solved, resid, factor)


def solution(mesh):
    return jax.shard_map(
        body,
        mesh=mesh,
        in_specs=(
            P(("wide", "narrow"), None),
            P(("wide", "narrow")),
            P(("wide", "narrow")),
            P(("wide", "narrow")),
            P(),
            P(("wide", "narrow")),
        ),
        out_specs=(P(), P(("wide", "narrow")), P()),
        check_vma=False,
    )
```

```python
import functools
import math

import jax
import jax.numpy as jnp
from jax import lax
from jax.experimental import pallas as pl
from jax.experimental.pallas import tpu as pltpu
from jax.sharding import PartitionSpec as P

COV = 128
LEVELS = 4
HB = 256
SKETCH = 1024
ITERS = 4
MIX_BITS = 3
MATES = 2**MIX_BITS

half_root = math.sqrt(0.5)
HIGHEST = lax.Precision.HIGHEST
f32, bf16 = jnp.float32, jnp.bfloat16
SUB, LANE = 8, 128
PACK = 16
COUNT = 4
NT = (((1,), (1,)), ((), ()))
VMEM = pl.BlockSpec(memory_space=pltpu.VMEM)
SMEM = pl.BlockSpec(memory_space=pltpu.SMEM)


def partner(value, axis, mask):
    pairs = [(source, source ^ mask) for source in range(lax.axis_size(axis))]
    return lax.ppermute(value, axis, pairs)


def whole_up(number, unit):
    return -(-number // unit) * unit


def eye():
    rows = lax.broadcasted_iota(jnp.int32, (LANE, LANE), 0)
    lanes = lax.broadcasted_iota(jnp.int32, (LANE, LANE), 1)
    return rows, lanes, rows == lanes


def to_column(row, same):
    return jnp.sum(jnp.where(same, row, 0.0), axis=1, keepdims=True)


def to_row(column, same):
    return jnp.sum(jnp.where(same, column, 0.0), axis=0, keepdims=True)


def split(value):
    parts = []
    for _ in range(3):
        parts.append(value.astype(bf16))
        value = value - parts[-1].astype(f32)
    return parts


def tree_sum(values):
    while len(values) > 1:
        values = [left + right for left, right in zip(values[0::2], values[1::2])]
    return values[0]


def put_sums(ref, start, share, extra):
    rows = share.shape[0]
    for k, part in enumerate(split(share)):
        ref[start : start + rows, k * LANE : (k + 1) * LANE] = part
    tail = jnp.zeros((rows - 3 * SUB, LANE), bf16)
    ref[start : start + rows, 3 * LANE :] = jnp.concatenate(split(extra) + [tail])


def take_sums(ref, start, rows):
    block = ref[start : start + rows, :].astype(f32)
    share = block[:, :LANE] + block[:, LANE : 2 * LANE] + block[:, 2 * LANE : 3 * LANE]
    tail = block[:, 3 * LANE :]
    return share, tail[:SUB] + tail[SUB : 2 * SUB] + tail[2 * SUB : 3 * SUB]


def local_kernel(samp, share, index_ref, want_ref, cov_ref, codes_ref, signs_ref, noise_ref, *refs):
    out_refs, (design, table, packed) = refs[:-3], refs[-3:]
    chunks = codes_ref.shape[0]
    rows, lanes, same = eye()
    zero = jnp.zeros((LANE, LANE), f32)

    masks, halves = [], []
    for c in range(want_ref.shape[0]):
        want = to_column(want_ref[c : c + 1, :].astype(f32), same).astype(jnp.int32)
        masks.append(jnp.right_shift(want, HB.bit_length() - 1))
        line = []
        for h in range(HB // LANE):
            common = jnp.bitwise_and(want, lanes + h * LANE)
            for shift in (4, 2, 1):
                common = jnp.bitwise_xor(common, jnp.right_shift(common, shift))
            line.append((1 - 2 * jnp.bitwise_and(common, 1)).astype(f32))
        halves.append(line)

    for r in range(chunks):
        here = slice(r * LANE, (r + 1) * LANE)
        code = codes_ref[r : r + 1, :]
        turned = cov_ref[here, :].astype(f32).T
        for level in range(LEVELS):
            design[level * LANE : (level + 1) * LANE, here] = jnp.where(code == level, turned, zero).astype(bf16)
        noise = jnp.concatenate([noise_ref[r : r + 1, :]] * LEVELS + [jnp.zeros((PACK - LEVELS, LANE), f32)])
        level = lax.broadcasted_iota(jnp.int32, (PACK, LANE), 0)
        noise = jnp.where(code == level, noise, 0.0)
        for k, part in enumerate(split(noise)):
            design[LEVELS * LANE + k * PACK : LEVELS * LANE + (k + 1) * PACK, here] = part
        sign = (1 - 2 * signs_ref[r : r + 1, :]).astype(f32)
        block, h = divmod(r * LANE, HB)
        for c, (mask, line) in enumerate(zip(masks, halves)):
            value = jnp.where(mask == block, line[h // LANE] * sign, zero)
            table[c * LANE : (c + 1) * LANE, here] = value.astype(bf16)

    sums = jnp.dot(design[...], cov_ref[...], preferred_element_type=f32)
    normal = [sums[level * LANE : (level + 1) * LANE] for level in range(LEVELS)]
    back = sums[LEVELS * LANE :]
    back = back[:SUB] + back[PACK : PACK + SUB] + back[2 * PACK : 2 * PACK + SUB]
    extra = [jnp.sum(jnp.where(same, normal[level], 0.0), axis=0, keepdims=True) for level in (1, 3)]
    extra = jnp.concatenate([back[:LEVELS]] + extra + [jnp.zeros((2, LANE), f32)])
    for pair in range(LEVELS // 2):
        packed[pair * LANE : (pair + 1) * LANE, :] = jnp.where(rows >= lanes, normal[2 * pair], normal[2 * pair + 1])
    if packed.shape[0] > 2 * LANE:
        packed[2 * LANE :, :] = jnp.zeros((packed.shape[0] - 2 * LANE, LANE), f32)

    local = lax.dot_general(table[...], design[: LEVELS * LANE, :], NT, preferred_element_type=f32)
    local = (local * (1.0 / math.sqrt(HB))).astype(bf16)
    for m, out_ref in enumerate(out_refs):
        start = 0
        if m < MATES:
            out_ref[:samp, :] = local[m * samp : (m + 1) * samp]
            start = samp
        at = pl.multiple_of(jnp.bitwise_xor(index_ref[0], m) * share, share)
        put_sums(out_ref, start, packed[pl.ds(at, share), :], extra)


def mix_kernel(samp, share, index_ref, *refs):
    piece_refs, out_ref = refs[:-1], refs[-1]
    pieces = [ref[:samp, :].astype(f32) for ref in piece_refs[:MATES]]
    for place in range(MIX_BITS):
        bit = jnp.bitwise_and(jnp.right_shift(index_ref[0], place), 1)
        sign = (1 - 2 * bit).astype(f32)
        pieces = [
            ((sign * own + other) * half_root).astype(bf16).astype(f32)
            for own, other in zip(pieces[0::2], pieces[1::2])
        ]
    out_ref[:samp, :] = pieces[0].astype(bf16)
    sums = [take_sums(ref, samp if m < MATES else 0, share) for m, ref in enumerate(piece_refs)]
    put_sums(out_ref, samp, tree_sum([one for one, _ in sums]), tree_sum([one for _, one in sums]))


def stack_kernel(samp, share, index_ref, *refs):
    piece_refs, out_ref = refs[:-1], refs[-1]
    for m, ref in enumerate(piece_refs):
        at = pl.multiple_of(jnp.bitwise_xor(index_ref[1], m) * samp, samp)
        out_ref[pl.ds(at, samp), :] = ref[:samp, :]
    sums = [take_sums(ref, samp, share) for ref in piece_refs]
    put_sums(
        out_ref, samp * len(piece_refs), tree_sum([one for one, _ in sums]), tree_sum([one for _, one in sums])
    )


def spread(value):
    return jnp.broadcast_to(value, (SUB, LANE))


def eliminate(tiles, count):
    lane = lax.broadcasted_iota(jnp.int32, (SUB, LANE), 1)
    sub = lax.broadcasted_iota(jnp.int32, (SUB, LANE), 0)
    tiles = list(tiles)
    scales = [None] * len(tiles)
    for first in range(0, LANE, count):
        tile, offset = divmod(first, SUB)
        window = (lane >= first) & (lane < first + count)
        columns = [
            [spread(tiles[i][:, first + k : first + k + 1]) for k in range(count)] for i in range(tile, len(tiles))
        ]
        pivot = [
            [spread(columns[0][m][offset + k : offset + k + 1, :]) if m >= k else None for m in range(count)]
            for k in range(count)
        ]
        rows = []
        for k in range(count):
            row = spread(tiles[tile][offset + k : offset + k + 1, :])
            row = jnp.where(window, 0.0, row)
            rows.append(jnp.where(lane == first + k, 1.0, row))
        inverse, ratio = [], [[None] * count for _ in range(count)]
        for k in range(count):
            inverse.append(1.0 / pivot[k][k])
            for m in range(k + 1, count):
                ratio[k][m] = pivot[k][m] * inverse[k]
                for n in range(m, count):
                    pivot[m][n] = pivot[m][n] - ratio[k][m] * pivot[k][n]
                rows[m] = rows[m] - ratio[k][m] * rows[k]
        steps = [None] * count
        for k in reversed(range(count)):
            steps[k] = rows[k] * inverse[k]
            for m in range(k + 1, count):
                steps[k] = steps[k] - ratio[k][m] * steps[m]
        old = tiles[tile]
        scale = scales[tile]
        for i in range(tile, len(tiles)):
            new = jnp.where(window, 0.0, tiles[i])
            for k in range(count):
                new = new - columns[i - tile][k] * steps[k]
            tiles[i] = new
        fixed = old
        if offset + count < SUB:
            fixed = jnp.where(sub >= offset + count, tiles[tile], old)
        for k in range(count):
            kept = rows[k]
            for m in range(k, count):
                kept = jnp.where(lane == first + m, pivot[k][m], kept)
            root = lax.rsqrt(pivot[k][k])
            fixed = jnp.where(sub == offset + k, kept, fixed)
            scale = root if scale is None else jnp.where(sub == offset + k, root, scale)
        tiles[tile] = fixed
        scales[tile] = scale
    return tiles, scales


def factor_kernel(ratio, apart, rows_in, index_ref, *refs):
    piece_refs, (factor_ref, inverse_ref, sketch, work, line) = refs[:-5], refs[-5:]
    cols = work.shape[0]
    for mask, ref in zip(apart, piece_refs):
        at = pl.multiple_of(jnp.bitwise_xor(index_ref[0], mask) * rows_in, rows_in)
        sketch[pl.ds(at, rows_in), :] = ref[:rows_in, :]
    rows = sketch[...]
    work[...] = lax.dot_general(rows, rows, (((0,), (0,)), ((), ())), preferred_element_type=f32)

    row_in = lax.broadcasted_iota(jnp.int32, (LANE, LANE), 0)
    lane_in = lax.broadcasted_iota(jnp.int32, (LANE, LANE), 1)
    lane_all = lax.broadcasted_iota(jnp.int32, (LANE, cols), 1)
    row_all = lax.broadcasted_iota(jnp.int32, (cols, LANE), 0)

    def block_step(block, _):
        base = pl.multiple_of(block * LANE, LANE)
        here = pl.ds(base, LANE)
        tiles = [work[pl.ds(base + SUB * i, SUB), here] for i in range(LANE // SUB)]
        tiles, scales = eliminate(tiles, COUNT)
        scale = jnp.concatenate(scales)
        inner = jnp.concatenate(tiles) * scale
        upper = jnp.where(lane_in >= row_in, inner, 0.0)
        lower = jnp.where(lane_in < row_in, inner, jnp.where(lane_in == row_in, scale, 0.0))
        line[...] = jnp.dot(lower, work[here, :], precision=HIGHEST, preferred_element_type=f32)
        whole = line[...]
        factor_ref[here, :] = jnp.where(lane_all >= base, whole, 0.0) * ratio
        factor_ref[here, here] = upper * ratio
        inverse_ref[here, :] = jnp.where(lane_all < base, whole, 0.0)
        inverse_ref[here, here] = lower

        @pl.when(block < cols // LANE - 1)
        def _():
            line[:, here] = lower
            steps = jnp.dot(lower.T, line[...], precision=HIGHEST, preferred_element_type=f32)
            panel = jnp.where(row_all >= base + LANE, work[:, here], 0.0)
            work[:, here] = jnp.where(row_all >= base + LANE, 0.0, work[:, here])
            work[...] -= jnp.dot(panel, steps, precision=HIGHEST, preferred_element_type=f32)

        return 0

    lax.fori_loop(0, cols // LANE, block_step, 0)


def solve_kernel(apart, rows_in, share, index_ref, inverse_ref, effects_ref, cov_ref, codes_ref, noise_ref, *refs):
    piece_refs, (solved_ref, resid_ref, packed, kernel) = refs[:-4], refs[-4:]
    rows, lanes, same = eye()
    extra = None
    for mask, ref in zip(apart, piece_refs):
        at = pl.multiple_of(jnp.bitwise_xor(index_ref[0], mask) * share, share)
        packed[pl.ds(at, share), :], more = take_sums(ref, rows_in, share)
        extra = more if extra is None else extra
    normal = []
    for pair in range(LEVELS // 2):
        both = packed[pair * LANE : (pair + 1) * LANE, :]
        turned = both.T
        normal.append(jnp.where(rows >= lanes, both, turned))
        diagonal = jnp.where(same, extra[LEVELS + pair : LEVELS + pair + 1], turned)
        normal.append(jnp.where(rows < lanes, both, diagonal))

    inverse = inverse_ref[...]
    for level in range(LEVELS):
        here = slice(level * LANE, (level + 1) * LANE)
        kernel[:, here] = jnp.dot(inverse[:, here], normal[level], precision=HIGHEST, preferred_element_type=f32)
    kernel[...] = lax.dot_general(kernel[...], inverse, NT, precision=HIGHEST, preferred_element_type=f32)
    square = kernel[...]

    gradient = []
    for level in range(LEVELS):
        column = to_column(effects_ref[level : level + 1, :], same)
        gradient.append(jnp.sum(normal[level] * column, axis=0, keepdims=True) + extra[level : level + 1])
    gradient = jnp.concatenate(gradient, axis=1)
    steer_col = jnp.sum(inverse * gradient, axis=1, keepdims=True)
    steer_row = jnp.concatenate(
        [to_row(steer_col[level * LANE : (level + 1) * LANE], same) for level in range(LEVELS)], axis=1
    )
    go_row, go_col = steer_row, steer_col
    gamma = jnp.sum(steer_row * steer_row, axis=1, keepdims=True)
    solved_col = jnp.zeros_like(steer_col)
    for step in range(ITERS):
        image_row = jnp.sum(square * go_col, axis=0, keepdims=True)
        alpha = gamma / jnp.sum(go_row * image_row, axis=1, keepdims=True)
        solved_col = solved_col + alpha * go_col
        if step == ITERS - 1:
            break
        image_col = jnp.sum(square * go_row, axis=1, keepdims=True)
        steer_row = steer_row - alpha * image_row
        steer_col = steer_col - alpha * image_col
        gamma_new = jnp.sum(steer_row * steer_row, axis=1, keepdims=True)
        go_row = steer_row + gamma_new / gamma * go_row
        go_col = steer_col + gamma_new / gamma * go_col
        gamma = gamma_new
    solved = jnp.sum(inverse * solved_col, axis=0, keepdims=True)
    solved = jnp.concatenate([solved[:, level * LANE : (level + 1) * LANE] for level in range(LEVELS)])
    solved_ref[...] = solved

    left = jnp.concatenate([effects_ref[...] - solved, jnp.zeros((PACK - LEVELS, LANE), f32)])
    values = jnp.zeros((SUB, cov_ref.shape[0]), f32)
    for part in split(left):
        values = values + lax.dot_general(part, cov_ref[...], NT, preferred_element_type=f32)[:SUB]
    for r in range(codes_ref.shape[0]):
        code = codes_ref[r : r + 1, :]
        total = noise_ref[r : r + 1, :]
        for level in range(LEVELS):
            total = total + jnp.where(code == level, values[level : level + 1, r * LANE : (r + 1) * LANE], 0.0)
        resid_ref[r : r + 1, :] = total


def call(kernel, name, outs, scratch, index, *operands):
    return pl.pallas_call(
        kernel,
        out_shape=[jax.ShapeDtypeStruct(shape, dtype) for shape, dtype in outs],
        in_specs=[SMEM] + [VMEM] * len(operands),
        out_specs=[VMEM] * len(outs),
        scratch_shapes=[pltpu.VMEM(shape, dtype) for shape, dtype in scratch],
        compiler_params=pltpu.CompilerParams(vmem_limit_bytes=40 * 2**20),
        name=name,
    )(index, *operands)


def body(covariates, level_codes, sign_bits, sample_rows, effects, noise):
    wide, narrow = lax.axis_size("wide"), lax.axis_size("narrow")
    index = jnp.stack([lax.axis_index("wide"), lax.axis_index("narrow")]).astype(jnp.int32)
    rows_dev, cols = covariates.shape[0], LEVELS * COV
    samp = whole_up(sample_rows.shape[0], PACK)
    share = whole_up(max(2 * LANE // wide, 3 * SUB), PACK)
    sample_rows = jnp.pad(sample_rows, (0, samp - sample_rows.shape[0]), constant_values=-1)
    codes, signs, noise = [array.reshape(-1, LANE) for array in (level_codes, sign_bits, noise)]
    effects = effects.reshape(LEVELS, COV)

    want = jnp.concatenate([sample_rows] + [partner(sample_rows, "wide", m) for m in range(1, MATES)])
    pieces = call(
        functools.partial(local_kernel, samp, share),
        "local",
        [((samp * (m < MATES) + share, cols), bf16) for m in range(wide)],
        [
            ((cols + 3 * PACK, rows_dev), bf16),
            ((MATES * samp, rows_dev), bf16),
            ((share * wide, LANE), f32),
        ],
        index,
        want.reshape(-1, LANE),
        covariates,
        codes,
        signs,
        noise,
    )
    pieces = [pieces[0]] + [partner(pieces[m], "wide", m) for m in range(1, wide)]
    (piece,) = call(
        functools.partial(mix_kernel, samp, share), "mix", [((samp + share, cols), bf16)], [], index, *pieces
    )
    pieces = [piece] + [partner(piece, "narrow", m) for m in range(1, narrow)]
    rows_in = samp * narrow
    (piece,) = call(
        functools.partial(stack_kernel, samp, share), "stack", [((rows_in + share, cols), bf16)], [], index, *pieces
    )
    pieces = [piece] + [partner(piece, "wide", m) for m in range(2, wide, 2)]
    pieces += [partner(piece, "wide", 1) for piece in pieces]
    apart = [2 * m + core for core in range(2) for m in range(wide // 2)]
    factor, inverse = call(
        functools.partial(factor_kernel, math.sqrt(LEVELS / SKETCH), apart, rows_in),
        "factor",
        [((cols, cols), f32)] * 2,
        [((rows_in * wide, cols), bf16), ((cols, cols), f32), ((LANE, cols), f32)],
        index,
        *pieces,
    )
    solved, resid = call(
        functools.partial(solve_kernel, apart, rows_in, share),
        "solve",
        [((LEVELS, COV), f32), (codes.shape, f32)],
        [((share * wide, LANE), f32), ((cols, cols), f32)],
        index,
        inverse,
        effects,
        covariates,
        codes,
        noise,
        *pieces,
    )
    return solved.reshape(-1), resid.reshape(-1), factor


def solution(mesh):
    return jax.shard_map(
        body,
        mesh=mesh,
        in_specs=(
            P(("wide", "narrow"), None),
            P(("wide", "narrow")),
            P(("wide", "narrow")),
            P(("wide", "narrow")),
            P(),
            P(("wide", "narrow")),
        ),
        out_specs=(P(), P(("wide", "narrow")), P()),
        check_vma=False,
    )
```

```python
import functools
import math

import jax
import jax.numpy as jnp
from jax import lax
from jax.experimental import pallas as pl
from jax.experimental.pallas import tpu as pltpu
from jax.sharding import PartitionSpec as P

COV = 128
LEVELS = 4
HB = 256
SKETCH = 1024
ITERS = 4
MIX_BITS = 3
MATES = 2**MIX_BITS

half_root = math.sqrt(0.5)
HIGHEST = lax.Precision.HIGHEST
f32, bf16 = jnp.float32, jnp.bfloat16
SUB, LANE = 8, 128
PACK = 16
NT = (((1,), (1,)), ((), ()))
VMEM = pl.BlockSpec(memory_space=pltpu.VMEM)
SMEM = pl.BlockSpec(memory_space=pltpu.SMEM)


def partner(value, axis, mask):
    pairs = [(source, source ^ mask) for source in range(lax.axis_size(axis))]
    return lax.ppermute(value, axis, pairs)


def whole_up(number, unit):
    return -(-number // unit) * unit


def eye():
    rows = lax.broadcasted_iota(jnp.int32, (LANE, LANE), 0)
    lanes = lax.broadcasted_iota(jnp.int32, (LANE, LANE), 1)
    return rows, lanes, rows == lanes


def to_column(row, same):
    return jnp.sum(jnp.where(same, row, 0.0), axis=1, keepdims=True)


def to_row(column, same):
    return jnp.sum(jnp.where(same, column, 0.0), axis=0, keepdims=True)


def split(value):
    parts = []
    for _ in range(3):
        parts.append(value.astype(bf16))
        value = value - parts[-1].astype(f32)
    return parts


def tree_sum(values):
    while len(values) > 1:
        values = [left + right for left, right in zip(values[0::2], values[1::2])]
    return values[0]


def put_sums(ref, start, share, extra):
    rows = share.shape[0]
    for k, part in enumerate(split(share)):
        ref[start : start + rows, k * LANE : (k + 1) * LANE] = part
    tail = jnp.zeros((rows - 3 * SUB, LANE), bf16)
    ref[start : start + rows, 3 * LANE :] = jnp.concatenate(split(extra) + [tail])


def take_sums(ref, start, rows):
    block = ref[start : start + rows, :].astype(f32)
    share = block[:, :LANE] + block[:, LANE : 2 * LANE] + block[:, 2 * LANE : 3 * LANE]
    tail = block[:, 3 * LANE :]
    return share, tail[:SUB] + tail[SUB : 2 * SUB] + tail[2 * SUB : 3 * SUB]


def local_kernel(samp, share, index_ref, want_ref, cov_ref, codes_ref, signs_ref, noise_ref, *refs):
    out_refs, (design, table, packed) = refs[:-3], refs[-3:]
    chunks = codes_ref.shape[0]
    rows, lanes, same = eye()
    zero = jnp.zeros((LANE, LANE), f32)

    masks, halves = [], []
    for c in range(want_ref.shape[0]):
        want = to_column(want_ref[c : c + 1, :].astype(f32), same).astype(jnp.int32)
        masks.append(jnp.right_shift(want, HB.bit_length() - 1))
        line = []
        for h in range(HB // LANE):
            common = jnp.bitwise_and(want, lanes + h * LANE)
            for shift in (4, 2, 1):
                common = jnp.bitwise_xor(common, jnp.right_shift(common, shift))
            line.append((1 - 2 * jnp.bitwise_and(common, 1)).astype(f32))
        halves.append(line)

    for r in range(chunks):
        here = slice(r * LANE, (r + 1) * LANE)
        code = codes_ref[r : r + 1, :]
        turned = cov_ref[here, :].astype(f32).T
        for level in range(LEVELS):
            design[level * LANE : (level + 1) * LANE, here] = jnp.where(code == level, turned, zero).astype(bf16)
        noise = jnp.concatenate([noise_ref[r : r + 1, :]] * LEVELS + [jnp.zeros((PACK - LEVELS, LANE), f32)])
        level = lax.broadcasted_iota(jnp.int32, (PACK, LANE), 0)
        noise = jnp.where(code == level, noise, 0.0)
        for k, part in enumerate(split(noise)):
            design[LEVELS * LANE + k * PACK : LEVELS * LANE + (k + 1) * PACK, here] = part
        sign = (1 - 2 * signs_ref[r : r + 1, :]).astype(f32)
        block, h = divmod(r * LANE, HB)
        for c, (mask, line) in enumerate(zip(masks, halves)):
            value = jnp.where(mask == block, line[h // LANE] * sign, zero)
            table[c * LANE : (c + 1) * LANE, here] = value.astype(bf16)

    sums = jnp.dot(design[...], cov_ref[...], preferred_element_type=f32)
    normal = [sums[level * LANE : (level + 1) * LANE] for level in range(LEVELS)]
    back = sums[LEVELS * LANE :]
    back = back[:SUB] + back[PACK : PACK + SUB] + back[2 * PACK : 2 * PACK + SUB]
    extra = [jnp.sum(jnp.where(same, normal[level], 0.0), axis=0, keepdims=True) for level in (1, 3)]
    extra = jnp.concatenate([back[:LEVELS]] + extra + [jnp.zeros((2, LANE), f32)])
    for pair in range(LEVELS // 2):
        packed[pair * LANE : (pair + 1) * LANE, :] = jnp.where(rows >= lanes, normal[2 * pair], normal[2 * pair + 1])
    if packed.shape[0] > 2 * LANE:
        packed[2 * LANE :, :] = jnp.zeros((packed.shape[0] - 2 * LANE, LANE), f32)

    local = lax.dot_general(table[...], design[: LEVELS * LANE, :], NT, preferred_element_type=f32)
    local = (local * (1.0 / math.sqrt(HB))).astype(bf16)
    for m, out_ref in enumerate(out_refs):
        start = 0
        if m < MATES:
            out_ref[:samp, :] = local[m * samp : (m + 1) * samp]
            start = samp
        at = pl.multiple_of(jnp.bitwise_xor(index_ref[0], m) * share, share)
        put_sums(out_ref, start, packed[pl.ds(at, share), :], extra)


def mix_kernel(samp, share, index_ref, *refs):
    piece_refs, out_ref = refs[:-1], refs[-1]
    pieces = [ref[:samp, :].astype(f32) for ref in piece_refs[:MATES]]
    for place in range(MIX_BITS):
        bit = jnp.bitwise_and(jnp.right_shift(index_ref[0], place), 1)
        sign = (1 - 2 * bit).astype(f32)
        pieces = [
            ((sign * own + other) * half_root).astype(bf16).astype(f32)
            for own, other in zip(pieces[0::2], pieces[1::2])
        ]
    out_ref[:samp, :] = pieces[0].astype(bf16)
    sums = [take_sums(ref, samp if m < MATES else 0, share) for m, ref in enumerate(piece_refs)]
    put_sums(out_ref, samp, tree_sum([one for one, _ in sums]), tree_sum([one for _, one in sums]))


def stack_kernel(samp, share, index_ref, *refs):
    piece_refs, out_ref = refs[:-1], refs[-1]
    for m, ref in enumerate(piece_refs):
        at = pl.multiple_of(jnp.bitwise_xor(index_ref[1], m) * samp, samp)
        out_ref[pl.ds(at, samp), :] = ref[:samp, :]
    sums = [take_sums(ref, samp, share) for ref in piece_refs]
    put_sums(
        out_ref, samp * len(piece_refs), tree_sum([one for one, _ in sums]), tree_sum([one for _, one in sums])
    )


def spread(value):
    return jnp.broadcast_to(value, (SUB, LANE))


def reciprocal(value):
    rough = pl.reciprocal(value, approx=True)
    rough = rough * (2.0 - value * rough)
    return rough * (2.0 - value * rough)


def eliminate(tiles):
    lane = lax.broadcasted_iota(jnp.int32, (SUB, LANE), 1)
    sub = lax.broadcasted_iota(jnp.int32, (SUB, LANE), 0)
    tiles = list(tiles)
    scales = []
    for tile in range(len(tiles)):
        first = tile * SUB
        window = (lane >= first) & (lane < first + SUB)
        marks = [lane == first + k for k in range(SUB)]
        old = tiles[tile]
        columns = [spread(old[:, first + k : first + k + 1]) for k in range(SUB)]
        pivot = [[spread(columns[m][k : k + 1, :]) if m >= k else None for m in range(SUB)] for k in range(SUB)]
        cleared = jnp.where(window, 0.0, old)
        rows = [jnp.where(marks[k], 1.0, spread(cleared[k : k + 1, :])) for k in range(SUB)]
        steps, near, far = [None] * SUB, {}, {}
        kept, scale = [None] * SUB, None
        for k in range(0, SUB, 2):
            low, cross, high = pivot[k][k], pivot[k][k + 1], pivot[k + 1][k + 1]
            area = low * high - cross * cross
            over = reciprocal(area)
            rest = range(k + 2, SUB)
            for m in rest:
                near[k, m] = high * pivot[k][m] - cross * pivot[k + 1][m]
                far[k, m] = low * pivot[k + 1][m] - cross * pivot[k][m]
            for m in rest:
                for n in range(m, SUB):
                    pivot[m][n] = pivot[m][n] - over * (pivot[k][m] * near[k, n] + pivot[k + 1][m] * far[k, n])
            for m in rest:
                near[k, m] = over * near[k, m]
                far[k, m] = over * far[k, m]
                rows[m] = rows[m] - (near[k, m] * rows[k] + far[k, m] * rows[k + 1])
            steps[k] = over * (high * rows[k] - cross * rows[k + 1])
            steps[k + 1] = over * (low * rows[k + 1] - cross * rows[k])
            inner = reciprocal(low)
            ratio = cross * inner
            kept[k] = rows[k]
            kept[k + 1] = rows[k + 1] - ratio * rows[k]
            for m in range(k, SUB):
                kept[k] = jnp.where(marks[m], pivot[k][m], kept[k])
            last = area * inner
            kept[k + 1] = jnp.where(marks[k + 1], last, kept[k + 1])
            for m in rest:
                kept[k + 1] = jnp.where(marks[m], pivot[k + 1][m] - ratio * pivot[k][m], kept[k + 1])
            roots = lax.rsqrt(low), lax.rsqrt(last)
            scale = roots[0] if scale is None else jnp.where(sub >= k, roots[0], scale)
            scale = jnp.where(sub >= k + 1, roots[1], scale)
        for k in reversed(range(0, SUB, 2)):
            for m in range(k + 2, SUB):
                steps[k] = steps[k] - near[k, m] * steps[m]
                steps[k + 1] = steps[k + 1] - far[k, m] * steps[m]
        for i in range(tile + 1, len(tiles)):
            change = [spread(tiles[i][:, first + k : first + k + 1]) * steps[k] for k in range(SUB)]
            tiles[i] = jnp.where(window, 0.0, tiles[i]) - tree_sum(change)
        new = kept[0]
        for k in range(1, SUB):
            new = jnp.where(sub >= k, kept[k], new)
        tiles[tile] = new
        scales.append(scale)
    return tiles, scales


def factor_kernel(ratio, apart, rows_in, index_ref, *refs):
    piece_refs, (factor_ref, inverse_ref, sketch, work, line) = refs[:-5], refs[-5:]
    cols = work.shape[0]
    for mask, ref in zip(apart, piece_refs):
        at = pl.multiple_of(jnp.bitwise_xor(index_ref[0], mask) * rows_in, rows_in)
        sketch[pl.ds(at, rows_in), :] = ref[:rows_in, :]
    rows = sketch[...]
    gram = lax.dot_general(rows, rows, (((0,), (0,)), ((), ())), preferred_element_type=f32)
    work[...] = gram
    _, _, same = eye()
    diagonal = []
    for at in range(0, cols, LANE):
        block = work[at : at + LANE, at : at + LANE]
        diagonal.append(jnp.sum(jnp.where(same, block, 0.0), axis=0, keepdims=True))
    unit = [lax.rsqrt(part) for part in diagonal]
    level = jnp.concatenate([part * one for part, one in zip(diagonal, unit)], axis=1) * ratio
    unit_row = jnp.concatenate(unit, axis=1)
    for at, one in zip(range(0, cols, LANE), unit):
        work[at : at + LANE, :] = work[at : at + LANE, :] * to_column(one, same) * unit_row

    row_in = lax.broadcasted_iota(jnp.int32, (LANE, LANE), 0)
    lane_in = lax.broadcasted_iota(jnp.int32, (LANE, LANE), 1)
    lane_all = lax.broadcasted_iota(jnp.int32, (LANE, cols), 1)
    row_all = lax.broadcasted_iota(jnp.int32, (cols, LANE), 0)

    def block_step(block, _):
        base = pl.multiple_of(block * LANE, LANE)
        here = pl.ds(base, LANE)
        tiles = [work[pl.ds(base + SUB * i, SUB), here] for i in range(LANE // SUB)]
        tiles, scales = eliminate(tiles)
        scale = jnp.concatenate(scales)
        inner = jnp.concatenate(tiles) * scale
        upper = jnp.where(lane_in >= row_in, inner, 0.0)
        lower = jnp.where(lane_in < row_in, inner, jnp.where(lane_in == row_in, scale, 0.0))
        line[...] = jnp.dot(lower, work[here, :], precision=HIGHEST, preferred_element_type=f32)
        line[:, here] = upper
        factor_ref[here, :] = jnp.where(lane_all >= base, line[...], 0.0) * level
        line[:, here] = lower
        inverse_ref[here, :] = jnp.where(lane_all < base + LANE, line[...], 0.0) * unit_row

        @pl.when(block < cols // LANE - 1)
        def _():
            steps = jnp.dot(lower.T, line[...], precision=HIGHEST, preferred_element_type=f32)
            panel = jnp.where(row_all >= base + LANE, work[:, here], 0.0)
            work[:, here] = jnp.where(row_all >= base + LANE, 0.0, work[:, here])
            work[...] -= jnp.dot(panel, steps, precision=HIGHEST, preferred_element_type=f32)

        return 0

    lax.fori_loop(0, cols // LANE, block_step, 0)


def solve_kernel(apart, rows_in, share, index_ref, inverse_ref, effects_ref, cov_ref, codes_ref, noise_ref, *refs):
    piece_refs, (solved_ref, resid_ref, packed) = refs[:-3], refs[-3:]
    rows, lanes, same = eye()
    extra = None
    for mask, ref in zip(apart, piece_refs):
        at = pl.multiple_of(jnp.bitwise_xor(index_ref[0], mask) * share, share)
        packed[pl.ds(at, share), :], more = take_sums(ref, rows_in, share)
        extra = more if extra is None else extra
    normal = []
    for pair in range(LEVELS // 2):
        both = packed[pair * LANE : (pair + 1) * LANE, :]
        turned = both.T
        normal.append(jnp.where(rows >= lanes, both, turned))
        diagonal = jnp.where(same, extra[LEVELS + pair : LEVELS + pair + 1], turned)
        normal.append(jnp.where(rows < lanes, both, diagonal))

    inverse = inverse_ref[...]
    spans = [slice(level * LANE, (level + 1) * LANE) for level in range(LEVELS)]
    gradient = []
    for level in range(LEVELS):
        column = to_column(effects_ref[level : level + 1, :], same)
        gradient.append(jnp.sum(normal[level] * column, axis=0, keepdims=True) + extra[level : level + 1])
    steer = jnp.sum(inverse * jnp.concatenate(gradient, axis=1), axis=1, keepdims=True)
    direction = steer
    gamma = jnp.sum(steer * steer, axis=0, keepdims=True)
    solved = jnp.zeros((1, cov_ref.shape[1] * LEVELS), f32)
    for step in range(ITERS):
        move = jnp.sum(inverse * direction, axis=0, keepdims=True)
        image = []
        for level, span in enumerate(spans):
            image.append(jnp.sum(normal[level] * to_column(move[:, span], same), axis=0, keepdims=True))
        image = jnp.concatenate(image, axis=1)
        alpha = gamma / jnp.sum(move * image, axis=1, keepdims=True)
        solved = solved + alpha * move
        if step == ITERS - 1:
            break
        steer = steer - alpha * jnp.sum(inverse * image, axis=1, keepdims=True)
        gamma_new = jnp.sum(steer * steer, axis=0, keepdims=True)
        direction = steer + gamma_new / gamma * direction
        gamma = gamma_new
    solved = jnp.concatenate([solved[:, span] for span in spans])
    solved_ref[...] = solved

    left = jnp.concatenate([effects_ref[...] - solved, jnp.zeros((PACK - LEVELS, LANE), f32)])
    values = jnp.zeros((SUB, cov_ref.shape[0]), f32)
    for part in split(left):
        values = values + lax.dot_general(part, cov_ref[...], NT, preferred_element_type=f32)[:SUB]
    for r in range(codes_ref.shape[0]):
        code = codes_ref[r : r + 1, :]
        total = noise_ref[r : r + 1, :]
        for level in range(LEVELS):
            total = total + jnp.where(code == level, values[level : level + 1, r * LANE : (r + 1) * LANE], 0.0)
        resid_ref[r : r + 1, :] = total


def call(kernel, name, outs, scratch, index, *operands):
    return pl.pallas_call(
        kernel,
        out_shape=[jax.ShapeDtypeStruct(shape, dtype) for shape, dtype in outs],
        in_specs=[SMEM] + [VMEM] * len(operands),
        out_specs=[VMEM] * len(outs),
        scratch_shapes=[pltpu.VMEM(shape, dtype) for shape, dtype in scratch],
        compiler_params=pltpu.CompilerParams(vmem_limit_bytes=40 * 2**20),
        name=name,
    )(index, *operands)


def body(covariates, level_codes, sign_bits, sample_rows, effects, noise):
    wide, narrow = lax.axis_size("wide"), lax.axis_size("narrow")
    index = jnp.stack([lax.axis_index("wide"), lax.axis_index("narrow")]).astype(jnp.int32)
    rows_dev, cols = covariates.shape[0], LEVELS * COV
    samp = whole_up(sample_rows.shape[0], PACK)
    share = whole_up(max(2 * LANE // wide, 3 * SUB), PACK)
    sample_rows = jnp.pad(sample_rows, (0, samp - sample_rows.shape[0]), constant_values=-1)
    codes, signs, noise = [array.reshape(-1, LANE) for array in (level_codes, sign_bits, noise)]
    effects = effects.reshape(LEVELS, COV)

    want = jnp.concatenate([sample_rows] + [partner(sample_rows, "wide", m) for m in range(1, MATES)])
    pieces = call(
        functools.partial(local_kernel, samp, share),
        "local",
        [((samp * (m < MATES) + share, cols), bf16) for m in range(wide)],
        [
            ((cols + 3 * PACK, rows_dev), bf16),
            ((MATES * samp, rows_dev), bf16),
            ((share * wide, LANE), f32),
        ],
        index,
        want.reshape(-1, LANE),
        covariates,
        codes,
        signs,
        noise,
    )
    pieces = [pieces[0]] + [partner(pieces[m], "wide", m) for m in range(1, wide)]
    (piece,) = call(
        functools.partial(mix_kernel, samp, share), "mix", [((samp + share, cols), bf16)], [], index, *pieces
    )
    pieces = [piece] + [partner(piece, "narrow", m) for m in range(1, narrow)]
    rows_in = samp * narrow
    (piece,) = call(
        functools.partial(stack_kernel, samp, share), "stack", [((rows_in + share, cols), bf16)], [], index, *pieces
    )
    pieces = [piece] + [partner(piece, "wide", m) for m in range(2, wide, 2)]
    pieces += [partner(piece, "wide", 1) for piece in pieces]
    apart = [2 * m + core for core in range(2) for m in range(wide // 2)]
    factor, inverse = call(
        functools.partial(factor_kernel, math.sqrt(LEVELS / SKETCH), apart, rows_in),
        "factor",
        [((cols, cols), f32)] * 2,
        [((rows_in * wide, cols), bf16), ((cols, cols), f32), ((LANE, cols), f32)],
        index,
        *pieces,
    )
    solved, resid = call(
        functools.partial(solve_kernel, apart, rows_in, share),
        "solve",
        [((LEVELS, COV), f32), (codes.shape, f32)],
        [((share * wide, LANE), f32)],
        index,
        inverse,
        effects,
        covariates,
        codes,
        noise,
        *pieces,
    )
    return solved.reshape(-1), resid.reshape(-1), factor


def solution(mesh):
    return jax.shard_map(
        body,
        mesh=mesh,
        in_specs=(
            P(("wide", "narrow"), None),
            P(("wide", "narrow")),
            P(("wide", "narrow")),
            P(("wide", "narrow")),
            P(),
            P(("wide", "narrow")),
        ),
        out_specs=(P(), P(("wide", "narrow")), P()),
        check_vma=False,
    )
```

```python
import functools
import math

import jax
import jax.numpy as jnp
from jax import lax
from jax.experimental import pallas as pl
from jax.experimental.pallas import tpu as pltpu
from jax.sharding import PartitionSpec as P

COV = 128
LEVELS = 4
HB = 256
SKETCH = 1024
ITERS = 4
MIX_BITS = 3
MATES = 2**MIX_BITS

half_root = math.sqrt(0.5)
HIGHEST = lax.Precision.HIGHEST
f32, bf16 = jnp.float32, jnp.bfloat16
SUB, LANE = 8, 128
PACK = 16
NT = (((1,), (1,)), ((), ()))
VMEM = pl.BlockSpec(memory_space=pltpu.VMEM)
SMEM = pl.BlockSpec(memory_space=pltpu.SMEM)


def partner(value, axis, mask):
    pairs = [(source, source ^ mask) for source in range(lax.axis_size(axis))]
    return lax.ppermute(value, axis, pairs)


def whole_up(number, unit):
    return -(-number // unit) * unit


def eye():
    rows = lax.broadcasted_iota(jnp.int32, (LANE, LANE), 0)
    lanes = lax.broadcasted_iota(jnp.int32, (LANE, LANE), 1)
    return rows, lanes, rows == lanes


def to_column(row, same):
    return jnp.sum(jnp.where(same, row, 0.0), axis=1, keepdims=True)


def to_row(column, same):
    return jnp.sum(jnp.where(same, column, 0.0), axis=0, keepdims=True)


def split(value):
    parts = []
    for _ in range(3):
        parts.append(value.astype(bf16))
        value = value - parts[-1].astype(f32)
    return parts


def tree_sum(values):
    while len(values) > 1:
        values = [left + right for left, right in zip(values[0::2], values[1::2])]
    return values[0]


def put_sums(ref, start, share, extra):
    rows = share.shape[0]
    for k, part in enumerate(split(share)):
        ref[start : start + rows, k * LANE : (k + 1) * LANE] = part
    tail = jnp.zeros((rows - 3 * SUB, LANE), bf16)
    ref[start : start + rows, 3 * LANE :] = jnp.concatenate(split(extra) + [tail])


def take_sums(ref, start, rows):
    block = ref[start : start + rows, :].astype(f32)
    share = block[:, :LANE] + block[:, LANE : 2 * LANE] + block[:, 2 * LANE : 3 * LANE]
    tail = block[:, 3 * LANE :]
    return share, tail[:SUB] + tail[SUB : 2 * SUB] + tail[2 * SUB : 3 * SUB]


def design_kernel(cov_ref, codes_ref, noise_ref, design, packed):
    rows, lanes, same = eye()
    zero = jnp.zeros((LANE, LANE), f32)
    for r in range(codes_ref.shape[0]):
        here = slice(r * LANE, (r + 1) * LANE)
        code = codes_ref[r : r + 1, :]
        turned = cov_ref[here, :].astype(f32).T
        for level in range(LEVELS):
            design[level * LANE : (level + 1) * LANE, here] = jnp.where(code == level, turned, zero).astype(bf16)
        noise = jnp.concatenate([noise_ref[r : r + 1, :]] * LEVELS + [jnp.zeros((PACK - LEVELS, LANE), f32)])
        level = lax.broadcasted_iota(jnp.int32, (PACK, LANE), 0)
        noise = jnp.where(code == level, noise, 0.0)
        for k, part in enumerate(split(noise)):
            design[LEVELS * LANE + k * PACK : LEVELS * LANE + (k + 1) * PACK, here] = part

    sums = jnp.dot(design[...], cov_ref[...], preferred_element_type=f32)
    normal = [sums[level * LANE : (level + 1) * LANE] for level in range(LEVELS)]
    back = sums[LEVELS * LANE :]
    back = back[:SUB] + back[PACK : PACK + SUB] + back[2 * PACK : 2 * PACK + SUB]
    extra = [jnp.sum(jnp.where(same, normal[level], 0.0), axis=0, keepdims=True) for level in (1, 3)]
    for pair in range(LEVELS // 2):
        packed[pair * LANE : (pair + 1) * LANE, :] = jnp.where(rows >= lanes, normal[2 * pair], normal[2 * pair + 1])
    rest = packed.shape[0] - SUB - 2 * LANE
    if rest:
        packed[2 * LANE : 2 * LANE + rest, :] = jnp.zeros((rest, LANE), f32)
    packed[2 * LANE + rest :, :] = jnp.concatenate([back[:LEVELS]] + extra + [jnp.zeros((2, LANE), f32)])


def local_kernel(samp, share, starts, index_ref, design_ref, packed_ref, signs_ref, *refs):
    want_refs, (stay_ref, go_ref, table) = refs[:-3], refs[-3:]
    chunks = signs_ref.shape[0]
    lanes = lax.broadcasted_iota(jnp.int32, (1, LANE), 1)
    wide_lanes, same = eye()[1:]
    zero = jnp.zeros((LANE, LANE), f32)
    pairs = LANE // (2 * samp)

    masks, halves = [], []
    for c in range(MATES // 2 // pairs):
        want = want_refs[c * pairs][...]
        for q in range(1, pairs):
            want = jnp.where(lanes >= 2 * samp * q, want_refs[c * pairs + q][...], want)
        want = to_column(want.astype(f32), same).astype(jnp.int32)
        masks.append(jnp.right_shift(want, HB.bit_length() - 1))
        line = []
        for h in range(HB // LANE):
            common = jnp.bitwise_and(want, wide_lanes + h * LANE)
            for shift in (4, 2, 1):
                common = jnp.bitwise_xor(common, jnp.right_shift(common, shift))
            line.append((1 - 2 * jnp.bitwise_and(common, 1)).astype(f32))
        halves.append(line)
    for r in range(chunks):
        sign = (1 - 2 * signs_ref[r : r + 1, :]).astype(f32)
        block, h = divmod(r * LANE, HB)
        for c, (mask, line) in enumerate(zip(masks, halves)):
            value = jnp.where(mask == block, line[h // LANE] * sign, zero)
            table[c * LANE : (c + 1) * LANE, r * LANE : (r + 1) * LANE] = value.astype(bf16)

    local = lax.dot_general(table[...], design_ref[: LEVELS * LANE, :], NT, preferred_element_type=f32)
    local = (local * (1.0 / math.sqrt(HB))).astype(bf16)
    extra = packed_ref[packed_ref.shape[0] - SUB :, :]
    for m in range(2 * len(starts)):
        out_ref, start = (stay_ref, go_ref)[m % 2], starts[m // 2]
        if m < MATES:
            out_ref[start : start + samp, :] = local[m * samp : (m + 1) * samp]
            start += samp
        at = pl.multiple_of(jnp.bitwise_xor(index_ref[0], m) * share, share)
        put_sums(out_ref, start, packed_ref[pl.ds(at, share), :], extra)


def butterfly(pieces, place, index):
    bit = jnp.bitwise_and(jnp.right_shift(index, place), 1)
    sign = (1 - 2 * bit).astype(f32)
    return [
        ((sign * own + other) * half_root).astype(bf16).astype(f32) for own, other in zip(pieces[0::2], pieces[1::2])
    ]


def pair_kernel(samp, share, starts, index_ref, stay_ref, came_ref, *out_refs):
    for m, (start, out_ref) in enumerate(zip(starts, out_refs)):
        put = 0
        if 2 * m < MATES:
            here = slice(start, start + samp)
            pieces = [ref[here, :].astype(f32) for ref in (stay_ref, came_ref)]
            out_ref[:samp, :] = butterfly(pieces, 0, index_ref[0])[0].astype(bf16)
            put, start = samp, start + samp
        (own, own_extra), (other, other_extra) = [take_sums(ref, start, share) for ref in (stay_ref, came_ref)]
        put_sums(out_ref, put, own + other, own_extra + other_extra)


def mix_kernel(samp, share, index_ref, *refs):
    piece_refs, out_ref = refs[:-1], refs[-1]
    pieces = [ref[:samp, :].astype(f32) for ref in piece_refs[: MATES // 2]]
    for place in range(1, MIX_BITS):
        pieces = butterfly(pieces, place, index_ref[0])
    out_ref[:samp, :] = pieces[0].astype(bf16)
    sums = [take_sums(ref, samp if 2 * m < MATES else 0, share) for m, ref in enumerate(piece_refs)]
    put_sums(out_ref, samp, tree_sum([one for one, _ in sums]), tree_sum([one for _, one in sums]))


def stack_kernel(samp, share, index_ref, *refs):
    piece_refs, out_ref = refs[:-1], refs[-1]
    for m, ref in enumerate(piece_refs):
        at = pl.multiple_of(jnp.bitwise_xor(index_ref[1], m) * samp, samp)
        out_ref[pl.ds(at, samp), :] = ref[:samp, :]
    sums = [take_sums(ref, samp, share) for ref in piece_refs]
    put_sums(
        out_ref, samp * len(piece_refs), tree_sum([one for one, _ in sums]), tree_sum([one for _, one in sums])
    )


def spread(value):
    return jnp.broadcast_to(value, (SUB, LANE))


def reciprocal(value):
    rough = pl.reciprocal(value, approx=True)
    rough = rough * (2.0 - value * rough)
    return rough * (2.0 - value * rough)


def eliminate(tiles):
    lane = lax.broadcasted_iota(jnp.int32, (SUB, LANE), 1)
    sub = lax.broadcasted_iota(jnp.int32, (SUB, LANE), 0)
    tiles = list(tiles)
    scales = []
    for tile in range(len(tiles)):
        first = tile * SUB
        window = (lane >= first) & (lane < first + SUB)
        marks = [lane == first + k for k in range(SUB)]
        old = tiles[tile]
        columns = [spread(old[:, first + k : first + k + 1]) for k in range(SUB)]
        pivot = [[spread(columns[m][k : k + 1, :]) if m >= k else None for m in range(SUB)] for k in range(SUB)]
        cleared = jnp.where(window, 0.0, old)
        rows = [jnp.where(marks[k], 1.0, spread(cleared[k : k + 1, :])) for k in range(SUB)]
        steps, near, far = [None] * SUB, {}, {}
        kept, scale = [None] * SUB, None
        for k in range(0, SUB, 2):
            low, cross, high = pivot[k][k], pivot[k][k + 1], pivot[k + 1][k + 1]
            area = low * high - cross * cross
            over = reciprocal(area)
            rest = range(k + 2, SUB)
            for m in rest:
                near[k, m] = high * pivot[k][m] - cross * pivot[k + 1][m]
                far[k, m] = low * pivot[k + 1][m] - cross * pivot[k][m]
            for m in rest:
                for n in range(m, SUB):
                    pivot[m][n] = pivot[m][n] - over * (pivot[k][m] * near[k, n] + pivot[k + 1][m] * far[k, n])
            for m in rest:
                near[k, m] = over * near[k, m]
                far[k, m] = over * far[k, m]
                rows[m] = rows[m] - (near[k, m] * rows[k] + far[k, m] * rows[k + 1])
            steps[k] = over * (high * rows[k] - cross * rows[k + 1])
            steps[k + 1] = over * (low * rows[k + 1] - cross * rows[k])
            inner = reciprocal(low)
            ratio = cross * inner
            kept[k] = rows[k]
            kept[k + 1] = rows[k + 1] - ratio * rows[k]
            for m in range(k, SUB):
                kept[k] = jnp.where(marks[m], pivot[k][m], kept[k])
            last = area * inner
            kept[k + 1] = jnp.where(marks[k + 1], last, kept[k + 1])
            for m in rest:
                kept[k + 1] = jnp.where(marks[m], pivot[k + 1][m] - ratio * pivot[k][m], kept[k + 1])
            roots = lax.rsqrt(low), lax.rsqrt(last)
            scale = roots[0] if scale is None else jnp.where(sub >= k, roots[0], scale)
            scale = jnp.where(sub >= k + 1, roots[1], scale)
        for k in reversed(range(0, SUB, 2)):
            for m in range(k + 2, SUB):
                steps[k] = steps[k] - near[k, m] * steps[m]
                steps[k + 1] = steps[k + 1] - far[k, m] * steps[m]
        for i in range(tile + 1, len(tiles)):
            change = [spread(tiles[i][:, first + k : first + k + 1]) * steps[k] for k in range(SUB)]
            tiles[i] = jnp.where(window, 0.0, tiles[i]) - tree_sum(change)
        new = kept[0]
        for k in range(1, SUB):
            new = jnp.where(sub >= k, kept[k], new)
        tiles[tile] = new
        scales.append(scale)
    return tiles, scales


def factor_kernel(ratio, apart, rows_in, index_ref, *refs):
    piece_refs, (factor_ref, inverse_ref, sketch, work, line) = refs[:-5], refs[-5:]
    cols = work.shape[0]
    for mask, ref in zip(apart, piece_refs):
        at = pl.multiple_of(jnp.bitwise_xor(index_ref[0], mask) * rows_in, rows_in)
        sketch[pl.ds(at, rows_in), :] = ref[:rows_in, :]
    rows = sketch[...]
    gram = lax.dot_general(rows, rows, (((0,), (0,)), ((), ())), preferred_element_type=f32)
    work[...] = gram
    _, _, same = eye()
    diagonal = []
    for at in range(0, cols, LANE):
        block = work[at : at + LANE, at : at + LANE]
        diagonal.append(jnp.sum(jnp.where(same, block, 0.0), axis=0, keepdims=True))
    unit = [lax.rsqrt(part) for part in diagonal]
    level = jnp.concatenate([part * one for part, one in zip(diagonal, unit)], axis=1) * ratio
    unit_row = jnp.concatenate(unit, axis=1)
    for at, one in zip(range(0, cols, LANE), unit):
        work[at : at + LANE, :] = work[at : at + LANE, :] * to_column(one, same) * unit_row

    row_in = lax.broadcasted_iota(jnp.int32, (LANE, LANE), 0)
    lane_in = lax.broadcasted_iota(jnp.int32, (LANE, LANE), 1)
    lane_all = lax.broadcasted_iota(jnp.int32, (LANE, cols), 1)
    row_all = lax.broadcasted_iota(jnp.int32, (cols, LANE), 0)

    def block_step(block, _):
        base = pl.multiple_of(block * LANE, LANE)
        here = pl.ds(base, LANE)
        tiles = [work[pl.ds(base + SUB * i, SUB), here] for i in range(LANE // SUB)]
        tiles, scales = eliminate(tiles)
        scale = jnp.concatenate(scales)
        inner = jnp.concatenate(tiles) * scale
        upper = jnp.where(lane_in >= row_in, inner, 0.0)
        lower = jnp.where(lane_in < row_in, inner, jnp.where(lane_in == row_in, scale, 0.0))
        line[...] = jnp.dot(lower, work[here, :], precision=HIGHEST, preferred_element_type=f32)
        line[:, here] = upper
        factor_ref[here, :] = jnp.where(lane_all >= base, line[...], 0.0) * level
        line[:, here] = lower
        inverse_ref[here, :] = jnp.where(lane_all < base + LANE, line[...], 0.0) * unit_row

        @pl.when(block < cols // LANE - 1)
        def _():
            steps = jnp.dot(lower.T, line[...], precision=HIGHEST, preferred_element_type=f32)
            panel = jnp.where(row_all >= base + LANE, work[:, here], 0.0)
            work[:, here] = jnp.where(row_all >= base + LANE, 0.0, work[:, here])
            work[...] -= jnp.dot(panel, steps, precision=HIGHEST, preferred_element_type=f32)

        return 0

    lax.fori_loop(0, cols // LANE, block_step, 0)


def solve_kernel(apart, rows_in, share, index_ref, inverse_ref, effects_ref, cov_ref, codes_ref, noise_ref, *refs):
    piece_refs, (solved_ref, resid_ref, packed) = refs[:-3], refs[-3:]
    rows, lanes, same = eye()
    extra = None
    for mask, ref in zip(apart, piece_refs):
        at = pl.multiple_of(jnp.bitwise_xor(index_ref[0], mask) * share, share)
        packed[pl.ds(at, share), :], more = take_sums(ref, rows_in, share)
        extra = more if extra is None else extra
    normal = []
    for pair in range(LEVELS // 2):
        both = packed[pair * LANE : (pair + 1) * LANE, :]
        turned = both.T
        normal.append(jnp.where(rows >= lanes, both, turned))
        diagonal = jnp.where(same, extra[LEVELS + pair : LEVELS + pair + 1], turned)
        normal.append(jnp.where(rows < lanes, both, diagonal))

    inverse = inverse_ref[...]
    spans = [slice(level * LANE, (level + 1) * LANE) for level in range(LEVELS)]
    gradient = []
    for level in range(LEVELS):
        column = to_column(effects_ref[level : level + 1, :], same)
        gradient.append(jnp.sum(normal[level] * column, axis=0, keepdims=True) + extra[level : level + 1])
    steer = jnp.sum(inverse * jnp.concatenate(gradient, axis=1), axis=1, keepdims=True)
    direction = steer
    gamma = jnp.sum(steer * steer, axis=0, keepdims=True)
    solved = jnp.zeros((1, cov_ref.shape[1] * LEVELS), f32)
    for step in range(ITERS):
        move = jnp.sum(inverse * direction, axis=0, keepdims=True)
        image = []
        for level, span in enumerate(spans):
            image.append(jnp.sum(normal[level] * to_column(move[:, span], same), axis=0, keepdims=True))
        image = jnp.concatenate(image, axis=1)
        alpha = gamma / jnp.sum(move * image, axis=1, keepdims=True)
        solved = solved + alpha * move
        if step == ITERS - 1:
            break
        steer = steer - alpha * jnp.sum(inverse * image, axis=1, keepdims=True)
        gamma_new = jnp.sum(steer * steer, axis=0, keepdims=True)
        direction = steer + gamma_new / gamma * direction
        gamma = gamma_new
    solved = jnp.concatenate([solved[:, span] for span in spans])
    solved_ref[...] = solved

    left = jnp.concatenate([effects_ref[...] - solved, jnp.zeros((PACK - LEVELS, LANE), f32)])
    values = jnp.zeros((SUB, cov_ref.shape[0]), f32)
    for part in split(left):
        values = values + lax.dot_general(part, cov_ref[...], NT, preferred_element_type=f32)[:SUB]
    for r in range(codes_ref.shape[0]):
        code = codes_ref[r : r + 1, :]
        total = noise_ref[r : r + 1, :]
        for level in range(LEVELS):
            total = total + jnp.where(code == level, values[level : level + 1, r * LANE : (r + 1) * LANE], 0.0)
        resid_ref[r : r + 1, :] = total


def call(kernel, name, outs, scratch, *operands):
    return pl.pallas_call(
        kernel,
        out_shape=[jax.ShapeDtypeStruct(shape, dtype) for shape, dtype in outs],
        in_specs=[SMEM if operand.ndim == 1 else VMEM for operand in operands],
        out_specs=[VMEM] * len(outs),
        scratch_shapes=[pltpu.VMEM(shape, dtype) for shape, dtype in scratch],
        compiler_params=pltpu.CompilerParams(vmem_limit_bytes=40 * 2**20),
        name=name,
    )(*operands)


def body(covariates, level_codes, sign_bits, sample_rows, effects, noise):
    wide, narrow = lax.axis_size("wide"), lax.axis_size("narrow")
    index = jnp.stack([lax.axis_index("wide"), lax.axis_index("narrow")]).astype(jnp.int32)
    rows_dev, cols = covariates.shape[0], LEVELS * COV
    samp = whole_up(sample_rows.shape[0], PACK)
    share = whole_up(max(2 * LANE // wide, 3 * SUB), PACK)
    sample_rows = jnp.pad(sample_rows, (0, samp - sample_rows.shape[0]), constant_values=-1)
    codes, signs, noise = [array.reshape(-1, LANE) for array in (level_codes, sign_bits, noise)]
    effects = effects.reshape(LEVELS, COV)

    lane = jnp.arange(LANE, dtype=jnp.int32)[None, :]
    want = jnp.tile(sample_rows, LANE // samp)[None, :]
    want = jnp.where(jnp.bitwise_and(lane // samp, 1) == 0, want, partner(want, "wide", 1))
    want = [want] + [partner(want, "wide", m) for m in range(2, MATES, 2)]

    design, packed = call(
        design_kernel,
        "design",
        [((cols + 3 * PACK, rows_dev), bf16), ((share * wide + SUB, LANE), f32)],
        [],
        covariates,
        codes,
        noise,
    )
    sizes = [samp * (2 * m < MATES) + share for m in range(wide // 2)]
    starts = [sum(sizes[:m]) for m in range(wide // 2)]
    stay, go = call(
        functools.partial(local_kernel, samp, share, starts),
        "local",
        [((sum(sizes), cols), bf16)] * 2,
        [((MATES * samp, rows_dev), bf16)],
        index,
        design,
        packed,
        signs,
        *want,
    )
    pieces = call(
        functools.partial(pair_kernel, samp, share, starts),
        "pair",
        [((size, cols), bf16) for size in sizes],
        [],
        index,
        stay,
        partner(go, "wide", 1),
    )
    pieces = [pieces[0]] + [partner(pieces[m], "wide", 2 * m) for m in range(1, wide // 2)]
    (piece,) = call(
        functools.partial(mix_kernel, samp, share), "mix", [((samp + share, cols), bf16)], [], index, *pieces
    )
    pieces = [piece] + [partner(piece, "narrow", m) for m in range(1, narrow)]
    rows_in = samp * narrow
    (piece,) = call(
        functools.partial(stack_kernel, samp, share), "stack", [((rows_in + share, cols), bf16)], [], index, *pieces
    )
    pieces = [piece] + [partner(piece, "wide", m) for m in range(2, wide, 2)]
    pieces += [partner(piece, "wide", 1) for piece in pieces]
    apart = [2 * m + core for core in range(2) for m in range(wide // 2)]
    factor, inverse = call(
        functools.partial(factor_kernel, math.sqrt(LEVELS / SKETCH), apart, rows_in),
        "factor",
        [((cols, cols), f32)] * 2,
        [((rows_in * wide, cols), bf16), ((cols, cols), f32), ((LANE, cols), f32)],
        index,
        *pieces,
    )
    solved, resid = call(
        functools.partial(solve_kernel, apart, rows_in, share),
        "solve",
        [((LEVELS, COV), f32), (codes.shape, f32)],
        [((share * wide, LANE), f32)],
        index,
        inverse,
        effects,
        covariates,
        codes,
        noise,
        *pieces,
    )
    return solved.reshape(-1), resid.reshape(-1), factor


def solution(mesh):
    return jax.shard_map(
        body,
        mesh=mesh,
        in_specs=(
            P(("wide", "narrow"), None),
            P(("wide", "narrow")),
            P(("wide", "narrow")),
            P(("wide", "narrow")),
            P(),
            P(("wide", "narrow")),
        ),
        out_specs=(P(), P(("wide", "narrow")), P()),
        check_vma=False,
    )
```

```python
import functools
import math

import jax
import jax.numpy as jnp
from jax import lax
from jax.experimental import pallas as pl
from jax.experimental.pallas import tpu as pltpu
from jax.sharding import PartitionSpec as P

COV = 128
LEVELS = 4
HB = 256
SKETCH = 1024
ITERS = 4
MIX_BITS = 3
MATES = 2**MIX_BITS

half_root = math.sqrt(0.5)
HIGHEST = lax.Precision.HIGHEST
f32, bf16 = jnp.float32, jnp.bfloat16
SUB, LANE = 8, 128
PACK = 16
NT = (((1,), (1,)), ((), ()))
VMEM = pl.BlockSpec(memory_space=pltpu.VMEM)
SMEM = pl.BlockSpec(memory_space=pltpu.SMEM)


def partner(value, axis, mask):
    pairs = [(source, source ^ mask) for source in range(lax.axis_size(axis))]
    return lax.ppermute(value, axis, pairs)


def whole_up(number, unit):
    return -(-number // unit) * unit


def eye():
    rows = lax.broadcasted_iota(jnp.int32, (LANE, LANE), 0)
    lanes = lax.broadcasted_iota(jnp.int32, (LANE, LANE), 1)
    return rows, lanes, rows == lanes


def to_column(row, same):
    return jnp.sum(jnp.where(same, row, 0.0), axis=1, keepdims=True)


def to_row(column, same):
    return jnp.sum(jnp.where(same, column, 0.0), axis=0, keepdims=True)


def split(value):
    parts = []
    for _ in range(3):
        parts.append(value.astype(bf16))
        value = value - parts[-1].astype(f32)
    return parts


def tree_sum(values):
    while len(values) > 1:
        values = [left + right for left, right in zip(values[0::2], values[1::2])]
    return values[0]


def put_sums(ref, start, share, extra):
    rows = share.shape[0]
    for k, part in enumerate(split(share)):
        ref[start : start + rows, k * LANE : (k + 1) * LANE] = part
    tail = jnp.zeros((rows - 3 * SUB, LANE), bf16)
    ref[start : start + rows, 3 * LANE :] = jnp.concatenate(split(extra) + [tail])


def take_sums(ref, start, rows):
    block = ref[start : start + rows, :].astype(f32)
    share = block[:, :LANE] + block[:, LANE : 2 * LANE] + block[:, 2 * LANE : 3 * LANE]
    tail = block[:, 3 * LANE :]
    return share, tail[:SUB] + tail[SUB : 2 * SUB] + tail[2 * SUB : 3 * SUB]


def design_kernel(cov_ref, codes_ref, noise_ref, design, packed):
    rows, lanes, same = eye()
    zero = jnp.zeros((LANE, LANE), f32)
    for r in range(codes_ref.shape[0]):
        here = slice(r * LANE, (r + 1) * LANE)
        code = codes_ref[r : r + 1, :]
        turned = cov_ref[here, :].astype(f32).T
        for level in range(LEVELS):
            design[level * LANE : (level + 1) * LANE, here] = jnp.where(code == level, turned, zero).astype(bf16)
        noise = jnp.concatenate([noise_ref[r : r + 1, :]] * LEVELS + [jnp.zeros((PACK - LEVELS, LANE), f32)])
        level = lax.broadcasted_iota(jnp.int32, (PACK, LANE), 0)
        noise = jnp.where(code == level, noise, 0.0)
        for k, part in enumerate(split(noise)):
            design[LEVELS * LANE + k * PACK : LEVELS * LANE + (k + 1) * PACK, here] = part

    sums = jnp.dot(design[...], cov_ref[...], preferred_element_type=f32)
    normal = [sums[level * LANE : (level + 1) * LANE] for level in range(LEVELS)]
    back = sums[LEVELS * LANE :]
    back = back[:SUB] + back[PACK : PACK + SUB] + back[2 * PACK : 2 * PACK + SUB]
    extra = [jnp.sum(jnp.where(same, normal[level], 0.0), axis=0, keepdims=True) for level in (1, 3)]
    for pair in range(LEVELS // 2):
        packed[pair * LANE : (pair + 1) * LANE, :] = jnp.where(rows >= lanes, normal[2 * pair], normal[2 * pair + 1])
    rest = packed.shape[0] - SUB - 2 * LANE
    if rest:
        packed[2 * LANE : 2 * LANE + rest, :] = jnp.zeros((rest, LANE), f32)
    packed[2 * LANE + rest :, :] = jnp.concatenate([back[:LEVELS]] + extra + [jnp.zeros((2, LANE), f32)])


def local_kernel(samp, share, starts, index_ref, design_ref, packed_ref, signs_ref, *refs):
    want_refs, (stay_ref, go_ref, table) = refs[:-3], refs[-3:]
    chunks = signs_ref.shape[0]
    lanes = lax.broadcasted_iota(jnp.int32, (1, LANE), 1)
    wide_lanes, same = eye()[1:]
    zero = jnp.zeros((LANE, LANE), f32)
    pairs = LANE // (2 * samp)

    masks, halves = [], []
    for c in range(MATES // 2 // pairs):
        want = want_refs[c * pairs][...]
        for q in range(1, pairs):
            want = jnp.where(lanes >= 2 * samp * q, want_refs[c * pairs + q][...], want)
        want = to_column(want.astype(f32), same).astype(jnp.int32)
        masks.append(jnp.right_shift(want, HB.bit_length() - 1))
        line = []
        for h in range(HB // LANE):
            common = jnp.bitwise_and(want, wide_lanes + h * LANE)
            for shift in (4, 2, 1):
                common = jnp.bitwise_xor(common, jnp.right_shift(common, shift))
            line.append((1 - 2 * jnp.bitwise_and(common, 1)).astype(f32))
        halves.append(line)
    for r in range(chunks):
        sign = (1 - 2 * signs_ref[r : r + 1, :]).astype(f32)
        block, h = divmod(r * LANE, HB)
        for c, (mask, line) in enumerate(zip(masks, halves)):
            value = jnp.where(mask == block, line[h // LANE] * sign, zero)
            table[c * LANE : (c + 1) * LANE, r * LANE : (r + 1) * LANE] = value.astype(bf16)

    local = lax.dot_general(table[...], design_ref[: LEVELS * LANE, :], NT, preferred_element_type=f32)
    local = (local * (1.0 / math.sqrt(HB))).astype(bf16)
    extra = packed_ref[packed_ref.shape[0] - SUB :, :]
    for m in range(2 * len(starts)):
        out_ref, start = (stay_ref, go_ref)[m % 2], starts[m // 2]
        if m < MATES:
            out_ref[start : start + samp, :] = local[m * samp : (m + 1) * samp]
            start += samp
        at = pl.multiple_of(jnp.bitwise_xor(index_ref[0], m) * share, share)
        put_sums(out_ref, start, packed_ref[pl.ds(at, share), :], extra)


def butterfly(pieces, place, index):
    bit = jnp.bitwise_and(jnp.right_shift(index, place), 1)
    sign = (1 - 2 * bit).astype(f32)
    return [
        ((sign * own + other) * half_root).astype(bf16).astype(f32) for own, other in zip(pieces[0::2], pieces[1::2])
    ]


def pair_kernel(samp, share, starts, index_ref, stay_ref, came_ref, *out_refs):
    for m, (start, out_ref) in enumerate(zip(starts, out_refs)):
        put = 0
        if 2 * m < MATES:
            here = slice(start, start + samp)
            pieces = [ref[here, :].astype(f32) for ref in (stay_ref, came_ref)]
            out_ref[:samp, :] = butterfly(pieces, 0, index_ref[0])[0].astype(bf16)
            put, start = samp, start + samp
        (own, own_extra), (other, other_extra) = [take_sums(ref, start, share) for ref in (stay_ref, came_ref)]
        put_sums(out_ref, put, own + other, own_extra + other_extra)


def mix_kernel(samp, share, index_ref, *refs):
    piece_refs, out_ref = refs[:-1], refs[-1]
    pieces = [ref[:samp, :].astype(f32) for ref in piece_refs[: MATES // 2]]
    for place in range(1, MIX_BITS):
        pieces = butterfly(pieces, place, index_ref[0])
    out_ref[:samp, :] = pieces[0].astype(bf16)
    sums = [take_sums(ref, samp if 2 * m < MATES else 0, share) for m, ref in enumerate(piece_refs)]
    put_sums(out_ref, samp, tree_sum([one for one, _ in sums]), tree_sum([one for _, one in sums]))


def stack_kernel(samp, share, index_ref, *refs):
    piece_refs, out_ref = refs[:-1], refs[-1]
    for m, ref in enumerate(piece_refs):
        at = pl.multiple_of(jnp.bitwise_xor(index_ref[1], m) * samp, samp)
        out_ref[pl.ds(at, samp), :] = ref[:samp, :]
    sums = [take_sums(ref, samp, share) for ref in piece_refs]
    put_sums(
        out_ref, samp * len(piece_refs), tree_sum([one for one, _ in sums]), tree_sum([one for _, one in sums])
    )


def spread(value):
    return jnp.broadcast_to(value, (SUB, LANE))


def reciprocal(value):
    return pltpu.reciprocal(value, approx=True)


def eliminate(tiles):
    lane = lax.broadcasted_iota(jnp.int32, (SUB, LANE), 1)
    sub = lax.broadcasted_iota(jnp.int32, (SUB, LANE), 0)
    tiles = list(tiles)
    scales = []
    for tile in range(len(tiles)):
        first = tile * SUB
        window = (lane >= first) & (lane < first + SUB)
        marks = [lane == first + k for k in range(SUB)]
        old = tiles[tile]
        columns = [spread(old[:, first + k : first + k + 1]) for k in range(SUB)]
        pivot = [[spread(columns[m][k : k + 1, :]) if m >= k else None for m in range(SUB)] for k in range(SUB)]
        cleared = jnp.where(window, 0.0, old)
        rows = [jnp.where(marks[k], 1.0, spread(cleared[k : k + 1, :])) for k in range(SUB)]
        steps, near, far = [None] * SUB, {}, {}
        kept, roots = [None] * SUB, [None] * SUB

        def keep(k, low, ratio, values, others):
            last = others[k + 1]
            kept[k] = rows[k]
            for m in range(k, SUB):
                kept[k] = jnp.where(marks[m], values[m], kept[k])
            kept[k + 1] = rows[k + 1] - ratio * rows[k]
            for m in range(k + 1, SUB):
                kept[k + 1] = jnp.where(marks[m], others[m], kept[k + 1])
            roots[k], roots[k + 1] = lax.rsqrt(low), lax.rsqrt(last)

        for k in range(0, SUB, 4):
            low, cross, high = pivot[k][k], pivot[k][k + 1], pivot[k + 1][k + 1]
            area = low * high - cross * cross
            drop = {}
            for m in range(k + 2, SUB):
                near[k, m] = high * pivot[k][m] - cross * pivot[k + 1][m]
                far[k, m] = low * pivot[k + 1][m] - cross * pivot[k][m]
            for m in range(k + 2, SUB):
                for n in range(m, SUB):
                    drop[m, n] = pivot[k][m] * near[k, n] + pivot[k + 1][m] * far[k, n]
            c, d = k + 2, k + 3
            grown = {(m, n): area * pivot[m][n] - drop[m, n] for m in (c, d) for n in range(m, SUB)}
            low2, cross2, high2 = grown[c, c], grown[c, d], grown[d, d]
            area2 = low2 * high2 - cross2 * cross2
            over, over2 = reciprocal(area), reciprocal(area2)
            for m in range(k + 4, SUB):
                near[c, m] = high2 * grown[c, m] - cross2 * grown[d, m]
                far[c, m] = low2 * grown[d, m] - cross2 * grown[c, m]
            for m in range(k + 4, SUB):
                for n in range(m, SUB):
                    drop2 = grown[c, m] * near[c, n] + grown[d, m] * far[c, n]
                    pivot[m][n] = pivot[m][n] - over * (drop[m, n] + over2 * drop2)
            for m in range(k + 2, SUB):
                near[k, m], far[k, m] = over * near[k, m], over * far[k, m]
                rows[m] = rows[m] - (near[k, m] * rows[k] + far[k, m] * rows[k + 1])
            for m in range(k + 4, SUB):
                near[c, m], far[c, m] = over2 * near[c, m], over2 * far[c, m]
                rows[m] = rows[m] - (near[c, m] * rows[c] + far[c, m] * rows[d])
            steps[k] = over * (high * rows[k] - cross * rows[k + 1])
            steps[k + 1] = over * (low * rows[k + 1] - cross * rows[k])
            both = area * over2
            steps[c] = both * (high2 * rows[c] - cross2 * rows[d])
            steps[d] = both * (low2 * rows[d] - cross2 * rows[c])

            inner = reciprocal(low)
            ratio = cross * inner
            values = {m: pivot[k][m] for m in range(k, SUB)}
            others = {m: pivot[k + 1][m] - ratio * pivot[k][m] for m in range(k + 2, SUB)}
            others[k + 1] = area * inner
            keep(k, low, ratio, values, others)
            inner = reciprocal(low2)
            ratio = cross2 * inner
            values = {m: over * grown[c, m] for m in range(c, SUB)}
            others = {m: over * (grown[d, m] - ratio * grown[c, m]) for m in range(c + 2, SUB)}
            others[d] = over * (area2 * inner)
            keep(c, values[c], ratio, values, others)
        for k in reversed(range(0, SUB, 2)):
            for m in reversed(range(k + 2, SUB)):
                steps[k] = steps[k] - near[k, m] * steps[m]
                steps[k + 1] = steps[k + 1] - far[k, m] * steps[m]
        for i in range(tile + 1, len(tiles)):
            change = [spread(tiles[i][:, first + k : first + k + 1]) * steps[k] for k in range(SUB)]
            tiles[i] = jnp.where(window, 0.0, tiles[i]) - tree_sum(change[::-1])
        new, scale = kept[0], roots[0]
        for k in range(1, SUB):
            new = jnp.where(sub >= k, kept[k], new)
            scale = jnp.where(sub >= k, roots[k], scale)
        tiles[tile] = new
        scales.append(scale)
    return tiles, scales


LEFT, RIGHT = (0, 1, 0, 1, 2, 0), (0, 0, 1, 1, 0, 2)


def parts_of(value, order, axis):
    parts = split(value)
    return jnp.concatenate([parts[k] for k in order], axis=axis)


def factor_kernel(ratio, apart, rows_in, index_ref, *refs):
    piece_refs, (factor_ref, inverse_ref, sketch, work) = refs[:-4], refs[-4:]
    cols = work.shape[0]
    for mask, ref in zip(apart, piece_refs):
        at = pl.multiple_of(jnp.bitwise_xor(index_ref[0], mask) * rows_in, rows_in)
        sketch[pl.ds(at, rows_in), :] = ref[:rows_in, :]
    rows = sketch[...]
    gram = lax.dot_general(rows, rows, (((0,), (0,)), ((), ())), preferred_element_type=f32)
    work[...] = gram
    _, _, same = eye()
    diagonal = []
    for at in range(0, cols, LANE):
        block = work[at : at + LANE, at : at + LANE]
        diagonal.append(jnp.sum(jnp.where(same, block, 0.0), axis=0, keepdims=True))
    unit = [lax.rsqrt(part) for part in diagonal]
    level = jnp.concatenate([part * one for part, one in zip(diagonal, unit)], axis=1) * ratio
    unit_row = jnp.concatenate(unit, axis=1)
    for at, one in zip(range(0, cols, LANE), unit):
        work[at : at + LANE, :] = work[at : at + LANE, :] * to_column(one, same) * unit_row

    row_in = lax.broadcasted_iota(jnp.int32, (LANE, LANE), 0)
    lane_in = lax.broadcasted_iota(jnp.int32, (LANE, LANE), 1)
    for base in range(0, cols, LANE):
        end = base + LANE
        here = slice(base, end)
        tiles = [work[base + SUB * i : base + SUB * (i + 1), here] for i in range(LANE // SUB)]
        tiles, scales = eliminate(tiles)
        scale = jnp.concatenate(scales)
        inner = jnp.concatenate(tiles) * scale
        upper = jnp.where(lane_in >= row_in, inner, 0.0)
        lower = jnp.where(lane_in < row_in, inner, jnp.where(lane_in == row_in, scale, 0.0))
        line = jnp.dot(parts_of(lower, LEFT, 1), parts_of(work[here, :], RIGHT, 0), preferred_element_type=f32)
        if end < cols:
            panel = parts_of(work[end:, here], LEFT, 1)
            panel = lax.dot_general(panel, parts_of(lower, RIGHT, 1), NT, preferred_element_type=f32)
            panel = parts_of(panel, LEFT, 1)
            steps = ([line[:, :base]] if base else []) + [lower, line[:, end:]]
            steps = parts_of(jnp.concatenate(steps, axis=1), RIGHT, 0)
            work[end:, here] = jnp.zeros((cols - end, LANE), f32)
            for start, stop in ((0, LANE), (LANE, cols - end)):
                if start < stop:
                    change = jnp.dot(panel[start:stop], steps, preferred_element_type=f32)
                    work[end + start : end + stop, :] = work[end + start : end + stop, :] - change
        factor_ref[here, here] = upper * level[:, here]
        inverse_ref[here, here] = lower * unit_row[:, here]
        if base:
            factor_ref[here, :base] = jnp.zeros((LANE, base), f32)
            inverse_ref[here, :base] = line[:, :base] * unit_row[:, :base]
        if end < cols:
            factor_ref[here, end:] = line[:, end:] * level[:, end:]
            inverse_ref[here, end:] = jnp.zeros((LANE, cols - end), f32)


def solve_kernel(apart, rows_in, share, index_ref, inverse_ref, effects_ref, cov_ref, codes_ref, noise_ref, *refs):
    piece_refs, (solved_ref, resid_ref, packed) = refs[:-3], refs[-3:]
    rows, lanes, same = eye()
    extra = None
    for mask, ref in zip(apart, piece_refs):
        at = pl.multiple_of(jnp.bitwise_xor(index_ref[0], mask) * share, share)
        packed[pl.ds(at, share), :], more = take_sums(ref, rows_in, share)
        extra = more if extra is None else extra
    normal = []
    for pair in range(LEVELS // 2):
        both = packed[pair * LANE : (pair + 1) * LANE, :]
        turned = both.T
        normal.append(jnp.where(rows >= lanes, both, turned))
        diagonal = jnp.where(same, extra[LEVELS + pair : LEVELS + pair + 1], turned)
        normal.append(jnp.where(rows < lanes, both, diagonal))

    inverse = inverse_ref[...]
    spans = [slice(level * LANE, (level + 1) * LANE) for level in range(LEVELS)]
    gradient = []
    for level in range(LEVELS):
        column = to_column(effects_ref[level : level + 1, :], same)
        gradient.append(jnp.sum(normal[level] * column, axis=0, keepdims=True) + extra[level : level + 1])
    steer = jnp.sum(inverse * jnp.concatenate(gradient, axis=1), axis=1, keepdims=True)
    direction = steer
    gamma = jnp.sum(steer * steer, axis=0, keepdims=True)
    solved = jnp.zeros((1, cov_ref.shape[1] * LEVELS), f32)
    for step in range(ITERS):
        move = jnp.sum(inverse * direction, axis=0, keepdims=True)
        image = []
        for level, span in enumerate(spans):
            image.append(jnp.sum(normal[level] * to_column(move[:, span], same), axis=0, keepdims=True))
        image = jnp.concatenate(image, axis=1)
        alpha = gamma / jnp.sum(move * image, axis=1, keepdims=True)
        solved = solved + alpha * move
        if step == ITERS - 1:
            break
        steer = steer - alpha * jnp.sum(inverse * image, axis=1, keepdims=True)
        gamma_new = jnp.sum(steer * steer, axis=0, keepdims=True)
        direction = steer + gamma_new / gamma * direction
        gamma = gamma_new
    solved = jnp.concatenate([solved[:, span] for span in spans])
    solved_ref[...] = solved

    left = jnp.concatenate([effects_ref[...] - solved, jnp.zeros((PACK - LEVELS, LANE), f32)])
    values = jnp.zeros((SUB, cov_ref.shape[0]), f32)
    for part in split(left):
        values = values + lax.dot_general(part, cov_ref[...], NT, preferred_element_type=f32)[:SUB]
    for r in range(codes_ref.shape[0]):
        code = codes_ref[r : r + 1, :]
        total = noise_ref[r : r + 1, :]
        for level in range(LEVELS):
            total = total + jnp.where(code == level, values[level : level + 1, r * LANE : (r + 1) * LANE], 0.0)
        resid_ref[r : r + 1, :] = total


def call(kernel, name, outs, scratch, *operands):
    return pl.pallas_call(
        kernel,
        out_shape=[jax.ShapeDtypeStruct(shape, dtype) for shape, dtype in outs],
        in_specs=[SMEM if operand.ndim == 1 else VMEM for operand in operands],
        out_specs=[VMEM] * len(outs),
        scratch_shapes=[pltpu.VMEM(shape, dtype) for shape, dtype in scratch],
        compiler_params=pltpu.CompilerParams(vmem_limit_bytes=40 * 2**20),
        name=name,
    )(*operands)


def body(covariates, level_codes, sign_bits, sample_rows, effects, noise):
    wide, narrow = lax.axis_size("wide"), lax.axis_size("narrow")
    index = jnp.stack([lax.axis_index("wide"), lax.axis_index("narrow")]).astype(jnp.int32)
    rows_dev, cols = covariates.shape[0], LEVELS * COV
    samp = whole_up(sample_rows.shape[0], PACK)
    share = whole_up(max(2 * LANE // wide, 3 * SUB), PACK)
    sample_rows = jnp.pad(sample_rows, (0, samp - sample_rows.shape[0]), constant_values=-1)
    codes, signs, noise = [array.reshape(-1, LANE) for array in (level_codes, sign_bits, noise)]
    effects = effects.reshape(LEVELS, COV)

    lane = jnp.arange(LANE, dtype=jnp.int32)[None, :]
    want = jnp.tile(sample_rows, LANE // samp)[None, :]
    want = jnp.where(jnp.bitwise_and(lane // samp, 1) == 0, want, partner(want, "wide", 1))
    want = [want] + [partner(want, "wide", m) for m in range(2, MATES, 2)]

    design, packed = call(
        design_kernel,
        "design",
        [((cols + 3 * PACK, rows_dev), bf16), ((share * wide + SUB, LANE), f32)],
        [],
        covariates,
        codes,
        noise,
    )
    sizes = [samp * (2 * m < MATES) + share for m in range(wide // 2)]
    starts = [sum(sizes[:m]) for m in range(wide // 2)]
    stay, go = call(
        functools.partial(local_kernel, samp, share, starts),
        "local",
        [((sum(sizes), cols), bf16)] * 2,
        [((MATES * samp, rows_dev), bf16)],
        index,
        design,
        packed,
        signs,
        *want,
    )
    pieces = call(
        functools.partial(pair_kernel, samp, share, starts),
        "pair",
        [((size, cols), bf16) for size in sizes],
        [],
        index,
        stay,
        partner(go, "wide", 1),
    )
    pieces = [pieces[0]] + [partner(pieces[m], "wide", 2 * m) for m in range(1, wide // 2)]
    (piece,) = call(
        functools.partial(mix_kernel, samp, share), "mix", [((samp + share, cols), bf16)], [], index, *pieces
    )
    pieces = [piece] + [partner(piece, "narrow", m) for m in range(1, narrow)]
    rows_in = samp * narrow
    (piece,) = call(
        functools.partial(stack_kernel, samp, share), "stack", [((rows_in + share, cols), bf16)], [], index, *pieces
    )
    pieces = [piece] + [partner(piece, "wide", m) for m in range(2, wide, 2)]
    pieces += [partner(piece, "wide", 1) for piece in pieces]
    apart = [2 * m + core for core in range(2) for m in range(wide // 2)]
    factor, inverse = call(
        functools.partial(factor_kernel, math.sqrt(LEVELS / SKETCH), apart, rows_in),
        "factor",
        [((cols, cols), f32)] * 2,
        [((rows_in * wide, cols), bf16), ((cols, cols), f32)],
        index,
        *pieces,
    )
    solved, resid = call(
        functools.partial(solve_kernel, apart, rows_in, share),
        "solve",
        [((LEVELS, COV), f32), (codes.shape, f32)],
        [((share * wide, LANE), f32)],
        index,
        inverse,
        effects,
        covariates,
        codes,
        noise,
        *pieces,
    )
    return solved.reshape(-1), resid.reshape(-1), factor


def solution(mesh):
    return jax.shard_map(
        body,
        mesh=mesh,
        in_specs=(
            P(("wide", "narrow"), None),
            P(("wide", "narrow")),
            P(("wide", "narrow")),
            P(("wide", "narrow")),
            P(),
            P(("wide", "narrow")),
        ),
        out_specs=(P(), P(("wide", "narrow")), P()),
        check_vma=False,
    )
```

```python
import functools
import math

import jax
import jax.numpy as jnp
from jax import lax
from jax.experimental import pallas as pl
from jax.experimental.pallas import tpu as pltpu
from jax.sharding import PartitionSpec as P

COV = 128
LEVELS = 4
HB = 256
SKETCH = 1024
ITERS = 4
MIX_BITS = 3
MATES = 2**MIX_BITS

half_root = math.sqrt(0.5)
HIGHEST = lax.Precision.HIGHEST
f32, bf16 = jnp.float32, jnp.bfloat16
SUB, LANE = 8, 128
PACK = 16
NT = (((1,), (1,)), ((), ()))
VMEM = pl.BlockSpec(memory_space=pltpu.VMEM)
SMEM = pl.BlockSpec(memory_space=pltpu.SMEM)


def partner(value, axis, mask):
    pairs = [(source, source ^ mask) for source in range(lax.axis_size(axis))]
    return lax.ppermute(value, axis, pairs)


def whole_up(number, unit):
    return -(-number // unit) * unit


def eye():
    rows = lax.broadcasted_iota(jnp.int32, (LANE, LANE), 0)
    lanes = lax.broadcasted_iota(jnp.int32, (LANE, LANE), 1)
    return rows, lanes, rows == lanes


def to_column(row, same):
    return jnp.sum(jnp.where(same, row, 0.0), axis=1, keepdims=True)


def to_row(column, same):
    return jnp.sum(jnp.where(same, column, 0.0), axis=0, keepdims=True)


def split(value):
    parts = []
    for _ in range(3):
        parts.append(value.astype(bf16))
        value = value - parts[-1].astype(f32)
    return parts


def tree_sum(values):
    while len(values) > 1:
        values = [left + right for left, right in zip(values[0::2], values[1::2])]
    return values[0]


def put_sums(ref, start, share, extra):
    rows = share.shape[0]
    for k, part in enumerate(split(share)):
        ref[start : start + rows, k * LANE : (k + 1) * LANE] = part
    tail = jnp.zeros((rows - 3 * SUB, LANE), bf16)
    ref[start : start + rows, 3 * LANE :] = jnp.concatenate(split(extra) + [tail])


def take_sums(ref, start, rows):
    block = ref[start : start + rows, :].astype(f32)
    share = block[:, :LANE] + block[:, LANE : 2 * LANE] + block[:, 2 * LANE : 3 * LANE]
    tail = block[:, 3 * LANE :]
    return share, tail[:SUB] + tail[SUB : 2 * SUB] + tail[2 * SUB : 3 * SUB]


def design_kernel(cov_hbm, codes_hbm, signs_hbm, noise_hbm, design, packed, signs, *scratch):
    cov_ref, codes_ref, signs_ref, noise_ref, arrived = scratch
    moves = [
        pltpu.make_async_copy(source, target, arrived.at[k])
        for k, (source, target) in enumerate(
            ((cov_hbm, cov_ref), (codes_hbm, codes_ref), (signs_hbm, signs_ref), (noise_hbm, noise_ref))
        )
    ]
    for move in moves:
        move.start()
    for move in moves:
        move.wait()
    signs[...] = (1 - 2 * signs_ref[...]).astype(f32)
    rows, lanes, same = eye()
    zero = jnp.zeros((LANE, LANE), f32)
    for r in range(codes_ref.shape[0]):
        here = slice(r * LANE, (r + 1) * LANE)
        code = codes_ref[r : r + 1, :]
        turned = cov_ref[here, :].astype(f32).T
        for level in range(LEVELS):
            design[level * LANE : (level + 1) * LANE, here] = jnp.where(code == level, turned, zero).astype(bf16)
        noise = jnp.concatenate([noise_ref[r : r + 1, :]] * LEVELS + [jnp.zeros((PACK - LEVELS, LANE), f32)])
        level = lax.broadcasted_iota(jnp.int32, (PACK, LANE), 0)
        noise = jnp.where(code == level, noise, 0.0)
        for k, part in enumerate(split(noise)):
            design[LEVELS * LANE + k * PACK : LEVELS * LANE + (k + 1) * PACK, here] = part

    sums = jnp.dot(design[...], cov_ref[...], preferred_element_type=f32)
    normal = [sums[level * LANE : (level + 1) * LANE] for level in range(LEVELS)]
    back = sums[LEVELS * LANE :]
    back = back[:SUB] + back[PACK : PACK + SUB] + back[2 * PACK : 2 * PACK + SUB]
    extra = [jnp.sum(jnp.where(same, normal[level], 0.0), axis=0, keepdims=True) for level in (1, 3)]
    for pair in range(LEVELS // 2):
        packed[pair * LANE : (pair + 1) * LANE, :] = jnp.where(rows >= lanes, normal[2 * pair], normal[2 * pair + 1])
    rest = packed.shape[0] - SUB - 2 * LANE
    if rest:
        packed[2 * LANE : 2 * LANE + rest, :] = jnp.zeros((rest, LANE), f32)
    packed[2 * LANE + rest :, :] = jnp.concatenate([back[:LEVELS]] + extra + [jnp.zeros((2, LANE), f32)])


def local_kernel(samp, share, starts, index_ref, design_ref, packed_ref, signs_ref, *refs):
    want_refs, (stay_ref, go_ref, table) = refs[:-3], refs[-3:]
    chunks = signs_ref.shape[0]
    lanes = lax.broadcasted_iota(jnp.int32, (1, LANE), 1)
    wide_lanes, same = eye()[1:]
    zero = jnp.zeros((LANE, LANE), f32)
    pairs = LANE // (2 * samp)

    masks, halves = [], []
    for c in range(MATES // 2 // pairs):
        want = want_refs[c * pairs][...]
        for q in range(1, pairs):
            want = jnp.where(lanes >= 2 * samp * q, want_refs[c * pairs + q][...], want)
        want = to_column(want.astype(f32), same).astype(jnp.int32)
        masks.append(jnp.right_shift(want, HB.bit_length() - 1))
        line = []
        for h in range(HB // LANE):
            common = jnp.bitwise_and(want, wide_lanes + h * LANE)
            for shift in (4, 2, 1):
                common = jnp.bitwise_xor(common, jnp.right_shift(common, shift))
            line.append((1 - 2 * jnp.bitwise_and(common, 1)).astype(f32))
        halves.append(line)
    for r in range(chunks):
        sign = signs_ref[r : r + 1, :]
        block, h = divmod(r * LANE, HB)
        for c, (mask, line) in enumerate(zip(masks, halves)):
            value = jnp.where(mask == block, line[h // LANE] * sign, zero)
            table[c * LANE : (c + 1) * LANE, r * LANE : (r + 1) * LANE] = value.astype(bf16)

    local = lax.dot_general(table[...], design_ref[: LEVELS * LANE, :], NT, preferred_element_type=f32)
    local = (local * (1.0 / math.sqrt(HB))).astype(bf16)
    extra = packed_ref[packed_ref.shape[0] - SUB :, :]
    for m in range(2 * len(starts)):
        out_ref, start = (stay_ref, go_ref)[m % 2], starts[m // 2]
        if m < MATES:
            out_ref[start : start + samp, :] = local[m * samp : (m + 1) * samp]
            start += samp
        at = pl.multiple_of(jnp.bitwise_xor(index_ref[0], m) * share, share)
        put_sums(out_ref, start, packed_ref[pl.ds(at, share), :], extra)


def butterfly(pieces, place, index):
    bit = jnp.bitwise_and(jnp.right_shift(index, place), 1)
    sign = (1 - 2 * bit).astype(f32)
    return [
        ((sign * own + other) * half_root).astype(bf16).astype(f32) for own, other in zip(pieces[0::2], pieces[1::2])
    ]


def pair_kernel(samp, share, starts, index_ref, stay_ref, came_ref, *out_refs):
    for m, (start, out_ref) in enumerate(zip(starts, out_refs)):
        put = 0
        if 2 * m < MATES:
            here = slice(start, start + samp)
            pieces = [ref[here, :].astype(f32) for ref in (stay_ref, came_ref)]
            out_ref[:samp, :] = butterfly(pieces, 0, index_ref[0])[0].astype(bf16)
            put, start = samp, start + samp
        (own, own_extra), (other, other_extra) = [take_sums(ref, start, share) for ref in (stay_ref, came_ref)]
        put_sums(out_ref, put, own + other, own_extra + other_extra)


def mix_kernel(samp, share, index_ref, *refs):
    piece_refs, out_ref = refs[:-1], refs[-1]
    pieces = [ref[:samp, :].astype(f32) for ref in piece_refs[: MATES // 2]]
    for place in range(1, MIX_BITS):
        pieces = butterfly(pieces, place, index_ref[0])
    out_ref[:samp, :] = pieces[0].astype(bf16)
    sums = [take_sums(ref, samp if 2 * m < MATES else 0, share) for m, ref in enumerate(piece_refs)]
    put_sums(out_ref, samp, tree_sum([one for one, _ in sums]), tree_sum([one for _, one in sums]))


def stack_kernel(samp, share, index_ref, *refs):
    piece_refs, out_ref = refs[:-1], refs[-1]
    for m, ref in enumerate(piece_refs):
        at = pl.multiple_of(jnp.bitwise_xor(index_ref[1], m) * samp, samp)
        out_ref[pl.ds(at, samp), :] = ref[:samp, :]
    sums = [take_sums(ref, samp, share) for ref in piece_refs]
    put_sums(
        out_ref, samp * len(piece_refs), tree_sum([one for one, _ in sums]), tree_sum([one for _, one in sums])
    )


def spread(value):
    return jnp.broadcast_to(value, (SUB, LANE))


def reciprocal(value):
    return pltpu.reciprocal(value, approx=True)


def eliminate(tiles):
    lane = lax.broadcasted_iota(jnp.int32, (SUB, LANE), 1)
    sub = lax.broadcasted_iota(jnp.int32, (SUB, LANE), 0)
    tiles = list(tiles)
    scales = []
    for tile in range(len(tiles)):
        first = tile * SUB
        window = (lane >= first) & (lane < first + SUB)
        marks = [lane == first + k for k in range(SUB)]
        old = tiles[tile]
        columns = [spread(old[:, first + k : first + k + 1]) for k in range(SUB)]
        pivot = [[spread(columns[m][k : k + 1, :]) if m >= k else None for m in range(SUB)] for k in range(SUB)]
        cleared = jnp.where(window, 0.0, old)
        rows = [jnp.where(marks[k], 1.0, spread(cleared[k : k + 1, :])) for k in range(SUB)]
        steps, near, far = [None] * SUB, {}, {}
        kept, roots = [None] * SUB, [None] * SUB

        def keep(k, low, ratio, values, others):
            last = others[k + 1]
            kept[k] = rows[k]
            for m in range(k, SUB):
                kept[k] = jnp.where(marks[m], values[m], kept[k])
            kept[k + 1] = rows[k + 1] - ratio * rows[k]
            for m in range(k + 1, SUB):
                kept[k + 1] = jnp.where(marks[m], others[m], kept[k + 1])
            roots[k], roots[k + 1] = lax.rsqrt(low), lax.rsqrt(last)

        for k in range(0, SUB, 4):
            low, cross, high = pivot[k][k], pivot[k][k + 1], pivot[k + 1][k + 1]
            area = low * high - cross * cross
            drop = {}
            for m in range(k + 2, SUB):
                near[k, m] = high * pivot[k][m] - cross * pivot[k + 1][m]
                far[k, m] = low * pivot[k + 1][m] - cross * pivot[k][m]
            for m in range(k + 2, SUB):
                for n in range(m, SUB):
                    drop[m, n] = pivot[k][m] * near[k, n] + pivot[k + 1][m] * far[k, n]
            c, d = k + 2, k + 3
            grown = {(m, n): area * pivot[m][n] - drop[m, n] for m in (c, d) for n in range(m, SUB)}
            low2, cross2, high2 = grown[c, c], grown[c, d], grown[d, d]
            area2 = low2 * high2 - cross2 * cross2
            over, over2 = reciprocal(area), reciprocal(area2)
            for m in range(k + 4, SUB):
                near[c, m] = high2 * grown[c, m] - cross2 * grown[d, m]
                far[c, m] = low2 * grown[d, m] - cross2 * grown[c, m]
            for m in range(k + 4, SUB):
                for n in range(m, SUB):
                    drop2 = grown[c, m] * near[c, n] + grown[d, m] * far[c, n]
                    pivot[m][n] = pivot[m][n] - over * (drop[m, n] + over2 * drop2)
            for m in range(k + 2, SUB):
                near[k, m], far[k, m] = over * near[k, m], over * far[k, m]
                rows[m] = rows[m] - (near[k, m] * rows[k] + far[k, m] * rows[k + 1])
            for m in range(k + 4, SUB):
                near[c, m], far[c, m] = over2 * near[c, m], over2 * far[c, m]
                rows[m] = rows[m] - (near[c, m] * rows[c] + far[c, m] * rows[d])
            steps[k] = over * (high * rows[k] - cross * rows[k + 1])
            steps[k + 1] = over * (low * rows[k + 1] - cross * rows[k])
            both = area * over2
            steps[c] = both * (high2 * rows[c] - cross2 * rows[d])
            steps[d] = both * (low2 * rows[d] - cross2 * rows[c])

            inner = reciprocal(low)
            ratio = cross * inner
            values = {m: pivot[k][m] for m in range(k, SUB)}
            others = {m: pivot[k + 1][m] - ratio * pivot[k][m] for m in range(k + 2, SUB)}
            others[k + 1] = area * inner
            keep(k, low, ratio, values, others)
            inner = reciprocal(low2)
            ratio = cross2 * inner
            values = {m: over * grown[c, m] for m in range(c, SUB)}
            others = {m: over * (grown[d, m] - ratio * grown[c, m]) for m in range(c + 2, SUB)}
            others[d] = over * (area2 * inner)
            keep(c, values[c], ratio, values, others)
        for k in reversed(range(0, SUB, 2)):
            for m in reversed(range(k + 2, SUB)):
                steps[k] = steps[k] - near[k, m] * steps[m]
                steps[k + 1] = steps[k + 1] - far[k, m] * steps[m]
        for i in range(tile + 1, len(tiles)):
            change = [spread(tiles[i][:, first + k : first + k + 1]) * steps[k] for k in range(SUB)]
            tiles[i] = jnp.where(window, 0.0, tiles[i]) - tree_sum(change[::-1])
        new, scale = kept[0], roots[0]
        for k in range(1, SUB):
            new = jnp.where(sub >= k, kept[k], new)
            scale = jnp.where(sub >= k, roots[k], scale)
        tiles[tile] = new
        scales.append(scale)
    return tiles, scales


LEFT, RIGHT = (0, 1, 0, 1, 2, 0), (0, 0, 1, 1, 0, 2)


def parts_of(value, order, axis):
    parts = split(value)
    return jnp.concatenate([parts[k] for k in order], axis=axis)


def take_gram(rows_in, index_ref, piece_refs, sketch):
    for m, ref in enumerate(piece_refs):
        at = jnp.bitwise_xor(jnp.right_shift(index_ref[0], 1), m) * rows_in
        sketch[pl.ds(pl.multiple_of(at, rows_in), rows_in), :] = ref[:rows_in, :]
    rows = sketch[...]
    return lax.dot_general(rows, rows, (((0,), (0,)), ((), ())), preferred_element_type=f32)


def gram_kernel(rows_in, index_ref, *refs):
    piece_refs, (gram_ref, sketch) = refs[:-2], refs[-2:]
    gram_ref[...] = take_gram(rows_in, index_ref, piece_refs, sketch)


def factor_kernel(ratio, rows_in, index_ref, gram_ref, *refs):
    piece_refs, (factor_ref, inverse_ref, sketch, work) = refs[:-4], refs[-4:]
    cols = work.shape[0]
    work[...] = gram_ref[...] + take_gram(rows_in, index_ref, piece_refs, sketch)
    _, _, same = eye()
    diagonal = []
    for at in range(0, cols, LANE):
        block = work[at : at + LANE, at : at + LANE]
        diagonal.append(jnp.sum(jnp.where(same, block, 0.0), axis=0, keepdims=True))
    unit = [lax.rsqrt(part) for part in diagonal]
    level = jnp.concatenate([part * one for part, one in zip(diagonal, unit)], axis=1) * ratio
    unit_row = jnp.concatenate(unit, axis=1)
    for at, one in zip(range(0, cols, LANE), unit):
        work[at : at + LANE, :] = work[at : at + LANE, :] * to_column(one, same) * unit_row

    row_in = lax.broadcasted_iota(jnp.int32, (LANE, LANE), 0)
    lane_in = lax.broadcasted_iota(jnp.int32, (LANE, LANE), 1)
    for base in range(0, cols, LANE):
        end = base + LANE
        here = slice(base, end)
        tiles = [work[base + SUB * i : base + SUB * (i + 1), here] for i in range(LANE // SUB)]
        tiles, scales = eliminate(tiles)
        scale = jnp.concatenate(scales)
        inner = jnp.concatenate(tiles) * scale
        upper = jnp.where(lane_in >= row_in, inner, 0.0)
        lower = jnp.where(lane_in < row_in, inner, jnp.where(lane_in == row_in, scale, 0.0))
        line = jnp.dot(parts_of(lower, LEFT, 1), parts_of(work[here, :], RIGHT, 0), preferred_element_type=f32)
        if end < cols:
            panel = parts_of(work[end:, here], LEFT, 1)
            panel = lax.dot_general(panel, parts_of(lower, RIGHT, 1), NT, preferred_element_type=f32)
            panel = parts_of(panel, LEFT, 1)
            steps = ([line[:, :base]] if base else []) + [lower, line[:, end:]]
            steps = parts_of(jnp.concatenate(steps, axis=1), RIGHT, 0)
            work[end:, here] = jnp.zeros((cols - end, LANE), f32)
            for start, stop in ((0, LANE), (LANE, cols - end)):
                if start < stop:
                    change = jnp.dot(panel[start:stop], steps, preferred_element_type=f32)
                    work[end + start : end + stop, :] = work[end + start : end + stop, :] - change
        factor_ref[here, here] = upper * level[:, here]
        inverse_ref[here, here] = lower * unit_row[:, here]
        if base:
            factor_ref[here, :base] = jnp.zeros((LANE, base), f32)
            inverse_ref[here, :base] = line[:, :base] * unit_row[:, :base]
        if end < cols:
            factor_ref[here, end:] = line[:, end:] * level[:, end:]
            inverse_ref[here, end:] = jnp.zeros((LANE, cols - end), f32)


def solve_kernel(apart, rows_in, share, index_ref, inverse_ref, effects_ref, cov_ref, codes_ref, noise_ref, *refs):
    piece_refs, (solved_ref, resid_ref, packed) = refs[:-3], refs[-3:]
    rows, lanes, same = eye()
    extra = None
    for mask, ref in zip(apart, piece_refs):
        at = pl.multiple_of(jnp.bitwise_xor(index_ref[0], mask) * share, share)
        packed[pl.ds(at, share), :], more = take_sums(ref, rows_in, share)
        extra = more if extra is None else extra
    normal = []
    for pair in range(LEVELS // 2):
        both = packed[pair * LANE : (pair + 1) * LANE, :]
        turned = both.T
        normal.append(jnp.where(rows >= lanes, both, turned))
        diagonal = jnp.where(same, extra[LEVELS + pair : LEVELS + pair + 1], turned)
        normal.append(jnp.where(rows < lanes, both, diagonal))

    inverse = inverse_ref[...]
    spans = [slice(level * LANE, (level + 1) * LANE) for level in range(LEVELS)]
    gradient = []
    for level in range(LEVELS):
        column = to_column(effects_ref[level : level + 1, :], same)
        gradient.append(jnp.sum(normal[level] * column, axis=0, keepdims=True) + extra[level : level + 1])
    steer = jnp.sum(inverse * jnp.concatenate(gradient, axis=1), axis=1, keepdims=True)
    direction = steer
    gamma = jnp.sum(steer * steer, axis=0, keepdims=True)
    solved = jnp.zeros((1, cov_ref.shape[1] * LEVELS), f32)
    for step in range(ITERS):
        move = jnp.sum(inverse * direction, axis=0, keepdims=True)
        image = []
        for level, span in enumerate(spans):
            image.append(jnp.sum(normal[level] * to_column(move[:, span], same), axis=0, keepdims=True))
        image = jnp.concatenate(image, axis=1)
        alpha = gamma / jnp.sum(move * image, axis=1, keepdims=True)
        solved = solved + alpha * move
        if step == ITERS - 1:
            break
        steer = steer - alpha * jnp.sum(inverse * image, axis=1, keepdims=True)
        gamma_new = jnp.sum(steer * steer, axis=0, keepdims=True)
        direction = steer + gamma_new / gamma * direction
        gamma = gamma_new
    solved = jnp.concatenate([solved[:, span] for span in spans])
    solved_ref[...] = solved

    left = jnp.concatenate([effects_ref[...] - solved, jnp.zeros((PACK - LEVELS, LANE), f32)])
    values = jnp.zeros((SUB, cov_ref.shape[0]), f32)
    for part in split(left):
        values = values + lax.dot_general(part, cov_ref[...], NT, preferred_element_type=f32)[:SUB]
    for r in range(codes_ref.shape[0]):
        code = codes_ref[r : r + 1, :]
        total = noise_ref[r : r + 1, :]
        for level in range(LEVELS):
            total = total + jnp.where(code == level, values[level : level + 1, r * LANE : (r + 1) * LANE], 0.0)
        resid_ref[r : r + 1, :] = total


def call(kernel, name, outs, scratch, *operands):
    return pl.pallas_call(
        kernel,
        out_shape=[jax.ShapeDtypeStruct(shape, dtype) for shape, dtype in outs],
        in_specs=[SMEM if operand.ndim == 1 else VMEM for operand in operands],
        out_specs=[VMEM] * len(outs),
        scratch_shapes=[pltpu.VMEM(shape, dtype) for shape, dtype in scratch],
        compiler_params=pltpu.CompilerParams(vmem_limit_bytes=40 * 2**20),
        name=name,
    )(*operands)


def body(covariates, level_codes, sign_bits, sample_rows, effects, noise):
    wide, narrow = lax.axis_size("wide"), lax.axis_size("narrow")
    index = jnp.stack([lax.axis_index("wide"), lax.axis_index("narrow")]).astype(jnp.int32)
    rows_dev, cols = covariates.shape[0], LEVELS * COV
    samp = whole_up(sample_rows.shape[0], PACK)
    share = whole_up(max(2 * LANE // wide, 3 * SUB), PACK)
    sample_rows = jnp.pad(sample_rows, (0, samp - sample_rows.shape[0]), constant_values=-1)
    codes, signs, noise = [array.reshape(-1, LANE) for array in (level_codes, sign_bits, noise)]
    effects = effects.reshape(LEVELS, COV)

    want = jnp.concatenate([sample_rows, partner(sample_rows, "wide", 1)] * (LANE // (2 * samp)))[None, :]
    want = [want] + [partner(want, "wide", m) for m in range(2, MATES, 2)]

    anywhere = pl.BlockSpec(memory_space=pl.ANY)
    operands = (covariates, codes, signs, noise)
    design, packed, signs = pl.pallas_call(
        design_kernel,
        out_shape=[
            jax.ShapeDtypeStruct((cols + 3 * PACK, rows_dev), bf16),
            jax.ShapeDtypeStruct((share * wide + SUB, LANE), f32),
            jax.ShapeDtypeStruct(signs.shape, f32),
        ],
        in_specs=[anywhere] * 4,
        out_specs=[VMEM] * 3,
        scratch_shapes=[pltpu.VMEM(operand.shape, operand.dtype) for operand in operands]
        + [pltpu.SemaphoreType.DMA((4,))],
        compiler_params=pltpu.CompilerParams(vmem_limit_bytes=40 * 2**20),
        name="design",
    )(*operands)
    sizes = [samp * (2 * m < MATES) + share for m in range(wide // 2)]
    starts = [sum(sizes[:m]) for m in range(wide // 2)]
    stay, go = call(
        functools.partial(local_kernel, samp, share, starts),
        "local",
        [((sum(sizes), cols), bf16)] * 2,
        [((MATES * samp, rows_dev), bf16)],
        index,
        design,
        packed,
        signs,
        *want,
    )
    pieces = call(
        functools.partial(pair_kernel, samp, share, starts),
        "pair",
        [((size, cols), bf16) for size in sizes],
        [],
        index,
        stay,
        partner(go, "wide", 1),
    )
    pieces = [pieces[0]] + [partner(pieces[m], "wide", 2 * m) for m in range(1, wide // 2)]
    (piece,) = call(
        functools.partial(mix_kernel, samp, share), "mix", [((samp + share, cols), bf16)], [], index, *pieces
    )
    pieces = [piece] + [partner(piece, "narrow", m) for m in range(1, narrow)]
    rows_in = samp * narrow
    (piece,) = call(
        functools.partial(stack_kernel, samp, share), "stack", [((rows_in + share, cols), bf16)], [], index, *pieces
    )
    pieces = [piece] + [partner(piece, "wide", m) for m in range(2, wide, 2)]
    theirs = [partner(piece, "wide", 1) for piece in pieces]
    sketch = [((rows_in * (wide // 2), cols), bf16)]
    square = ((cols, cols), f32)
    (gram,) = call(functools.partial(gram_kernel, rows_in), "gram", [square], sketch, index, *pieces)
    factor, inverse = call(
        functools.partial(factor_kernel, math.sqrt(LEVELS / SKETCH), rows_in),
        "factor",
        [square] * 2,
        sketch + [square],
        index,
        gram,
        *theirs,
    )
    pieces += theirs
    apart = [2 * m + core for core in range(2) for m in range(wide // 2)]
    solved, resid = call(
        functools.partial(solve_kernel, apart, rows_in, share),
        "solve",
        [((LEVELS, COV), f32), (codes.shape, f32)],
        [((share * wide, LANE), f32)],
        index,
        inverse,
        effects,
        covariates,
        codes,
        noise,
        *pieces,
    )
    return solved.reshape(-1), resid.reshape(-1), factor


def solution(mesh):
    return jax.shard_map(
        body,
        mesh=mesh,
        in_specs=(
            P(("wide", "narrow"), None),
            P(("wide", "narrow")),
            P(("wide", "narrow")),
            P(("wide", "narrow")),
            P(),
            P(("wide", "narrow")),
        ),
        out_specs=(P(), P(("wide", "narrow")), P()),
        check_vma=False,
    )
```

```python
import functools
import math

import jax
import jax.numpy as jnp
from jax import lax
from jax.experimental import pallas as pl
from jax.experimental.pallas import tpu as pltpu
from jax.sharding import PartitionSpec as P

COV = 128
LEVELS = 4
HB = 256
SKETCH = 1024
ITERS = 4
MIX_BITS = 3
MATES = 2**MIX_BITS

half_root = math.sqrt(0.5)
HIGHEST = lax.Precision.HIGHEST
f32, bf16 = jnp.float32, jnp.bfloat16
SUB, LANE = 8, 128
PACK = 16
NT = (((1,), (1,)), ((), ()))
VMEM = pl.BlockSpec(memory_space=pltpu.VMEM)
SMEM = pl.BlockSpec(memory_space=pltpu.SMEM)


def partner(value, axis, mask):
    pairs = [(source, source ^ mask) for source in range(lax.axis_size(axis))]
    return lax.ppermute(value, axis, pairs)


def whole_up(number, unit):
    return -(-number // unit) * unit


def eye():
    rows = lax.broadcasted_iota(jnp.int32, (LANE, LANE), 0)
    lanes = lax.broadcasted_iota(jnp.int32, (LANE, LANE), 1)
    return rows, lanes, rows == lanes


def to_column(row, same):
    return jnp.sum(jnp.where(same, row, 0.0), axis=1, keepdims=True)


def to_row(column, same):
    return jnp.sum(jnp.where(same, column, 0.0), axis=0, keepdims=True)


def split(value):
    parts = []
    for _ in range(3):
        parts.append(value.astype(bf16))
        value = value - parts[-1].astype(f32)
    return parts


def tree_sum(values):
    while len(values) > 1:
        values = [left + right for left, right in zip(values[0::2], values[1::2])]
    return values[0]


def put_sums(ref, start, share, extra):
    rows = share.shape[0]
    for k, part in enumerate(split(share)):
        ref[start : start + rows, k * LANE : (k + 1) * LANE] = part
    tail = jnp.zeros((rows - 3 * SUB, LANE), bf16)
    ref[start : start + rows, 3 * LANE :] = jnp.concatenate(split(extra) + [tail])


def take_sums(ref, start, rows):
    block = ref[start : start + rows, :].astype(f32)
    share = block[:, :LANE] + block[:, LANE : 2 * LANE] + block[:, 2 * LANE : 3 * LANE]
    tail = block[:, 3 * LANE :]
    return share, tail[:SUB] + tail[SUB : 2 * SUB] + tail[2 * SUB : 3 * SUB]


def design_kernel(cov_hbm, codes_hbm, signs_hbm, noise_hbm, design, packed, signs, *scratch):
    cov_ref, codes_ref, signs_ref, noise_ref, arrived = scratch
    moves = [
        pltpu.make_async_copy(source, target, arrived.at[k])
        for k, (source, target) in enumerate(
            ((cov_hbm, cov_ref), (codes_hbm, codes_ref), (signs_hbm, signs_ref), (noise_hbm, noise_ref))
        )
    ]
    for move in moves:
        move.start()
    for move in moves:
        move.wait()
    signs[...] = (1 - 2 * signs_ref[...]).astype(f32)
    rows, lanes, same = eye()
    zero = jnp.zeros((LANE, LANE), f32)
    for r in range(codes_ref.shape[0]):
        here = slice(r * LANE, (r + 1) * LANE)
        code = codes_ref[r : r + 1, :]
        turned = cov_ref[here, :].astype(f32).T
        for level in range(LEVELS):
            design[level * LANE : (level + 1) * LANE, here] = jnp.where(code == level, turned, zero).astype(bf16)
        noise = jnp.concatenate([noise_ref[r : r + 1, :]] * LEVELS + [jnp.zeros((PACK - LEVELS, LANE), f32)])
        level = lax.broadcasted_iota(jnp.int32, (PACK, LANE), 0)
        noise = jnp.where(code == level, noise, 0.0)
        for k, part in enumerate(split(noise)):
            design[LEVELS * LANE + k * PACK : LEVELS * LANE + (k + 1) * PACK, here] = part

    sums = jnp.dot(design[...], cov_ref[...], preferred_element_type=f32)
    normal = [sums[level * LANE : (level + 1) * LANE] for level in range(LEVELS)]
    back = sums[LEVELS * LANE :]
    back = back[:SUB] + back[PACK : PACK + SUB] + back[2 * PACK : 2 * PACK + SUB]
    extra = [jnp.sum(jnp.where(same, normal[level], 0.0), axis=0, keepdims=True) for level in (1, 3)]
    for pair in range(LEVELS // 2):
        packed[pair * LANE : (pair + 1) * LANE, :] = jnp.where(rows >= lanes, normal[2 * pair], normal[2 * pair + 1])
    rest = packed.shape[0] - SUB - 2 * LANE
    if rest:
        packed[2 * LANE : 2 * LANE + rest, :] = jnp.zeros((rest, LANE), f32)
    packed[2 * LANE + rest :, :] = jnp.concatenate([back[:LEVELS]] + extra + [jnp.zeros((2, LANE), f32)])


def local_kernel(samp, share, starts, index_ref, design_ref, packed_ref, signs_ref, *refs):
    want_refs, (stay_ref, go_ref, table) = refs[:-3], refs[-3:]
    chunks = signs_ref.shape[0]
    lanes = lax.broadcasted_iota(jnp.int32, (1, LANE), 1)
    wide_lanes, same = eye()[1:]
    zero = jnp.zeros((LANE, LANE), f32)
    pairs = LANE // (2 * samp)

    masks, halves = [], []
    for c in range(MATES // 2 // pairs):
        want = want_refs[c * pairs][...]
        for q in range(1, pairs):
            want = jnp.where(lanes >= 2 * samp * q, want_refs[c * pairs + q][...], want)
        want = to_column(want.astype(f32), same).astype(jnp.int32)
        masks.append(jnp.right_shift(want, HB.bit_length() - 1))
        line = []
        for h in range(HB // LANE):
            common = jnp.bitwise_and(want, wide_lanes + h * LANE)
            for shift in (4, 2, 1):
                common = jnp.bitwise_xor(common, jnp.right_shift(common, shift))
            line.append((1 - 2 * jnp.bitwise_and(common, 1)).astype(f32))
        halves.append(line)
    for r in range(chunks):
        sign = signs_ref[r : r + 1, :]
        block, h = divmod(r * LANE, HB)
        for c, (mask, line) in enumerate(zip(masks, halves)):
            value = jnp.where(mask == block, line[h // LANE] * sign, zero)
            table[c * LANE : (c + 1) * LANE, r * LANE : (r + 1) * LANE] = value.astype(bf16)

    local = lax.dot_general(table[...], design_ref[: LEVELS * LANE, :], NT, preferred_element_type=f32)
    local = (local * (1.0 / math.sqrt(HB))).astype(bf16)
    extra = packed_ref[packed_ref.shape[0] - SUB :, :]
    for m in range(2 * len(starts)):
        out_ref, start = (stay_ref, go_ref)[m % 2], starts[m // 2]
        if m < MATES:
            out_ref[start : start + samp, :] = local[m * samp : (m + 1) * samp]
            start += samp
        at = pl.multiple_of(jnp.bitwise_xor(index_ref[0], m) * share, share)
        put_sums(out_ref, start, packed_ref[pl.ds(at, share), :], extra)


def butterfly(pieces, place, index):
    bit = jnp.bitwise_and(jnp.right_shift(index, place), 1)
    sign = (1 - 2 * bit).astype(f32)
    return [
        ((sign * own + other) * half_root).astype(bf16).astype(f32) for own, other in zip(pieces[0::2], pieces[1::2])
    ]


def pair_kernel(samp, share, starts, index_ref, stay_ref, came_ref, *out_refs):
    for m, (start, out_ref) in enumerate(zip(starts, out_refs)):
        put = 0
        if 2 * m < MATES:
            here = slice(start, start + samp)
            pieces = [ref[here, :].astype(f32) for ref in (stay_ref, came_ref)]
            out_ref[:samp, :] = butterfly(pieces, 0, index_ref[0])[0].astype(bf16)
            put, start = samp, start + samp
        (own, own_extra), (other, other_extra) = [take_sums(ref, start, share) for ref in (stay_ref, came_ref)]
        put_sums(out_ref, put, own + other, own_extra + other_extra)


def mix_kernel(samp, share, index_ref, *refs):
    piece_refs, out_ref = refs[:-1], refs[-1]
    pieces = [ref[:samp, :].astype(f32) for ref in piece_refs[: MATES // 2]]
    for place in range(1, MIX_BITS):
        pieces = butterfly(pieces, place, index_ref[0])
    out_ref[:samp, :] = pieces[0].astype(bf16)
    sums = [take_sums(ref, samp if 2 * m < MATES else 0, share) for m, ref in enumerate(piece_refs)]
    put_sums(out_ref, samp, tree_sum([one for one, _ in sums]), tree_sum([one for _, one in sums]))


def stack_kernel(samp, share, index_ref, *refs):
    piece_refs, out_ref = refs[:-1], refs[-1]
    for m, ref in enumerate(piece_refs):
        at = pl.multiple_of(jnp.bitwise_xor(index_ref[1], m) * samp, samp)
        out_ref[pl.ds(at, samp), :] = ref[:samp, :]
    sums = [take_sums(ref, samp, share) for ref in piece_refs]
    put_sums(
        out_ref, samp * len(piece_refs), tree_sum([one for one, _ in sums]), tree_sum([one for _, one in sums])
    )


def spread(value):
    return jnp.broadcast_to(value, (SUB, LANE))


def reciprocal(value):
    return pltpu.reciprocal(value, approx=True)


def eliminate(tiles):
    lane = lax.broadcasted_iota(jnp.int32, (SUB, LANE), 1)
    sub = lax.broadcasted_iota(jnp.int32, (SUB, LANE), 0)
    tiles = list(tiles)
    scales = []
    for tile in range(len(tiles)):
        first = tile * SUB
        window = (lane >= first) & (lane < first + SUB)
        marks = [lane == first + k for k in range(SUB)]
        old = tiles[tile]
        columns = [spread(old[:, first + k : first + k + 1]) for k in range(SUB)]
        pivot = [[spread(columns[m][k : k + 1, :]) if m >= k else None for m in range(SUB)] for k in range(SUB)]
        cleared = jnp.where(window, 0.0, old)
        rows = [jnp.where(marks[k], 1.0, spread(cleared[k : k + 1, :])) for k in range(SUB)]
        steps, near, far = [None] * SUB, {}, {}
        kept, roots = [None] * SUB, [None] * SUB

        def keep(k, low, ratio, values, others):
            last = others[k + 1]
            kept[k] = rows[k]
            for m in range(k, SUB):
                kept[k] = jnp.where(marks[m], values[m], kept[k])
            kept[k + 1] = rows[k + 1] - ratio * rows[k]
            for m in range(k + 1, SUB):
                kept[k + 1] = jnp.where(marks[m], others[m], kept[k + 1])
            roots[k], roots[k + 1] = lax.rsqrt(low), lax.rsqrt(last)

        for k in range(0, SUB, 4):
            low, cross, high = pivot[k][k], pivot[k][k + 1], pivot[k + 1][k + 1]
            area = low * high - cross * cross
            drop = {}
            for m in range(k + 2, SUB):
                near[k, m] = high * pivot[k][m] - cross * pivot[k + 1][m]
                far[k, m] = low * pivot[k + 1][m] - cross * pivot[k][m]
            for m in range(k + 2, SUB):
                for n in range(m, SUB):
                    drop[m, n] = pivot[k][m] * near[k, n] + pivot[k + 1][m] * far[k, n]
            c, d = k + 2, k + 3
            grown = {(m, n): area * pivot[m][n] - drop[m, n] for m in (c, d) for n in range(m, SUB)}
            low2, cross2, high2 = grown[c, c], grown[c, d], grown[d, d]
            area2 = low2 * high2 - cross2 * cross2
            over, over2 = reciprocal(area), reciprocal(area2)
            for m in range(k + 4, SUB):
                near[c, m] = high2 * grown[c, m] - cross2 * grown[d, m]
                far[c, m] = low2 * grown[d, m] - cross2 * grown[c, m]
            for m in range(k + 4, SUB):
                for n in range(m, SUB):
                    drop2 = grown[c, m] * near[c, n] + grown[d, m] * far[c, n]
                    pivot[m][n] = pivot[m][n] - over * (drop[m, n] + over2 * drop2)
            for m in range(k + 2, SUB):
                near[k, m], far[k, m] = over * near[k, m], over * far[k, m]
                rows[m] = rows[m] - (near[k, m] * rows[k] + far[k, m] * rows[k + 1])
            for m in range(k + 4, SUB):
                near[c, m], far[c, m] = over2 * near[c, m], over2 * far[c, m]
                rows[m] = rows[m] - (near[c, m] * rows[c] + far[c, m] * rows[d])
            steps[k] = over * (high * rows[k] - cross * rows[k + 1])
            steps[k + 1] = over * (low * rows[k + 1] - cross * rows[k])
            both = area * over2
            steps[c] = both * (high2 * rows[c] - cross2 * rows[d])
            steps[d] = both * (low2 * rows[d] - cross2 * rows[c])

            inner = reciprocal(low)
            ratio = cross * inner
            values = {m: pivot[k][m] for m in range(k, SUB)}
            others = {m: pivot[k + 1][m] - ratio * pivot[k][m] for m in range(k + 2, SUB)}
            others[k + 1] = area * inner
            keep(k, low, ratio, values, others)
            inner = reciprocal(low2)
            ratio = cross2 * inner
            values = {m: over * grown[c, m] for m in range(c, SUB)}
            others = {m: over * (grown[d, m] - ratio * grown[c, m]) for m in range(c + 2, SUB)}
            others[d] = over * (area2 * inner)
            keep(c, values[c], ratio, values, others)
        if tile + 1 < len(tiles):
            after = tiles[tile + 1]
            ahead = [spread(after[:, first + k : first + k + 1]) for k in range(SUB)]
            fresh = jnp.where(window, 0.0, after)
            for k in range(0, SUB, 2):
                for m in range(k + 2, SUB):
                    ahead[m] = ahead[m] - (near[k, m] * ahead[k] + far[k, m] * ahead[k + 1])
                fresh = fresh - (ahead[k] * steps[k] + ahead[k + 1] * steps[k + 1])
        for k in reversed(range(0, SUB, 2)):
            for m in reversed(range(k + 2, SUB)):
                steps[k] = steps[k] - near[k, m] * steps[m]
                steps[k + 1] = steps[k + 1] - far[k, m] * steps[m]
        for i in range(tile + 2, len(tiles)):
            change = [spread(tiles[i][:, first + k : first + k + 1]) * steps[k] for k in range(SUB)]
            tiles[i] = jnp.where(window, 0.0, tiles[i]) - tree_sum(change[::-1])
        if tile + 1 < len(tiles):
            tiles[tile + 1] = fresh
        new, scale = kept[0], roots[0]
        for k in range(1, SUB):
            new = jnp.where(sub >= k, kept[k], new)
            scale = jnp.where(sub >= k, roots[k], scale)
        tiles[tile] = new
        scales.append(scale)
    return tiles, scales


LEFT, RIGHT = (0, 1, 0, 1, 2, 0), (0, 0, 1, 1, 0, 2)


def parts_of(value, order, axis):
    parts = split(value)
    return jnp.concatenate([parts[k] for k in order], axis=axis)


def take_gram(rows_in, index_ref, piece_refs, sketch):
    for m, ref in enumerate(piece_refs):
        at = jnp.bitwise_xor(jnp.right_shift(index_ref[0], 1), m) * rows_in
        sketch[pl.ds(pl.multiple_of(at, rows_in), rows_in), :] = ref[:rows_in, :]
    rows = sketch[...]
    return lax.dot_general(rows, rows, (((0,), (0,)), ((), ())), preferred_element_type=f32)


def gram_kernel(rows_in, index_ref, *refs):
    piece_refs, (gram_ref, sketch) = refs[:-2], refs[-2:]
    gram_ref[...] = take_gram(rows_in, index_ref, piece_refs, sketch)


def factor_kernel(ratio, rows_in, index_ref, gram_ref, *refs):
    piece_refs, (factor_ref, inverse_ref, sketch, work) = refs[:-4], refs[-4:]
    cols = work.shape[0]
    work[...] = gram_ref[...] + take_gram(rows_in, index_ref, piece_refs, sketch)
    _, _, same = eye()
    diagonal = []
    for at in range(0, cols, LANE):
        block = work[at : at + LANE, at : at + LANE]
        diagonal.append(jnp.sum(jnp.where(same, block, 0.0), axis=0, keepdims=True))
    unit = [lax.rsqrt(part) for part in diagonal]
    level = jnp.concatenate([part * one for part, one in zip(diagonal, unit)], axis=1) * ratio
    unit_row = jnp.concatenate(unit, axis=1)
    for at, one in zip(range(0, cols, LANE), unit):
        work[at : at + LANE, :] = work[at : at + LANE, :] * to_column(one, same) * unit_row

    row_in = lax.broadcasted_iota(jnp.int32, (LANE, LANE), 0)
    lane_in = lax.broadcasted_iota(jnp.int32, (LANE, LANE), 1)
    for base in range(0, cols, LANE):
        end = base + LANE
        here = slice(base, end)
        tiles = [work[base + SUB * i : base + SUB * (i + 1), here] for i in range(LANE // SUB)]
        tiles, scales = eliminate(tiles)
        scale = jnp.concatenate(scales)
        inner = jnp.concatenate(tiles) * scale
        upper = jnp.where(lane_in >= row_in, inner, 0.0)
        lower = jnp.where(lane_in < row_in, inner, jnp.where(lane_in == row_in, scale, 0.0))
        line = jnp.dot(parts_of(lower, LEFT, 1), parts_of(work[here, :], RIGHT, 0), preferred_element_type=f32)
        if end < cols:
            panel = parts_of(work[end:, here], LEFT, 1)
            panel = lax.dot_general(panel, parts_of(lower, RIGHT, 1), NT, preferred_element_type=f32)
            panel = parts_of(panel, LEFT, 1)
            steps = ([line[:, :base]] if base else []) + [lower, line[:, end:]]
            steps = parts_of(jnp.concatenate(steps, axis=1), RIGHT, 0)
            work[end:, here] = jnp.zeros((cols - end, LANE), f32)
            for start, stop in ((0, LANE), (LANE, cols - end)):
                if start < stop:
                    change = jnp.dot(panel[start:stop], steps, preferred_element_type=f32)
                    work[end + start : end + stop, :] = work[end + start : end + stop, :] - change
        factor_ref[here, here] = upper * level[:, here]
        inverse_ref[here, here] = lower * unit_row[:, here]
        if base:
            factor_ref[here, :base] = jnp.zeros((LANE, base), f32)
            inverse_ref[here, :base] = line[:, :base] * unit_row[:, :base]
        if end < cols:
            factor_ref[here, end:] = line[:, end:] * level[:, end:]
            inverse_ref[here, end:] = jnp.zeros((LANE, cols - end), f32)


def solve_kernel(apart, rows_in, share, index_ref, inverse_ref, effects_ref, cov_ref, codes_ref, noise_ref, *refs):
    piece_refs, (solved_ref, resid_ref, packed) = refs[:-3], refs[-3:]
    rows, lanes, same = eye()
    extra = None
    for mask, ref in zip(apart, piece_refs):
        at = pl.multiple_of(jnp.bitwise_xor(index_ref[0], mask) * share, share)
        packed[pl.ds(at, share), :], more = take_sums(ref, rows_in, share)
        extra = more if extra is None else extra
    normal = []
    for pair in range(LEVELS // 2):
        both = packed[pair * LANE : (pair + 1) * LANE, :]
        turned = both.T
        normal.append(jnp.where(rows >= lanes, both, turned))
        diagonal = jnp.where(same, extra[LEVELS + pair : LEVELS + pair + 1], turned)
        normal.append(jnp.where(rows < lanes, both, diagonal))

    inverse = inverse_ref[...]
    spans = [slice(level * LANE, (level + 1) * LANE) for level in range(LEVELS)]
    gradient = []
    for level in range(LEVELS):
        column = to_column(effects_ref[level : level + 1, :], same)
        gradient.append(jnp.sum(normal[level] * column, axis=0, keepdims=True) + extra[level : level + 1])
    steer = jnp.sum(inverse * jnp.concatenate(gradient, axis=1), axis=1, keepdims=True)
    direction = steer
    gamma = jnp.sum(steer * steer, axis=0, keepdims=True)
    solved = jnp.zeros((1, cov_ref.shape[1] * LEVELS), f32)
    for step in range(ITERS):
        move = jnp.sum(inverse * direction, axis=0, keepdims=True)
        image = []
        for level, span in enumerate(spans):
            image.append(jnp.sum(normal[level] * to_column(move[:, span], same), axis=0, keepdims=True))
        image = jnp.concatenate(image, axis=1)
        alpha = gamma / jnp.sum(move * image, axis=1, keepdims=True)
        solved = solved + alpha * move
        if step == ITERS - 1:
            break
        steer = steer - alpha * jnp.sum(inverse * image, axis=1, keepdims=True)
        gamma_new = jnp.sum(steer * steer, axis=0, keepdims=True)
        direction = steer + gamma_new / gamma * direction
        gamma = gamma_new
    solved = jnp.concatenate([solved[:, span] for span in spans])
    solved_ref[...] = solved

    left = jnp.concatenate([effects_ref[...] - solved, jnp.zeros((PACK - LEVELS, LANE), f32)])
    values = jnp.zeros((SUB, cov_ref.shape[0]), f32)
    for part in split(left):
        values = values + lax.dot_general(part, cov_ref[...], NT, preferred_element_type=f32)[:SUB]
    for r in range(codes_ref.shape[0]):
        code = codes_ref[r : r + 1, :]
        total = noise_ref[r : r + 1, :]
        for level in range(LEVELS):
            total = total + jnp.where(code == level, values[level : level + 1, r * LANE : (r + 1) * LANE], 0.0)
        resid_ref[r : r + 1, :] = total


def call(kernel, name, outs, scratch, *operands):
    return pl.pallas_call(
        kernel,
        out_shape=[jax.ShapeDtypeStruct(shape, dtype) for shape, dtype in outs],
        in_specs=[SMEM if operand.ndim == 1 else VMEM for operand in operands],
        out_specs=[VMEM] * len(outs),
        scratch_shapes=[pltpu.VMEM(shape, dtype) for shape, dtype in scratch],
        compiler_params=pltpu.CompilerParams(vmem_limit_bytes=40 * 2**20),
        name=name,
    )(*operands)


def body(covariates, level_codes, sign_bits, sample_rows, effects, noise):
    wide, narrow = lax.axis_size("wide"), lax.axis_size("narrow")
    index = jnp.stack([lax.axis_index("wide"), lax.axis_index("narrow")]).astype(jnp.int32)
    rows_dev, cols = covariates.shape[0], LEVELS * COV
    samp = whole_up(sample_rows.shape[0], PACK)
    share = whole_up(max(2 * LANE // wide, 3 * SUB), PACK)
    sample_rows = jnp.pad(sample_rows, (0, samp - sample_rows.shape[0]), constant_values=-1)
    codes, signs, noise = [array.reshape(-1, LANE) for array in (level_codes, sign_bits, noise)]
    effects = effects.reshape(LEVELS, COV)

    want = jnp.concatenate([sample_rows, partner(sample_rows, "wide", 1)] * (LANE // (2 * samp)))[None, :]
    want = [want] + [partner(want, "wide", m) for m in range(2, MATES, 2)]

    in_hbm = pl.BlockSpec(memory_space=pltpu.HBM)
    operands = (covariates, codes, signs, noise)
    design, packed, signs = pl.pallas_call(
        design_kernel,
        out_shape=[
            jax.ShapeDtypeStruct((cols + 3 * PACK, rows_dev), bf16),
            jax.ShapeDtypeStruct((share * wide + SUB, LANE), f32),
            jax.ShapeDtypeStruct(signs.shape, f32),
        ],
        in_specs=[in_hbm] * 4,
        out_specs=[VMEM] * 3,
        scratch_shapes=[pltpu.VMEM(operand.shape, operand.dtype) for operand in operands]
        + [pltpu.SemaphoreType.DMA((4,))],
        compiler_params=pltpu.CompilerParams(vmem_limit_bytes=40 * 2**20),
        name="design",
    )(*operands)
    sizes = [samp * (2 * m < MATES) + share for m in range(wide // 2)]
    starts = [sum(sizes[:m]) for m in range(wide // 2)]
    stay, go = call(
        functools.partial(local_kernel, samp, share, starts),
        "local",
        [((sum(sizes), cols), bf16)] * 2,
        [((MATES * samp, rows_dev), bf16)],
        index,
        design,
        packed,
        signs,
        *want,
    )
    pieces = call(
        functools.partial(pair_kernel, samp, share, starts),
        "pair",
        [((size, cols), bf16) for size in sizes],
        [],
        index,
        stay,
        partner(go, "wide", 1),
    )
    pieces = [pieces[0]] + [partner(pieces[m], "wide", 2 * m) for m in range(1, wide // 2)]
    (piece,) = call(
        functools.partial(mix_kernel, samp, share), "mix", [((samp + share, cols), bf16)], [], index, *pieces
    )
    pieces = [piece] + [partner(piece, "narrow", m) for m in range(1, narrow)]
    rows_in = samp * narrow
    (piece,) = call(
        functools.partial(stack_kernel, samp, share), "stack", [((rows_in + share, cols), bf16)], [], index, *pieces
    )
    pieces = [piece] + [partner(piece, "wide", m) for m in range(2, wide, 2)]
    theirs = [partner(piece, "wide", 1) for piece in pieces]
    sketch = [((rows_in * (wide // 2), cols), bf16)]
    square = ((cols, cols), f32)
    (gram,) = call(functools.partial(gram_kernel, rows_in), "gram", [square], sketch, index, *pieces)
    factor, inverse = call(
        functools.partial(factor_kernel, math.sqrt(LEVELS / SKETCH), rows_in),
        "factor",
        [square] * 2,
        sketch + [square],
        index,
        gram,
        *theirs,
    )
    pieces += theirs
    apart = [2 * m + core for core in range(2) for m in range(wide // 2)]
    solved, resid = call(
        functools.partial(solve_kernel, apart, rows_in, share),
        "solve",
        [((LEVELS, COV), f32), (codes.shape, f32)],
        [((share * wide, LANE), f32)],
        index,
        inverse,
        effects,
        covariates,
        codes,
        noise,
        *pieces,
    )
    return solved.reshape(-1), resid.reshape(-1), factor


def solution(mesh):
    return jax.shard_map(
        body,
        mesh=mesh,
        in_specs=(
            P(("wide", "narrow"), None),
            P(("wide", "narrow")),
            P(("wide", "narrow")),
            P(("wide", "narrow")),
            P(),
            P(("wide", "narrow")),
        ),
        out_specs=(P(), P(("wide", "narrow")), P()),
        check_vma=False,
    )
```

```python
import functools
import math

import jax
import jax.numpy as jnp
from jax import lax
from jax.experimental import pallas as pl
from jax.experimental.pallas import tpu as pltpu
from jax.sharding import PartitionSpec as P

COV = 128
LEVELS = 4
HB = 256
SKETCH = 1024
ITERS = 4
MIX_BITS = 3
MATES = 2**MIX_BITS

half_root = math.sqrt(0.5)
HIGHEST = lax.Precision.HIGHEST
f32, bf16 = jnp.float32, jnp.bfloat16
SUB, LANE = 8, 128
PACK = 16
NT = (((1,), (1,)), ((), ()))
VMEM = pl.BlockSpec(memory_space=pltpu.VMEM)
SMEM = pl.BlockSpec(memory_space=pltpu.SMEM)


def partner(value, axis, mask):
    pairs = [(source, source ^ mask) for source in range(lax.axis_size(axis))]
    return lax.ppermute(value, axis, pairs)


def whole_up(number, unit):
    return -(-number // unit) * unit


def eye():
    rows = lax.broadcasted_iota(jnp.int32, (LANE, LANE), 0)
    lanes = lax.broadcasted_iota(jnp.int32, (LANE, LANE), 1)
    return rows, lanes, rows == lanes


def to_column(row, same):
    return jnp.sum(jnp.where(same, row, 0.0), axis=1, keepdims=True)


def to_row(column, same):
    return jnp.sum(jnp.where(same, column, 0.0), axis=0, keepdims=True)


def split(value):
    parts = []
    for _ in range(3):
        parts.append(value.astype(bf16))
        value = value - parts[-1].astype(f32)
    return parts


def tree_sum(values):
    while len(values) > 1:
        values = [left + right for left, right in zip(values[0::2], values[1::2])]
    return values[0]


def put_sums(ref, start, share, extra):
    rows = share.shape[0]
    for k, part in enumerate(split(share)):
        ref[start : start + rows, k * LANE : (k + 1) * LANE] = part
    tail = jnp.zeros((rows - 3 * SUB, LANE), bf16)
    ref[start : start + rows, 3 * LANE :] = jnp.concatenate(split(extra) + [tail])


def take_sums(ref, start, rows):
    block = ref[start : start + rows, :].astype(f32)
    share = block[:, :LANE] + block[:, LANE : 2 * LANE] + block[:, 2 * LANE : 3 * LANE]
    tail = block[:, 3 * LANE :]
    return share, tail[:SUB] + tail[SUB : 2 * SUB] + tail[2 * SUB : 3 * SUB]


def design_kernel(cov_ref, marks_ref, noise_ref, design, packed):
    rows, lanes, same = eye()
    zero = jnp.zeros((LANE, LANE), f32)
    for r in range(marks_ref.shape[0]):
        here = slice(r * LANE, (r + 1) * LANE)
        code = jnp.bitwise_and(marks_ref[r : r + 1, :], LEVELS - 1)
        turned = cov_ref[here, :].astype(f32).T
        for level in range(LEVELS):
            design[level * LANE : (level + 1) * LANE, here] = jnp.where(code == level, turned, zero).astype(bf16)
        noise = jnp.concatenate([noise_ref[r : r + 1, :]] * LEVELS + [jnp.zeros((PACK - LEVELS, LANE), f32)])
        level = lax.broadcasted_iota(jnp.int32, (PACK, LANE), 0)
        noise = jnp.where(code == level, noise, 0.0)
        for k, part in enumerate(split(noise)):
            design[LEVELS * LANE + k * PACK : LEVELS * LANE + (k + 1) * PACK, here] = part

    sums = jnp.dot(design[...], cov_ref[...], preferred_element_type=f32)
    normal = [sums[level * LANE : (level + 1) * LANE] for level in range(LEVELS)]
    back = sums[LEVELS * LANE :]
    back = back[:SUB] + back[PACK : PACK + SUB] + back[2 * PACK : 2 * PACK + SUB]
    extra = [jnp.sum(jnp.where(same, normal[level], 0.0), axis=0, keepdims=True) for level in (1, 3)]
    for pair in range(LEVELS // 2):
        packed[pair * LANE : (pair + 1) * LANE, :] = jnp.where(rows >= lanes, normal[2 * pair], normal[2 * pair + 1])
    rest = packed.shape[0] - SUB - 2 * LANE
    if rest:
        packed[2 * LANE : 2 * LANE + rest, :] = jnp.zeros((rest, LANE), f32)
    packed[2 * LANE + rest :, :] = jnp.concatenate([back[:LEVELS]] + extra + [jnp.zeros((2, LANE), f32)])


def local_kernel(samp, share, starts, index_ref, design_ref, packed_ref, marks_ref, *refs):
    want_refs, (stay_ref, go_ref, table) = refs[:-3], refs[-3:]
    chunks = marks_ref.shape[0]
    lanes = eye()[1]
    zero = jnp.zeros((LANE, LANE), f32)
    per = LANE // samp
    small = lax.broadcasted_iota(jnp.int32, (samp, samp), 0) == lax.broadcasted_iota(jnp.int32, (samp, samp), 1)

    masks, halves = [], []
    for c in range(MATES // per):
        want = [to_column(ref[...].astype(f32), small) for ref in want_refs[c * per : (c + 1) * per]]
        want = jnp.concatenate(want).astype(jnp.int32)
        masks.append(jnp.right_shift(want, HB.bit_length() - 1))
        line = []
        for h in range(HB // LANE):
            common = jnp.bitwise_and(want, lanes + h * LANE)
            for shift in (4, 2, 1):
                common = jnp.bitwise_xor(common, jnp.right_shift(common, shift))
            line.append((1 - 2 * jnp.bitwise_and(common, 1)).astype(f32))
        halves.append(line)
    for r in range(chunks):
        sign = jnp.where(marks_ref[r : r + 1, :] < LEVELS, 1.0, -1.0)
        block, h = divmod(r * LANE, HB)
        for c, (mask, line) in enumerate(zip(masks, halves)):
            value = jnp.where(mask == block, line[h // LANE] * sign, zero)
            table[c * LANE : (c + 1) * LANE, r * LANE : (r + 1) * LANE] = value.astype(bf16)

    local = lax.dot_general(table[...], design_ref[: LEVELS * LANE, :], NT, preferred_element_type=f32)
    local = (local * (1.0 / math.sqrt(HB))).astype(bf16)
    extra = packed_ref[packed_ref.shape[0] - SUB :, :]
    for m in range(2 * len(starts)):
        out_ref, start = (stay_ref, go_ref)[m % 2], starts[m // 2]
        if m < MATES:
            out_ref[start : start + samp, :] = local[m * samp : (m + 1) * samp]
            start += samp
        at = pl.multiple_of(jnp.bitwise_xor(index_ref[0], m) * share, share)
        put_sums(out_ref, start, packed_ref[pl.ds(at, share), :], extra)


def butterfly(pieces, place, index):
    bit = jnp.bitwise_and(jnp.right_shift(index, place), 1)
    sign = (1 - 2 * bit).astype(f32)
    return [
        ((sign * own + other) * half_root).astype(bf16).astype(f32) for own, other in zip(pieces[0::2], pieces[1::2])
    ]


def pair_kernel(samp, share, starts, index_ref, stay_ref, came_ref, *out_refs):
    for m, (start, out_ref) in enumerate(zip(starts, out_refs)):
        put = 0
        if 2 * m < MATES:
            here = slice(start, start + samp)
            pieces = [ref[here, :].astype(f32) for ref in (stay_ref, came_ref)]
            out_ref[:samp, :] = butterfly(pieces, 0, index_ref[0])[0].astype(bf16)
            put, start = samp, start + samp
        (own, own_extra), (other, other_extra) = [take_sums(ref, start, share) for ref in (stay_ref, came_ref)]
        put_sums(out_ref, put, own + other, own_extra + other_extra)


def mix_kernel(samp, share, index_ref, *refs):
    piece_refs, out_ref = refs[:-1], refs[-1]
    pieces = [ref[:samp, :].astype(f32) for ref in piece_refs[: MATES // 2]]
    for place in range(1, MIX_BITS):
        pieces = butterfly(pieces, place, index_ref[0])
    out_ref[:samp, :] = pieces[0].astype(bf16)
    sums = [take_sums(ref, samp if 2 * m < MATES else 0, share) for m, ref in enumerate(piece_refs)]
    put_sums(out_ref, samp, tree_sum([one for one, _ in sums]), tree_sum([one for _, one in sums]))


def stack_kernel(samp, share, index_ref, *refs):
    piece_refs, out_ref = refs[:-1], refs[-1]
    for m, ref in enumerate(piece_refs):
        at = pl.multiple_of(jnp.bitwise_xor(index_ref[1], m) * samp, samp)
        out_ref[pl.ds(at, samp), :] = ref[:samp, :]
    sums = [take_sums(ref, samp, share) for ref in piece_refs]
    put_sums(
        out_ref, samp * len(piece_refs), tree_sum([one for one, _ in sums]), tree_sum([one for _, one in sums])
    )


def spread(value):
    return jnp.broadcast_to(value, (SUB, LANE))


def reciprocal(value):
    return pltpu.reciprocal(value, approx=True)


def eliminate(tiles):
    lane = lax.broadcasted_iota(jnp.int32, (SUB, LANE), 1)
    sub = lax.broadcasted_iota(jnp.int32, (SUB, LANE), 0)
    tiles = list(tiles)
    scales = []
    for tile in range(len(tiles)):
        first = tile * SUB
        window = (lane >= first) & (lane < first + SUB)
        marks = [lane == first + k for k in range(SUB)]
        old = tiles[tile]
        columns = [spread(old[:, first + k : first + k + 1]) for k in range(SUB)]
        pivot = [[spread(columns[m][k : k + 1, :]) if m >= k else None for m in range(SUB)] for k in range(SUB)]
        cleared = jnp.where(window, 0.0, old)
        rows = [jnp.where(marks[k], 1.0, spread(cleared[k : k + 1, :])) for k in range(SUB)]
        steps, near, far = [None] * SUB, {}, {}
        kept, roots = [None] * SUB, [None] * SUB

        def keep(k, low, ratio, values, others):
            last = others[k + 1]
            kept[k] = rows[k]
            for m in range(k, SUB):
                kept[k] = jnp.where(marks[m], values[m], kept[k])
            kept[k + 1] = rows[k + 1] - ratio * rows[k]
            for m in range(k + 1, SUB):
                kept[k + 1] = jnp.where(marks[m], others[m], kept[k + 1])
            roots[k], roots[k + 1] = lax.rsqrt(low), lax.rsqrt(last)

        for k in range(0, SUB, 4):
            low, cross, high = pivot[k][k], pivot[k][k + 1], pivot[k + 1][k + 1]
            area = low * high - cross * cross
            drop = {}
            for m in range(k + 2, SUB):
                near[k, m] = high * pivot[k][m] - cross * pivot[k + 1][m]
                far[k, m] = low * pivot[k + 1][m] - cross * pivot[k][m]
            for m in range(k + 2, SUB):
                for n in range(m, SUB):
                    drop[m, n] = pivot[k][m] * near[k, n] + pivot[k + 1][m] * far[k, n]
            c, d = k + 2, k + 3
            grown = {(m, n): area * pivot[m][n] - drop[m, n] for m in (c, d) for n in range(m, SUB)}
            low2, cross2, high2 = grown[c, c], grown[c, d], grown[d, d]
            area2 = low2 * high2 - cross2 * cross2
            over, over2 = reciprocal(area), reciprocal(area2)
            for m in range(k + 4, SUB):
                near[c, m] = high2 * grown[c, m] - cross2 * grown[d, m]
                far[c, m] = low2 * grown[d, m] - cross2 * grown[c, m]
            for m in range(k + 4, SUB):
                for n in range(m, SUB):
                    drop2 = grown[c, m] * near[c, n] + grown[d, m] * far[c, n]
                    pivot[m][n] = pivot[m][n] - over * (drop[m, n] + over2 * drop2)
            for m in range(k + 2, SUB):
                near[k, m], far[k, m] = over * near[k, m], over * far[k, m]
                rows[m] = rows[m] - (near[k, m] * rows[k] + far[k, m] * rows[k + 1])
            for m in range(k + 4, SUB):
                near[c, m], far[c, m] = over2 * near[c, m], over2 * far[c, m]
                rows[m] = rows[m] - (near[c, m] * rows[c] + far[c, m] * rows[d])
            steps[k] = over * (high * rows[k] - cross * rows[k + 1])
            steps[k + 1] = over * (low * rows[k + 1] - cross * rows[k])
            both = area * over2
            steps[c] = both * (high2 * rows[c] - cross2 * rows[d])
            steps[d] = both * (low2 * rows[d] - cross2 * rows[c])

            inner = reciprocal(low)
            ratio = cross * inner
            values = {m: pivot[k][m] for m in range(k, SUB)}
            others = {m: pivot[k + 1][m] - ratio * pivot[k][m] for m in range(k + 2, SUB)}
            others[k + 1] = area * inner
            keep(k, low, ratio, values, others)
            inner = reciprocal(low2)
            ratio = cross2 * inner
            values = {m: over * grown[c, m] for m in range(c, SUB)}
            others = {m: over * (grown[d, m] - ratio * grown[c, m]) for m in range(c + 2, SUB)}
            others[d] = over * (area2 * inner)
            keep(c, values[c], ratio, values, others)
        if tile + 1 < len(tiles):
            after = tiles[tile + 1]
            ahead = [spread(after[:, first + k : first + k + 1]) for k in range(SUB)]
            fresh = jnp.where(window, 0.0, after)
            for k in range(0, SUB, 2):
                for m in range(k + 2, SUB):
                    ahead[m] = ahead[m] - (near[k, m] * ahead[k] + far[k, m] * ahead[k + 1])
                fresh = fresh - (ahead[k] * steps[k] + ahead[k + 1] * steps[k + 1])
        for k in reversed(range(0, SUB, 2)):
            for m in reversed(range(k + 2, SUB)):
                steps[k] = steps[k] - near[k, m] * steps[m]
                steps[k + 1] = steps[k + 1] - far[k, m] * steps[m]
        for i in range(tile + 2, len(tiles)):
            change = [spread(tiles[i][:, first + k : first + k + 1]) * steps[k] for k in range(SUB)]
            tiles[i] = jnp.where(window, 0.0, tiles[i]) - tree_sum(change[::-1])
        if tile + 1 < len(tiles):
            tiles[tile + 1] = fresh
        new, scale = kept[0], roots[0]
        for k in range(1, SUB):
            new = jnp.where(sub >= k, kept[k], new)
            scale = jnp.where(sub >= k, roots[k], scale)
        tiles[tile] = new
        scales.append(scale)
    return tiles, scales


LEFT, RIGHT = (0, 1, 0, 1, 2, 0), (0, 0, 1, 1, 0, 2)


def parts_of(value, order, axis):
    parts = split(value)
    return jnp.concatenate([parts[k] for k in order], axis=axis)


def take_gram(rows_in, index_ref, piece_refs, sketch):
    for m, ref in enumerate(piece_refs):
        at = jnp.bitwise_xor(jnp.right_shift(index_ref[0], 1), m) * rows_in
        sketch[pl.ds(pl.multiple_of(at, rows_in), rows_in), :] = ref[:rows_in, :]
    rows = sketch[...]
    return lax.dot_general(rows, rows, (((0,), (0,)), ((), ())), preferred_element_type=f32)


def gram_kernel(rows_in, index_ref, *refs):
    piece_refs, (gram_ref, sketch) = refs[:-2], refs[-2:]
    gram_ref[...] = take_gram(rows_in, index_ref, piece_refs, sketch)


def factor_kernel(ratio, rows_in, index_ref, gram_ref, *refs):
    piece_refs, (factor_ref, inverse_ref, sketch, work) = refs[:-4], refs[-4:]
    cols = work.shape[0]
    work[...] = gram_ref[...] + take_gram(rows_in, index_ref, piece_refs, sketch)
    _, _, same = eye()
    diagonal = []
    for at in range(0, cols, LANE):
        block = work[at : at + LANE, at : at + LANE]
        diagonal.append(jnp.sum(jnp.where(same, block, 0.0), axis=0, keepdims=True))
    unit = [lax.rsqrt(part) for part in diagonal]
    level = jnp.concatenate([part * one for part, one in zip(diagonal, unit)], axis=1) * ratio
    unit_row = jnp.concatenate(unit, axis=1)
    for at, one in zip(range(0, cols, LANE), unit):
        work[at : at + LANE, :] = work[at : at + LANE, :] * to_column(one, same) * unit_row

    row_in = lax.broadcasted_iota(jnp.int32, (LANE, LANE), 0)
    lane_in = lax.broadcasted_iota(jnp.int32, (LANE, LANE), 1)
    for base in range(0, cols, LANE):
        end = base + LANE
        here = slice(base, end)
        tiles = [work[base + SUB * i : base + SUB * (i + 1), here] for i in range(LANE // SUB)]
        tiles, scales = eliminate(tiles)
        scale = jnp.concatenate(scales)
        inner = jnp.concatenate(tiles) * scale
        upper = jnp.where(lane_in >= row_in, inner, 0.0)
        lower = jnp.where(lane_in < row_in, inner, jnp.where(lane_in == row_in, scale, 0.0))
        line = jnp.dot(parts_of(lower, LEFT, 1), parts_of(work[here, :], RIGHT, 0), preferred_element_type=f32)
        if end < cols:
            panel = parts_of(work[end:, here], LEFT, 1)
            panel = lax.dot_general(panel, parts_of(lower, RIGHT, 1), NT, preferred_element_type=f32)
            panel = parts_of(panel, LEFT, 1)
            steps = ([line[:, :base]] if base else []) + [lower, line[:, end:]]
            steps = parts_of(jnp.concatenate(steps, axis=1), RIGHT, 0)
            work[end:, here] = jnp.zeros((cols - end, LANE), f32)
            for start, stop in ((0, LANE), (LANE, cols - end)):
                if start < stop:
                    change = jnp.dot(panel[start:stop], steps, preferred_element_type=f32)
                    work[end + start : end + stop, :] = work[end + start : end + stop, :] - change
        factor_ref[here, here] = upper * level[:, here]
        inverse_ref[here, here] = lower * unit_row[:, here]
        if base:
            factor_ref[here, :base] = jnp.zeros((LANE, base), f32)
            inverse_ref[here, :base] = line[:, :base] * unit_row[:, :base]
        if end < cols:
            factor_ref[here, end:] = line[:, end:] * level[:, end:]
            inverse_ref[here, end:] = jnp.zeros((LANE, cols - end), f32)


def solve_kernel(apart, rows_in, share, index_ref, inverse_ref, effects_ref, cov_ref, marks_ref, noise_ref, *refs):
    piece_refs, (solved_ref, resid_ref, packed) = refs[:-3], refs[-3:]
    rows, lanes, same = eye()
    extra = None
    for mask, ref in zip(apart, piece_refs):
        at = pl.multiple_of(jnp.bitwise_xor(index_ref[0], mask) * share, share)
        packed[pl.ds(at, share), :], more = take_sums(ref, rows_in, share)
        extra = more if extra is None else extra
    normal = []
    for pair in range(LEVELS // 2):
        both = packed[pair * LANE : (pair + 1) * LANE, :]
        turned = both.T
        normal.append(jnp.where(rows >= lanes, both, turned))
        diagonal = jnp.where(same, extra[LEVELS + pair : LEVELS + pair + 1], turned)
        normal.append(jnp.where(rows < lanes, both, diagonal))

    inverse = inverse_ref[...]
    spans = [slice(level * LANE, (level + 1) * LANE) for level in range(LEVELS)]
    gradient = []
    for level in range(LEVELS):
        column = to_column(effects_ref[level : level + 1, :], same)
        gradient.append(jnp.sum(normal[level] * column, axis=0, keepdims=True) + extra[level : level + 1])
    steer = jnp.sum(inverse * jnp.concatenate(gradient, axis=1), axis=1, keepdims=True)
    direction = steer
    gamma = jnp.sum(steer * steer, axis=0, keepdims=True)
    solved = jnp.zeros((1, cov_ref.shape[1] * LEVELS), f32)
    for step in range(ITERS):
        move = jnp.sum(inverse * direction, axis=0, keepdims=True)
        image = []
        for level, span in enumerate(spans):
            image.append(jnp.sum(normal[level] * to_column(move[:, span], same), axis=0, keepdims=True))
        image = jnp.concatenate(image, axis=1)
        alpha = gamma / jnp.sum(move * image, axis=1, keepdims=True)
        solved = solved + alpha * move
        if step == ITERS - 1:
            break
        steer = steer - alpha * jnp.sum(inverse * image, axis=1, keepdims=True)
        gamma_new = jnp.sum(steer * steer, axis=0, keepdims=True)
        direction = steer + gamma_new / gamma * direction
        gamma = gamma_new
    solved = jnp.concatenate([solved[:, span] for span in spans])
    solved_ref[...] = solved

    left = jnp.concatenate([effects_ref[...] - solved, jnp.zeros((PACK - LEVELS, LANE), f32)])
    values = jnp.zeros((SUB, cov_ref.shape[0]), f32)
    for part in split(left):
        values = values + lax.dot_general(part, cov_ref[...], NT, preferred_element_type=f32)[:SUB]
    for r in range(marks_ref.shape[0]):
        code = jnp.bitwise_and(marks_ref[r : r + 1, :], LEVELS - 1)
        total = noise_ref[r : r + 1, :]
        for level in range(LEVELS):
            total = total + jnp.where(code == level, values[level : level + 1, r * LANE : (r + 1) * LANE], 0.0)
        resid_ref[r : r + 1, :] = total


def call(kernel, name, outs, scratch, *operands):
    return pl.pallas_call(
        kernel,
        out_shape=[jax.ShapeDtypeStruct(shape, dtype) for shape, dtype in outs],
        in_specs=[SMEM if operand.ndim == 1 else VMEM for operand in operands],
        out_specs=[VMEM] * len(outs),
        scratch_shapes=[pltpu.VMEM(shape, dtype) for shape, dtype in scratch],
        compiler_params=pltpu.CompilerParams(vmem_limit_bytes=40 * 2**20),
        name=name,
    )(*operands)


def body(covariates, level_codes, sign_bits, sample_rows, effects, noise):
    wide, narrow = lax.axis_size("wide"), lax.axis_size("narrow")
    index = jnp.stack([lax.axis_index("wide"), lax.axis_index("narrow")]).astype(jnp.int32)
    rows_dev, cols = covariates.shape[0], LEVELS * COV
    samp = whole_up(sample_rows.shape[0], PACK)
    share = whole_up(max(2 * LANE // wide, 3 * SUB), PACK)
    sample_rows = jnp.pad(sample_rows, (0, samp - sample_rows.shape[0]), constant_values=-1)
    marks = (level_codes + LEVELS * sign_bits).reshape(-1, LANE)
    noise = noise.reshape(-1, LANE)
    effects = effects.reshape(LEVELS, COV)

    want = sample_rows[None, :]
    want = [want] + [partner(want, "wide", m) for m in range(2, MATES, 2)]
    want = [one for piece in want for one in (piece, partner(piece, "wide", 1))]

    design, packed = call(
        design_kernel,
        "design",
        [((cols + 3 * PACK, rows_dev), bf16), ((share * wide + SUB, LANE), f32)],
        [],
        covariates,
        marks,
        noise,
    )
    sizes = [samp * (2 * m < MATES) + share for m in range(wide // 2)]
    starts = [sum(sizes[:m]) for m in range(wide // 2)]
    stay, go = call(
        functools.partial(local_kernel, samp, share, starts),
        "local",
        [((sum(sizes), cols), bf16)] * 2,
        [((MATES * samp, rows_dev), bf16)],
        index,
        design,
        packed,
        marks,
        *want,
    )
    pieces = call(
        functools.partial(pair_kernel, samp, share, starts),
        "pair",
        [((size, cols), bf16) for size in sizes],
        [],
        index,
        stay,
        partner(go, "wide", 1),
    )
    pieces = [pieces[0]] + [partner(pieces[m], "wide", 2 * m) for m in range(1, wide // 2)]
    (piece,) = call(
        functools.partial(mix_kernel, samp, share), "mix", [((samp + share, cols), bf16)], [], index, *pieces
    )
    pieces = [piece] + [partner(piece, "narrow", m) for m in range(1, narrow)]
    rows_in = samp * narrow
    (piece,) = call(
        functools.partial(stack_kernel, samp, share), "stack", [((rows_in + share, cols), bf16)], [], index, *pieces
    )
    pieces = [piece] + [partner(piece, "wide", m) for m in range(2, wide, 2)]
    theirs = [partner(piece, "wide", 1) for piece in pieces]
    sketch = [((rows_in * (wide // 2), cols), bf16)]
    square = ((cols, cols), f32)
    (gram,) = call(functools.partial(gram_kernel, rows_in), "gram", [square], sketch, index, *pieces)
    factor, inverse = call(
        functools.partial(factor_kernel, math.sqrt(LEVELS / SKETCH), rows_in),
        "factor",
        [square] * 2,
        sketch + [square],
        index,
        gram,
        *theirs,
    )
    pieces += theirs
    apart = [2 * m + core for core in range(2) for m in range(wide // 2)]
    solved, resid = call(
        functools.partial(solve_kernel, apart, rows_in, share),
        "solve",
        [((LEVELS, COV), f32), (noise.shape, f32)],
        [((share * wide, LANE), f32)],
        index,
        inverse,
        effects,
        covariates,
        marks,
        noise,
        *pieces,
    )
    return solved.reshape(-1), resid.reshape(-1), factor


def solution(mesh):
    return jax.shard_map(
        body,
        mesh=mesh,
        in_specs=(
            P(("wide", "narrow"), None),
            P(("wide", "narrow")),
            P(("wide", "narrow")),
            P(("wide", "narrow")),
            P(),
            P(("wide", "narrow")),
        ),
        out_specs=(P(), P(("wide", "narrow")), P()),
        check_vma=False,
    )
```

```python
import functools
import math

import jax
import jax.numpy as jnp
from jax import lax
from jax.experimental import pallas as pl
from jax.experimental.pallas import tpu as pltpu
from jax.sharding import PartitionSpec as P

COV = 128
LEVELS = 4
HB = 256
SKETCH = 1024
ITERS = 4
MIX_BITS = 3
MATES = 2**MIX_BITS

half_root = math.sqrt(0.5)
HIGHEST = lax.Precision.HIGHEST
f32, bf16 = jnp.float32, jnp.bfloat16
SUB, LANE = 8, 128
PACK = 16
NT = (((1,), (1,)), ((), ()))
VMEM = pl.BlockSpec(memory_space=pltpu.VMEM)
SMEM = pl.BlockSpec(memory_space=pltpu.SMEM)


def partner(value, axis, mask):
    pairs = [(source, source ^ mask) for source in range(lax.axis_size(axis))]
    return lax.ppermute(value, axis, pairs)


def whole_up(number, unit):
    return -(-number // unit) * unit


def eye():
    rows = lax.broadcasted_iota(jnp.int32, (LANE, LANE), 0)
    lanes = lax.broadcasted_iota(jnp.int32, (LANE, LANE), 1)
    return rows, lanes, rows == lanes


def to_column(row, same):
    return jnp.sum(jnp.where(same, row, 0.0), axis=1, keepdims=True)


def to_row(column, same):
    return jnp.sum(jnp.where(same, column, 0.0), axis=0, keepdims=True)


def split(value):
    parts = []
    for _ in range(3):
        parts.append(value.astype(bf16))
        value = value - parts[-1].astype(f32)
    return parts


def tree_sum(values):
    while len(values) > 1:
        values = [left + right for left, right in zip(values[0::2], values[1::2])]
    return values[0]


def put_sums(ref, start, share, extra):
    rows = share.shape[0]
    for k, part in enumerate(split(share)):
        ref[start : start + rows, k * LANE : (k + 1) * LANE] = part
    tail = jnp.zeros((rows - 3 * SUB, LANE), bf16)
    ref[start : start + rows, 3 * LANE :] = jnp.concatenate(split(extra) + [tail])


def take_sums(ref, start, rows):
    block = ref[start : start + rows, :].astype(f32)
    share = block[:, :LANE] + block[:, LANE : 2 * LANE] + block[:, 2 * LANE : 3 * LANE]
    tail = block[:, 3 * LANE :]
    return share, tail[:SUB] + tail[SUB : 2 * SUB] + tail[2 * SUB : 3 * SUB]


def design_kernel(cov_ref, marks_ref, noise_ref, design, packed):
    rows, lanes, same = eye()
    zero = jnp.zeros((LANE, LANE), f32)
    for r in range(marks_ref.shape[0]):
        here = slice(r * LANE, (r + 1) * LANE)
        code = jnp.bitwise_and(marks_ref[r : r + 1, :], LEVELS - 1)
        turned = cov_ref[here, :].astype(f32).T
        for level in range(LEVELS):
            design[level * LANE : (level + 1) * LANE, here] = jnp.where(code == level, turned, zero).astype(bf16)
        noise = jnp.concatenate([noise_ref[r : r + 1, :]] * LEVELS + [jnp.zeros((PACK - LEVELS, LANE), f32)])
        level = lax.broadcasted_iota(jnp.int32, (PACK, LANE), 0)
        noise = jnp.where(code == level, noise, 0.0)
        for k, part in enumerate(split(noise)):
            design[LEVELS * LANE + k * PACK : LEVELS * LANE + (k + 1) * PACK, here] = part

    sums = jnp.dot(design[...], cov_ref[...], preferred_element_type=f32)
    normal = [sums[level * LANE : (level + 1) * LANE] for level in range(LEVELS)]
    back = sums[LEVELS * LANE :]
    back = back[:SUB] + back[PACK : PACK + SUB] + back[2 * PACK : 2 * PACK + SUB]
    extra = [jnp.sum(jnp.where(same, normal[level], 0.0), axis=0, keepdims=True) for level in (1, 3)]
    for pair in range(LEVELS // 2):
        packed[pair * LANE : (pair + 1) * LANE, :] = jnp.where(rows >= lanes, normal[2 * pair], normal[2 * pair + 1])
    rest = packed.shape[0] - SUB - 2 * LANE
    if rest:
        packed[2 * LANE : 2 * LANE + rest, :] = jnp.zeros((rest, LANE), f32)
    packed[2 * LANE + rest :, :] = jnp.concatenate([back[:LEVELS]] + extra + [jnp.zeros((2, LANE), f32)])


def local_kernel(samp, share, starts, index_ref, design_ref, packed_ref, marks_ref, *refs):
    want_refs, (stay_ref, go_ref, table) = refs[:-3], refs[-3:]
    chunks = marks_ref.shape[0]
    lanes = eye()[1]
    zero = jnp.zeros((LANE, LANE), f32)
    per = LANE // samp
    small = lax.broadcasted_iota(jnp.int32, (samp, samp), 0) == lax.broadcasted_iota(jnp.int32, (samp, samp), 1)

    masks, halves = [], []
    for c in range(MATES // per):
        want = [to_column(ref[...].astype(f32), small) for ref in want_refs[c * per : (c + 1) * per]]
        want = jnp.concatenate(want).astype(jnp.int32)
        masks.append(jnp.right_shift(want, HB.bit_length() - 1))
        line = []
        for h in range(HB // LANE):
            common = jnp.bitwise_and(want, lanes + h * LANE)
            for shift in (4, 2, 1):
                common = jnp.bitwise_xor(common, jnp.right_shift(common, shift))
            line.append((1 - 2 * jnp.bitwise_and(common, 1)).astype(f32))
        halves.append(line)
    for r in range(chunks):
        sign = jnp.where(marks_ref[r : r + 1, :] < LEVELS, 1.0, -1.0)
        block, h = divmod(r * LANE, HB)
        for c, (mask, line) in enumerate(zip(masks, halves)):
            value = jnp.where(mask == block, line[h // LANE] * sign, zero)
            table[c * LANE : (c + 1) * LANE, r * LANE : (r + 1) * LANE] = value.astype(bf16)

    local = lax.dot_general(table[...], design_ref[: LEVELS * LANE, :], NT, preferred_element_type=f32)
    local = (local * (1.0 / math.sqrt(HB))).astype(bf16)
    extra = packed_ref[packed_ref.shape[0] - SUB :, :]
    for m in range(2 * len(starts)):
        out_ref, start = (stay_ref, go_ref)[m % 2], starts[m // 2]
        if m < MATES:
            out_ref[start : start + samp, :] = local[m * samp : (m + 1) * samp]
            start += samp
        at = pl.multiple_of(jnp.bitwise_xor(index_ref[0], m) * share, share)
        put_sums(out_ref, start, packed_ref[pl.ds(at, share), :], extra)


def butterfly(pieces, place, index):
    bit = jnp.bitwise_and(jnp.right_shift(index, place), 1)
    sign = (1 - 2 * bit).astype(f32)
    return [
        ((sign * own + other) * half_root).astype(bf16).astype(f32) for own, other in zip(pieces[0::2], pieces[1::2])
    ]


def pair_kernel(samp, share, starts, index_ref, stay_ref, came_ref, *out_refs):
    for m, (start, out_ref) in enumerate(zip(starts, out_refs)):
        put = 0
        if 2 * m < MATES:
            here = slice(start, start + samp)
            pieces = [ref[here, :].astype(f32) for ref in (stay_ref, came_ref)]
            out_ref[:samp, :] = butterfly(pieces, 0, index_ref[0])[0].astype(bf16)
            put, start = samp, start + samp
        (own, own_extra), (other, other_extra) = [take_sums(ref, start, share) for ref in (stay_ref, came_ref)]
        put_sums(out_ref, put, own + other, own_extra + other_extra)


def mix_kernel(samp, share, index_ref, *refs):
    piece_refs, out_ref = refs[:-1], refs[-1]
    pieces = [ref[:samp, :].astype(f32) for ref in piece_refs[: MATES // 2]]
    for place in range(1, MIX_BITS):
        pieces = butterfly(pieces, place, index_ref[0])
    out_ref[:samp, :] = pieces[0].astype(bf16)
    sums = [take_sums(ref, samp if 2 * m < MATES else 0, share) for m, ref in enumerate(piece_refs)]
    put_sums(out_ref, samp, tree_sum([one for one, _ in sums]), tree_sum([one for _, one in sums]))


def stack_kernel(samp, share, index_ref, *refs):
    piece_refs, out_ref = refs[:-1], refs[-1]
    for m, ref in enumerate(piece_refs):
        at = pl.multiple_of(jnp.bitwise_xor(index_ref[1], m) * samp, samp)
        out_ref[pl.ds(at, samp), :] = ref[:samp, :]
    sums = [take_sums(ref, samp, share) for ref in piece_refs]
    put_sums(
        out_ref, samp * len(piece_refs), tree_sum([one for one, _ in sums]), tree_sum([one for _, one in sums])
    )


def spread(value):
    return jnp.broadcast_to(value, (SUB, LANE))


def reciprocal(value):
    return pltpu.reciprocal(value, approx=True)


def eliminate(tiles, aside):
    share = -(-len(aside) // len(tiles))
    lane = lax.broadcasted_iota(jnp.int32, (SUB, LANE), 1)
    sub = lax.broadcasted_iota(jnp.int32, (SUB, LANE), 0)
    tiles = list(tiles)
    scales = []
    for tile in range(len(tiles)):
        first = tile * SUB
        window = (lane >= first) & (lane < first + SUB)
        marks = [lane == first + k for k in range(SUB)]
        old = tiles[tile]
        columns = [spread(old[:, first + k : first + k + 1]) for k in range(SUB)]
        pivot = [[spread(columns[m][k : k + 1, :]) if m >= k else None for m in range(SUB)] for k in range(SUB)]
        cleared = jnp.where(window, 0.0, old)
        rows = [jnp.where(marks[k], 1.0, spread(cleared[k : k + 1, :])) for k in range(SUB)]
        steps, near, far = [None] * SUB, {}, {}
        kept, roots = [None] * SUB, [None] * SUB

        def keep(k, low, ratio, values, others):
            last = others[k + 1]
            kept[k] = rows[k]
            for m in range(k, SUB):
                kept[k] = jnp.where(marks[m], values[m], kept[k])
            kept[k + 1] = rows[k + 1] - ratio * rows[k]
            for m in range(k + 1, SUB):
                kept[k + 1] = jnp.where(marks[m], others[m], kept[k + 1])
            roots[k], roots[k + 1] = lax.rsqrt(low), lax.rsqrt(last)

        for k in range(0, SUB, 4):
            low, cross, high = pivot[k][k], pivot[k][k + 1], pivot[k + 1][k + 1]
            area = low * high - cross * cross
            drop = {}
            for m in range(k + 2, SUB):
                near[k, m] = high * pivot[k][m] - cross * pivot[k + 1][m]
                far[k, m] = low * pivot[k + 1][m] - cross * pivot[k][m]
            for m in range(k + 2, SUB):
                for n in range(m, SUB):
                    drop[m, n] = pivot[k][m] * near[k, n] + pivot[k + 1][m] * far[k, n]
            c, d = k + 2, k + 3
            grown = {(m, n): area * pivot[m][n] - drop[m, n] for m in (c, d) for n in range(m, SUB)}
            low2, cross2, high2 = grown[c, c], grown[c, d], grown[d, d]
            area2 = low2 * high2 - cross2 * cross2
            over, over2 = reciprocal(area), reciprocal(area2)
            for m in range(k + 4, SUB):
                near[c, m] = high2 * grown[c, m] - cross2 * grown[d, m]
                far[c, m] = low2 * grown[d, m] - cross2 * grown[c, m]
            for m in range(k + 4, SUB):
                for n in range(m, SUB):
                    drop2 = grown[c, m] * near[c, n] + grown[d, m] * far[c, n]
                    pivot[m][n] = pivot[m][n] - over * (drop[m, n] + over2 * drop2)
            for m in range(k + 2, SUB):
                near[k, m], far[k, m] = over * near[k, m], over * far[k, m]
                rows[m] = rows[m] - (near[k, m] * rows[k] + far[k, m] * rows[k + 1])
            for m in range(k + 4, SUB):
                near[c, m], far[c, m] = over2 * near[c, m], over2 * far[c, m]
                rows[m] = rows[m] - (near[c, m] * rows[c] + far[c, m] * rows[d])
            steps[k] = over * (high * rows[k] - cross * rows[k + 1])
            steps[k + 1] = over * (low * rows[k + 1] - cross * rows[k])
            both = area * over2
            steps[c] = both * (high2 * rows[c] - cross2 * rows[d])
            steps[d] = both * (low2 * rows[d] - cross2 * rows[c])

            inner = reciprocal(low)
            ratio = cross * inner
            values = {m: pivot[k][m] for m in range(k, SUB)}
            others = {m: pivot[k + 1][m] - ratio * pivot[k][m] for m in range(k + 2, SUB)}
            others[k + 1] = area * inner
            keep(k, low, ratio, values, others)
            inner = reciprocal(low2)
            ratio = cross2 * inner
            values = {m: over * grown[c, m] for m in range(c, SUB)}
            others = {m: over * (grown[d, m] - ratio * grown[c, m]) for m in range(c + 2, SUB)}
            others[d] = over * (area2 * inner)
            keep(c, values[c], ratio, values, others)
        if tile + 1 < len(tiles):
            after = tiles[tile + 1]
            ahead = [spread(after[:, first + k : first + k + 1]) for k in range(SUB)]
            fresh = jnp.where(window, 0.0, after)
            for k in range(0, SUB, 2):
                for m in range(k + 2, SUB):
                    ahead[m] = ahead[m] - (near[k, m] * ahead[k] + far[k, m] * ahead[k + 1])
                fresh = fresh - (ahead[k] * steps[k] + ahead[k + 1] * steps[k + 1])
        for k in reversed(range(0, SUB, 2)):
            for m in reversed(range(k + 2, SUB)):
                steps[k] = steps[k] - near[k, m] * steps[m]
                steps[k + 1] = steps[k + 1] - far[k, m] * steps[m]
        for i in range(tile + 2, len(tiles)):
            change = [spread(tiles[i][:, first + k : first + k + 1]) * steps[k] for k in range(SUB)]
            tiles[i] = jnp.where(window, 0.0, tiles[i]) - tree_sum(change[::-1])
        if tile + 1 < len(tiles):
            tiles[tile + 1] = fresh
        new, scale = kept[0], roots[0]
        for k in range(1, SUB):
            new = jnp.where(sub >= k, kept[k], new)
            scale = jnp.where(sub >= k, roots[k], scale)
        tiles[tile] = new
        scales.append(scale)
        for work in aside[tile * share : (tile + 1) * share]:
            work()
    return tiles, scales


LEFT, RIGHT = (0, 1, 0, 1, 2, 0), (0, 0, 1, 1, 0, 2)


def parts_of(value, order, axis):
    parts = split(value)
    return jnp.concatenate([parts[k] for k in order], axis=axis)


def put_pieces(rows_in, index_ref, piece_refs, sketch):
    for m, ref in enumerate(piece_refs):
        at = jnp.bitwise_xor(jnp.right_shift(index_ref[0], 1), m) * rows_in
        sketch[pl.ds(pl.multiple_of(at, rows_in), rows_in), :] = ref[:rows_in, :]


def gram_rows(sketch, here):
    return lax.dot_general(sketch[:, here], sketch[...], (((0,), (0,)), ((), ())), preferred_element_type=f32)


def gram_kernel(rows_in, index_ref, *refs):
    piece_refs, (gram_ref, sketch) = refs[:-2], refs[-2:]
    put_pieces(rows_in, index_ref, piece_refs, sketch)
    for at in range(0, gram_ref.shape[0], LANE):
        gram_ref[at : at + LANE, :] = gram_rows(sketch, slice(at, at + LANE))


def factor_kernel(ratio, rows_in, index_ref, gram_ref, *refs):
    piece_refs, (factor_ref, inverse_ref, sketch, work) = refs[:-4], refs[-4:]
    count = work.shape[0] // LANE
    spans = [slice(at, at + LANE) for at in range(0, work.shape[0], LANE)]
    row_in, lane_in, same = eye()
    diagonals, units = [None] * count, [None] * count
    put_pieces(rows_in, index_ref, piece_refs, sketch)

    def take_rows(i):
        work[spans[i], :] = gram_ref[spans[i], :] + gram_rows(sketch, spans[i])

    def take_unit(i):
        diagonals[i] = jnp.sum(jnp.where(same, work[spans[i], spans[i]], 0.0), axis=0, keepdims=True)
        units[i] = lax.rsqrt(diagonals[i])

    def scale_rows(i):
        work[spans[i], :] = work[spans[i], :] * to_column(units[i], same) * jnp.concatenate(units, axis=1)

    take_rows(0)
    take_unit(0)
    fresh = work[spans[0], spans[0]] * to_column(units[0], same) * units[0]
    aside = [functools.partial(take_rows, i) for i in range(1, count)]
    aside += [functools.partial(take_unit, i) for i in range(1, count)]
    aside += [functools.partial(scale_rows, i) for i in range(count)]
    for b, here in enumerate(spans):
        tiles, scales = eliminate([fresh[at : at + SUB] for at in range(0, LANE, SUB)], aside)
        scale = jnp.concatenate(scales)
        inner = jnp.concatenate(tiles) * scale
        lower = jnp.where(lane_in < row_in, inner, jnp.where(lane_in == row_in, scale, 0.0))
        lower_left, lower_right = parts_of(lower, LEFT, 1), parts_of(lower, RIGHT, 1)
        panels, steps = {}, {}

        def take_line(j, b=b, here=here, lower_left=lower_left, steps=steps):
            line = jnp.dot(lower_left, parts_of(work[here, spans[j]], RIGHT, 0), preferred_element_type=f32)
            steps[j] = parts_of(line, RIGHT, 0)
            if j > b:
                factor_ref[here, spans[j]] = line * (diagonals[j] * units[j] * ratio)
                inverse_ref[here, spans[j]] = jnp.zeros((LANE, LANE), f32)
            else:
                factor_ref[here, spans[j]] = jnp.zeros((LANE, LANE), f32)
                inverse_ref[here, spans[j]] = line * units[j]

        def take_panel(i, here=here, lower_right=lower_right, panels=panels):
            panel = parts_of(work[spans[i], here], LEFT, 1)
            panels[i] = parts_of(lax.dot_general(panel, lower_right, NT, preferred_element_type=f32), LEFT, 1)

        def take_change(i, j, b=b, panels=panels, steps=steps):
            change = jnp.dot(panels[i], steps[j], preferred_element_type=f32)
            work[spans[i], spans[j]] = -change if j == b else work[spans[i], spans[j]] - change

        def put_own(here=here, inner=inner, lower=lower, b=b, steps=steps):
            steps[b] = parts_of(lower, RIGHT, 0)
            factor_ref[here, here] = jnp.where(lane_in >= row_in, inner, 0.0) * (diagonals[b] * units[b] * ratio)
            inverse_ref[here, here] = lower * units[b]

        if b + 1 < count:
            take_line(b + 1)
            take_panel(b + 1)
            fresh = work[spans[b + 1], spans[b + 1]]
            fresh = fresh - jnp.dot(panels[b + 1], steps[b + 1], preferred_element_type=f32)
        others = [j for j in range(count) if j not in (b, b + 1)]
        aside = [put_own] + [functools.partial(take_line, j) for j in others]
        aside += [functools.partial(take_panel, i) for i in range(b + 2, count)]
        aside += [
            functools.partial(take_change, i, j)
            for i in range(b + 1, count)
            for j in range(count)
            if (i, j) != (b + 1, b + 1)
        ]
    for call_it in aside:
        call_it()


def solve_kernel(apart, rows_in, share, index_ref, inverse_ref, effects_ref, cov_ref, marks_ref, noise_ref, *refs):
    piece_refs, (solved_ref, resid_ref, packed) = refs[:-3], refs[-3:]
    rows, lanes, same = eye()
    extra = None
    for mask, ref in zip(apart, piece_refs):
        at = pl.multiple_of(jnp.bitwise_xor(index_ref[0], mask) * share, share)
        packed[pl.ds(at, share), :], more = take_sums(ref, rows_in, share)
        extra = more if extra is None else extra
    normal = []
    for pair in range(LEVELS // 2):
        both = packed[pair * LANE : (pair + 1) * LANE, :]
        turned = both.T
        normal.append(jnp.where(rows >= lanes, both, turned))
        diagonal = jnp.where(same, extra[LEVELS + pair : LEVELS + pair + 1], turned)
        normal.append(jnp.where(rows < lanes, both, diagonal))

    inverse = inverse_ref[...]
    spans = [slice(level * LANE, (level + 1) * LANE) for level in range(LEVELS)]
    gradient = []
    for level in range(LEVELS):
        column = to_column(effects_ref[level : level + 1, :], same)
        gradient.append(jnp.sum(normal[level] * column, axis=0, keepdims=True) + extra[level : level + 1])
    steer = jnp.sum(inverse * jnp.concatenate(gradient, axis=1), axis=1, keepdims=True)
    direction = steer
    gamma = jnp.sum(steer * steer, axis=0, keepdims=True)
    solved = jnp.zeros((1, cov_ref.shape[1] * LEVELS), f32)
    for step in range(ITERS):
        move = jnp.sum(inverse * direction, axis=0, keepdims=True)
        image = []
        for level, span in enumerate(spans):
            image.append(jnp.sum(normal[level] * to_column(move[:, span], same), axis=0, keepdims=True))
        image = jnp.concatenate(image, axis=1)
        alpha = gamma / jnp.sum(move * image, axis=1, keepdims=True)
        solved = solved + alpha * move
        if step == ITERS - 1:
            break
        steer = steer - alpha * jnp.sum(inverse * image, axis=1, keepdims=True)
        gamma_new = jnp.sum(steer * steer, axis=0, keepdims=True)
        direction = steer + gamma_new / gamma * direction
        gamma = gamma_new
    solved = jnp.concatenate([solved[:, span] for span in spans])
    solved_ref[...] = solved

    left = jnp.concatenate([effects_ref[...] - solved, jnp.zeros((PACK - LEVELS, LANE), f32)])
    values = jnp.zeros((SUB, cov_ref.shape[0]), f32)
    for part in split(left):
        values = values + lax.dot_general(part, cov_ref[...], NT, preferred_element_type=f32)[:SUB]
    for r in range(marks_ref.shape[0]):
        code = jnp.bitwise_and(marks_ref[r : r + 1, :], LEVELS - 1)
        total = noise_ref[r : r + 1, :]
        for level in range(LEVELS):
            total = total + jnp.where(code == level, values[level : level + 1, r * LANE : (r + 1) * LANE], 0.0)
        resid_ref[r : r + 1, :] = total


def call(kernel, name, outs, scratch, *operands):
    return pl.pallas_call(
        kernel,
        out_shape=[jax.ShapeDtypeStruct(shape, dtype) for shape, dtype in outs],
        in_specs=[SMEM if operand.ndim == 1 else VMEM for operand in operands],
        out_specs=[VMEM] * len(outs),
        scratch_shapes=[pltpu.VMEM(shape, dtype) for shape, dtype in scratch],
        compiler_params=pltpu.CompilerParams(vmem_limit_bytes=40 * 2**20),
        name=name,
    )(*operands)


def body(covariates, level_codes, sign_bits, sample_rows, effects, noise):
    wide, narrow = lax.axis_size("wide"), lax.axis_size("narrow")
    index = jnp.stack([lax.axis_index("wide"), lax.axis_index("narrow")]).astype(jnp.int32)
    rows_dev, cols = covariates.shape[0], LEVELS * COV
    samp = whole_up(sample_rows.shape[0], PACK)
    share = whole_up(max(2 * LANE // wide, 3 * SUB), PACK)
    sample_rows = jnp.pad(sample_rows, (0, samp - sample_rows.shape[0]), constant_values=-1)
    marks = (level_codes + LEVELS * sign_bits).reshape(-1, LANE)
    noise = noise.reshape(-1, LANE)
    effects = effects.reshape(LEVELS, COV)

    want = sample_rows[None, :]
    want = [want] + [partner(want, "wide", m) for m in range(2, MATES, 2)]
    want = [one for piece in want for one in (piece, partner(piece, "wide", 1))]

    design, packed = call(
        design_kernel,
        "design",
        [((cols + 3 * PACK, rows_dev), bf16), ((share * wide + SUB, LANE), f32)],
        [],
        covariates,
        marks,
        noise,
    )
    sizes = [samp * (2 * m < MATES) + share for m in range(wide // 2)]
    starts = [sum(sizes[:m]) for m in range(wide // 2)]
    stay, go = call(
        functools.partial(local_kernel, samp, share, starts),
        "local",
        [((sum(sizes), cols), bf16)] * 2,
        [((MATES * samp, rows_dev), bf16)],
        index,
        design,
        packed,
        marks,
        *want,
    )
    pieces = call(
        functools.partial(pair_kernel, samp, share, starts),
        "pair",
        [((size, cols), bf16) for size in sizes],
        [],
        index,
        stay,
        partner(go, "wide", 1),
    )
    pieces = [pieces[0]] + [partner(pieces[m], "wide", 2 * m) for m in range(1, wide // 2)]
    (piece,) = call(
        functools.partial(mix_kernel, samp, share), "mix", [((samp + share, cols), bf16)], [], index, *pieces
    )
    pieces = [piece] + [partner(piece, "narrow", m) for m in range(1, narrow)]
    rows_in = samp * narrow
    (piece,) = call(
        functools.partial(stack_kernel, samp, share), "stack", [((rows_in + share, cols), bf16)], [], index, *pieces
    )
    pieces = [piece] + [partner(piece, "wide", m) for m in range(2, wide, 2)]
    theirs = [partner(piece, "wide", 1) for piece in pieces]
    sketch = [((rows_in * (wide // 2), cols), bf16)]
    square = ((cols, cols), f32)
    (gram,) = call(functools.partial(gram_kernel, rows_in), "gram", [square], sketch, index, *pieces)
    factor, inverse = call(
        functools.partial(factor_kernel, math.sqrt(LEVELS / SKETCH), rows_in),
        "factor",
        [square] * 2,
        sketch + [square],
        index,
        gram,
        *theirs,
    )
    pieces += theirs
    apart = [2 * m + core for core in range(2) for m in range(wide // 2)]
    solved, resid = call(
        functools.partial(solve_kernel, apart, rows_in, share),
        "solve",
        [((LEVELS, COV), f32), (noise.shape, f32)],
        [((share * wide, LANE), f32)],
        index,
        inverse,
        effects,
        covariates,
        marks,
        noise,
        *pieces,
    )
    return solved.reshape(-1), resid.reshape(-1), factor


def solution(mesh):
    return jax.shard_map(
        body,
        mesh=mesh,
        in_specs=(
            P(("wide", "narrow"), None),
            P(("wide", "narrow")),
            P(("wide", "narrow")),
            P(("wide", "narrow")),
            P(),
            P(("wide", "narrow")),
        ),
        out_specs=(P(), P(("wide", "narrow")), P()),
        check_vma=False,
    )
```

```python
import functools
import math

import jax
import jax.numpy as jnp
from jax import lax
from jax.experimental import pallas as pl
from jax.experimental.pallas import tpu as pltpu
from jax.sharding import PartitionSpec as P

COV = 128
LEVELS = 4
HB = 256
SKETCH = 1024
ITERS = 4
MIX_BITS = 3
MATES = 2**MIX_BITS

half_root = math.sqrt(0.5)
HIGHEST = lax.Precision.HIGHEST
f32, bf16 = jnp.float32, jnp.bfloat16
SUB, LANE = 8, 128
PACK = 16
NT = (((1,), (1,)), ((), ()))
VMEM = pl.BlockSpec(memory_space=pltpu.VMEM)
SMEM = pl.BlockSpec(memory_space=pltpu.SMEM)


def partner(value, axis, mask):
    pairs = [(source, source ^ mask) for source in range(lax.axis_size(axis))]
    return lax.ppermute(value, axis, pairs)


def whole_up(number, unit):
    return -(-number // unit) * unit


def eye():
    rows = lax.broadcasted_iota(jnp.int32, (LANE, LANE), 0)
    lanes = lax.broadcasted_iota(jnp.int32, (LANE, LANE), 1)
    return rows, lanes, rows == lanes


def to_column(row, same):
    return jnp.sum(jnp.where(same, row, 0.0), axis=1, keepdims=True)


def to_row(column, same):
    return jnp.sum(jnp.where(same, column, 0.0), axis=0, keepdims=True)


def split(value):
    parts = []
    for _ in range(3):
        parts.append(value.astype(bf16))
        value = value - parts[-1].astype(f32)
    return parts


def tree_sum(values):
    while len(values) > 1:
        values = [left + right for left, right in zip(values[0::2], values[1::2])]
    return values[0]


def put_sums(ref, start, share, extra):
    rows = share.shape[0]
    for k, part in enumerate(split(share)):
        ref[start : start + rows, k * LANE : (k + 1) * LANE] = part
    tail = jnp.zeros((rows - 3 * SUB, LANE), bf16)
    ref[start : start + rows, 3 * LANE :] = jnp.concatenate(split(extra) + [tail])


def take_sums(ref, start, rows):
    block = ref[start : start + rows, :].astype(f32)
    share = block[:, :LANE] + block[:, LANE : 2 * LANE] + block[:, 2 * LANE : 3 * LANE]
    tail = block[:, 3 * LANE :]
    return share, tail[:SUB] + tail[SUB : 2 * SUB] + tail[2 * SUB : 3 * SUB]


def design_kernel(cov_ref, marks_ref, noise_ref, design, packed):
    rows, lanes, same = eye()
    zero = jnp.zeros((LANE, LANE), f32)
    for r in range(marks_ref.shape[0]):
        here = slice(r * LANE, (r + 1) * LANE)
        code = jnp.bitwise_and(marks_ref[r : r + 1, :], LEVELS - 1)
        turned = cov_ref[here, :].astype(f32).T
        for level in range(LEVELS):
            design[level * LANE : (level + 1) * LANE, here] = jnp.where(code == level, turned, zero).astype(bf16)
        noise = jnp.concatenate([noise_ref[r : r + 1, :]] * LEVELS + [jnp.zeros((PACK - LEVELS, LANE), f32)])
        level = lax.broadcasted_iota(jnp.int32, (PACK, LANE), 0)
        noise = jnp.where(code == level, noise, 0.0)
        for k, part in enumerate(split(noise)):
            design[LEVELS * LANE + k * PACK : LEVELS * LANE + (k + 1) * PACK, here] = part

    sums = jnp.dot(design[...], cov_ref[...], preferred_element_type=f32)
    normal = [sums[level * LANE : (level + 1) * LANE] for level in range(LEVELS)]
    back = sums[LEVELS * LANE :]
    back = back[:SUB] + back[PACK : PACK + SUB] + back[2 * PACK : 2 * PACK + SUB]
    extra = [jnp.sum(jnp.where(same, normal[level], 0.0), axis=0, keepdims=True) for level in (1, 3)]
    for pair in range(LEVELS // 2):
        packed[pair * LANE : (pair + 1) * LANE, :] = jnp.where(rows >= lanes, normal[2 * pair], normal[2 * pair + 1])
    rest = packed.shape[0] - SUB - 2 * LANE
    if rest:
        packed[2 * LANE : 2 * LANE + rest, :] = jnp.zeros((rest, LANE), f32)
    packed[2 * LANE + rest :, :] = jnp.concatenate([back[:LEVELS]] + extra + [jnp.zeros((2, LANE), f32)])


def local_kernel(samp, share, starts, index_ref, design_ref, packed_ref, marks_ref, *refs):
    want_refs, (stay_ref, go_ref, table) = refs[:-3], refs[-3:]
    chunks = marks_ref.shape[0]
    lanes = eye()[1]
    zero = jnp.zeros((LANE, LANE), f32)
    per = LANE // samp
    small = lax.broadcasted_iota(jnp.int32, (samp, samp), 0) == lax.broadcasted_iota(jnp.int32, (samp, samp), 1)

    masks, halves = [], []
    for c in range(MATES // per):
        want = [to_column(ref[...].astype(f32), small) for ref in want_refs[c * per : (c + 1) * per]]
        want = jnp.concatenate(want).astype(jnp.int32)
        masks.append(jnp.right_shift(want, HB.bit_length() - 1))
        line = []
        for h in range(HB // LANE):
            common = jnp.bitwise_and(want, lanes + h * LANE)
            for shift in (4, 2, 1):
                common = jnp.bitwise_xor(common, jnp.right_shift(common, shift))
            line.append((1 - 2 * jnp.bitwise_and(common, 1)).astype(f32))
        halves.append(line)
    for r in range(chunks):
        sign = jnp.where(marks_ref[r : r + 1, :] < LEVELS, 1.0, -1.0)
        block, h = divmod(r * LANE, HB)
        for c, (mask, line) in enumerate(zip(masks, halves)):
            value = jnp.where(mask == block, line[h // LANE] * sign, zero)
            table[c * LANE : (c + 1) * LANE, r * LANE : (r + 1) * LANE] = value.astype(bf16)

    local = lax.dot_general(table[...], design_ref[: LEVELS * LANE, :], NT, preferred_element_type=f32)
    local = (local * (1.0 / math.sqrt(HB))).astype(bf16)
    extra = packed_ref[packed_ref.shape[0] - SUB :, :]
    for m in range(2 * len(starts)):
        out_ref, start = (stay_ref, go_ref)[m % 2], starts[m // 2]
        if m < MATES:
            out_ref[start : start + samp, :] = local[m * samp : (m + 1) * samp]
            start += samp
        at = pl.multiple_of(jnp.bitwise_xor(index_ref[0], m) * share, share)
        put_sums(out_ref, start, packed_ref[pl.ds(at, share), :], extra)


def butterfly(pieces, place, index):
    bit = jnp.bitwise_and(jnp.right_shift(index, place), 1)
    sign = (1 - 2 * bit).astype(f32)
    return [
        ((sign * own + other) * half_root).astype(bf16).astype(f32) for own, other in zip(pieces[0::2], pieces[1::2])
    ]


def pair_kernel(samp, share, starts, index_ref, stay_ref, came_ref, *out_refs):
    for m, (start, out_ref) in enumerate(zip(starts, out_refs)):
        put = 0
        if 2 * m < MATES:
            here = slice(start, start + samp)
            pieces = [ref[here, :].astype(f32) for ref in (stay_ref, came_ref)]
            out_ref[:samp, :] = butterfly(pieces, 0, index_ref[0])[0].astype(bf16)
            put, start = samp, start + samp
        (own, own_extra), (other, other_extra) = [take_sums(ref, start, share) for ref in (stay_ref, came_ref)]
        put_sums(out_ref, put, own + other, own_extra + other_extra)


def mix_kernel(samp, share, index_ref, *refs):
    piece_refs, out_ref = refs[:-1], refs[-1]
    pieces = [ref[:samp, :].astype(f32) for ref in piece_refs[: MATES // 2]]
    for place in range(1, MIX_BITS):
        pieces = butterfly(pieces, place, index_ref[0])
    out_ref[:samp, :] = pieces[0].astype(bf16)
    sums = [take_sums(ref, samp if 2 * m < MATES else 0, share) for m, ref in enumerate(piece_refs)]
    put_sums(out_ref, samp, tree_sum([one for one, _ in sums]), tree_sum([one for _, one in sums]))


def stack_kernel(samp, share, index_ref, *refs):
    piece_refs, out_ref = refs[:-1], refs[-1]
    for m, ref in enumerate(piece_refs):
        at = pl.multiple_of(jnp.bitwise_xor(index_ref[1], m) * samp, samp)
        out_ref[pl.ds(at, samp), :] = ref[:samp, :]
    sums = [take_sums(ref, samp, share) for ref in piece_refs]
    put_sums(
        out_ref, samp * len(piece_refs), tree_sum([one for one, _ in sums]), tree_sum([one for _, one in sums])
    )


def spread(value):
    return jnp.broadcast_to(value, (SUB, LANE))


def reciprocal(value):
    return pltpu.reciprocal(value, approx=True)


def eliminate(tiles, aside, shelf):
    share = -(-len(aside) // len(tiles))
    lane = lax.broadcasted_iota(jnp.int32, (SUB, LANE), 1)
    sub = lax.broadcasted_iota(jnp.int32, (SUB, LANE), 0)
    tiles = list(tiles)
    scales = []
    for tile in range(len(tiles)):
        first = tile * SUB
        window = (lane >= first) & (lane < first + SUB)
        marks = [lane == first + k for k in range(SUB)]
        old = tiles[tile]
        columns = [spread(old[:, first + k : first + k + 1]) for k in range(SUB)]
        base = tile % 2 * (SUB + 1) * SUB
        shelf[base : base + SUB, :] = jnp.where(window, 0.0, old)
        for m in range(SUB):
            shelf[base + (m + 1) * SUB : base + (m + 2) * SUB, :] = columns[m]

        def take(m, k):
            at = base + m * SUB + k
            return spread(shelf[at : at + 1, :])

        pivot = [[take(m + 1, k) if m >= k else None for m in range(SUB)] for k in range(SUB)]
        rows = [jnp.where(marks[k], 1.0, take(0, k)) for k in range(SUB)]
        steps, near, far = [None] * SUB, {}, {}
        kept, roots = [None] * SUB, [None] * SUB

        def keep(k, low, ratio, values, others):
            last = others[k + 1]
            kept[k] = rows[k]
            for m in range(k, SUB):
                kept[k] = jnp.where(marks[m], values[m], kept[k])
            kept[k + 1] = rows[k + 1] - ratio * rows[k]
            for m in range(k + 1, SUB):
                kept[k + 1] = jnp.where(marks[m], others[m], kept[k + 1])
            roots[k], roots[k + 1] = lax.rsqrt(low), lax.rsqrt(last)

        for k in range(0, SUB, 4):
            low, cross, high = pivot[k][k], pivot[k][k + 1], pivot[k + 1][k + 1]
            area = low * high - cross * cross
            drop = {}
            for m in range(k + 2, SUB):
                near[k, m] = high * pivot[k][m] - cross * pivot[k + 1][m]
                far[k, m] = low * pivot[k + 1][m] - cross * pivot[k][m]
            for m in range(k + 2, SUB):
                for n in range(m, SUB):
                    drop[m, n] = pivot[k][m] * near[k, n] + pivot[k + 1][m] * far[k, n]
            c, d = k + 2, k + 3
            grown = {(m, n): area * pivot[m][n] - drop[m, n] for m in (c, d) for n in range(m, SUB)}
            low2, cross2, high2 = grown[c, c], grown[c, d], grown[d, d]
            area2 = low2 * high2 - cross2 * cross2
            over, over2 = reciprocal(area), reciprocal(area2)
            for m in range(k + 4, SUB):
                near[c, m] = high2 * grown[c, m] - cross2 * grown[d, m]
                far[c, m] = low2 * grown[d, m] - cross2 * grown[c, m]
            for m in range(k + 4, SUB):
                for n in range(m, SUB):
                    drop2 = grown[c, m] * near[c, n] + grown[d, m] * far[c, n]
                    pivot[m][n] = pivot[m][n] - over * (drop[m, n] + over2 * drop2)
            for m in range(k + 2, SUB):
                near[k, m], far[k, m] = over * near[k, m], over * far[k, m]
                rows[m] = rows[m] - (near[k, m] * rows[k] + far[k, m] * rows[k + 1])
            for m in range(k + 4, SUB):
                near[c, m], far[c, m] = over2 * near[c, m], over2 * far[c, m]
                rows[m] = rows[m] - (near[c, m] * rows[c] + far[c, m] * rows[d])
            steps[k] = over * (high * rows[k] - cross * rows[k + 1])
            steps[k + 1] = over * (low * rows[k + 1] - cross * rows[k])
            both = area * over2
            steps[c] = both * (high2 * rows[c] - cross2 * rows[d])
            steps[d] = both * (low2 * rows[d] - cross2 * rows[c])

            inner = reciprocal(low)
            ratio = cross * inner
            values = {m: pivot[k][m] for m in range(k, SUB)}
            others = {m: pivot[k + 1][m] - ratio * pivot[k][m] for m in range(k + 2, SUB)}
            others[k + 1] = area * inner
            keep(k, low, ratio, values, others)
            inner = reciprocal(low2)
            ratio = cross2 * inner
            values = {m: over * grown[c, m] for m in range(c, SUB)}
            others = {m: over * (grown[d, m] - ratio * grown[c, m]) for m in range(c + 2, SUB)}
            others[d] = over * (area2 * inner)
            keep(c, values[c], ratio, values, others)
        if tile + 1 < len(tiles):
            after = tiles[tile + 1]
            ahead = [spread(after[:, first + k : first + k + 1]) for k in range(SUB)]
            fresh = jnp.where(window, 0.0, after)
            for k in range(0, SUB, 2):
                for m in range(k + 2, SUB):
                    ahead[m] = ahead[m] - (near[k, m] * ahead[k] + far[k, m] * ahead[k + 1])
                fresh = fresh - (ahead[k] * steps[k] + ahead[k + 1] * steps[k + 1])
        for k in reversed(range(0, SUB, 2)):
            for m in reversed(range(k + 2, SUB)):
                steps[k] = steps[k] - near[k, m] * steps[m]
                steps[k + 1] = steps[k + 1] - far[k, m] * steps[m]
        for i in range(tile + 2, len(tiles)):
            change = [spread(tiles[i][:, first + k : first + k + 1]) * steps[k] for k in range(SUB)]
            tiles[i] = jnp.where(window, 0.0, tiles[i]) - tree_sum(change[::-1])
        if tile + 1 < len(tiles):
            tiles[tile + 1] = fresh
        new, scale = kept[0], roots[0]
        for k in range(1, SUB):
            new = jnp.where(sub >= k, kept[k], new)
            scale = jnp.where(sub >= k, roots[k], scale)
        tiles[tile] = new
        scales.append(scale)
        for work in aside[tile * share : (tile + 1) * share]:
            work()
    return tiles, scales


LEFT, RIGHT = (0, 1, 0, 1, 2, 0), (0, 0, 1, 1, 0, 2)


def parts_of(value, order, axis):
    parts = split(value)
    return jnp.concatenate([parts[k] for k in order], axis=axis)


def put_pieces(rows_in, index_ref, piece_refs, sketch):
    for m, ref in enumerate(piece_refs):
        at = jnp.bitwise_xor(jnp.right_shift(index_ref[0], 1), m) * rows_in
        sketch[pl.ds(pl.multiple_of(at, rows_in), rows_in), :] = ref[:rows_in, :]


def gram_rows(sketch, here):
    return lax.dot_general(sketch[:, here], sketch[...], (((0,), (0,)), ((), ())), preferred_element_type=f32)


def gram_kernel(rows_in, index_ref, *refs):
    piece_refs, (gram_ref, sketch) = refs[:-2], refs[-2:]
    put_pieces(rows_in, index_ref, piece_refs, sketch)
    for at in range(0, gram_ref.shape[0], LANE):
        gram_ref[at : at + LANE, :] = gram_rows(sketch, slice(at, at + LANE))


def factor_kernel(ratio, rows_in, index_ref, gram_ref, *refs):
    piece_refs, (factor_ref, inverse_ref, sketch, work, shelf) = refs[:-5], refs[-5:]
    count = work.shape[0] // LANE
    spans = [slice(at, at + LANE) for at in range(0, work.shape[0], LANE)]
    row_in, lane_in, same = eye()
    diagonals, units = [None] * count, [None] * count
    put_pieces(rows_in, index_ref, piece_refs, sketch)

    def take_rows(i):
        work[spans[i], :] = gram_ref[spans[i], :] + gram_rows(sketch, spans[i])

    def take_unit(i):
        diagonals[i] = jnp.sum(jnp.where(same, work[spans[i], spans[i]], 0.0), axis=0, keepdims=True)
        units[i] = lax.rsqrt(diagonals[i])

    def scale_rows(i):
        work[spans[i], :] = work[spans[i], :] * to_column(units[i], same) * jnp.concatenate(units, axis=1)

    take_rows(0)
    take_unit(0)
    fresh = work[spans[0], spans[0]] * to_column(units[0], same) * units[0]
    aside = [functools.partial(take_rows, i) for i in range(1, count)]
    aside += [functools.partial(take_unit, i) for i in range(1, count)]
    aside += [functools.partial(scale_rows, i) for i in range(count)]
    for b, here in enumerate(spans):
        tiles, scales = eliminate([fresh[at : at + SUB] for at in range(0, LANE, SUB)], aside, shelf)
        scale = jnp.concatenate(scales)
        inner = jnp.concatenate(tiles) * scale
        lower = jnp.where(lane_in < row_in, inner, jnp.where(lane_in == row_in, scale, 0.0))
        lower_left, lower_right = parts_of(lower, LEFT, 1), parts_of(lower, RIGHT, 1)
        panels, steps = {}, {}

        def take_line(j, b=b, here=here, lower_left=lower_left, steps=steps):
            line = jnp.dot(lower_left, parts_of(work[here, spans[j]], RIGHT, 0), preferred_element_type=f32)
            steps[j] = parts_of(line, RIGHT, 0)
            if j > b:
                factor_ref[here, spans[j]] = line * (diagonals[j] * units[j] * ratio)
                inverse_ref[here, spans[j]] = jnp.zeros((LANE, LANE), f32)
            else:
                factor_ref[here, spans[j]] = jnp.zeros((LANE, LANE), f32)
                inverse_ref[here, spans[j]] = line * units[j]

        def take_panel(i, here=here, lower_right=lower_right, panels=panels):
            panel = parts_of(work[spans[i], here], LEFT, 1)
            panels[i] = parts_of(lax.dot_general(panel, lower_right, NT, preferred_element_type=f32), LEFT, 1)

        def take_change(i, j, b=b, panels=panels, steps=steps):
            change = jnp.dot(panels[i], steps[j], preferred_element_type=f32)
            work[spans[i], spans[j]] = -change if j == b else work[spans[i], spans[j]] - change

        def put_own(here=here, inner=inner, lower=lower, b=b, steps=steps):
            steps[b] = parts_of(lower, RIGHT, 0)
            factor_ref[here, here] = jnp.where(lane_in >= row_in, inner, 0.0) * (diagonals[b] * units[b] * ratio)
            inverse_ref[here, here] = lower * units[b]

        if b + 1 < count:
            take_line(b + 1)
            take_panel(b + 1)
            fresh = work[spans[b + 1], spans[b + 1]]
            fresh = fresh - jnp.dot(panels[b + 1], steps[b + 1], preferred_element_type=f32)
        others = [j for j in range(count) if j not in (b, b + 1)]
        aside = [put_own] + [functools.partial(take_line, j) for j in others]
        aside += [functools.partial(take_panel, i) for i in range(b + 2, count)]
        aside += [
            functools.partial(take_change, i, j)
            for i in range(b + 1, count)
            for j in range(count)
            if (i, j) != (b + 1, b + 1)
        ]
    for call_it in aside:
        call_it()


def solve_kernel(apart, rows_in, share, index_ref, inverse_ref, effects_ref, cov_ref, marks_ref, noise_ref, *refs):
    piece_refs, (solved_ref, resid_ref, packed) = refs[:-3], refs[-3:]
    rows, lanes, same = eye()
    extra = None
    for mask, ref in zip(apart, piece_refs):
        at = pl.multiple_of(jnp.bitwise_xor(index_ref[0], mask) * share, share)
        packed[pl.ds(at, share), :], more = take_sums(ref, rows_in, share)
        extra = more if extra is None else extra
    normal = []
    for pair in range(LEVELS // 2):
        both = packed[pair * LANE : (pair + 1) * LANE, :]
        turned = both.T
        normal.append(jnp.where(rows >= lanes, both, turned))
        diagonal = jnp.where(same, extra[LEVELS + pair : LEVELS + pair + 1], turned)
        normal.append(jnp.where(rows < lanes, both, diagonal))

    inverse = inverse_ref[...]
    spans = [slice(level * LANE, (level + 1) * LANE) for level in range(LEVELS)]
    gradient = []
    for level in range(LEVELS):
        column = to_column(effects_ref[level : level + 1, :], same)
        gradient.append(jnp.sum(normal[level] * column, axis=0, keepdims=True) + extra[level : level + 1])
    steer = jnp.sum(inverse * jnp.concatenate(gradient, axis=1), axis=1, keepdims=True)
    direction = steer
    gamma = jnp.sum(steer * steer, axis=0, keepdims=True)
    solved = jnp.zeros((1, cov_ref.shape[1] * LEVELS), f32)
    for step in range(ITERS):
        move = jnp.sum(inverse * direction, axis=0, keepdims=True)
        image = []
        for level, span in enumerate(spans):
            image.append(jnp.sum(normal[level] * to_column(move[:, span], same), axis=0, keepdims=True))
        image = jnp.concatenate(image, axis=1)
        alpha = gamma / jnp.sum(move * image, axis=1, keepdims=True)
        solved = solved + alpha * move
        if step == ITERS - 1:
            break
        steer = steer - alpha * jnp.sum(inverse * image, axis=1, keepdims=True)
        gamma_new = jnp.sum(steer * steer, axis=0, keepdims=True)
        direction = steer + gamma_new / gamma * direction
        gamma = gamma_new
    solved = jnp.concatenate([solved[:, span] for span in spans])
    solved_ref[...] = solved

    left = jnp.concatenate([effects_ref[...] - solved, jnp.zeros((PACK - LEVELS, LANE), f32)])
    values = jnp.zeros((SUB, cov_ref.shape[0]), f32)
    for part in split(left):
        values = values + lax.dot_general(part, cov_ref[...], NT, preferred_element_type=f32)[:SUB]
    for r in range(marks_ref.shape[0]):
        code = jnp.bitwise_and(marks_ref[r : r + 1, :], LEVELS - 1)
        total = noise_ref[r : r + 1, :]
        for level in range(LEVELS):
            total = total + jnp.where(code == level, values[level : level + 1, r * LANE : (r + 1) * LANE], 0.0)
        resid_ref[r : r + 1, :] = total


def call(kernel, name, outs, scratch, *operands):
    return pl.pallas_call(
        kernel,
        out_shape=[jax.ShapeDtypeStruct(shape, dtype) for shape, dtype in outs],
        in_specs=[SMEM if operand.ndim == 1 else VMEM for operand in operands],
        out_specs=[VMEM] * len(outs),
        scratch_shapes=[pltpu.VMEM(shape, dtype) for shape, dtype in scratch],
        compiler_params=pltpu.CompilerParams(vmem_limit_bytes=40 * 2**20),
        name=name,
    )(*operands)


def body(covariates, level_codes, sign_bits, sample_rows, effects, noise):
    wide, narrow = lax.axis_size("wide"), lax.axis_size("narrow")
    index = jnp.stack([lax.axis_index("wide"), lax.axis_index("narrow")]).astype(jnp.int32)
    rows_dev, cols = covariates.shape[0], LEVELS * COV
    samp = whole_up(sample_rows.shape[0], PACK)
    share = whole_up(max(2 * LANE // wide, 3 * SUB), PACK)
    sample_rows = jnp.pad(sample_rows, (0, samp - sample_rows.shape[0]), constant_values=-1)
    marks = (level_codes + LEVELS * sign_bits).reshape(-1, LANE)
    noise = noise.reshape(-1, LANE)
    effects = effects.reshape(LEVELS, COV)

    want = sample_rows[None, :]
    want = [want] + [partner(want, "wide", m) for m in range(2, MATES, 2)]
    want = [one for piece in want for one in (piece, partner(piece, "wide", 1))]

    design, packed = call(
        design_kernel,
        "design",
        [((cols + 3 * PACK, rows_dev), bf16), ((share * wide + SUB, LANE), f32)],
        [],
        covariates,
        marks,
        noise,
    )
    sizes = [samp * (2 * m < MATES) + share for m in range(wide // 2)]
    starts = [sum(sizes[:m]) for m in range(wide // 2)]
    stay, go = call(
        functools.partial(local_kernel, samp, share, starts),
        "local",
        [((sum(sizes), cols), bf16)] * 2,
        [((MATES * samp, rows_dev), bf16)],
        index,
        design,
        packed,
        marks,
        *want,
    )
    pieces = call(
        functools.partial(pair_kernel, samp, share, starts),
        "pair",
        [((size, cols), bf16) for size in sizes],
        [],
        index,
        stay,
        partner(go, "wide", 1),
    )
    pieces = [pieces[0]] + [partner(pieces[m], "wide", 2 * m) for m in range(1, wide // 2)]
    (piece,) = call(
        functools.partial(mix_kernel, samp, share), "mix", [((samp + share, cols), bf16)], [], index, *pieces
    )
    pieces = [piece] + [partner(piece, "narrow", m) for m in range(1, narrow)]
    rows_in = samp * narrow
    (piece,) = call(
        functools.partial(stack_kernel, samp, share), "stack", [((rows_in + share, cols), bf16)], [], index, *pieces
    )
    pieces = [piece] + [partner(piece, "wide", m) for m in range(2, wide, 2)]
    theirs = [partner(piece, "wide", 1) for piece in pieces]
    sketch = [((rows_in * (wide // 2), cols), bf16)]
    square = ((cols, cols), f32)
    (gram,) = call(functools.partial(gram_kernel, rows_in), "gram", [square], sketch, index, *pieces)
    factor, inverse = call(
        functools.partial(factor_kernel, math.sqrt(LEVELS / SKETCH), rows_in),
        "factor",
        [square] * 2,
        sketch + [square, ((2 * (SUB + 1) * SUB, LANE), f32)],
        index,
        gram,
        *theirs,
    )
    pieces += theirs
    apart = [2 * m + core for core in range(2) for m in range(wide // 2)]
    solved, resid = call(
        functools.partial(solve_kernel, apart, rows_in, share),
        "solve",
        [((LEVELS, COV), f32), (noise.shape, f32)],
        [((share * wide, LANE), f32)],
        index,
        inverse,
        effects,
        covariates,
        marks,
        noise,
        *pieces,
    )
    return solved.reshape(-1), resid.reshape(-1), factor


def solution(mesh):
    return jax.shard_map(
        body,
        mesh=mesh,
        in_specs=(
            P(("wide", "narrow"), None),
            P(("wide", "narrow")),
            P(("wide", "narrow")),
            P(("wide", "narrow")),
            P(),
            P(("wide", "narrow")),
        ),
        out_specs=(P(), P(("wide", "narrow")), P()),
        check_vma=False,
    )
```

```python
import functools
import math

import jax
import jax.numpy as jnp
from jax import lax
from jax.experimental import pallas as pl
from jax.experimental.pallas import tpu as pltpu
from jax.sharding import PartitionSpec as P

COV = 128
LEVELS = 4
HB = 256
SKETCH = 1024
ITERS = 4
MIX_BITS = 3
MATES = 2**MIX_BITS

half_root = math.sqrt(0.5)
HIGHEST = lax.Precision.HIGHEST
f32, bf16 = jnp.float32, jnp.bfloat16
SUB, LANE = 8, 128
PACK = 16
NT = (((1,), (1,)), ((), ()))
VMEM = pl.BlockSpec(memory_space=pltpu.VMEM)
SMEM = pl.BlockSpec(memory_space=pltpu.SMEM)


def partner(value, axis, mask):
    pairs = [(source, source ^ mask) for source in range(lax.axis_size(axis))]
    return lax.ppermute(value, axis, pairs)


def whole_up(number, unit):
    return -(-number // unit) * unit


def eye():
    rows = lax.broadcasted_iota(jnp.int32, (LANE, LANE), 0)
    lanes = lax.broadcasted_iota(jnp.int32, (LANE, LANE), 1)
    return rows, lanes, rows == lanes


def to_column(row, same):
    return jnp.sum(jnp.where(same, row, 0.0), axis=1, keepdims=True)


def to_row(column, same):
    return jnp.sum(jnp.where(same, column, 0.0), axis=0, keepdims=True)


def split(value):
    parts = []
    for _ in range(3):
        parts.append(value.astype(bf16))
        value = value - parts[-1].astype(f32)
    return parts


def tree_sum(values):
    while len(values) > 1:
        values = [left + right for left, right in zip(values[0::2], values[1::2])]
    return values[0]


def put_sums(ref, start, share, extra):
    rows = share.shape[0]
    for k, part in enumerate(split(share)):
        ref[start : start + rows, k * LANE : (k + 1) * LANE] = part
    tail = jnp.zeros((rows - 3 * SUB, LANE), bf16)
    ref[start : start + rows, 3 * LANE :] = jnp.concatenate(split(extra) + [tail])


def take_sums(ref, start, rows):
    block = ref[start : start + rows, :].astype(f32)
    share = block[:, :LANE] + block[:, LANE : 2 * LANE] + block[:, 2 * LANE : 3 * LANE]
    tail = block[:, 3 * LANE :]
    return share, tail[:SUB] + tail[SUB : 2 * SUB] + tail[2 * SUB : 3 * SUB]


def design_kernel(cov_ref, marks_ref, noise_ref, design, packed):
    rows, lanes, same = eye()
    zero = jnp.zeros((LANE, LANE), f32)
    for r in range(marks_ref.shape[0]):
        here = slice(r * LANE, (r + 1) * LANE)
        code = jnp.bitwise_and(marks_ref[r : r + 1, :], LEVELS - 1)
        turned = cov_ref[here, :].astype(f32).T
        for level in range(LEVELS):
            design[level * LANE : (level + 1) * LANE, here] = jnp.where(code == level, turned, zero).astype(bf16)
        noise = jnp.concatenate([noise_ref[r : r + 1, :]] * LEVELS + [jnp.zeros((PACK - LEVELS, LANE), f32)])
        level = lax.broadcasted_iota(jnp.int32, (PACK, LANE), 0)
        noise = jnp.where(code == level, noise, 0.0)
        for k, part in enumerate(split(noise)):
            design[LEVELS * LANE + k * PACK : LEVELS * LANE + (k + 1) * PACK, here] = part

    sums = jnp.dot(design[...], cov_ref[...], preferred_element_type=f32)
    normal = [sums[level * LANE : (level + 1) * LANE] for level in range(LEVELS)]
    back = sums[LEVELS * LANE :]
    back = back[:SUB] + back[PACK : PACK + SUB] + back[2 * PACK : 2 * PACK + SUB]
    extra = [jnp.sum(jnp.where(same, normal[level], 0.0), axis=0, keepdims=True) for level in (1, 3)]
    for pair in range(LEVELS // 2):
        packed[pair * LANE : (pair + 1) * LANE, :] = jnp.where(rows >= lanes, normal[2 * pair], normal[2 * pair + 1])
    rest = packed.shape[0] - SUB - 2 * LANE
    if rest:
        packed[2 * LANE : 2 * LANE + rest, :] = jnp.zeros((rest, LANE), f32)
    packed[2 * LANE + rest :, :] = jnp.concatenate([back[:LEVELS]] + extra + [jnp.zeros((2, LANE), f32)])


def local_kernel(samp, share, starts, index_ref, design_ref, packed_ref, marks_ref, *refs):
    want_refs, (stay_ref, go_ref, table) = refs[:-3], refs[-3:]
    chunks = marks_ref.shape[0]
    lanes = eye()[1]
    zero = jnp.zeros((LANE, LANE), f32)
    per = LANE // samp
    small = lax.broadcasted_iota(jnp.int32, (samp, samp), 0) == lax.broadcasted_iota(jnp.int32, (samp, samp), 1)

    masks, halves = [], []
    for c in range(MATES // per):
        want = [to_column(ref[...].astype(f32), small) for ref in want_refs[c * per : (c + 1) * per]]
        want = jnp.concatenate(want).astype(jnp.int32)
        masks.append(jnp.right_shift(want, HB.bit_length() - 1))
        line = []
        for h in range(HB // LANE):
            common = jnp.bitwise_and(want, lanes + h * LANE)
            for shift in (4, 2, 1):
                common = jnp.bitwise_xor(common, jnp.right_shift(common, shift))
            line.append((1 - 2 * jnp.bitwise_and(common, 1)).astype(f32))
        halves.append(line)
    for r in range(chunks):
        sign = jnp.where(marks_ref[r : r + 1, :] < LEVELS, 1.0, -1.0)
        block, h = divmod(r * LANE, HB)
        for c, (mask, line) in enumerate(zip(masks, halves)):
            value = jnp.where(mask == block, line[h // LANE] * sign, zero)
            table[c * LANE : (c + 1) * LANE, r * LANE : (r + 1) * LANE] = value.astype(bf16)

    local = lax.dot_general(table[...], design_ref[: LEVELS * LANE, :], NT, preferred_element_type=f32)
    local = (local * (1.0 / math.sqrt(HB))).astype(bf16)
    extra = packed_ref[packed_ref.shape[0] - SUB :, :]
    for m in range(2 * len(starts)):
        out_ref, start = (stay_ref, go_ref)[m % 2], starts[m // 2]
        if m < MATES:
            out_ref[start : start + samp, :] = local[m * samp : (m + 1) * samp]
            start += samp
        at = pl.multiple_of(jnp.bitwise_xor(index_ref[0], m) * share, share)
        put_sums(out_ref, start, packed_ref[pl.ds(at, share), :], extra)


def butterfly(pieces, place, index):
    bit = jnp.bitwise_and(jnp.right_shift(index, place), 1)
    sign = (1 - 2 * bit).astype(f32)
    return [
        ((sign * own + other) * half_root).astype(bf16).astype(f32) for own, other in zip(pieces[0::2], pieces[1::2])
    ]


def pair_kernel(samp, share, starts, index_ref, stay_ref, came_ref, *out_refs):
    for m, (start, out_ref) in enumerate(zip(starts, out_refs)):
        put = 0
        if 2 * m < MATES:
            here = slice(start, start + samp)
            pieces = [ref[here, :].astype(f32) for ref in (stay_ref, came_ref)]
            out_ref[:samp, :] = butterfly(pieces, 0, index_ref[0])[0].astype(bf16)
            put, start = samp, start + samp
        (own, own_extra), (other, other_extra) = [take_sums(ref, start, share) for ref in (stay_ref, came_ref)]
        put_sums(out_ref, put, own + other, own_extra + other_extra)


def mix_kernel(samp, share, index_ref, *refs):
    piece_refs, out_ref = refs[:-1], refs[-1]
    pieces = [ref[:samp, :].astype(f32) for ref in piece_refs[: MATES // 2]]
    for place in range(1, MIX_BITS):
        pieces = butterfly(pieces, place, index_ref[0])
    out_ref[:samp, :] = pieces[0].astype(bf16)
    sums = [take_sums(ref, samp if 2 * m < MATES else 0, share) for m, ref in enumerate(piece_refs)]
    put_sums(out_ref, samp, tree_sum([one for one, _ in sums]), tree_sum([one for _, one in sums]))


def stack_kernel(samp, share, index_ref, *refs):
    piece_refs, out_ref = refs[:-1], refs[-1]
    for m, ref in enumerate(piece_refs):
        at = pl.multiple_of(jnp.bitwise_xor(index_ref[1], m) * samp, samp)
        out_ref[pl.ds(at, samp), :] = ref[:samp, :]
    sums = [take_sums(ref, samp, share) for ref in piece_refs]
    put_sums(
        out_ref, samp * len(piece_refs), tree_sum([one for one, _ in sums]), tree_sum([one for _, one in sums])
    )


def spread(value):
    return jnp.broadcast_to(value, (SUB, LANE))


def reciprocal(value):
    return pltpu.reciprocal(value, approx=True)


def eliminate(tiles, aside, shelf):
    share = -(-len(aside) // len(tiles))
    lane = lax.broadcasted_iota(jnp.int32, (SUB, LANE), 1)
    sub = lax.broadcasted_iota(jnp.int32, (SUB, LANE), 0)
    tiles = list(tiles)
    scales = []
    for tile in range(len(tiles)):
        first = tile * SUB
        window = (lane >= first) & (lane < first + SUB)
        marks = [lane == first + k for k in range(SUB)]
        old = tiles[tile]
        columns = [spread(old[:, first + k : first + k + 1]) for k in range(SUB)]
        base = tile % 2 * (SUB + 1) * SUB
        shelf[base : base + SUB, :] = jnp.where(window, 0.0, old)
        for m in range(SUB):
            shelf[base + (m + 1) * SUB : base + (m + 2) * SUB, :] = columns[m]

        def take(m, k):
            at = base + m * SUB + k
            return spread(shelf[at : at + 1, :])

        pivot = [[take(m + 1, k) if m >= k else None for m in range(SUB)] for k in range(SUB)]
        rows = [jnp.where(marks[k], 1.0, take(0, k)) for k in range(SUB)]
        steps, near, far = [None] * SUB, {}, {}
        kept, roots = [None] * SUB, [None] * SUB

        def keep(k, low, ratio, values, others):
            last = others[k + 1]
            kept[k] = rows[k]
            for m in range(k, SUB):
                kept[k] = jnp.where(marks[m], values[m], kept[k])
            kept[k + 1] = rows[k + 1] - ratio * rows[k]
            for m in range(k + 1, SUB):
                kept[k + 1] = jnp.where(marks[m], others[m], kept[k + 1])
            roots[k], roots[k + 1] = lax.rsqrt(low), lax.rsqrt(last)

        for k in range(0, SUB, 4):
            low, cross, high = pivot[k][k], pivot[k][k + 1], pivot[k + 1][k + 1]
            area = low * high - cross * cross
            drop = {}
            for m in range(k + 2, SUB):
                near[k, m] = high * pivot[k][m] - cross * pivot[k + 1][m]
                far[k, m] = low * pivot[k + 1][m] - cross * pivot[k][m]
            for m in range(k + 2, SUB):
                for n in range(m, SUB):
                    drop[m, n] = pivot[k][m] * near[k, n] + pivot[k + 1][m] * far[k, n]
            c, d = k + 2, k + 3
            grown = {(m, n): area * pivot[m][n] - drop[m, n] for m in (c, d) for n in range(m, SUB)}
            low2, cross2, high2 = grown[c, c], grown[c, d], grown[d, d]
            area2 = low2 * high2 - cross2 * cross2
            over, over2 = reciprocal(area), reciprocal(area2)
            for m in range(k + 4, SUB):
                near[c, m] = high2 * grown[c, m] - cross2 * grown[d, m]
                far[c, m] = low2 * grown[d, m] - cross2 * grown[c, m]
            for m in range(k + 4, SUB):
                for n in range(m, SUB):
                    drop2 = grown[c, m] * near[c, n] + grown[d, m] * far[c, n]
                    pivot[m][n] = pivot[m][n] - over * (drop[m, n] + over2 * drop2)
            for m in range(k + 2, SUB):
                near[k, m], far[k, m] = over * near[k, m], over * far[k, m]
                rows[m] = rows[m] - (near[k, m] * rows[k] + far[k, m] * rows[k + 1])
            for m in range(k + 4, SUB):
                near[c, m], far[c, m] = over2 * near[c, m], over2 * far[c, m]
                rows[m] = rows[m] - (near[c, m] * rows[c] + far[c, m] * rows[d])
            steps[k] = over * (high * rows[k] - cross * rows[k + 1])
            steps[k + 1] = over * (low * rows[k + 1] - cross * rows[k])
            both = area * over2
            steps[c] = both * (high2 * rows[c] - cross2 * rows[d])
            steps[d] = both * (low2 * rows[d] - cross2 * rows[c])

            inner = reciprocal(low)
            ratio = cross * inner
            values = {m: pivot[k][m] for m in range(k, SUB)}
            others = {m: pivot[k + 1][m] - ratio * pivot[k][m] for m in range(k + 2, SUB)}
            others[k + 1] = area * inner
            keep(k, low, ratio, values, others)
            inner = reciprocal(low2)
            ratio = cross2 * inner
            values = {m: over * grown[c, m] for m in range(c, SUB)}
            others = {m: over * (grown[d, m] - ratio * grown[c, m]) for m in range(c + 2, SUB)}
            others[d] = over * (area2 * inner)
            keep(c, values[c], ratio, values, others)
        if tile + 1 < len(tiles):
            after = tiles[tile + 1]
            ahead = [spread(after[:, first + k : first + k + 1]) for k in range(SUB)]
            fresh = jnp.where(window, 0.0, after)
            for k in range(0, SUB, 2):
                for m in range(k + 2, SUB):
                    ahead[m] = ahead[m] - (near[k, m] * ahead[k] + far[k, m] * ahead[k + 1])
                fresh = fresh - (ahead[k] * steps[k] + ahead[k + 1] * steps[k + 1])
        for k in reversed(range(0, SUB, 2)):
            for m in reversed(range(k + 2, SUB)):
                steps[k] = steps[k] - near[k, m] * steps[m]
                steps[k + 1] = steps[k + 1] - far[k, m] * steps[m]
        for i in range(tile + 2, min(tile + 3, len(tiles))):
            change = [spread(tiles[i][:, first + k : first + k + 1]) * steps[k] for k in range(SUB)]
            tiles[i] = jnp.where(window, 0.0, tiles[i]) - tree_sum(change[::-1])
        if tile + 3 < len(tiles):
            stacked = steps[0]
            for k in range(1, SUB):
                stacked = jnp.where(sub >= k, steps[k], stacked)
            blank = jnp.zeros_like(stacked)
            stacked = jnp.concatenate([stacked, blank] if tile % 2 == 0 else [blank, stacked])
            none = jnp.zeros((PACK, LANE), bf16)
            before, after = tile // 2, len(tiles) // 2 - 1 - tile // 2
            parts = [jnp.concatenate([none] * before + [part] + [none] * after) for part in split(stacked)]
            change = jnp.dot(
                parts_of(jnp.concatenate(tiles[tile + 3 :]), LEFT, 1),
                jnp.concatenate([parts[k] for k in RIGHT]),
                preferred_element_type=f32,
            )
            for i in range(tile + 3, len(tiles)):
                at = (i - tile - 3) * SUB
                tiles[i] = jnp.where(window, 0.0, tiles[i]) - change[at : at + SUB]
        if tile + 1 < len(tiles):
            tiles[tile + 1] = fresh
        new, scale = kept[0], roots[0]
        for k in range(1, SUB):
            new = jnp.where(sub >= k, kept[k], new)
            scale = jnp.where(sub >= k, roots[k], scale)
        tiles[tile] = new
        scales.append(scale)
        for work in aside[tile * share : (tile + 1) * share]:
            work()
    return tiles, scales


LEFT, RIGHT = (0, 1, 0, 1, 2, 0), (0, 0, 1, 1, 0, 2)


def parts_of(value, order, axis):
    parts = split(value)
    return jnp.concatenate([parts[k] for k in order], axis=axis)


def put_pieces(rows_in, index_ref, piece_refs, sketch):
    for m, ref in enumerate(piece_refs):
        at = jnp.bitwise_xor(jnp.right_shift(index_ref[0], 1), m) * rows_in
        sketch[pl.ds(pl.multiple_of(at, rows_in), rows_in), :] = ref[:rows_in, :]


def gram_rows(sketch, here):
    return lax.dot_general(sketch[:, here], sketch[...], (((0,), (0,)), ((), ())), preferred_element_type=f32)


def gram_kernel(rows_in, index_ref, *refs):
    piece_refs, (gram_ref, sketch) = refs[:-2], refs[-2:]
    put_pieces(rows_in, index_ref, piece_refs, sketch)
    for at in range(0, gram_ref.shape[0], LANE):
        gram_ref[at : at + LANE, :] = gram_rows(sketch, slice(at, at + LANE))


def factor_kernel(ratio, rows_in, index_ref, gram_ref, *refs):
    piece_refs, (factor_ref, inverse_ref, sketch, work, shelf) = refs[:-5], refs[-5:]
    count = work.shape[0] // LANE
    spans = [slice(at, at + LANE) for at in range(0, work.shape[0], LANE)]
    row_in, lane_in, same = eye()
    diagonals, units = [None] * count, [None] * count
    put_pieces(rows_in, index_ref, piece_refs, sketch)

    def take_rows(i):
        work[spans[i], :] = gram_ref[spans[i], :] + gram_rows(sketch, spans[i])

    def take_unit(i):
        diagonals[i] = jnp.sum(jnp.where(same, work[spans[i], spans[i]], 0.0), axis=0, keepdims=True)
        units[i] = lax.rsqrt(diagonals[i])

    def scale_rows(i):
        work[spans[i], :] = work[spans[i], :] * to_column(units[i], same) * jnp.concatenate(units, axis=1)

    take_rows(0)
    take_unit(0)
    fresh = work[spans[0], spans[0]] * to_column(units[0], same) * units[0]
    aside = [functools.partial(take_rows, i) for i in range(1, count)]
    aside += [functools.partial(take_unit, i) for i in range(1, count)]
    aside += [functools.partial(scale_rows, i) for i in range(count)]
    for b, here in enumerate(spans):
        tiles, scales = eliminate([fresh[at : at + SUB] for at in range(0, LANE, SUB)], aside, shelf)
        scale = jnp.concatenate(scales)
        inner = jnp.concatenate(tiles) * scale
        lower = jnp.where(lane_in < row_in, inner, jnp.where(lane_in == row_in, scale, 0.0))
        lower_left, lower_right = parts_of(lower, LEFT, 1), parts_of(lower, RIGHT, 1)
        panels, steps = {}, {}

        def take_line(j, b=b, here=here, lower_left=lower_left, steps=steps):
            line = jnp.dot(lower_left, parts_of(work[here, spans[j]], RIGHT, 0), preferred_element_type=f32)
            steps[j] = parts_of(line, RIGHT, 0)
            if j > b:
                factor_ref[here, spans[j]] = line * (diagonals[j] * units[j] * ratio)
                inverse_ref[here, spans[j]] = jnp.zeros((LANE, LANE), f32)
            else:
                factor_ref[here, spans[j]] = jnp.zeros((LANE, LANE), f32)
                inverse_ref[here, spans[j]] = line * units[j]

        def take_panel(i, here=here, lower_right=lower_right, panels=panels):
            panel = parts_of(work[spans[i], here], LEFT, 1)
            panels[i] = parts_of(lax.dot_general(panel, lower_right, NT, preferred_element_type=f32), LEFT, 1)

        def take_change(i, j, b=b, panels=panels, steps=steps):
            change = jnp.dot(panels[i], steps[j], preferred_element_type=f32)
            work[spans[i], spans[j]] = -change if j == b else work[spans[i], spans[j]] - change

        def put_own(here=here, inner=inner, lower=lower, b=b, steps=steps):
            steps[b] = parts_of(lower, RIGHT, 0)
            factor_ref[here, here] = jnp.where(lane_in >= row_in, inner, 0.0) * (diagonals[b] * units[b] * ratio)
            inverse_ref[here, here] = lower * units[b]

        if b + 1 < count:
            take_line(b + 1)
            take_panel(b + 1)
            fresh = work[spans[b + 1], spans[b + 1]]
            fresh = fresh - jnp.dot(panels[b + 1], steps[b + 1], preferred_element_type=f32)
        others = [j for j in range(count) if j not in (b, b + 1)]
        aside = [put_own] + [functools.partial(take_line, j) for j in others]
        aside += [functools.partial(take_panel, i) for i in range(b + 2, count)]
        aside += [
            functools.partial(take_change, i, j)
            for i in range(b + 1, count)
            for j in range(count)
            if (i, j) != (b + 1, b + 1)
        ]
    for call_it in aside:
        call_it()


def solve_kernel(apart, rows_in, share, index_ref, inverse_ref, effects_ref, cov_ref, marks_ref, noise_ref, *refs):
    piece_refs, (solved_ref, resid_ref, packed) = refs[:-3], refs[-3:]
    rows, lanes, same = eye()
    extra = None
    for mask, ref in zip(apart, piece_refs):
        at = pl.multiple_of(jnp.bitwise_xor(index_ref[0], mask) * share, share)
        packed[pl.ds(at, share), :], more = take_sums(ref, rows_in, share)
        extra = more if extra is None else extra
    normal = []
    for pair in range(LEVELS // 2):
        both = packed[pair * LANE : (pair + 1) * LANE, :]
        turned = both.T
        normal.append(jnp.where(rows >= lanes, both, turned))
        diagonal = jnp.where(same, extra[LEVELS + pair : LEVELS + pair + 1], turned)
        normal.append(jnp.where(rows < lanes, both, diagonal))

    inverse = inverse_ref[...]
    spans = [slice(level * LANE, (level + 1) * LANE) for level in range(LEVELS)]
    gradient = []
    for level in range(LEVELS):
        column = to_column(effects_ref[level : level + 1, :], same)
        gradient.append(jnp.sum(normal[level] * column, axis=0, keepdims=True) + extra[level : level + 1])
    steer = jnp.sum(inverse * jnp.concatenate(gradient, axis=1), axis=1, keepdims=True)
    direction = steer
    gamma = jnp.sum(steer * steer, axis=0, keepdims=True)
    solved = jnp.zeros((1, cov_ref.shape[1] * LEVELS), f32)
    for step in range(ITERS):
        move = jnp.sum(inverse * direction, axis=0, keepdims=True)
        image = []
        for level, span in enumerate(spans):
            image.append(jnp.sum(normal[level] * to_column(move[:, span], same), axis=0, keepdims=True))
        image = jnp.concatenate(image, axis=1)
        alpha = gamma / jnp.sum(move * image, axis=1, keepdims=True)
        solved = solved + alpha * move
        if step == ITERS - 1:
            break
        steer = steer - alpha * jnp.sum(inverse * image, axis=1, keepdims=True)
        gamma_new = jnp.sum(steer * steer, axis=0, keepdims=True)
        direction = steer + gamma_new / gamma * direction
        gamma = gamma_new
    solved = jnp.concatenate([solved[:, span] for span in spans])
    solved_ref[...] = solved

    left = jnp.concatenate([effects_ref[...] - solved, jnp.zeros((PACK - LEVELS, LANE), f32)])
    values = jnp.zeros((SUB, cov_ref.shape[0]), f32)
    for part in split(left):
        values = values + lax.dot_general(part, cov_ref[...], NT, preferred_element_type=f32)[:SUB]
    for r in range(marks_ref.shape[0]):
        code = jnp.bitwise_and(marks_ref[r : r + 1, :], LEVELS - 1)
        total = noise_ref[r : r + 1, :]
        for level in range(LEVELS):
            total = total + jnp.where(code == level, values[level : level + 1, r * LANE : (r + 1) * LANE], 0.0)
        resid_ref[r : r + 1, :] = total


def call(kernel, name, outs, scratch, *operands):
    return pl.pallas_call(
        kernel,
        out_shape=[jax.ShapeDtypeStruct(shape, dtype) for shape, dtype in outs],
        in_specs=[SMEM if operand.ndim == 1 else VMEM for operand in operands],
        out_specs=[VMEM] * len(outs),
        scratch_shapes=[pltpu.VMEM(shape, dtype) for shape, dtype in scratch],
        compiler_params=pltpu.CompilerParams(vmem_limit_bytes=40 * 2**20),
        name=name,
    )(*operands)


def body(covariates, level_codes, sign_bits, sample_rows, effects, noise):
    wide, narrow = lax.axis_size("wide"), lax.axis_size("narrow")
    index = jnp.stack([lax.axis_index("wide"), lax.axis_index("narrow")]).astype(jnp.int32)
    rows_dev, cols = covariates.shape[0], LEVELS * COV
    samp = whole_up(sample_rows.shape[0], PACK)
    share = whole_up(max(2 * LANE // wide, 3 * SUB), PACK)
    sample_rows = jnp.pad(sample_rows, (0, samp - sample_rows.shape[0]), constant_values=-1)
    marks = (level_codes + LEVELS * sign_bits).reshape(-1, LANE)
    noise = noise.reshape(-1, LANE)
    effects = effects.reshape(LEVELS, COV)

    want = sample_rows[None, :]
    want = [want] + [partner(want, "wide", m) for m in range(2, MATES, 2)]
    want = [one for piece in want for one in (piece, partner(piece, "wide", 1))]

    design, packed = call(
        design_kernel,
        "design",
        [((cols + 3 * PACK, rows_dev), bf16), ((share * wide + SUB, LANE), f32)],
        [],
        covariates,
        marks,
        noise,
    )
    sizes = [samp * (2 * m < MATES) + share for m in range(wide // 2)]
    starts = [sum(sizes[:m]) for m in range(wide // 2)]
    stay, go = call(
        functools.partial(local_kernel, samp, share, starts),
        "local",
        [((sum(sizes), cols), bf16)] * 2,
        [((MATES * samp, rows_dev), bf16)],
        index,
        design,
        packed,
        marks,
        *want,
    )
    pieces = call(
        functools.partial(pair_kernel, samp, share, starts),
        "pair",
        [((size, cols), bf16) for size in sizes],
        [],
        index,
        stay,
        partner(go, "wide", 1),
    )
    pieces = [pieces[0]] + [partner(pieces[m], "wide", 2 * m) for m in range(1, wide // 2)]
    (piece,) = call(
        functools.partial(mix_kernel, samp, share), "mix", [((samp + share, cols), bf16)], [], index, *pieces
    )
    pieces = [piece] + [partner(piece, "narrow", m) for m in range(1, narrow)]
    rows_in = samp * narrow
    (piece,) = call(
        functools.partial(stack_kernel, samp, share), "stack", [((rows_in + share, cols), bf16)], [], index, *pieces
    )
    pieces = [piece] + [partner(piece, "wide", m) for m in range(2, wide, 2)]
    theirs = [partner(piece, "wide", 1) for piece in pieces]
    sketch = [((rows_in * (wide // 2), cols), bf16)]
    square = ((cols, cols), f32)
    (gram,) = call(functools.partial(gram_kernel, rows_in), "gram", [square], sketch, index, *pieces)
    factor, inverse = call(
        functools.partial(factor_kernel, math.sqrt(LEVELS / SKETCH), rows_in),
        "factor",
        [square] * 2,
        sketch + [square, ((2 * (SUB + 1) * SUB, LANE), f32)],
        index,
        gram,
        *theirs,
    )
    pieces += theirs
    apart = [2 * m + core for core in range(2) for m in range(wide // 2)]
    solved, resid = call(
        functools.partial(solve_kernel, apart, rows_in, share),
        "solve",
        [((LEVELS, COV), f32), (noise.shape, f32)],
        [((share * wide, LANE), f32)],
        index,
        inverse,
        effects,
        covariates,
        marks,
        noise,
        *pieces,
    )
    return solved.reshape(-1), resid.reshape(-1), factor


def solution(mesh):
    return jax.shard_map(
        body,
        mesh=mesh,
        in_specs=(
            P(("wide", "narrow"), None),
            P(("wide", "narrow")),
            P(("wide", "narrow")),
            P(("wide", "narrow")),
            P(),
            P(("wide", "narrow")),
        ),
        out_specs=(P(), P(("wide", "narrow")), P()),
        check_vma=False,
    )
```

```python
import functools
import math

import jax
import jax.numpy as jnp
from jax import lax
from jax.experimental import pallas as pl
from jax.experimental.pallas import tpu as pltpu
from jax.sharding import PartitionSpec as P

COV = 128
LEVELS = 4
HB = 256
SKETCH = 1024
ITERS = 4
MIX_BITS = 3
MATES = 2**MIX_BITS

half_root = math.sqrt(0.5)
HIGHEST = lax.Precision.HIGHEST
f32, bf16 = jnp.float32, jnp.bfloat16
SUB, LANE = 8, 128
PACK = 16
NT = (((1,), (1,)), ((), ()))
VMEM = pl.BlockSpec(memory_space=pltpu.VMEM)
SMEM = pl.BlockSpec(memory_space=pltpu.SMEM)


def partner(value, axis, mask):
    pairs = [(source, source ^ mask) for source in range(lax.axis_size(axis))]
    return lax.ppermute(value, axis, pairs)


def whole_up(number, unit):
    return -(-number // unit) * unit


def eye():
    rows = lax.broadcasted_iota(jnp.int32, (LANE, LANE), 0)
    lanes = lax.broadcasted_iota(jnp.int32, (LANE, LANE), 1)
    return rows, lanes, rows == lanes


def to_column(row, same):
    return jnp.sum(jnp.where(same, row, 0.0), axis=1, keepdims=True)


def to_row(column, same):
    return jnp.sum(jnp.where(same, column, 0.0), axis=0, keepdims=True)


def split(value):
    parts = []
    for _ in range(3):
        parts.append(value.astype(bf16))
        value = value - parts[-1].astype(f32)
    return parts


def tree_sum(values):
    while len(values) > 1:
        values = [left + right for left, right in zip(values[0::2], values[1::2])]
    return values[0]


def put_sums(ref, start, share, extra):
    rows = share.shape[0]
    for k, part in enumerate(split(share)):
        ref[start : start + rows, k * LANE : (k + 1) * LANE] = part
    tail = jnp.zeros((rows - 3 * SUB, LANE), bf16)
    ref[start : start + rows, 3 * LANE :] = jnp.concatenate(split(extra) + [tail])


def take_sums(ref, start, rows):
    block = ref[start : start + rows, :].astype(f32)
    share = block[:, :LANE] + block[:, LANE : 2 * LANE] + block[:, 2 * LANE : 3 * LANE]
    tail = block[:, 3 * LANE :]
    return share, tail[:SUB] + tail[SUB : 2 * SUB] + tail[2 * SUB : 3 * SUB]


def design_kernel(cov_ref, marks_ref, noise_ref, design, packed):
    rows, lanes, same = eye()
    zero = jnp.zeros((LANE, LANE), f32)
    for r in range(marks_ref.shape[0]):
        here = slice(r * LANE, (r + 1) * LANE)
        code = jnp.bitwise_and(marks_ref[r : r + 1, :], LEVELS - 1)
        turned = cov_ref[here, :].astype(f32).T
        for level in range(LEVELS):
            design[level * LANE : (level + 1) * LANE, here] = jnp.where(code == level, turned, zero).astype(bf16)
        noise = jnp.concatenate([noise_ref[r : r + 1, :]] * LEVELS + [jnp.zeros((PACK - LEVELS, LANE), f32)])
        level = lax.broadcasted_iota(jnp.int32, (PACK, LANE), 0)
        noise = jnp.where(code == level, noise, 0.0)
        for k, part in enumerate(split(noise)):
            design[LEVELS * LANE + k * PACK : LEVELS * LANE + (k + 1) * PACK, here] = part

    sums = jnp.dot(design[...], cov_ref[...], preferred_element_type=f32)
    normal = [sums[level * LANE : (level + 1) * LANE] for level in range(LEVELS)]
    back = sums[LEVELS * LANE :]
    back = back[:SUB] + back[PACK : PACK + SUB] + back[2 * PACK : 2 * PACK + SUB]
    extra = [jnp.sum(jnp.where(same, normal[level], 0.0), axis=0, keepdims=True) for level in (1, 3)]
    for pair in range(LEVELS // 2):
        packed[pair * LANE : (pair + 1) * LANE, :] = jnp.where(rows >= lanes, normal[2 * pair], normal[2 * pair + 1])
    rest = packed.shape[0] - SUB - 2 * LANE
    if rest:
        packed[2 * LANE : 2 * LANE + rest, :] = jnp.zeros((rest, LANE), f32)
    packed[2 * LANE + rest :, :] = jnp.concatenate([back[:LEVELS]] + extra + [jnp.zeros((2, LANE), f32)])


def local_kernel(samp, share, starts, index_ref, design_ref, packed_ref, marks_ref, *refs):
    want_refs, (stay_ref, go_ref, table) = refs[:-3], refs[-3:]
    chunks = marks_ref.shape[0]
    lanes = eye()[1]
    zero = jnp.zeros((LANE, LANE), f32)
    per = LANE // samp
    small = lax.broadcasted_iota(jnp.int32, (samp, samp), 0) == lax.broadcasted_iota(jnp.int32, (samp, samp), 1)

    masks, halves = [], []
    for c in range(MATES // per):
        want = [to_column(ref[...].astype(f32), small) for ref in want_refs[c * per : (c + 1) * per]]
        want = jnp.concatenate(want).astype(jnp.int32)
        masks.append(jnp.right_shift(want, HB.bit_length() - 1))
        line = []
        for h in range(HB // LANE):
            common = jnp.bitwise_and(want, lanes + h * LANE)
            for shift in (4, 2, 1):
                common = jnp.bitwise_xor(common, jnp.right_shift(common, shift))
            line.append((1 - 2 * jnp.bitwise_and(common, 1)).astype(f32))
        halves.append(line)
    for r in range(chunks):
        sign = jnp.where(marks_ref[r : r + 1, :] < LEVELS, 1.0, -1.0)
        block, h = divmod(r * LANE, HB)
        for c, (mask, line) in enumerate(zip(masks, halves)):
            value = jnp.where(mask == block, line[h // LANE] * sign, zero)
            table[c * LANE : (c + 1) * LANE, r * LANE : (r + 1) * LANE] = value.astype(bf16)

    local = lax.dot_general(table[...], design_ref[: LEVELS * LANE, :], NT, preferred_element_type=f32)
    local = (local * (1.0 / math.sqrt(HB))).astype(bf16)
    extra = packed_ref[packed_ref.shape[0] - SUB :, :]
    for m in range(2 * len(starts)):
        out_ref, start = (stay_ref, go_ref)[m % 2], starts[m // 2]
        if m < MATES:
            out_ref[start : start + samp, :] = local[m * samp : (m + 1) * samp]
            start += samp
        at = pl.multiple_of(jnp.bitwise_xor(index_ref[0], m) * share, share)
        put_sums(out_ref, start, packed_ref[pl.ds(at, share), :], extra)


def butterfly(pieces, place, index):
    bit = jnp.bitwise_and(jnp.right_shift(index, place), 1)
    sign = (1 - 2 * bit).astype(f32)
    return [
        ((sign * own + other) * half_root).astype(bf16).astype(f32) for own, other in zip(pieces[0::2], pieces[1::2])
    ]


def pair_kernel(samp, share, starts, index_ref, stay_ref, came_ref, *out_refs):
    for m, (start, out_ref) in enumerate(zip(starts, out_refs)):
        put = 0
        if 2 * m < MATES:
            here = slice(start, start + samp)
            pieces = [ref[here, :].astype(f32) for ref in (stay_ref, came_ref)]
            out_ref[:samp, :] = butterfly(pieces, 0, index_ref[0])[0].astype(bf16)
            put, start = samp, start + samp
        (own, own_extra), (other, other_extra) = [take_sums(ref, start, share) for ref in (stay_ref, came_ref)]
        put_sums(out_ref, put, own + other, own_extra + other_extra)


def mix_kernel(samp, share, index_ref, *refs):
    piece_refs, out_ref = refs[:-1], refs[-1]
    pieces = [ref[:samp, :].astype(f32) for ref in piece_refs[: MATES // 2]]
    for place in range(1, MIX_BITS):
        pieces = butterfly(pieces, place, index_ref[0])
    out_ref[:samp, :] = pieces[0].astype(bf16)
    sums = [take_sums(ref, samp if 2 * m < MATES else 0, share) for m, ref in enumerate(piece_refs)]
    put_sums(out_ref, samp, tree_sum([one for one, _ in sums]), tree_sum([one for _, one in sums]))


def stack_kernel(samp, share, index_ref, *refs):
    piece_refs, out_ref = refs[:-1], refs[-1]
    for m, ref in enumerate(piece_refs):
        at = pl.multiple_of(jnp.bitwise_xor(index_ref[1], m) * samp, samp)
        out_ref[pl.ds(at, samp), :] = ref[:samp, :]
    sums = [take_sums(ref, samp, share) for ref in piece_refs]
    put_sums(
        out_ref, samp * len(piece_refs), tree_sum([one for one, _ in sums]), tree_sum([one for _, one in sums])
    )


def spread(value):
    return jnp.broadcast_to(value, (SUB, LANE))


def reciprocal(value):
    return pltpu.reciprocal(value, approx=True)


def eliminate(tiles, aside, shelf):
    share = -(-len(aside) // len(tiles))
    lane = lax.broadcasted_iota(jnp.int32, (SUB, LANE), 1)
    sub = lax.broadcasted_iota(jnp.int32, (SUB, LANE), 0)
    tiles = list(tiles)
    scales = []
    for tile in range(len(tiles)):
        first = tile * SUB
        window = (lane >= first) & (lane < first + SUB)
        marks = [lane == first + k for k in range(SUB)]
        old = tiles[tile]
        columns = [spread(old[:, first + k : first + k + 1]) for k in range(SUB)]
        base = tile % 2 * (SUB + 1) * SUB
        shelf[base : base + SUB, :] = jnp.where(window, 0.0, old)
        for m in range(SUB):
            shelf[base + (m + 1) * SUB : base + (m + 2) * SUB, :] = columns[m]

        def take(m, k):
            at = base + m * SUB + k
            return spread(shelf[at : at + 1, :])

        pivot = [[take(m + 1, k) if m >= k else None for m in range(SUB)] for k in range(SUB)]
        rows = [jnp.where(marks[k], 1.0, take(0, k)) for k in range(SUB)]
        steps, near, far = [None] * SUB, {}, {}
        kept, roots = [None] * SUB, [None] * SUB

        def keep(k, low, ratio, values, others):
            last = others[k + 1]
            kept[k] = rows[k]
            for m in range(k, SUB):
                kept[k] = jnp.where(marks[m], values[m], kept[k])
            kept[k + 1] = rows[k + 1] - ratio * rows[k]
            for m in range(k + 1, SUB):
                kept[k + 1] = jnp.where(marks[m], others[m], kept[k + 1])
            roots[k], roots[k + 1] = lax.rsqrt(low), lax.rsqrt(last)

        for k in range(0, SUB, 4):
            low, cross, high = pivot[k][k], pivot[k][k + 1], pivot[k + 1][k + 1]
            area = low * high - cross * cross
            drop = {}
            for m in range(k + 2, SUB):
                near[k, m] = high * pivot[k][m] - cross * pivot[k + 1][m]
                far[k, m] = low * pivot[k + 1][m] - cross * pivot[k][m]
            for m in range(k + 2, SUB):
                for n in range(m, SUB):
                    drop[m, n] = pivot[k][m] * near[k, n] + pivot[k + 1][m] * far[k, n]
            c, d = k + 2, k + 3
            grown = {(m, n): area * pivot[m][n] - drop[m, n] for m in (c, d) for n in range(m, SUB)}
            low2, cross2, high2 = grown[c, c], grown[c, d], grown[d, d]
            area2 = low2 * high2 - cross2 * cross2
            over, over2 = reciprocal(area), reciprocal(area2)
            for m in range(k + 4, SUB):
                near[c, m] = high2 * grown[c, m] - cross2 * grown[d, m]
                far[c, m] = low2 * grown[d, m] - cross2 * grown[c, m]
            for m in range(k + 4, SUB):
                for n in range(m, SUB):
                    drop2 = grown[c, m] * near[c, n] + grown[d, m] * far[c, n]
                    pivot[m][n] = pivot[m][n] - over * (drop[m, n] + over2 * drop2)
            for m in range(k + 2, SUB):
                near[k, m], far[k, m] = over * near[k, m], over * far[k, m]
                rows[m] = rows[m] - (near[k, m] * rows[k] + far[k, m] * rows[k + 1])
            for m in range(k + 4, SUB):
                near[c, m], far[c, m] = over2 * near[c, m], over2 * far[c, m]
                rows[m] = rows[m] - (near[c, m] * rows[c] + far[c, m] * rows[d])
            steps[k] = over * (high * rows[k] - cross * rows[k + 1])
            steps[k + 1] = over * (low * rows[k + 1] - cross * rows[k])
            both = area * over2
            steps[c] = both * (high2 * rows[c] - cross2 * rows[d])
            steps[d] = both * (low2 * rows[d] - cross2 * rows[c])

            inner = reciprocal(low)
            ratio = cross * inner
            values = {m: pivot[k][m] for m in range(k, SUB)}
            others = {m: pivot[k + 1][m] - ratio * pivot[k][m] for m in range(k + 2, SUB)}
            others[k + 1] = area * inner
            keep(k, low, ratio, values, others)
            inner = reciprocal(low2)
            ratio = cross2 * inner
            values = {m: over * grown[c, m] for m in range(c, SUB)}
            others = {m: over * (grown[d, m] - ratio * grown[c, m]) for m in range(c + 2, SUB)}
            others[d] = over * (area2 * inner)
            keep(c, values[c], ratio, values, others)
        if tile + 1 < len(tiles):
            after = tiles[tile + 1]
            ahead = [spread(after[:, first + k : first + k + 1]) for k in range(SUB)]
            fresh = jnp.where(window, 0.0, after)
            for k in range(0, SUB, 2):
                for m in range(k + 2, SUB):
                    ahead[m] = ahead[m] - (near[k, m] * ahead[k] + far[k, m] * ahead[k + 1])
                fresh = fresh - (ahead[k] * steps[k] + ahead[k + 1] * steps[k + 1])
        for k in reversed(range(0, SUB, 2)):
            for m in reversed(range(k + 2, SUB)):
                steps[k] = steps[k] - near[k, m] * steps[m]
                steps[k + 1] = steps[k + 1] - far[k, m] * steps[m]
        for i in range(tile + 2, min(tile + 3, len(tiles))):
            change = [spread(tiles[i][:, first + k : first + k + 1]) * steps[k] for k in range(SUB)]
            tiles[i] = jnp.where(window, 0.0, tiles[i]) - tree_sum(change[::-1])
        if tile + 3 < len(tiles):
            stacked = steps[0]
            for k in range(1, SUB):
                stacked = jnp.where(sub >= k, steps[k], stacked)
            blank = jnp.zeros_like(stacked)
            stacked = jnp.concatenate([stacked, blank] if tile % 2 == 0 else [blank, stacked])
            none = jnp.zeros((PACK, LANE), bf16)
            before, after = tile // 2, len(tiles) // 2 - 1 - tile // 2
            parts = [jnp.concatenate([none] * before + [part] + [none] * after) for part in split(stacked)]
            change = jnp.dot(
                parts_of(jnp.concatenate(tiles[tile + 3 :]), LEFT, 1),
                jnp.concatenate([parts[k] for k in RIGHT]),
                preferred_element_type=f32,
            )
            for i in range(tile + 3, len(tiles)):
                at = (i - tile - 3) * SUB
                tiles[i] = jnp.where(window, 0.0, tiles[i]) - change[at : at + SUB]
        if tile + 1 < len(tiles):
            tiles[tile + 1] = fresh
        new, scale = kept[0], roots[0]
        for k in range(1, SUB):
            new = jnp.where(sub >= k, kept[k], new)
            scale = jnp.where(sub >= k, roots[k], scale)
        tiles[tile] = new
        scales.append(scale)
        for work in aside[tile * share : (tile + 1) * share]:
            work()
    return tiles, scales


LEFT, RIGHT = (0, 1, 0, 1, 2, 0), (0, 0, 1, 1, 0, 2)


def parts_of(value, order, axis):
    parts = split(value)
    return jnp.concatenate([parts[k] for k in order], axis=axis)


def put_pieces(rows_in, index_ref, piece_refs, sketch):
    for m, ref in enumerate(piece_refs):
        at = jnp.bitwise_xor(jnp.right_shift(index_ref[0], 1), m) * rows_in
        sketch[pl.ds(pl.multiple_of(at, rows_in), rows_in), :] = ref[:rows_in, :]


def gram_rows(sketch, here):
    return lax.dot_general(sketch[:, here], sketch[...], (((0,), (0,)), ((), ())), preferred_element_type=f32)


def gram_kernel(rows_in, index_ref, *refs):
    piece_refs, (gram_ref, sketch) = refs[:-2], refs[-2:]
    put_pieces(rows_in, index_ref, piece_refs, sketch)
    for at in range(0, gram_ref.shape[0], LANE):
        gram_ref[at : at + LANE, :] = gram_rows(sketch, slice(at, at + LANE))


def solve_kernel(
    ratio, apart, rows_in, share, index_ref, gram_ref, effects_ref, cov_ref, marks_ref, noise_ref, *refs
):
    piece_refs, (factor_hbm, solved_ref, resid_ref), scratch = refs[:-11], refs[-11:-8], refs[-8:]
    sketch, work, shelf, factor_ref, inverse_ref, packed, normal, sent = scratch
    count = work.shape[0] // LANE
    spans = [slice(at, at + LANE) for at in range(0, work.shape[0], LANE)]
    row_in, lane_in, same = eye()
    diagonals, units = [None] * count, [None] * count
    put_pieces(rows_in, index_ref, piece_refs[len(piece_refs) // 2 :], sketch)

    def take_rows(i):
        work[spans[i], :] = gram_ref[spans[i], :] + gram_rows(sketch, spans[i])

    def take_unit(i):
        diagonals[i] = jnp.sum(jnp.where(same, work[spans[i], spans[i]], 0.0), axis=0, keepdims=True)
        units[i] = lax.rsqrt(diagonals[i])

    def scale_rows(i):
        work[spans[i], :] = work[spans[i], :] * to_column(units[i], same) * jnp.concatenate(units, axis=1)

    extras, gradient = [], [None] * LEVELS

    def take_share(mask, ref):
        at = pl.multiple_of(jnp.bitwise_xor(index_ref[0], mask) * share, share)
        packed[pl.ds(at, share), :], extra = take_sums(ref, rows_in, share)
        extras.append(extra)

    def unpack(pair):
        both = packed[spans[pair], :]
        turned = both.T
        normal[spans[2 * pair], :] = jnp.where(row_in >= lane_in, both, turned)
        diagonal = jnp.where(same, extras[0][LEVELS + pair : LEVELS + pair + 1], turned)
        normal[spans[2 * pair + 1], :] = jnp.where(row_in < lane_in, both, diagonal)

    def take_gradient(level):
        column = to_column(effects_ref[level : level + 1, :], same)
        image = jnp.sum(normal[spans[level], :] * column, axis=0, keepdims=True)
        gradient[level] = image + extras[0][level : level + 1]

    def send_factor(i):
        return pltpu.make_async_copy(factor_ref.at[spans[i], :], factor_hbm.at[spans[i], :], sent.at[i])

    take_rows(0)
    take_unit(0)
    fresh = work[spans[0], spans[0]] * to_column(units[0], same) * units[0]
    aside = [functools.partial(take_rows, i) for i in range(1, count)]
    aside += [functools.partial(take_unit, i) for i in range(1, count)]
    aside += [functools.partial(scale_rows, i) for i in range(count)]
    later = [functools.partial(take_share, mask, ref) for mask, ref in zip(apart, piece_refs)]
    later += [functools.partial(unpack, pair) for pair in range(LEVELS // 2)]
    later += [functools.partial(take_gradient, level) for level in range(LEVELS)]
    for b, here in enumerate(spans):
        tiles, scales = eliminate([fresh[at : at + SUB] for at in range(0, LANE, SUB)], aside, shelf)
        scale = jnp.concatenate(scales)
        inner = jnp.concatenate(tiles) * scale
        lower = jnp.where(lane_in < row_in, inner, jnp.where(lane_in == row_in, scale, 0.0))
        lower_left, lower_right = parts_of(lower, LEFT, 1), parts_of(lower, RIGHT, 1)
        panels, steps = {}, {}

        def take_line(j, b=b, here=here, lower_left=lower_left, steps=steps):
            line = jnp.dot(lower_left, parts_of(work[here, spans[j]], RIGHT, 0), preferred_element_type=f32)
            steps[j] = parts_of(line, RIGHT, 0)
            if j > b:
                factor_ref[here, spans[j]] = line * (diagonals[j] * units[j] * ratio)
                inverse_ref[here, spans[j]] = jnp.zeros((LANE, LANE), f32)
            else:
                factor_ref[here, spans[j]] = jnp.zeros((LANE, LANE), f32)
                inverse_ref[here, spans[j]] = line * units[j]

        def take_panel(i, here=here, lower_right=lower_right, panels=panels):
            panel = parts_of(work[spans[i], here], LEFT, 1)
            panels[i] = parts_of(lax.dot_general(panel, lower_right, NT, preferred_element_type=f32), LEFT, 1)

        def take_change(i, j, b=b, panels=panels, steps=steps):
            change = jnp.dot(panels[i], steps[j], preferred_element_type=f32)
            work[spans[i], spans[j]] = -change if j == b else work[spans[i], spans[j]] - change

        def put_own(here=here, inner=inner, lower=lower, b=b, steps=steps):
            steps[b] = parts_of(lower, RIGHT, 0)
            factor_ref[here, here] = jnp.where(lane_in >= row_in, inner, 0.0) * (diagonals[b] * units[b] * ratio)
            inverse_ref[here, here] = lower * units[b]

        if b + 1 < count:
            take_line(b + 1)
            take_panel(b + 1)
            fresh = work[spans[b + 1], spans[b + 1]]
            fresh = fresh - jnp.dot(panels[b + 1], steps[b + 1], preferred_element_type=f32)
        others = [j for j in range(count) if j not in (b, b + 1)]
        aside = [put_own] + [functools.partial(take_line, j) for j in others]
        aside += [functools.partial(take_panel, i) for i in range(b + 2, count)]
        aside += [
            functools.partial(take_change, i, j)
            for i in range(b + 1, count)
            for j in range(count)
            if (i, j) != (b + 1, b + 1)
        ]
        aside.append(lambda b=b: send_factor(b).start())
        if b == 1:
            aside += later
    for call_it in aside:
        call_it()

    inverse = inverse_ref[...]
    steer = jnp.sum(inverse * jnp.concatenate(gradient, axis=1), axis=1, keepdims=True)
    direction = steer
    gamma = jnp.sum(steer * steer, axis=0, keepdims=True)
    solved = jnp.zeros((1, cov_ref.shape[1] * LEVELS), f32)
    for step in range(ITERS):
        move = jnp.sum(inverse * direction, axis=0, keepdims=True)
        image = []
        for span in spans:
            image.append(jnp.sum(normal[span, :] * to_column(move[:, span], same), axis=0, keepdims=True))
        image = jnp.concatenate(image, axis=1)
        alpha = gamma / jnp.sum(move * image, axis=1, keepdims=True)
        solved = solved + alpha * move
        if step == ITERS - 1:
            break
        steer = steer - alpha * jnp.sum(inverse * image, axis=1, keepdims=True)
        gamma_new = jnp.sum(steer * steer, axis=0, keepdims=True)
        direction = steer + gamma_new / gamma * direction
        gamma = gamma_new
    solved = jnp.concatenate([solved[:, span] for span in spans])
    solved_ref[...] = solved

    left = [part.astype(f32) for part in split(effects_ref[...] - solved)]
    left = jnp.concatenate(left + [jnp.zeros((PACK - 3 * LEVELS, LANE), f32)]).astype(bf16)
    values = lax.dot_general(left, cov_ref[...], NT, preferred_element_type=f32)
    values = values[:LEVELS] + values[LEVELS : 2 * LEVELS] + values[2 * LEVELS : 3 * LEVELS]
    for r in range(marks_ref.shape[0]):
        code = jnp.bitwise_and(marks_ref[r : r + 1, :], LEVELS - 1)
        total = noise_ref[r : r + 1, :]
        for level in range(LEVELS):
            total = total + jnp.where(code == level, values[level : level + 1, r * LANE : (r + 1) * LANE], 0.0)
        resid_ref[r : r + 1, :] = total
    for i in range(count):
        send_factor(i).wait()


def call(kernel, name, outs, scratch, *operands):
    return pl.pallas_call(
        kernel,
        out_shape=[jax.ShapeDtypeStruct(shape, dtype) for shape, dtype in outs],
        in_specs=[SMEM if operand.ndim == 1 else VMEM for operand in operands],
        out_specs=[VMEM] * len(outs),
        scratch_shapes=[pltpu.VMEM(shape, dtype) for shape, dtype in scratch],
        compiler_params=pltpu.CompilerParams(vmem_limit_bytes=40 * 2**20),
        name=name,
    )(*operands)


def body(covariates, level_codes, sign_bits, sample_rows, effects, noise):
    wide, narrow = lax.axis_size("wide"), lax.axis_size("narrow")
    index = jnp.stack([lax.axis_index("wide"), lax.axis_index("narrow")]).astype(jnp.int32)
    rows_dev, cols = covariates.shape[0], LEVELS * COV
    samp = whole_up(sample_rows.shape[0], PACK)
    share = whole_up(max(2 * LANE // wide, 3 * SUB), PACK)
    sample_rows = jnp.pad(sample_rows, (0, samp - sample_rows.shape[0]), constant_values=-1)
    marks = (level_codes + LEVELS * sign_bits).reshape(-1, LANE)
    noise = noise.reshape(-1, LANE)
    effects = effects.reshape(LEVELS, COV)

    want = sample_rows[None, :]
    want = [want] + [partner(want, "wide", m) for m in range(2, MATES, 2)]
    want = [one for piece in want for one in (piece, partner(piece, "wide", 1))]

    design, packed = call(
        design_kernel,
        "design",
        [((cols + 3 * PACK, rows_dev), bf16), ((share * wide + SUB, LANE), f32)],
        [],
        covariates,
        marks,
        noise,
    )
    sizes = [samp * (2 * m < MATES) + share for m in range(wide // 2)]
    starts = [sum(sizes[:m]) for m in range(wide // 2)]
    stay, go = call(
        functools.partial(local_kernel, samp, share, starts),
        "local",
        [((sum(sizes), cols), bf16)] * 2,
        [((MATES * samp, rows_dev), bf16)],
        index,
        design,
        packed,
        marks,
        *want,
    )
    pieces = call(
        functools.partial(pair_kernel, samp, share, starts),
        "pair",
        [((size, cols), bf16) for size in sizes],
        [],
        index,
        stay,
        partner(go, "wide", 1),
    )
    pieces = [pieces[0]] + [partner(pieces[m], "wide", 2 * m) for m in range(1, wide // 2)]
    (piece,) = call(
        functools.partial(mix_kernel, samp, share), "mix", [((samp + share, cols), bf16)], [], index, *pieces
    )
    pieces = [piece] + [partner(piece, "narrow", m) for m in range(1, narrow)]
    rows_in = samp * narrow
    (piece,) = call(
        functools.partial(stack_kernel, samp, share), "stack", [((rows_in + share, cols), bf16)], [], index, *pieces
    )
    pieces = [piece] + [partner(piece, "wide", m) for m in range(2, wide, 2)]
    theirs = [partner(piece, "wide", 1) for piece in pieces]
    sketch = [((rows_in * (wide // 2), cols), bf16)]
    square = ((cols, cols), f32)
    (gram,) = call(functools.partial(gram_kernel, rows_in), "gram", [square], sketch, index, *pieces)
    apart = [2 * m + core for core in range(2) for m in range(wide // 2)]
    operands = (gram, effects, covariates, marks, noise, *pieces, *theirs)
    scratch = sketch + [
        square,
        ((2 * (SUB + 1) * SUB, LANE), f32),
        square,
        square,
        ((share * wide, LANE), f32),
        ((cols, LANE), f32),
    ]
    factor, solved, resid = pl.pallas_call(
        functools.partial(solve_kernel, math.sqrt(LEVELS / SKETCH), apart, rows_in, share),
        out_shape=[jax.ShapeDtypeStruct(shape, f32) for shape in ((cols, cols), (LEVELS, COV), noise.shape)],
        in_specs=[SMEM] + [VMEM] * len(operands),
        out_specs=[pl.BlockSpec(memory_space=pl.ANY), VMEM, VMEM],
        scratch_shapes=[pltpu.VMEM(shape, dtype) for shape, dtype in scratch]
        + [pltpu.SemaphoreType.DMA((cols // LANE,))],
        compiler_params=pltpu.CompilerParams(vmem_limit_bytes=40 * 2**20),
        name="solve",
    )(index, *operands)
    return solved.reshape(-1), resid.reshape(-1), factor


def solution(mesh):
    return jax.shard_map(
        body,
        mesh=mesh,
        in_specs=(
            P(("wide", "narrow"), None),
            P(("wide", "narrow")),
            P(("wide", "narrow")),
            P(("wide", "narrow")),
            P(),
            P(("wide", "narrow")),
        ),
        out_specs=(P(), P(("wide", "narrow")), P()),
        check_vma=False,
    )
```

```python
import functools
import math

import jax
import jax.numpy as jnp
from jax import lax
from jax.experimental import pallas as pl
from jax.experimental.pallas import tpu as pltpu
from jax.sharding import PartitionSpec as P

COV = 128
LEVELS = 4
HB = 256
SKETCH = 1024
ITERS = 4
MIX_BITS = 3
MATES = 2**MIX_BITS

half_root = math.sqrt(0.5)
HIGHEST = lax.Precision.HIGHEST
f32, bf16 = jnp.float32, jnp.bfloat16
SUB, LANE = 8, 128
PACK = 16
NT = (((1,), (1,)), ((), ()))
VMEM = pl.BlockSpec(memory_space=pltpu.VMEM)
SMEM = pl.BlockSpec(memory_space=pltpu.SMEM)


def partner(value, axis, mask):
    pairs = [(source, source ^ mask) for source in range(lax.axis_size(axis))]
    return lax.ppermute(value, axis, pairs)


def whole_up(number, unit):
    return -(-number // unit) * unit


def eye():
    rows = lax.broadcasted_iota(jnp.int32, (LANE, LANE), 0)
    lanes = lax.broadcasted_iota(jnp.int32, (LANE, LANE), 1)
    return rows, lanes, rows == lanes


def to_column(row, same):
    return jnp.sum(jnp.where(same, row, 0.0), axis=1, keepdims=True)


def to_row(column, same):
    return jnp.sum(jnp.where(same, column, 0.0), axis=0, keepdims=True)


def split(value):
    parts = []
    for _ in range(3):
        parts.append(value.astype(bf16))
        value = value - parts[-1].astype(f32)
    return parts


def tree_sum(values):
    while len(values) > 1:
        values = [left + right for left, right in zip(values[0::2], values[1::2])]
    return values[0]


def put_sums(ref, start, share, extra):
    rows = share.shape[0]
    for k, part in enumerate(split(share)):
        ref[start : start + rows, k * LANE : (k + 1) * LANE] = part
    tail = jnp.zeros((rows - 3 * SUB, LANE), bf16)
    ref[start : start + rows, 3 * LANE :] = jnp.concatenate(split(extra) + [tail])


def take_sums(ref, start, rows):
    block = ref[start : start + rows, :].astype(f32)
    share = block[:, :LANE] + block[:, LANE : 2 * LANE] + block[:, 2 * LANE : 3 * LANE]
    tail = block[:, 3 * LANE :]
    return share, tail[:SUB] + tail[SUB : 2 * SUB] + tail[2 * SUB : 3 * SUB]


def design_kernel(cov_ref, marks_ref, noise_ref, design, packed):
    rows, lanes, same = eye()
    zero = jnp.zeros((LANE, LANE), f32)
    for r in range(marks_ref.shape[0]):
        here = slice(r * LANE, (r + 1) * LANE)
        code = jnp.bitwise_and(marks_ref[r : r + 1, :], LEVELS - 1)
        turned = cov_ref[here, :].astype(f32).T
        for level in range(LEVELS):
            design[level * LANE : (level + 1) * LANE, here] = jnp.where(code == level, turned, zero).astype(bf16)
        noise = jnp.concatenate([noise_ref[r : r + 1, :]] * LEVELS + [jnp.zeros((PACK - LEVELS, LANE), f32)])
        level = lax.broadcasted_iota(jnp.int32, (PACK, LANE), 0)
        noise = jnp.where(code == level, noise, 0.0)
        for k, part in enumerate(split(noise)):
            design[LEVELS * LANE + k * PACK : LEVELS * LANE + (k + 1) * PACK, here] = part

    sums = jnp.dot(design[...], cov_ref[...], preferred_element_type=f32)
    normal = [sums[level * LANE : (level + 1) * LANE] for level in range(LEVELS)]
    back = sums[LEVELS * LANE :]
    back = back[:SUB] + back[PACK : PACK + SUB] + back[2 * PACK : 2 * PACK + SUB]
    extra = [jnp.sum(jnp.where(same, normal[level], 0.0), axis=0, keepdims=True) for level in (1, 3)]
    for pair in range(LEVELS // 2):
        packed[pair * LANE : (pair + 1) * LANE, :] = jnp.where(rows >= lanes, normal[2 * pair], normal[2 * pair + 1])
    rest = packed.shape[0] - SUB - 2 * LANE
    if rest:
        packed[2 * LANE : 2 * LANE + rest, :] = jnp.zeros((rest, LANE), f32)
    packed[2 * LANE + rest :, :] = jnp.concatenate([back[:LEVELS]] + extra + [jnp.zeros((2, LANE), f32)])


def local_kernel(samp, share, starts, index_ref, design_ref, packed_ref, marks_ref, *refs):
    want_refs, (stay_ref, go_ref, table) = refs[:-3], refs[-3:]
    chunks = marks_ref.shape[0]
    lanes = eye()[1]
    zero = jnp.zeros((LANE, LANE), f32)
    per = LANE // samp
    small = lax.broadcasted_iota(jnp.int32, (samp, samp), 0) == lax.broadcasted_iota(jnp.int32, (samp, samp), 1)

    masks, halves = [], []
    for c in range(MATES // per):
        want = [to_column(ref[...].astype(f32), small) for ref in want_refs[c * per : (c + 1) * per]]
        want = jnp.concatenate(want).astype(jnp.int32)
        masks.append(jnp.right_shift(want, HB.bit_length() - 1))
        line = []
        for h in range(HB // LANE):
            common = jnp.bitwise_and(want, lanes + h * LANE)
            for shift in (4, 2, 1):
                common = jnp.bitwise_xor(common, jnp.right_shift(common, shift))
            line.append((1 - 2 * jnp.bitwise_and(common, 1)).astype(f32))
        halves.append(line)
    for r in range(chunks):
        sign = jnp.where(marks_ref[r : r + 1, :] < LEVELS, 1.0, -1.0)
        block, h = divmod(r * LANE, HB)
        for c, (mask, line) in enumerate(zip(masks, halves)):
            value = jnp.where(mask == block, line[h // LANE] * sign, zero)
            table[c * LANE : (c + 1) * LANE, r * LANE : (r + 1) * LANE] = value.astype(bf16)

    local = lax.dot_general(table[...], design_ref[: LEVELS * LANE, :], NT, preferred_element_type=f32)
    local = (local * (1.0 / math.sqrt(HB))).astype(bf16)
    extra = packed_ref[packed_ref.shape[0] - SUB :, :]
    for m in range(2 * len(starts)):
        out_ref, start = (stay_ref, go_ref)[m % 2], starts[m // 2]
        if m < MATES:
            out_ref[start : start + samp, :] = local[m * samp : (m + 1) * samp]
            start += samp
        at = pl.multiple_of(jnp.bitwise_xor(index_ref[0], m) * share, share)
        put_sums(out_ref, start, packed_ref[pl.ds(at, share), :], extra)


def butterfly(pieces, place, index):
    bit = jnp.bitwise_and(jnp.right_shift(index, place), 1)
    sign = (1 - 2 * bit).astype(f32)
    return [
        ((sign * own + other) * half_root).astype(bf16).astype(f32) for own, other in zip(pieces[0::2], pieces[1::2])
    ]


def pair_kernel(samp, share, starts, index_ref, stay_ref, came_ref, *out_refs):
    for m, (start, out_ref) in enumerate(zip(starts, out_refs)):
        put = 0
        if 2 * m < MATES:
            here = slice(start, start + samp)
            pieces = [ref[here, :].astype(f32) for ref in (stay_ref, came_ref)]
            out_ref[:samp, :] = butterfly(pieces, 0, index_ref[0])[0].astype(bf16)
            put, start = samp, start + samp
        (own, own_extra), (other, other_extra) = [take_sums(ref, start, share) for ref in (stay_ref, came_ref)]
        put_sums(out_ref, put, own + other, own_extra + other_extra)


def mix_kernel(samp, share, index_ref, *refs):
    piece_refs, out_ref = refs[:-1], refs[-1]
    pieces = [ref[:samp, :].astype(f32) for ref in piece_refs[: MATES // 2]]
    for place in range(1, MIX_BITS):
        pieces = butterfly(pieces, place, index_ref[0])
    out_ref[:samp, :] = pieces[0].astype(bf16)
    sums = [take_sums(ref, samp if 2 * m < MATES else 0, share) for m, ref in enumerate(piece_refs)]
    put_sums(out_ref, samp, tree_sum([one for one, _ in sums]), tree_sum([one for _, one in sums]))


def stack_kernel(samp, share, index_ref, *refs):
    piece_refs, out_ref = refs[:-1], refs[-1]
    for m, ref in enumerate(piece_refs):
        at = pl.multiple_of(jnp.bitwise_xor(index_ref[1], m) * samp, samp)
        out_ref[pl.ds(at, samp), :] = ref[:samp, :]
    sums = [take_sums(ref, samp, share) for ref in piece_refs]
    put_sums(
        out_ref, samp * len(piece_refs), tree_sum([one for one, _ in sums]), tree_sum([one for _, one in sums])
    )


def spread(value):
    return jnp.broadcast_to(value, (SUB, LANE))


def reciprocal(value):
    return pltpu.reciprocal(value, approx=True)


def eliminate(tiles, aside, shelf):
    share = -(-len(aside) // len(tiles))
    lane = lax.broadcasted_iota(jnp.int32, (SUB, LANE), 1)
    sub = lax.broadcasted_iota(jnp.int32, (SUB, LANE), 0)
    tiles = list(tiles)
    scales = []
    for tile in range(len(tiles)):
        first = tile * SUB
        window = (lane >= first) & (lane < first + SUB)
        marks = [lane == first + k for k in range(SUB)]
        old = tiles[tile]
        columns = [spread(old[:, first + k : first + k + 1]) for k in range(SUB)]
        base = tile % 2 * (SUB + 1) * SUB
        shelf[base : base + SUB, :] = jnp.where(window, 0.0, old)
        for m in range(SUB):
            shelf[base + (m + 1) * SUB : base + (m + 2) * SUB, :] = columns[m]

        def take(m, k):
            at = base + m * SUB + k
            return spread(shelf[at : at + 1, :])

        pivot = [[take(m + 1, k) if m >= k else None for m in range(SUB)] for k in range(SUB)]
        rows = [jnp.where(marks[k], 1.0, take(0, k)) for k in range(SUB)]
        steps, near, far = [None] * SUB, {}, {}
        kept, roots = [None] * SUB, [None] * SUB

        def keep(k, low, ratio, values, others):
            last = others[k + 1]
            kept[k] = rows[k]
            for m in range(k, SUB):
                kept[k] = jnp.where(marks[m], values[m], kept[k])
            kept[k + 1] = rows[k + 1] - ratio * rows[k]
            for m in range(k + 1, SUB):
                kept[k + 1] = jnp.where(marks[m], others[m], kept[k + 1])
            roots[k], roots[k + 1] = lax.rsqrt(low), lax.rsqrt(last)

        ahead = []
        if tile + 1 < len(tiles):
            ahead = [spread(tiles[tile + 1][:, first + k : first + k + 1]) for k in range(SUB)]
            fresh = jnp.where(window, 0.0, tiles[tile + 1])

        for k in range(0, SUB, 4):
            low, cross, high = pivot[k][k], pivot[k][k + 1], pivot[k + 1][k + 1]
            area = low * high - cross * cross
            drop = {}
            for m in range(k + 2, SUB):
                near[k, m] = high * pivot[k][m] - cross * pivot[k + 1][m]
                far[k, m] = low * pivot[k + 1][m] - cross * pivot[k][m]
            for m in range(k + 2, SUB):
                for n in range(m, SUB):
                    drop[m, n] = pivot[k][m] * near[k, n] + pivot[k + 1][m] * far[k, n]
            c, d = k + 2, k + 3
            grown = {(m, n): area * pivot[m][n] - drop[m, n] for m in (c, d) for n in range(m, SUB)}
            low2, cross2, high2 = grown[c, c], grown[c, d], grown[d, d]
            area2 = low2 * high2 - cross2 * cross2
            over, over2 = reciprocal(area), reciprocal(area2)
            for m in range(k + 4, SUB):
                near[c, m] = high2 * grown[c, m] - cross2 * grown[d, m]
                far[c, m] = low2 * grown[d, m] - cross2 * grown[c, m]
            for m in range(k + 4, SUB):
                for n in range(m, SUB):
                    drop2 = grown[c, m] * near[c, n] + grown[d, m] * far[c, n]
                    pivot[m][n] = pivot[m][n] - over * (drop[m, n] + over2 * drop2)

            def past(lines):
                pair = [area * lines[m] - (near[k, m] * lines[k] + far[k, m] * lines[k + 1]) for m in (c, d)]
                for m in range(k + 4, SUB):
                    inner = near[c, m] * pair[0] + far[c, m] * pair[1]
                    lines[m] = lines[m] - over * (near[k, m] * lines[k] + far[k, m] * lines[k + 1] + over2 * inner)
                return pair

            wide = past(rows)
            first_pair = [high * rows[k] - cross * rows[k + 1], low * rows[k + 1] - cross * rows[k]]
            second_pair = [high2 * wide[0] - cross2 * wide[1], low2 * wide[1] - cross2 * wide[0]]
            if ahead:
                tall = past(ahead)
                inner = tall[0] * second_pair[0] + tall[1] * second_pair[1]
                outer = ahead[k] * first_pair[0] + ahead[k + 1] * first_pair[1]
                fresh = fresh - over * (outer + over2 * inner)
            steps[k], steps[k + 1] = [over * value for value in first_pair]
            steps[c], steps[d] = [over2 * value for value in second_pair]
            rows[c], rows[d] = [over * value for value in wide]
            for m in range(k + 2, SUB):
                near[k, m], far[k, m] = over * near[k, m], over * far[k, m]
            for m in range(k + 4, SUB):
                near[c, m], far[c, m] = over2 * near[c, m], over2 * far[c, m]

            inner = reciprocal(low)
            ratio = cross * inner
            values = {m: pivot[k][m] for m in range(k, SUB)}
            others = {m: pivot[k + 1][m] - ratio * pivot[k][m] for m in range(k + 2, SUB)}
            others[k + 1] = area * inner
            keep(k, low, ratio, values, others)
            inner = reciprocal(low2)
            ratio = cross2 * inner
            values = {m: over * grown[c, m] for m in range(c, SUB)}
            others = {m: over * (grown[d, m] - ratio * grown[c, m]) for m in range(c + 2, SUB)}
            others[d] = over * (area2 * inner)
            keep(c, values[c], ratio, values, others)
        for k in reversed(range(0, SUB, 2)):
            for m in reversed(range(k + 2, SUB)):
                steps[k] = steps[k] - near[k, m] * steps[m]
                steps[k + 1] = steps[k + 1] - far[k, m] * steps[m]
        for i in range(tile + 2, min(tile + 3, len(tiles))):
            change = [spread(tiles[i][:, first + k : first + k + 1]) * steps[k] for k in range(SUB)]
            tiles[i] = jnp.where(window, 0.0, tiles[i]) - tree_sum(change[::-1])
        if tile + 3 < len(tiles):
            stacked = steps[0]
            for k in range(1, SUB):
                stacked = jnp.where(sub >= k, steps[k], stacked)
            blank = jnp.zeros_like(stacked)
            stacked = jnp.concatenate([stacked, blank] if tile % 2 == 0 else [blank, stacked])
            none = jnp.zeros((PACK, LANE), bf16)
            before, after = tile // 2, len(tiles) // 2 - 1 - tile // 2
            parts = [jnp.concatenate([none] * before + [part] + [none] * after) for part in split(stacked)]
            change = jnp.dot(
                parts_of(jnp.concatenate(tiles[tile + 3 :]), LEFT, 1),
                jnp.concatenate([parts[k] for k in RIGHT]),
                preferred_element_type=f32,
            )
            for i in range(tile + 3, len(tiles)):
                at = (i - tile - 3) * SUB
                tiles[i] = jnp.where(window, 0.0, tiles[i]) - change[at : at + SUB]
        if tile + 1 < len(tiles):
            tiles[tile + 1] = fresh
        new, scale = kept[0], roots[0]
        for k in range(1, SUB):
            new = jnp.where(sub >= k, kept[k], new)
            scale = jnp.where(sub >= k, roots[k], scale)
        tiles[tile] = new
        scales.append(scale)
        for work in aside[tile * share : (tile + 1) * share]:
            work()
    return tiles, scales


LEFT, RIGHT = (0, 1, 0, 1, 2, 0), (0, 0, 1, 1, 0, 2)


def parts_of(value, order, axis):
    parts = split(value)
    return jnp.concatenate([parts[k] for k in order], axis=axis)


def put_pieces(rows_in, index_ref, piece_refs, sketch):
    for m, ref in enumerate(piece_refs):
        at = jnp.bitwise_xor(jnp.right_shift(index_ref[0], 1), m) * rows_in
        sketch[pl.ds(pl.multiple_of(at, rows_in), rows_in), :] = ref[:rows_in, :]


def gram_rows(sketch, here):
    return lax.dot_general(sketch[:, here], sketch[...], (((0,), (0,)), ((), ())), preferred_element_type=f32)


def gram_kernel(rows_in, index_ref, *refs):
    piece_refs, (gram_ref, sketch) = refs[:-2], refs[-2:]
    put_pieces(rows_in, index_ref, piece_refs, sketch)
    for at in range(0, gram_ref.shape[0], LANE):
        gram_ref[at : at + LANE, :] = gram_rows(sketch, slice(at, at + LANE))


def solve_kernel(
    ratio, apart, rows_in, share, index_ref, gram_ref, effects_ref, cov_ref, marks_ref, noise_ref, *refs
):
    piece_refs, (factor_hbm, solved_ref, resid_ref), scratch = refs[:-11], refs[-11:-8], refs[-8:]
    sketch, work, shelf, factor_ref, inverse_ref, packed, normal, sent = scratch
    count = work.shape[0] // LANE
    spans = [slice(at, at + LANE) for at in range(0, work.shape[0], LANE)]
    row_in, lane_in, same = eye()
    diagonals, units = [None] * count, [None] * count
    put_pieces(rows_in, index_ref, piece_refs[len(piece_refs) // 2 :], sketch)

    def take_rows(i):
        work[spans[i], :] = gram_ref[spans[i], :] + gram_rows(sketch, spans[i])

    def take_unit(i):
        diagonals[i] = jnp.sum(jnp.where(same, work[spans[i], spans[i]], 0.0), axis=0, keepdims=True)
        units[i] = lax.rsqrt(diagonals[i])

    def scale_rows(i):
        work[spans[i], :] = work[spans[i], :] * to_column(units[i], same) * jnp.concatenate(units, axis=1)

    extras, gradient = [], [None] * LEVELS

    def take_share(mask, ref):
        at = pl.multiple_of(jnp.bitwise_xor(index_ref[0], mask) * share, share)
        packed[pl.ds(at, share), :], extra = take_sums(ref, rows_in, share)
        extras.append(extra)

    def unpack(pair):
        both = packed[spans[pair], :]
        turned = both.T
        normal[spans[2 * pair], :] = jnp.where(row_in >= lane_in, both, turned)
        diagonal = jnp.where(same, extras[0][LEVELS + pair : LEVELS + pair + 1], turned)
        normal[spans[2 * pair + 1], :] = jnp.where(row_in < lane_in, both, diagonal)

    def take_gradient(level):
        column = to_column(effects_ref[level : level + 1, :], same)
        image = jnp.sum(normal[spans[level], :] * column, axis=0, keepdims=True)
        gradient[level] = image + extras[0][level : level + 1]

    def send_factor(i):
        return pltpu.make_async_copy(factor_ref.at[spans[i], :], factor_hbm.at[spans[i], :], sent.at[i])

    take_rows(0)
    take_unit(0)
    fresh = work[spans[0], spans[0]] * to_column(units[0], same) * units[0]
    aside = [functools.partial(take_rows, i) for i in range(1, count)]
    aside += [functools.partial(take_unit, i) for i in range(1, count)]
    aside += [functools.partial(scale_rows, i) for i in range(count)]
    later = [functools.partial(take_share, mask, ref) for mask, ref in zip(apart, piece_refs)]
    later += [functools.partial(unpack, pair) for pair in range(LEVELS // 2)]
    later += [functools.partial(take_gradient, level) for level in range(LEVELS)]
    for b, here in enumerate(spans):
        tiles, scales = eliminate([fresh[at : at + SUB] for at in range(0, LANE, SUB)], aside, shelf)
        scale = jnp.concatenate(scales)
        inner = jnp.concatenate(tiles) * scale
        lower = jnp.where(lane_in < row_in, inner, jnp.where(lane_in == row_in, scale, 0.0))
        lower_left, lower_right = parts_of(lower, LEFT, 1), parts_of(lower, RIGHT, 1)
        panels, steps = {}, {}

        def take_line(j, b=b, here=here, lower_left=lower_left, steps=steps):
            line = jnp.dot(lower_left, parts_of(work[here, spans[j]], RIGHT, 0), preferred_element_type=f32)
            steps[j] = parts_of(line, RIGHT, 0)
            if j > b:
                factor_ref[here, spans[j]] = line * (diagonals[j] * units[j] * ratio)
                inverse_ref[here, spans[j]] = jnp.zeros((LANE, LANE), f32)
            else:
                factor_ref[here, spans[j]] = jnp.zeros((LANE, LANE), f32)
                inverse_ref[here, spans[j]] = line * units[j]

        def take_panel(i, here=here, lower_right=lower_right, panels=panels):
            panel = parts_of(work[spans[i], here], LEFT, 1)
            panels[i] = parts_of(lax.dot_general(panel, lower_right, NT, preferred_element_type=f32), LEFT, 1)

        def take_change(i, j, b=b, panels=panels, steps=steps):
            change = jnp.dot(panels[i], steps[j], preferred_element_type=f32)
            work[spans[i], spans[j]] = -change if j == b else work[spans[i], spans[j]] - change

        def put_own(here=here, inner=inner, lower=lower, b=b, steps=steps):
            steps[b] = parts_of(lower, RIGHT, 0)
            factor_ref[here, here] = jnp.where(lane_in >= row_in, inner, 0.0) * (diagonals[b] * units[b] * ratio)
            inverse_ref[here, here] = lower * units[b]

        if b + 1 < count:
            take_line(b + 1)
            take_panel(b + 1)
            fresh = work[spans[b + 1], spans[b + 1]]
            fresh = fresh - jnp.dot(panels[b + 1], steps[b + 1], preferred_element_type=f32)
        others = [j for j in range(count) if j not in (b, b + 1)]
        aside = [put_own] + [functools.partial(take_line, j) for j in others]
        aside += [functools.partial(take_panel, i) for i in range(b + 2, count)]
        aside += [
            functools.partial(take_change, i, j)
            for i in range(b + 1, count)
            for j in range(count)
            if (i, j) != (b + 1, b + 1)
        ]
        aside.append(lambda b=b: send_factor(b).start())
        if b == 1:
            aside += later
    for call_it in aside:
        call_it()

    inverse = inverse_ref[...]
    steer = jnp.sum(inverse * jnp.concatenate(gradient, axis=1), axis=1, keepdims=True)
    direction = steer
    gamma = jnp.sum(steer * steer, axis=0, keepdims=True)
    solved = jnp.zeros((1, cov_ref.shape[1] * LEVELS), f32)
    for step in range(ITERS):
        move = jnp.sum(inverse * direction, axis=0, keepdims=True)
        image = []
        for span in spans:
            image.append(jnp.sum(normal[span, :] * to_column(move[:, span], same), axis=0, keepdims=True))
        image = jnp.concatenate(image, axis=1)
        alpha = gamma / jnp.sum(move * image, axis=1, keepdims=True)
        solved = solved + alpha * move
        if step == ITERS - 1:
            break
        steer = steer - alpha * jnp.sum(inverse * image, axis=1, keepdims=True)
        gamma_new = jnp.sum(steer * steer, axis=0, keepdims=True)
        direction = steer + gamma_new / gamma * direction
        gamma = gamma_new
    solved = jnp.concatenate([solved[:, span] for span in spans])
    solved_ref[...] = solved

    left = [part.astype(f32) for part in split(effects_ref[...] - solved)]
    left = jnp.concatenate(left + [jnp.zeros((PACK - 3 * LEVELS, LANE), f32)]).astype(bf16)
    values = lax.dot_general(left, cov_ref[...], NT, preferred_element_type=f32)
    values = values[:LEVELS] + values[LEVELS : 2 * LEVELS] + values[2 * LEVELS : 3 * LEVELS]
    for r in range(marks_ref.shape[0]):
        code = jnp.bitwise_and(marks_ref[r : r + 1, :], LEVELS - 1)
        total = noise_ref[r : r + 1, :]
        for level in range(LEVELS):
            total = total + jnp.where(code == level, values[level : level + 1, r * LANE : (r + 1) * LANE], 0.0)
        resid_ref[r : r + 1, :] = total
    for i in range(count):
        send_factor(i).wait()


def call(kernel, name, outs, scratch, *operands):
    return pl.pallas_call(
        kernel,
        out_shape=[jax.ShapeDtypeStruct(shape, dtype) for shape, dtype in outs],
        in_specs=[SMEM if operand.ndim == 1 else VMEM for operand in operands],
        out_specs=[VMEM] * len(outs),
        scratch_shapes=[pltpu.VMEM(shape, dtype) for shape, dtype in scratch],
        compiler_params=pltpu.CompilerParams(vmem_limit_bytes=40 * 2**20),
        name=name,
    )(*operands)


def body(covariates, level_codes, sign_bits, sample_rows, effects, noise):
    wide, narrow = lax.axis_size("wide"), lax.axis_size("narrow")
    index = jnp.stack([lax.axis_index("wide"), lax.axis_index("narrow")]).astype(jnp.int32)
    rows_dev, cols = covariates.shape[0], LEVELS * COV
    samp = whole_up(sample_rows.shape[0], PACK)
    share = whole_up(max(2 * LANE // wide, 3 * SUB), PACK)
    sample_rows = jnp.pad(sample_rows, (0, samp - sample_rows.shape[0]), constant_values=-1)
    marks = (level_codes + LEVELS * sign_bits).reshape(-1, LANE)
    noise = noise.reshape(-1, LANE)
    effects = effects.reshape(LEVELS, COV)

    want = sample_rows[None, :]
    want = [want] + [partner(want, "wide", m) for m in range(2, MATES, 2)]
    want = [one for piece in want for one in (piece, partner(piece, "wide", 1))]

    design, packed = call(
        design_kernel,
        "design",
        [((cols + 3 * PACK, rows_dev), bf16), ((share * wide + SUB, LANE), f32)],
        [],
        covariates,
        marks,
        noise,
    )
    sizes = [samp * (2 * m < MATES) + share for m in range(wide // 2)]
    starts = [sum(sizes[:m]) for m in range(wide // 2)]
    stay, go = call(
        functools.partial(local_kernel, samp, share, starts),
        "local",
        [((sum(sizes), cols), bf16)] * 2,
        [((MATES * samp, rows_dev), bf16)],
        index,
        design,
        packed,
        marks,
        *want,
    )
    pieces = call(
        functools.partial(pair_kernel, samp, share, starts),
        "pair",
        [((size, cols), bf16) for size in sizes],
        [],
        index,
        stay,
        partner(go, "wide", 1),
    )
    pieces = [pieces[0]] + [partner(pieces[m], "wide", 2 * m) for m in range(1, wide // 2)]
    (piece,) = call(
        functools.partial(mix_kernel, samp, share), "mix", [((samp + share, cols), bf16)], [], index, *pieces
    )
    pieces = [piece] + [partner(piece, "narrow", m) for m in range(1, narrow)]
    rows_in = samp * narrow
    (piece,) = call(
        functools.partial(stack_kernel, samp, share), "stack", [((rows_in + share, cols), bf16)], [], index, *pieces
    )
    pieces = [piece] + [partner(piece, "wide", m) for m in range(2, wide, 2)]
    theirs = [partner(piece, "wide", 1) for piece in pieces]
    sketch = [((rows_in * (wide // 2), cols), bf16)]
    square = ((cols, cols), f32)
    (gram,) = call(functools.partial(gram_kernel, rows_in), "gram", [square], sketch, index, *pieces)
    apart = [2 * m + core for core in range(2) for m in range(wide // 2)]
    operands = (gram, effects, covariates, marks, noise, *pieces, *theirs)
    scratch = sketch + [
        square,
        ((2 * (SUB + 1) * SUB, LANE), f32),
        square,
        square,
        ((share * wide, LANE), f32),
        ((cols, LANE), f32),
    ]
    factor, solved, resid = pl.pallas_call(
        functools.partial(solve_kernel, math.sqrt(LEVELS / SKETCH), apart, rows_in, share),
        out_shape=[jax.ShapeDtypeStruct(shape, f32) for shape in ((cols, cols), (LEVELS, COV), noise.shape)],
        in_specs=[SMEM] + [VMEM] * len(operands),
        out_specs=[pl.BlockSpec(memory_space=pl.ANY), VMEM, VMEM],
        scratch_shapes=[pltpu.VMEM(shape, dtype) for shape, dtype in scratch]
        + [pltpu.SemaphoreType.DMA((cols // LANE,))],
        compiler_params=pltpu.CompilerParams(vmem_limit_bytes=40 * 2**20),
        name="solve",
    )(index, *operands)
    return solved.reshape(-1), resid.reshape(-1), factor


def solution(mesh):
    return jax.shard_map(
        body,
        mesh=mesh,
        in_specs=(
            P(("wide", "narrow"), None),
            P(("wide", "narrow")),
            P(("wide", "narrow")),
            P(("wide", "narrow")),
            P(),
            P(("wide", "narrow")),
        ),
        out_specs=(P(), P(("wide", "narrow")), P()),
        check_vma=False,
    )
```

```python
import functools
import math

import jax
import jax.numpy as jnp
from jax import lax
from jax.experimental import pallas as pl
from jax.experimental.pallas import tpu as pltpu
from jax.sharding import PartitionSpec as P

COV = 128
LEVELS = 4
HB = 256
SKETCH = 1024
ITERS = 4
MIX_BITS = 3
MATES = 2**MIX_BITS

half_root = math.sqrt(0.5)
HIGHEST = lax.Precision.HIGHEST
f32, bf16 = jnp.float32, jnp.bfloat16
SUB, LANE = 8, 128
PACK = 16
NT = (((1,), (1,)), ((), ()))
VMEM = pl.BlockSpec(memory_space=pltpu.VMEM)
SMEM = pl.BlockSpec(memory_space=pltpu.SMEM)


def partner(value, axis, mask):
    pairs = [(source, source ^ mask) for source in range(lax.axis_size(axis))]
    return lax.ppermute(value, axis, pairs)


def whole_up(number, unit):
    return -(-number // unit) * unit


def eye():
    rows = lax.broadcasted_iota(jnp.int32, (LANE, LANE), 0)
    lanes = lax.broadcasted_iota(jnp.int32, (LANE, LANE), 1)
    return rows, lanes, rows == lanes


def to_column(row, same):
    return jnp.sum(jnp.where(same, row, 0.0), axis=1, keepdims=True)


def to_row(column, same):
    return jnp.sum(jnp.where(same, column, 0.0), axis=0, keepdims=True)


def split(value):
    parts = []
    for _ in range(3):
        parts.append(value.astype(bf16))
        value = value - parts[-1].astype(f32)
    return parts


def tree_sum(values):
    while len(values) > 1:
        values = [left + right for left, right in zip(values[0::2], values[1::2])]
    return values[0]


def put_sums(ref, start, share, extra):
    rows = share.shape[0]
    for k, part in enumerate(split(share)):
        ref[start : start + rows, k * LANE : (k + 1) * LANE] = part
    tail = jnp.zeros((rows - 3 * SUB, LANE), bf16)
    ref[start : start + rows, 3 * LANE :] = jnp.concatenate(split(extra) + [tail])


def take_sums(ref, start, rows):
    block = ref[start : start + rows, :].astype(f32)
    share = block[:, :LANE] + block[:, LANE : 2 * LANE] + block[:, 2 * LANE : 3 * LANE]
    tail = block[:, 3 * LANE :]
    return share, tail[:SUB] + tail[SUB : 2 * SUB] + tail[2 * SUB : 3 * SUB]


def design_kernel(cov_ref, marks_ref, noise_ref, design, packed):
    rows, lanes, same = eye()
    zero = jnp.zeros((LANE, LANE), f32)
    for r in range(marks_ref.shape[0]):
        here = slice(r * LANE, (r + 1) * LANE)
        code = jnp.bitwise_and(marks_ref[r : r + 1, :], LEVELS - 1)
        turned = cov_ref[here, :].astype(f32).T
        for level in range(LEVELS):
            design[level * LANE : (level + 1) * LANE, here] = jnp.where(code == level, turned, zero).astype(bf16)
        noise = jnp.concatenate([noise_ref[r : r + 1, :]] * LEVELS + [jnp.zeros((PACK - LEVELS, LANE), f32)])
        level = lax.broadcasted_iota(jnp.int32, (PACK, LANE), 0)
        noise = jnp.where(code == level, noise, 0.0)
        for k, part in enumerate(split(noise)):
            design[LEVELS * LANE + k * PACK : LEVELS * LANE + (k + 1) * PACK, here] = part

    sums = jnp.dot(design[...], cov_ref[...], preferred_element_type=f32)
    normal = [sums[level * LANE : (level + 1) * LANE] for level in range(LEVELS)]
    back = sums[LEVELS * LANE :]
    back = back[:SUB] + back[PACK : PACK + SUB] + back[2 * PACK : 2 * PACK + SUB]
    extra = [jnp.sum(jnp.where(same, normal[level], 0.0), axis=0, keepdims=True) for level in (1, 3)]
    for pair in range(LEVELS // 2):
        packed[pair * LANE : (pair + 1) * LANE, :] = jnp.where(rows >= lanes, normal[2 * pair], normal[2 * pair + 1])
    rest = packed.shape[0] - SUB - 2 * LANE
    if rest:
        packed[2 * LANE : 2 * LANE + rest, :] = jnp.zeros((rest, LANE), f32)
    packed[2 * LANE + rest :, :] = jnp.concatenate([back[:LEVELS]] + extra + [jnp.zeros((2, LANE), f32)])


def local_kernel(samp, share, starts, index_ref, design_ref, packed_ref, marks_ref, *refs):
    want_refs, (stay_ref, go_ref, table) = refs[:-3], refs[-3:]
    chunks = marks_ref.shape[0]
    lanes = eye()[1]
    zero = jnp.zeros((LANE, LANE), f32)
    per = LANE // samp
    small = lax.broadcasted_iota(jnp.int32, (samp, samp), 0) == lax.broadcasted_iota(jnp.int32, (samp, samp), 1)

    masks, halves = [], []
    for c in range(MATES // per):
        want = [to_column(ref[...].astype(f32), small) for ref in want_refs[c * per : (c + 1) * per]]
        want = jnp.concatenate(want).astype(jnp.int32)
        masks.append(jnp.right_shift(want, HB.bit_length() - 1))
        line = []
        for h in range(HB // LANE):
            common = jnp.bitwise_and(want, lanes + h * LANE)
            for shift in (4, 2, 1):
                common = jnp.bitwise_xor(common, jnp.right_shift(common, shift))
            line.append((1 - 2 * jnp.bitwise_and(common, 1)).astype(f32))
        halves.append(line)
    for r in range(chunks):
        sign = jnp.where(marks_ref[r : r + 1, :] < LEVELS, 1.0, -1.0)
        block, h = divmod(r * LANE, HB)
        for c, (mask, line) in enumerate(zip(masks, halves)):
            value = jnp.where(mask == block, line[h // LANE] * sign, zero)
            table[c * LANE : (c + 1) * LANE, r * LANE : (r + 1) * LANE] = value.astype(bf16)

    local = lax.dot_general(table[...], design_ref[: LEVELS * LANE, :], NT, preferred_element_type=f32)
    local = (local * (1.0 / math.sqrt(HB))).astype(bf16)
    extra = packed_ref[packed_ref.shape[0] - SUB :, :]
    for m in range(2 * len(starts)):
        out_ref, start = (stay_ref, go_ref)[m % 2], starts[m // 2]
        if m < MATES:
            out_ref[start : start + samp, :] = local[m * samp : (m + 1) * samp]
            start += samp
        at = pl.multiple_of(jnp.bitwise_xor(index_ref[0], m) * share, share)
        put_sums(out_ref, start, packed_ref[pl.ds(at, share), :], extra)


def butterfly(pieces, place, index):
    bit = jnp.bitwise_and(jnp.right_shift(index, place), 1)
    sign = (1 - 2 * bit).astype(f32)
    return [
        ((sign * own + other) * half_root).astype(bf16).astype(f32) for own, other in zip(pieces[0::2], pieces[1::2])
    ]


def pair_kernel(samp, share, starts, index_ref, stay_ref, came_ref, *out_refs):
    for m, (start, out_ref) in enumerate(zip(starts, out_refs)):
        put = 0
        if 2 * m < MATES:
            here = slice(start, start + samp)
            pieces = [ref[here, :].astype(f32) for ref in (stay_ref, came_ref)]
            out_ref[:samp, :] = butterfly(pieces, 0, index_ref[0])[0].astype(bf16)
            put, start = samp, start + samp
        (own, own_extra), (other, other_extra) = [take_sums(ref, start, share) for ref in (stay_ref, came_ref)]
        put_sums(out_ref, put, own + other, own_extra + other_extra)


def mix_kernel(samp, share, index_ref, *refs):
    piece_refs, out_ref = refs[:-1], refs[-1]
    pieces = [ref[:samp, :].astype(f32) for ref in piece_refs[: MATES // 2]]
    for place in range(1, MIX_BITS):
        pieces = butterfly(pieces, place, index_ref[0])
    out_ref[:samp, :] = pieces[0].astype(bf16)
    sums = [take_sums(ref, samp if 2 * m < MATES else 0, share) for m, ref in enumerate(piece_refs)]
    put_sums(out_ref, samp, tree_sum([one for one, _ in sums]), tree_sum([one for _, one in sums]))


def stack_kernel(samp, share, index_ref, *refs):
    piece_refs, out_ref = refs[:-1], refs[-1]
    for m, ref in enumerate(piece_refs):
        at = pl.multiple_of(jnp.bitwise_xor(index_ref[1], m) * samp, samp)
        out_ref[pl.ds(at, samp), :] = ref[:samp, :]
    sums = [take_sums(ref, samp, share) for ref in piece_refs]
    put_sums(
        out_ref, samp * len(piece_refs), tree_sum([one for one, _ in sums]), tree_sum([one for _, one in sums])
    )


def spread(value):
    return jnp.broadcast_to(value, (SUB, LANE))


def reciprocal(value):
    return pltpu.reciprocal(value, approx=True)


def finish(tiles, scales, tile, window, marks, pivot, rows, near, far, quads, aside):
    first = tile * SUB
    sub = lax.broadcasted_iota(jnp.int32, (SUB, LANE), 0)
    kept, roots, steps = [None] * SUB, [None] * SUB, [None] * SUB

    def keep(k, low, ratio, values, others):
        last = others[k + 1]
        kept[k] = rows[k]
        for m in range(k, SUB):
            kept[k] = jnp.where(marks[m], values[m], kept[k])
        kept[k + 1] = rows[k + 1] - ratio * rows[k]
        for m in range(k + 1, SUB):
            kept[k + 1] = jnp.where(marks[m], others[m], kept[k + 1])
        roots[k], roots[k + 1] = lax.rsqrt(low), lax.rsqrt(last)

    for k, low, cross, area, low2, cross2, area2, over, over2, grown, first_pair, second_pair, wide in quads:
        c, d = k + 2, k + 3
        steps[k], steps[k + 1] = [over * value for value in first_pair]
        steps[c], steps[d] = [over2 * value for value in second_pair]
        rows[c], rows[d] = [over * value for value in wide]
        for m in range(k + 2, SUB):
            near[k, m], far[k, m] = over * near[k, m], over * far[k, m]
        for m in range(k + 4, SUB):
            near[c, m], far[c, m] = over2 * near[c, m], over2 * far[c, m]
        inner = reciprocal(low)
        ratio = cross * inner
        values = {m: pivot[k][m] for m in range(k, SUB)}
        others = {m: pivot[k + 1][m] - ratio * pivot[k][m] for m in range(k + 2, SUB)}
        others[k + 1] = area * inner
        keep(k, low, ratio, values, others)
        inner = reciprocal(low2)
        ratio = cross2 * inner
        values = {m: over * grown[c, m] for m in range(c, SUB)}
        others = {m: over * (grown[d, m] - ratio * grown[c, m]) for m in range(c + 2, SUB)}
        others[d] = over * (area2 * inner)
        keep(c, values[c], ratio, values, others)
    for k in reversed(range(0, SUB, 2)):
        for m in reversed(range(k + 2, SUB)):
            steps[k] = steps[k] - near[k, m] * steps[m]
            steps[k + 1] = steps[k + 1] - far[k, m] * steps[m]
    for i in range(tile + 2, min(tile + 3, len(tiles))):
        change = [spread(tiles[i][:, first + k : first + k + 1]) * steps[k] for k in range(SUB)]
        tiles[i] = jnp.where(window, 0.0, tiles[i]) - tree_sum(change[::-1])
    if tile + 3 < len(tiles):
        stacked = steps[0]
        for k in range(1, SUB):
            stacked = jnp.where(sub >= k, steps[k], stacked)
        blank = jnp.zeros_like(stacked)
        stacked = jnp.concatenate([stacked, blank] if tile % 2 == 0 else [blank, stacked])
        none = jnp.zeros((PACK, LANE), bf16)
        before, after = tile // 2, len(tiles) // 2 - 1 - tile // 2
        parts = [jnp.concatenate([none] * before + [part] + [none] * after) for part in split(stacked)]
        change = jnp.dot(
            parts_of(jnp.concatenate(tiles[tile + 3 :]), LEFT, 1),
            jnp.concatenate([parts[k] for k in RIGHT]),
            preferred_element_type=f32,
        )
        for i in range(tile + 3, len(tiles)):
            at = (i - tile - 3) * SUB
            tiles[i] = jnp.where(window, 0.0, tiles[i]) - change[at : at + SUB]
    new, scale = kept[0], roots[0]
    for k in range(1, SUB):
        new = jnp.where(sub >= k, kept[k], new)
        scale = jnp.where(sub >= k, roots[k], scale)
    tiles[tile] = new
    scales.append(scale)
    for work in aside:
        work()


def eliminate(tiles, aside, shelf):
    share = -(-len(aside) // len(tiles))
    behind = None
    lane = lax.broadcasted_iota(jnp.int32, (SUB, LANE), 1)
    tiles = list(tiles)
    scales = []
    for tile in range(len(tiles)):
        first = tile * SUB
        window = (lane >= first) & (lane < first + SUB)
        marks = [lane == first + k for k in range(SUB)]
        old = tiles[tile]
        columns = [spread(old[:, first + k : first + k + 1]) for k in range(SUB)]
        base = tile % 2 * (SUB + 1) * SUB
        shelf[base : base + SUB, :] = jnp.where(window, 0.0, old)
        for m in range(SUB):
            shelf[base + (m + 1) * SUB : base + (m + 2) * SUB, :] = columns[m]

        def take(m, k):
            at = base + m * SUB + k
            return spread(shelf[at : at + 1, :])

        pivot = [[take(m + 1, k) if m >= k else None for m in range(SUB)] for k in range(SUB)]
        rows = [jnp.where(marks[k], 1.0, take(0, k)) for k in range(SUB)]
        near, far, quads = {}, {}, []
        if behind:
            behind()

        ahead = []
        if tile + 1 < len(tiles):
            ahead = [spread(tiles[tile + 1][:, first + k : first + k + 1]) for k in range(SUB)]
            fresh = jnp.where(window, 0.0, tiles[tile + 1])

        for k in range(0, SUB, 4):
            low, cross, high = pivot[k][k], pivot[k][k + 1], pivot[k + 1][k + 1]
            area = low * high - cross * cross
            drop = {}
            for m in range(k + 2, SUB):
                near[k, m] = high * pivot[k][m] - cross * pivot[k + 1][m]
                far[k, m] = low * pivot[k + 1][m] - cross * pivot[k][m]
            for m in range(k + 2, SUB):
                for n in range(m, SUB):
                    drop[m, n] = pivot[k][m] * near[k, n] + pivot[k + 1][m] * far[k, n]
            c, d = k + 2, k + 3
            grown = {(m, n): area * pivot[m][n] - drop[m, n] for m in (c, d) for n in range(m, SUB)}
            low2, cross2, high2 = grown[c, c], grown[c, d], grown[d, d]
            area2 = low2 * high2 - cross2 * cross2
            over, over2 = reciprocal(area), reciprocal(area2)
            for m in range(k + 4, SUB):
                near[c, m] = high2 * grown[c, m] - cross2 * grown[d, m]
                far[c, m] = low2 * grown[d, m] - cross2 * grown[c, m]
            for m in range(k + 4, SUB):
                for n in range(m, SUB):
                    drop2 = grown[c, m] * near[c, n] + grown[d, m] * far[c, n]
                    pivot[m][n] = pivot[m][n] - over * (drop[m, n] + over2 * drop2)

            def past(lines):
                pair = [area * lines[m] - (near[k, m] * lines[k] + far[k, m] * lines[k + 1]) for m in (c, d)]
                for m in range(k + 4, SUB):
                    inner = near[c, m] * pair[0] + far[c, m] * pair[1]
                    lines[m] = lines[m] - over * (near[k, m] * lines[k] + far[k, m] * lines[k + 1] + over2 * inner)
                return pair

            wide = past(rows)
            first_pair = [high * rows[k] - cross * rows[k + 1], low * rows[k + 1] - cross * rows[k]]
            second_pair = [high2 * wide[0] - cross2 * wide[1], low2 * wide[1] - cross2 * wide[0]]
            if ahead:
                tall = past(ahead)
                inner = tall[0] * second_pair[0] + tall[1] * second_pair[1]
                outer = ahead[k] * first_pair[0] + ahead[k + 1] * first_pair[1]
                fresh = fresh - over * (outer + over2 * inner)
            quads.append((k, low, cross, area, low2, cross2, area2, over, over2, grown, first_pair, second_pair, wide))
        if ahead:
            tiles[tile + 1] = fresh
        behind = functools.partial(
            finish, tiles, scales, tile, window, marks, pivot, rows, near, far, quads, aside[tile * share :][:share]
        )
    behind()
    return tiles, scales


LEFT, RIGHT = (0, 1, 0, 1, 2, 0), (0, 0, 1, 1, 0, 2)


def parts_of(value, order, axis):
    parts = split(value)
    return jnp.concatenate([parts[k] for k in order], axis=axis)


def put_pieces(rows_in, index_ref, piece_refs, sketch):
    for m, ref in enumerate(piece_refs):
        at = jnp.bitwise_xor(jnp.right_shift(index_ref[0], 1), m) * rows_in
        sketch[pl.ds(pl.multiple_of(at, rows_in), rows_in), :] = ref[:rows_in, :]


def gram_rows(sketch, here):
    return lax.dot_general(sketch[:, here], sketch[...], (((0,), (0,)), ((), ())), preferred_element_type=f32)


def gram_kernel(rows_in, index_ref, *refs):
    piece_refs, (gram_ref, sketch) = refs[:-2], refs[-2:]
    put_pieces(rows_in, index_ref, piece_refs, sketch)
    for at in range(0, gram_ref.shape[0], LANE):
        gram_ref[at : at + LANE, :] = gram_rows(sketch, slice(at, at + LANE))


def solve_kernel(
    ratio, apart, rows_in, share, index_ref, gram_ref, effects_ref, cov_ref, marks_ref, noise_ref, *refs
):
    piece_refs, (factor_hbm, solved_ref, resid_ref), scratch = refs[:-11], refs[-11:-8], refs[-8:]
    sketch, work, shelf, factor_ref, inverse_ref, packed, normal, sent = scratch
    count = work.shape[0] // LANE
    spans = [slice(at, at + LANE) for at in range(0, work.shape[0], LANE)]
    row_in, lane_in, same = eye()
    diagonals, units = [None] * count, [None] * count
    put_pieces(rows_in, index_ref, piece_refs[len(piece_refs) // 2 :], sketch)

    def take_rows(i):
        work[spans[i], :] = gram_ref[spans[i], :] + gram_rows(sketch, spans[i])

    def take_unit(i):
        diagonals[i] = jnp.sum(jnp.where(same, work[spans[i], spans[i]], 0.0), axis=0, keepdims=True)
        units[i] = lax.rsqrt(diagonals[i])

    def scale_rows(i):
        work[spans[i], :] = work[spans[i], :] * to_column(units[i], same) * jnp.concatenate(units, axis=1)

    extras, gradient = [], [None] * LEVELS

    def take_share(mask, ref):
        at = pl.multiple_of(jnp.bitwise_xor(index_ref[0], mask) * share, share)
        packed[pl.ds(at, share), :], extra = take_sums(ref, rows_in, share)
        extras.append(extra)

    def unpack(pair):
        both = packed[spans[pair], :]
        turned = both.T
        normal[spans[2 * pair], :] = jnp.where(row_in >= lane_in, both, turned)
        diagonal = jnp.where(same, extras[0][LEVELS + pair : LEVELS + pair + 1], turned)
        normal[spans[2 * pair + 1], :] = jnp.where(row_in < lane_in, both, diagonal)

    def take_gradient(level):
        column = to_column(effects_ref[level : level + 1, :], same)
        image = jnp.sum(normal[spans[level], :] * column, axis=0, keepdims=True)
        gradient[level] = image + extras[0][level : level + 1]

    def send_factor(i):
        return pltpu.make_async_copy(factor_ref.at[spans[i], :], factor_hbm.at[spans[i], :], sent.at[i])

    take_rows(0)
    take_unit(0)
    fresh = work[spans[0], spans[0]] * to_column(units[0], same) * units[0]
    aside = [functools.partial(take_rows, i) for i in range(1, count)]
    aside += [functools.partial(take_unit, i) for i in range(1, count)]
    aside += [functools.partial(scale_rows, i) for i in range(count)]
    later = [functools.partial(take_share, mask, ref) for mask, ref in zip(apart, piece_refs)]
    later += [functools.partial(unpack, pair) for pair in range(LEVELS // 2)]
    later += [functools.partial(take_gradient, level) for level in range(LEVELS)]
    for b, here in enumerate(spans):
        tiles, scales = eliminate([fresh[at : at + SUB] for at in range(0, LANE, SUB)], aside, shelf)
        scale = jnp.concatenate(scales)
        inner = jnp.concatenate(tiles) * scale
        lower = jnp.where(lane_in < row_in, inner, jnp.where(lane_in == row_in, scale, 0.0))
        lower_left, lower_right = parts_of(lower, LEFT, 1), parts_of(lower, RIGHT, 1)
        panels, steps = {}, {}

        def take_line(j, b=b, here=here, lower_left=lower_left, steps=steps):
            line = jnp.dot(lower_left, parts_of(work[here, spans[j]], RIGHT, 0), preferred_element_type=f32)
            steps[j] = parts_of(line, RIGHT, 0)
            if j > b:
                factor_ref[here, spans[j]] = line * (diagonals[j] * units[j] * ratio)
                inverse_ref[here, spans[j]] = jnp.zeros((LANE, LANE), f32)
            else:
                factor_ref[here, spans[j]] = jnp.zeros((LANE, LANE), f32)
                inverse_ref[here, spans[j]] = line * units[j]

        def take_panel(i, here=here, lower_right=lower_right, panels=panels):
            panel = parts_of(work[spans[i], here], LEFT, 1)
            panels[i] = parts_of(lax.dot_general(panel, lower_right, NT, preferred_element_type=f32), LEFT, 1)

        def take_change(i, j, b=b, panels=panels, steps=steps):
            change = jnp.dot(panels[i], steps[j], preferred_element_type=f32)
            work[spans[i], spans[j]] = -change if j == b else work[spans[i], spans[j]] - change

        def put_own(here=here, inner=inner, lower=lower, b=b, steps=steps):
            steps[b] = parts_of(lower, RIGHT, 0)
            factor_ref[here, here] = jnp.where(lane_in >= row_in, inner, 0.0) * (diagonals[b] * units[b] * ratio)
            inverse_ref[here, here] = lower * units[b]

        if b + 1 < count:
            take_line(b + 1)
            take_panel(b + 1)
            fresh = work[spans[b + 1], spans[b + 1]]
            fresh = fresh - jnp.dot(panels[b + 1], steps[b + 1], preferred_element_type=f32)
        others = [j for j in range(count) if j not in (b, b + 1)]
        aside = [put_own] + [functools.partial(take_line, j) for j in others]
        aside += [functools.partial(take_panel, i) for i in range(b + 2, count)]
        aside += [
            functools.partial(take_change, i, j)
            for i in range(b + 1, count)
            for j in range(count)
            if (i, j) != (b + 1, b + 1)
        ]
        aside.append(lambda b=b: send_factor(b).start())
        if b == 1:
            aside += later
    for call_it in aside:
        call_it()

    inverse = inverse_ref[...]
    steer = jnp.sum(inverse * jnp.concatenate(gradient, axis=1), axis=1, keepdims=True)
    direction = steer
    gamma = jnp.sum(steer * steer, axis=0, keepdims=True)
    solved = jnp.zeros((1, cov_ref.shape[1] * LEVELS), f32)
    for step in range(ITERS):
        move = jnp.sum(inverse * direction, axis=0, keepdims=True)
        image = []
        for span in spans:
            image.append(jnp.sum(normal[span, :] * to_column(move[:, span], same), axis=0, keepdims=True))
        image = jnp.concatenate(image, axis=1)
        alpha = gamma / jnp.sum(move * image, axis=1, keepdims=True)
        solved = solved + alpha * move
        if step == ITERS - 1:
            break
        steer = steer - alpha * jnp.sum(inverse * image, axis=1, keepdims=True)
        gamma_new = jnp.sum(steer * steer, axis=0, keepdims=True)
        direction = steer + gamma_new / gamma * direction
        gamma = gamma_new
    solved = jnp.concatenate([solved[:, span] for span in spans])
    solved_ref[...] = solved

    left = [part.astype(f32) for part in split(effects_ref[...] - solved)]
    left = jnp.concatenate(left + [jnp.zeros((PACK - 3 * LEVELS, LANE), f32)]).astype(bf16)
    values = lax.dot_general(left, cov_ref[...], NT, preferred_element_type=f32)
    values = values[:LEVELS] + values[LEVELS : 2 * LEVELS] + values[2 * LEVELS : 3 * LEVELS]
    for r in range(marks_ref.shape[0]):
        code = jnp.bitwise_and(marks_ref[r : r + 1, :], LEVELS - 1)
        total = noise_ref[r : r + 1, :]
        for level in range(LEVELS):
            total = total + jnp.where(code == level, values[level : level + 1, r * LANE : (r + 1) * LANE], 0.0)
        resid_ref[r : r + 1, :] = total
    for i in range(count):
        send_factor(i).wait()


def call(kernel, name, outs, scratch, *operands):
    return pl.pallas_call(
        kernel,
        out_shape=[jax.ShapeDtypeStruct(shape, dtype) for shape, dtype in outs],
        in_specs=[SMEM if operand.ndim == 1 else VMEM for operand in operands],
        out_specs=[VMEM] * len(outs),
        scratch_shapes=[pltpu.VMEM(shape, dtype) for shape, dtype in scratch],
        compiler_params=pltpu.CompilerParams(vmem_limit_bytes=40 * 2**20),
        name=name,
    )(*operands)


def body(covariates, level_codes, sign_bits, sample_rows, effects, noise):
    wide, narrow = lax.axis_size("wide"), lax.axis_size("narrow")
    index = jnp.stack([lax.axis_index("wide"), lax.axis_index("narrow")]).astype(jnp.int32)
    rows_dev, cols = covariates.shape[0], LEVELS * COV
    samp = whole_up(sample_rows.shape[0], PACK)
    share = whole_up(max(2 * LANE // wide, 3 * SUB), PACK)
    sample_rows = jnp.pad(sample_rows, (0, samp - sample_rows.shape[0]), constant_values=-1)
    marks = (level_codes + LEVELS * sign_bits).reshape(-1, LANE)
    noise = noise.reshape(-1, LANE)
    effects = effects.reshape(LEVELS, COV)

    want = sample_rows[None, :]
    want = [want] + [partner(want, "wide", m) for m in range(2, MATES, 2)]
    want = [one for piece in want for one in (piece, partner(piece, "wide", 1))]

    design, packed = call(
        design_kernel,
        "design",
        [((cols + 3 * PACK, rows_dev), bf16), ((share * wide + SUB, LANE), f32)],
        [],
        covariates,
        marks,
        noise,
    )
    sizes = [samp * (2 * m < MATES) + share for m in range(wide // 2)]
    starts = [sum(sizes[:m]) for m in range(wide // 2)]
    stay, go = call(
        functools.partial(local_kernel, samp, share, starts),
        "local",
        [((sum(sizes), cols), bf16)] * 2,
        [((MATES * samp, rows_dev), bf16)],
        index,
        design,
        packed,
        marks,
        *want,
    )
    pieces = call(
        functools.partial(pair_kernel, samp, share, starts),
        "pair",
        [((size, cols), bf16) for size in sizes],
        [],
        index,
        stay,
        partner(go, "wide", 1),
    )
    pieces = [pieces[0]] + [partner(pieces[m], "wide", 2 * m) for m in range(1, wide // 2)]
    (piece,) = call(
        functools.partial(mix_kernel, samp, share), "mix", [((samp + share, cols), bf16)], [], index, *pieces
    )
    pieces = [piece] + [partner(piece, "narrow", m) for m in range(1, narrow)]
    rows_in = samp * narrow
    (piece,) = call(
        functools.partial(stack_kernel, samp, share), "stack", [((rows_in + share, cols), bf16)], [], index, *pieces
    )
    pieces = [piece] + [partner(piece, "wide", m) for m in range(2, wide, 2)]
    theirs = [partner(piece, "wide", 1) for piece in pieces]
    sketch = [((rows_in * (wide // 2), cols), bf16)]
    square = ((cols, cols), f32)
    (gram,) = call(functools.partial(gram_kernel, rows_in), "gram", [square], sketch, index, *pieces)
    apart = [2 * m + core for core in range(2) for m in range(wide // 2)]
    operands = (gram, effects, covariates, marks, noise, *pieces, *theirs)
    scratch = sketch + [
        square,
        ((2 * (SUB + 1) * SUB, LANE), f32),
        square,
        square,
        ((share * wide, LANE), f32),
        ((cols, LANE), f32),
    ]
    factor, solved, resid = pl.pallas_call(
        functools.partial(solve_kernel, math.sqrt(LEVELS / SKETCH), apart, rows_in, share),
        out_shape=[jax.ShapeDtypeStruct(shape, f32) for shape in ((cols, cols), (LEVELS, COV), noise.shape)],
        in_specs=[SMEM] + [VMEM] * len(operands),
        out_specs=[pl.BlockSpec(memory_space=pl.ANY), VMEM, VMEM],
        scratch_shapes=[pltpu.VMEM(shape, dtype) for shape, dtype in scratch]
        + [pltpu.SemaphoreType.DMA((cols // LANE,))],
        compiler_params=pltpu.CompilerParams(vmem_limit_bytes=40 * 2**20),
        name="solve",
    )(index, *operands)
    return solved.reshape(-1), resid.reshape(-1), factor


def solution(mesh):
    return jax.shard_map(
        body,
        mesh=mesh,
        in_specs=(
            P(("wide", "narrow"), None),
            P(("wide", "narrow")),
            P(("wide", "narrow")),
            P(("wide", "narrow")),
            P(),
            P(("wide", "narrow")),
        ),
        out_specs=(P(), P(("wide", "narrow")), P()),
        check_vma=False,
    )
```

```python
import functools
import math

import jax
import jax.numpy as jnp
from jax import lax
from jax.experimental import pallas as pl
from jax.experimental.pallas import tpu as pltpu
from jax.sharding import PartitionSpec as P

COV = 128
LEVELS = 4
HB = 256
SKETCH = 1024
ITERS = 4
MIX_BITS = 3
MATES = 2**MIX_BITS

half_root = math.sqrt(0.5)
HIGHEST = lax.Precision.HIGHEST
f32, bf16 = jnp.float32, jnp.bfloat16
SUB, LANE = 8, 128
PACK = 16
NT = (((1,), (1,)), ((), ()))
VMEM = pl.BlockSpec(memory_space=pltpu.VMEM)
SMEM = pl.BlockSpec(memory_space=pltpu.SMEM)


def partner(value, axis, mask):
    pairs = [(source, source ^ mask) for source in range(lax.axis_size(axis))]
    return lax.ppermute(value, axis, pairs)


def whole_up(number, unit):
    return -(-number // unit) * unit


def eye():
    rows = lax.broadcasted_iota(jnp.int32, (LANE, LANE), 0)
    lanes = lax.broadcasted_iota(jnp.int32, (LANE, LANE), 1)
    return rows, lanes, rows == lanes


def to_column(row, same):
    return jnp.sum(jnp.where(same, row, 0.0), axis=1, keepdims=True)


def to_row(column, same):
    return jnp.sum(jnp.where(same, column, 0.0), axis=0, keepdims=True)


def split(value):
    parts = []
    for _ in range(3):
        parts.append(value.astype(bf16))
        value = value - parts[-1].astype(f32)
    return parts


def tree_sum(values):
    while len(values) > 1:
        values = [left + right for left, right in zip(values[0::2], values[1::2])]
    return values[0]


def put_sums(ref, start, share, extra):
    rows = share.shape[0]
    for k, part in enumerate(split(share)):
        ref[start : start + rows, k * LANE : (k + 1) * LANE] = part
    tail = jnp.zeros((rows - 3 * SUB, LANE), bf16)
    ref[start : start + rows, 3 * LANE :] = jnp.concatenate(split(extra) + [tail])


def take_sums(ref, start, rows):
    block = ref[start : start + rows, :].astype(f32)
    share = block[:, :LANE] + block[:, LANE : 2 * LANE] + block[:, 2 * LANE : 3 * LANE]
    tail = block[:, 3 * LANE :]
    return share, tail[:SUB] + tail[SUB : 2 * SUB] + tail[2 * SUB : 3 * SUB]


def design_kernel(cov_ref, marks_ref, noise_ref, design, packed):
    rows, lanes, same = eye()
    zero = jnp.zeros((LANE, LANE), f32)
    for r in range(marks_ref.shape[0]):
        here = slice(r * LANE, (r + 1) * LANE)
        code = jnp.bitwise_and(marks_ref[r : r + 1, :], LEVELS - 1)
        turned = cov_ref[here, :].astype(f32).T
        for level in range(LEVELS):
            design[level * LANE : (level + 1) * LANE, here] = jnp.where(code == level, turned, zero).astype(bf16)
        noise = jnp.concatenate([noise_ref[r : r + 1, :]] * LEVELS + [jnp.zeros((PACK - LEVELS, LANE), f32)])
        level = lax.broadcasted_iota(jnp.int32, (PACK, LANE), 0)
        noise = jnp.where(code == level, noise, 0.0)
        for k, part in enumerate(split(noise)):
            design[LEVELS * LANE + k * PACK : LEVELS * LANE + (k + 1) * PACK, here] = part

    sums = jnp.dot(design[...], cov_ref[...], preferred_element_type=f32)
    normal = [sums[level * LANE : (level + 1) * LANE] for level in range(LEVELS)]
    back = sums[LEVELS * LANE :]
    back = back[:SUB] + back[PACK : PACK + SUB] + back[2 * PACK : 2 * PACK + SUB]
    extra = [jnp.sum(jnp.where(same, normal[level], 0.0), axis=0, keepdims=True) for level in (1, 3)]
    for pair in range(LEVELS // 2):
        packed[pair * LANE : (pair + 1) * LANE, :] = jnp.where(rows >= lanes, normal[2 * pair], normal[2 * pair + 1])
    rest = packed.shape[0] - SUB - 2 * LANE
    if rest:
        packed[2 * LANE : 2 * LANE + rest, :] = jnp.zeros((rest, LANE), f32)
    packed[2 * LANE + rest :, :] = jnp.concatenate([back[:LEVELS]] + extra + [jnp.zeros((2, LANE), f32)])


def local_kernel(samp, share, starts, index_ref, design_ref, packed_ref, marks_ref, *refs):
    want_refs, (stay_ref, go_ref, table) = refs[:-3], refs[-3:]
    chunks = marks_ref.shape[0]
    lanes = eye()[1]
    zero = jnp.zeros((LANE, LANE), f32)
    per = LANE // samp
    small = lax.broadcasted_iota(jnp.int32, (samp, samp), 0) == lax.broadcasted_iota(jnp.int32, (samp, samp), 1)

    masks, halves = [], []
    for c in range(MATES // per):
        want = [to_column(ref[...].astype(f32), small) for ref in want_refs[c * per : (c + 1) * per]]
        want = jnp.concatenate(want).astype(jnp.int32)
        masks.append(jnp.right_shift(want, HB.bit_length() - 1))
        line = []
        for h in range(HB // LANE):
            common = jnp.bitwise_and(want, lanes + h * LANE)
            for shift in (4, 2, 1):
                common = jnp.bitwise_xor(common, jnp.right_shift(common, shift))
            line.append((1 - 2 * jnp.bitwise_and(common, 1)).astype(f32))
        halves.append(line)
    for r in range(chunks):
        sign = jnp.where(marks_ref[r : r + 1, :] < LEVELS, 1.0, -1.0)
        block, h = divmod(r * LANE, HB)
        for c, (mask, line) in enumerate(zip(masks, halves)):
            value = jnp.where(mask == block, line[h // LANE] * sign, zero)
            table[c * LANE : (c + 1) * LANE, r * LANE : (r + 1) * LANE] = value.astype(bf16)

    local = lax.dot_general(table[...], design_ref[: LEVELS * LANE, :], NT, preferred_element_type=f32)
    local = (local * (1.0 / math.sqrt(HB))).astype(bf16)
    extra = packed_ref[packed_ref.shape[0] - SUB :, :]
    for m in range(2 * len(starts)):
        out_ref, start = (stay_ref, go_ref)[m % 2], starts[m // 2]
        if m < MATES:
            out_ref[start : start + samp, :] = local[m * samp : (m + 1) * samp]
            start += samp
        at = pl.multiple_of(jnp.bitwise_xor(index_ref[0], m) * share, share)
        put_sums(out_ref, start, packed_ref[pl.ds(at, share), :], extra)


def butterfly(pieces, place, index):
    bit = jnp.bitwise_and(jnp.right_shift(index, place), 1)
    sign = (1 - 2 * bit).astype(f32)
    return [
        ((sign * own + other) * half_root).astype(bf16).astype(f32) for own, other in zip(pieces[0::2], pieces[1::2])
    ]


def pair_kernel(samp, share, starts, index_ref, stay_ref, came_ref, *out_refs):
    for m, (start, out_ref) in enumerate(zip(starts, out_refs)):
        put = 0
        if 2 * m < MATES:
            here = slice(start, start + samp)
            pieces = [ref[here, :].astype(f32) for ref in (stay_ref, came_ref)]
            out_ref[:samp, :] = butterfly(pieces, 0, index_ref[0])[0].astype(bf16)
            put, start = samp, start + samp
        (own, own_extra), (other, other_extra) = [take_sums(ref, start, share) for ref in (stay_ref, came_ref)]
        put_sums(out_ref, put, own + other, own_extra + other_extra)


def mix_kernel(samp, share, index_ref, *refs):
    piece_refs, out_ref = refs[:-1], refs[-1]
    pieces = [ref[:samp, :].astype(f32) for ref in piece_refs[: MATES // 2]]
    for place in range(1, MIX_BITS):
        pieces = butterfly(pieces, place, index_ref[0])
    out_ref[:samp, :] = pieces[0].astype(bf16)
    sums = [take_sums(ref, samp if 2 * m < MATES else 0, share) for m, ref in enumerate(piece_refs)]
    put_sums(out_ref, samp, tree_sum([one for one, _ in sums]), tree_sum([one for _, one in sums]))


def stack_kernel(samp, share, index_ref, *refs):
    piece_refs, out_ref = refs[:-1], refs[-1]
    for m, ref in enumerate(piece_refs):
        at = pl.multiple_of(jnp.bitwise_xor(index_ref[1], m) * samp, samp)
        out_ref[pl.ds(at, samp), :] = ref[:samp, :]
    sums = [take_sums(ref, samp, share) for ref in piece_refs]
    put_sums(
        out_ref, samp * len(piece_refs), tree_sum([one for one, _ in sums]), tree_sum([one for _, one in sums])
    )


def spread(value):
    return jnp.broadcast_to(value, (SUB, LANE))


def reciprocal(value):
    return pltpu.reciprocal(value, approx=True)


def eliminate(tiles, aside, shelf):
    share = -(-len(aside) // len(tiles))
    lane = lax.broadcasted_iota(jnp.int32, (SUB, LANE), 1)
    sub = lax.broadcasted_iota(jnp.int32, (SUB, LANE), 0)
    tiles = list(tiles)
    scales = []
    for tile in range(len(tiles)):
        first = tile * SUB
        window = (lane >= first) & (lane < first + SUB)
        marks = [lane == first + k for k in range(SUB)]
        old = tiles[tile]
        columns = [spread(old[:, first + k : first + k + 1]) for k in range(SUB)]
        base = tile % 2 * (SUB + 1) * SUB
        shelf[base : base + SUB, :] = jnp.where(window, 0.0, old)
        for m in range(SUB):
            shelf[base + (m + 1) * SUB : base + (m + 2) * SUB, :] = columns[m]

        def take(m, k):
            at = base + m * SUB + k
            return spread(shelf[at : at + 1, :])

        pivot = [[take(m + 1, k) if m >= k else None for m in range(SUB)] for k in range(SUB)]
        rows = [jnp.where(marks[k], 1.0, take(0, k)) for k in range(SUB)]
        steps, near, far = [None] * SUB, {}, {}
        kept, roots = [None] * SUB, [None] * SUB

        def keep(k, low, ratio, values, others):
            last = others[k + 1]
            kept[k] = rows[k]
            for m in range(k, SUB):
                kept[k] = jnp.where(marks[m], values[m], kept[k])
            kept[k + 1] = rows[k + 1] - ratio * rows[k]
            for m in range(k + 1, SUB):
                kept[k + 1] = jnp.where(marks[m], others[m], kept[k + 1])
            roots[k], roots[k + 1] = lax.rsqrt(low), lax.rsqrt(last)

        for k in range(0, SUB, 4):
            low, cross, high = pivot[k][k], pivot[k][k + 1], pivot[k + 1][k + 1]
            area = low * high - cross * cross
            drop = {}
            for m in range(k + 2, SUB):
                near[k, m] = high * pivot[k][m] - cross * pivot[k + 1][m]
                far[k, m] = low * pivot[k + 1][m] - cross * pivot[k][m]
            for m in range(k + 2, SUB):
                for n in range(m, SUB):
                    drop[m, n] = pivot[k][m] * near[k, n] + pivot[k + 1][m] * far[k, n]
            c, d = k + 2, k + 3
            grown = {(m, n): area * pivot[m][n] - drop[m, n] for m in (c, d) for n in range(m, SUB)}
            low2, cross2, high2 = grown[c, c], grown[c, d], grown[d, d]
            area2 = low2 * high2 - cross2 * cross2
            over, over2 = reciprocal(area), reciprocal(area2)
            for m in range(k + 4, SUB):
                near[c, m] = high2 * grown[c, m] - cross2 * grown[d, m]
                far[c, m] = low2 * grown[d, m] - cross2 * grown[c, m]
            for m in range(k + 4, SUB):
                for n in range(m, SUB):
                    drop2 = grown[c, m] * near[c, n] + grown[d, m] * far[c, n]
                    pivot[m][n] = pivot[m][n] - over * (drop[m, n] + over2 * drop2)
            for m in range(k + 2, SUB):
                near[k, m], far[k, m] = over * near[k, m], over * far[k, m]
                rows[m] = rows[m] - (near[k, m] * rows[k] + far[k, m] * rows[k + 1])
            for m in range(k + 4, SUB):
                near[c, m], far[c, m] = over2 * near[c, m], over2 * far[c, m]
                rows[m] = rows[m] - (near[c, m] * rows[c] + far[c, m] * rows[d])
            steps[k] = over * (high * rows[k] - cross * rows[k + 1])
            steps[k + 1] = over * (low * rows[k + 1] - cross * rows[k])
            both = area * over2
            steps[c] = both * (high2 * rows[c] - cross2 * rows[d])
            steps[d] = both * (low2 * rows[d] - cross2 * rows[c])

            inner = reciprocal(low)
            ratio = cross * inner
            values = {m: pivot[k][m] for m in range(k, SUB)}
            others = {m: pivot[k + 1][m] - ratio * pivot[k][m] for m in range(k + 2, SUB)}
            others[k + 1] = area * inner
            keep(k, low, ratio, values, others)
            inner = reciprocal(low2)
            ratio = cross2 * inner
            values = {m: over * grown[c, m] for m in range(c, SUB)}
            others = {m: over * (grown[d, m] - ratio * grown[c, m]) for m in range(c + 2, SUB)}
            others[d] = over * (area2 * inner)
            keep(c, values[c], ratio, values, others)
        if tile + 1 < len(tiles):
            after = tiles[tile + 1]
            ahead = [spread(after[:, first + k : first + k + 1]) for k in range(SUB)]
            fresh = jnp.where(window, 0.0, after)
            for k in range(0, SUB, 2):
                for m in range(k + 2, SUB):
                    ahead[m] = ahead[m] - (near[k, m] * ahead[k] + far[k, m] * ahead[k + 1])
                fresh = fresh - (ahead[k] * steps[k] + ahead[k + 1] * steps[k + 1])
        for k in reversed(range(0, SUB, 2)):
            for m in reversed(range(k + 2, SUB)):
                steps[k] = steps[k] - near[k, m] * steps[m]
                steps[k + 1] = steps[k + 1] - far[k, m] * steps[m]
        for i in range(tile + 2, min(tile + 3, len(tiles))):
            change = [spread(tiles[i][:, first + k : first + k + 1]) * steps[k] for k in range(SUB)]
            tiles[i] = jnp.where(window, 0.0, tiles[i]) - tree_sum(change[::-1])
        if tile + 3 < len(tiles):
            stacked = steps[0]
            for k in range(1, SUB):
                stacked = jnp.where(sub >= k, steps[k], stacked)
            blank = jnp.zeros_like(stacked)
            stacked = jnp.concatenate([stacked, blank] if tile % 2 == 0 else [blank, stacked])
            none = jnp.zeros((PACK, LANE), bf16)
            before, after = tile // 2, len(tiles) // 2 - 1 - tile // 2
            parts = [jnp.concatenate([none] * before + [part] + [none] * after) for part in split(stacked)]
            change = jnp.dot(
                parts_of(jnp.concatenate(tiles[tile + 3 :]), LEFT, 1),
                jnp.concatenate([parts[k] for k in RIGHT]),
                preferred_element_type=f32,
            )
            for i in range(tile + 3, len(tiles)):
                at = (i - tile - 3) * SUB
                tiles[i] = jnp.where(window, 0.0, tiles[i]) - change[at : at + SUB]
        if tile + 1 < len(tiles):
            tiles[tile + 1] = fresh
        new, scale = kept[0], roots[0]
        for k in range(1, SUB):
            new = jnp.where(sub >= k, kept[k], new)
            scale = jnp.where(sub >= k, roots[k], scale)
        tiles[tile] = new
        scales.append(scale)
        for work in aside[tile * share : (tile + 1) * share]:
            work()
    return tiles, scales


LEFT, RIGHT = (0, 1, 0, 1, 2, 0), (0, 0, 1, 1, 0, 2)


def parts_of(value, order, axis):
    parts = split(value)
    return jnp.concatenate([parts[k] for k in order], axis=axis)


def put_pieces(rows_in, index_ref, piece_refs, sketch):
    for m, ref in enumerate(piece_refs):
        at = jnp.bitwise_xor(jnp.right_shift(index_ref[0], 1), m) * rows_in
        sketch[pl.ds(pl.multiple_of(at, rows_in), rows_in), :] = ref[:rows_in, :]


def gram_rows(sketch, here):
    return lax.dot_general(sketch[:, here], sketch[...], (((0,), (0,)), ((), ())), preferred_element_type=f32)


def gram_kernel(rows_in, index_ref, *refs):
    piece_refs, (gram_ref, sketch) = refs[:-2], refs[-2:]
    put_pieces(rows_in, index_ref, piece_refs, sketch)
    for at in range(0, gram_ref.shape[0], LANE):
        gram_ref[at : at + LANE, :] = gram_rows(sketch, slice(at, at + LANE))


def solve_kernel(
    ratio, apart, rows_in, share, index_ref, gram_ref, effects_ref, cov_ref, marks_ref, noise_ref, *refs
):
    piece_refs, (factor_hbm, solved_ref, resid_ref), scratch = refs[:-11], refs[-11:-8], refs[-8:]
    sketch, work, shelf, factor_ref, inverse_ref, packed, normal, sent = scratch
    count = work.shape[0] // LANE
    spans = [slice(at, at + LANE) for at in range(0, work.shape[0], LANE)]
    row_in, lane_in, same = eye()
    diagonals, units = [None] * count, [None] * count
    put_pieces(rows_in, index_ref, piece_refs[len(piece_refs) // 2 :], sketch)

    def take_rows(i):
        work[spans[i], :] = gram_ref[spans[i], :] + gram_rows(sketch, spans[i])

    def take_unit(i):
        diagonals[i] = jnp.sum(jnp.where(same, work[spans[i], spans[i]], 0.0), axis=0, keepdims=True)
        units[i] = lax.rsqrt(diagonals[i])

    def scale_rows(i):
        work[spans[i], :] = work[spans[i], :] * to_column(units[i], same) * jnp.concatenate(units, axis=1)

    extras, gradient = [], [None] * LEVELS

    def take_share(mask, ref):
        at = pl.multiple_of(jnp.bitwise_xor(index_ref[0], mask) * share, share)
        packed[pl.ds(at, share), :], extra = take_sums(ref, rows_in, share)
        extras.append(extra)

    def unpack(pair):
        both = packed[spans[pair], :]
        turned = both.T
        normal[spans[2 * pair], :] = jnp.where(row_in >= lane_in, both, turned)
        diagonal = jnp.where(same, extras[0][LEVELS + pair : LEVELS + pair + 1], turned)
        normal[spans[2 * pair + 1], :] = jnp.where(row_in < lane_in, both, diagonal)

    def take_gradient(level):
        column = to_column(effects_ref[level : level + 1, :], same)
        image = jnp.sum(normal[spans[level], :] * column, axis=0, keepdims=True)
        gradient[level] = image + extras[0][level : level + 1]

    def send_factor(i):
        return pltpu.make_async_copy(factor_ref.at[spans[i], :], factor_hbm.at[spans[i], :], sent.at[i])

    take_rows(0)
    take_unit(0)
    fresh = work[spans[0], spans[0]] * to_column(units[0], same) * units[0]
    aside = [functools.partial(take_rows, i) for i in range(1, count)]
    aside += [functools.partial(take_unit, i) for i in range(1, count)]
    aside += [functools.partial(scale_rows, i) for i in range(count)]
    later = [functools.partial(take_share, mask, ref) for mask, ref in zip(apart, piece_refs)]
    later += [functools.partial(unpack, pair) for pair in range(LEVELS // 2)]
    later += [functools.partial(take_gradient, level) for level in range(LEVELS)]
    for b, here in enumerate(spans):
        tiles, scales = eliminate([fresh[at : at + SUB] for at in range(0, LANE, SUB)], aside, shelf)
        scale = jnp.concatenate(scales)
        inner = jnp.concatenate(tiles) * scale
        lower = jnp.where(lane_in < row_in, inner, jnp.where(lane_in == row_in, scale, 0.0))
        lower_left, lower_right = parts_of(lower, LEFT, 1), parts_of(lower, RIGHT, 1)
        panels, steps = {}, {}

        def take_line(j, b=b, here=here, lower_left=lower_left, steps=steps):
            line = jnp.dot(lower_left, parts_of(work[here, spans[j]], RIGHT, 0), preferred_element_type=f32)
            steps[j] = parts_of(line, RIGHT, 0)
            if j > b:
                factor_ref[here, spans[j]] = line * (diagonals[j] * units[j] * ratio)
                inverse_ref[here, spans[j]] = jnp.zeros((LANE, LANE), f32)
            else:
                factor_ref[here, spans[j]] = jnp.zeros((LANE, LANE), f32)
                inverse_ref[here, spans[j]] = line * units[j]

        def take_panel(i, here=here, lower_right=lower_right, panels=panels):
            panel = parts_of(work[spans[i], here], LEFT, 1)
            panels[i] = parts_of(lax.dot_general(panel, lower_right, NT, preferred_element_type=f32), LEFT, 1)

        def take_change(i, j, b=b, panels=panels, steps=steps):
            change = jnp.dot(panels[i], steps[j], preferred_element_type=f32)
            work[spans[i], spans[j]] = -change if j == b else work[spans[i], spans[j]] - change

        def put_own(here=here, inner=inner, lower=lower, b=b, steps=steps):
            steps[b] = parts_of(lower, RIGHT, 0)
            factor_ref[here, here] = jnp.where(lane_in >= row_in, inner, 0.0) * (diagonals[b] * units[b] * ratio)
            inverse_ref[here, here] = lower * units[b]

        if b + 1 < count:
            take_line(b + 1)
            take_panel(b + 1)
            fresh = work[spans[b + 1], spans[b + 1]]
            fresh = fresh - jnp.dot(panels[b + 1], steps[b + 1], preferred_element_type=f32)
        others = [j for j in range(count) if j not in (b, b + 1)]
        aside = [put_own] + [functools.partial(take_line, j) for j in others]
        aside += [functools.partial(take_panel, i) for i in range(b + 2, count)]
        aside += [
            functools.partial(take_change, i, j)
            for i in range(b + 1, count)
            for j in range(count)
            if (i, j) != (b + 1, b + 1)
        ]
        aside.append(lambda b=b: send_factor(b).start())
        if b == 1:
            aside += later
    for call_it in aside:
        call_it()

    inverse = inverse_ref[...]
    steer = jnp.sum(inverse * jnp.concatenate(gradient, axis=1), axis=1, keepdims=True)
    direction = steer
    gamma = jnp.sum(steer * steer, axis=0, keepdims=True)
    solved = jnp.zeros((1, cov_ref.shape[1] * LEVELS), f32)
    for step in range(ITERS):
        move = jnp.sum(inverse * direction, axis=0, keepdims=True)
        image = []
        for span in spans:
            image.append(jnp.sum(normal[span, :] * to_column(move[:, span], same), axis=0, keepdims=True))
        image = jnp.concatenate(image, axis=1)
        alpha = gamma / jnp.sum(move * image, axis=1, keepdims=True)
        solved = solved + alpha * move
        if step == ITERS - 1:
            break
        steer = steer - alpha * jnp.sum(inverse * image, axis=1, keepdims=True)
        gamma_new = jnp.sum(steer * steer, axis=0, keepdims=True)
        direction = steer + gamma_new / gamma * direction
        gamma = gamma_new
    solved = jnp.concatenate([solved[:, span] for span in spans])
    solved_ref[...] = solved

    left = [part.astype(f32) for part in split(effects_ref[...] - solved)]
    left = jnp.concatenate(left + [jnp.zeros((PACK - 3 * LEVELS, LANE), f32)]).astype(bf16)
    values = lax.dot_general(left, cov_ref[...], NT, preferred_element_type=f32)
    values = values[:LEVELS] + values[LEVELS : 2 * LEVELS] + values[2 * LEVELS : 3 * LEVELS]
    for r in range(marks_ref.shape[0]):
        code = jnp.bitwise_and(marks_ref[r : r + 1, :], LEVELS - 1)
        total = noise_ref[r : r + 1, :]
        for level in range(LEVELS):
            total = total + jnp.where(code == level, values[level : level + 1, r * LANE : (r + 1) * LANE], 0.0)
        resid_ref[r : r + 1, :] = total
    for i in range(count):
        send_factor(i).wait()


def call(kernel, name, outs, scratch, *operands):
    return pl.pallas_call(
        kernel,
        out_shape=[jax.ShapeDtypeStruct(shape, dtype) for shape, dtype in outs],
        in_specs=[SMEM if operand.ndim == 1 else VMEM for operand in operands],
        out_specs=[VMEM] * len(outs),
        scratch_shapes=[pltpu.VMEM(shape, dtype) for shape, dtype in scratch],
        compiler_params=pltpu.CompilerParams(vmem_limit_bytes=40 * 2**20),
        name=name,
    )(*operands)


def body(covariates, level_codes, sign_bits, sample_rows, effects, noise):
    wide, narrow = lax.axis_size("wide"), lax.axis_size("narrow")
    index = jnp.stack([lax.axis_index("wide"), lax.axis_index("narrow")]).astype(jnp.int32)
    rows_dev, cols = covariates.shape[0], LEVELS * COV
    samp = whole_up(sample_rows.shape[0], PACK)
    share = whole_up(max(2 * LANE // wide, 3 * SUB), PACK)
    sample_rows = jnp.pad(sample_rows, (0, samp - sample_rows.shape[0]), constant_values=-1)
    marks = (level_codes + LEVELS * sign_bits).reshape(-1, LANE)
    noise = noise.reshape(-1, LANE)
    effects = effects.reshape(LEVELS, COV)

    want = sample_rows[None, :]
    want = [want] + [partner(want, "wide", m) for m in range(2, MATES, 2)]
    want = [one for piece in want for one in (piece, partner(piece, "wide", 1))]
    want[0] = jnp.maximum(want[0], -1)

    design, packed = call(
        design_kernel,
        "design",
        [((cols + 3 * PACK, rows_dev), bf16), ((share * wide + SUB, LANE), f32)],
        [],
        covariates,
        marks,
        noise,
    )
    sizes = [samp * (2 * m < MATES) + share for m in range(wide // 2)]
    starts = [sum(sizes[:m]) for m in range(wide // 2)]
    stay, go = call(
        functools.partial(local_kernel, samp, share, starts),
        "local",
        [((sum(sizes), cols), bf16)] * 2,
        [((MATES * samp, rows_dev), bf16)],
        index,
        design,
        packed,
        marks,
        *want,
    )
    pieces = call(
        functools.partial(pair_kernel, samp, share, starts),
        "pair",
        [((size, cols), bf16) for size in sizes],
        [],
        index,
        stay,
        partner(go, "wide", 1),
    )
    pieces = [pieces[0]] + [partner(pieces[m], "wide", 2 * m) for m in range(1, wide // 2)]
    (piece,) = call(
        functools.partial(mix_kernel, samp, share), "mix", [((samp + share, cols), bf16)], [], index, *pieces
    )
    pieces = [piece] + [partner(piece, "narrow", m) for m in range(1, narrow)]
    rows_in = samp * narrow
    (piece,) = call(
        functools.partial(stack_kernel, samp, share), "stack", [((rows_in + share, cols), bf16)], [], index, *pieces
    )
    pieces = [piece] + [partner(piece, "wide", m) for m in range(2, wide, 2)]
    theirs = [partner(piece, "wide", 1) for piece in pieces]
    sketch = [((rows_in * (wide // 2), cols), bf16)]
    square = ((cols, cols), f32)
    (gram,) = call(functools.partial(gram_kernel, rows_in), "gram", [square], sketch, index, *pieces)
    apart = [2 * m + core for core in range(2) for m in range(wide // 2)]
    operands = (gram, effects, covariates, marks, noise, *pieces, *theirs)
    scratch = sketch + [
        square,
        ((2 * (SUB + 1) * SUB, LANE), f32),
        square,
        square,
        ((share * wide, LANE), f32),
        ((cols, LANE), f32),
    ]
    factor, solved, resid = pl.pallas_call(
        functools.partial(solve_kernel, math.sqrt(LEVELS / SKETCH), apart, rows_in, share),
        out_shape=[jax.ShapeDtypeStruct(shape, f32) for shape in ((cols, cols), (LEVELS, COV), noise.shape)],
        in_specs=[SMEM] + [VMEM] * len(operands),
        out_specs=[pl.BlockSpec(memory_space=pl.ANY), VMEM, VMEM],
        scratch_shapes=[pltpu.VMEM(shape, dtype) for shape, dtype in scratch]
        + [pltpu.SemaphoreType.DMA((cols // LANE,))],
        compiler_params=pltpu.CompilerParams(vmem_limit_bytes=40 * 2**20),
        name="solve",
    )(index, *operands)
    return solved.reshape(-1), resid.reshape(-1), factor


def solution(mesh):
    return jax.shard_map(
        body,
        mesh=mesh,
        in_specs=(
            P(("wide", "narrow"), None),
            P(("wide", "narrow")),
            P(("wide", "narrow")),
            P(("wide", "narrow")),
            P(),
            P(("wide", "narrow")),
        ),
        out_specs=(P(), P(("wide", "narrow")), P()),
        check_vma=False,
    )
```

```python
import functools
import math

import jax
import jax.numpy as jnp
from jax import lax
from jax.experimental import pallas as pl
from jax.experimental.pallas import tpu as pltpu
from jax.sharding import PartitionSpec as P

COV = 128
LEVELS = 4
HB = 256
SKETCH = 1024
ITERS = 4
MIX_BITS = 3
MATES = 2**MIX_BITS

half_root = math.sqrt(0.5)
HIGHEST = lax.Precision.HIGHEST
f32, bf16 = jnp.float32, jnp.bfloat16
SUB, LANE = 8, 128
PACK = 16
NT = (((1,), (1,)), ((), ()))
VMEM = pl.BlockSpec(memory_space=pltpu.VMEM)
SMEM = pl.BlockSpec(memory_space=pltpu.SMEM)


def partner(value, axis, mask):
    pairs = [(source, source ^ mask) for source in range(lax.axis_size(axis))]
    return lax.ppermute(value, axis, pairs)


def whole_up(number, unit):
    return -(-number // unit) * unit


def eye():
    rows = lax.broadcasted_iota(jnp.int32, (LANE, LANE), 0)
    lanes = lax.broadcasted_iota(jnp.int32, (LANE, LANE), 1)
    return rows, lanes, rows == lanes


def to_column(row, same):
    return jnp.sum(jnp.where(same, row, 0.0), axis=1, keepdims=True)


def to_row(column, same):
    return jnp.sum(jnp.where(same, column, 0.0), axis=0, keepdims=True)


def split(value):
    parts = []
    for _ in range(3):
        parts.append(value.astype(bf16))
        value = value - parts[-1].astype(f32)
    return parts


def tree_sum(values):
    while len(values) > 1:
        values = [left + right for left, right in zip(values[0::2], values[1::2])]
    return values[0]


def put_sums(ref, start, share, extra):
    rows = share.shape[0]
    for k, part in enumerate(split(share)):
        ref[start : start + rows, k * LANE : (k + 1) * LANE] = part
    tail = jnp.zeros((rows - 3 * SUB, LANE), bf16)
    ref[start : start + rows, 3 * LANE :] = jnp.concatenate(split(extra) + [tail])


def take_sums(ref, start, rows):
    block = ref[start : start + rows, :].astype(f32)
    share = block[:, :LANE] + block[:, LANE : 2 * LANE] + block[:, 2 * LANE : 3 * LANE]
    tail = block[:, 3 * LANE :]
    return share, tail[:SUB] + tail[SUB : 2 * SUB] + tail[2 * SUB : 3 * SUB]


def design_kernel(cov_ref, marks_ref, noise_ref, design, packed):
    rows, lanes, same = eye()
    zero = jnp.zeros((LANE, LANE), f32)
    for r in range(marks_ref.shape[0]):
        here = slice(r * LANE, (r + 1) * LANE)
        code = jnp.bitwise_and(marks_ref[r : r + 1, :], LEVELS - 1)
        turned = cov_ref[here, :].astype(f32).T
        for level in range(LEVELS):
            design[level * LANE : (level + 1) * LANE, here] = jnp.where(code == level, turned, zero).astype(bf16)
        noise = jnp.concatenate([noise_ref[r : r + 1, :]] * LEVELS + [jnp.zeros((PACK - LEVELS, LANE), f32)])
        level = lax.broadcasted_iota(jnp.int32, (PACK, LANE), 0)
        noise = jnp.where(code == level, noise, 0.0)
        for k, part in enumerate(split(noise)):
            design[LEVELS * LANE + k * PACK : LEVELS * LANE + (k + 1) * PACK, here] = part

    sums = jnp.dot(design[...], cov_ref[...], preferred_element_type=f32)
    normal = [sums[level * LANE : (level + 1) * LANE] for level in range(LEVELS)]
    back = sums[LEVELS * LANE :]
    back = back[:SUB] + back[PACK : PACK + SUB] + back[2 * PACK : 2 * PACK + SUB]
    extra = [jnp.sum(jnp.where(same, normal[level], 0.0), axis=0, keepdims=True) for level in (1, 3)]
    for pair in range(LEVELS // 2):
        packed[pair * LANE : (pair + 1) * LANE, :] = jnp.where(rows >= lanes, normal[2 * pair], normal[2 * pair + 1])
    rest = packed.shape[0] - SUB - 2 * LANE
    if rest:
        packed[2 * LANE : 2 * LANE + rest, :] = jnp.zeros((rest, LANE), f32)
    packed[2 * LANE + rest :, :] = jnp.concatenate([back[:LEVELS]] + extra + [jnp.zeros((2, LANE), f32)])


def local_kernel(samp, share, starts, index_ref, design_ref, packed_ref, marks_ref, *refs):
    want_refs, (stay_ref, go_ref, table) = refs[:-3], refs[-3:]
    chunks = marks_ref.shape[0]
    lanes = eye()[1]
    zero = jnp.zeros((LANE, LANE), f32)
    per = LANE // samp
    small = lax.broadcasted_iota(jnp.int32, (samp, samp), 0) == lax.broadcasted_iota(jnp.int32, (samp, samp), 1)

    masks, halves = [], []
    for c in range(MATES // per):
        want = [to_column(ref[...].astype(f32), small) for ref in want_refs[c * per : (c + 1) * per]]
        want = jnp.concatenate(want).astype(jnp.int32)
        masks.append(jnp.right_shift(want, HB.bit_length() - 1))
        line = []
        for h in range(HB // LANE):
            common = jnp.bitwise_and(want, lanes + h * LANE)
            for shift in (4, 2, 1):
                common = jnp.bitwise_xor(common, jnp.right_shift(common, shift))
            line.append((1 - 2 * jnp.bitwise_and(common, 1)).astype(f32))
        halves.append(line)
    for r in range(chunks):
        sign = jnp.where(marks_ref[r : r + 1, :] < LEVELS, 1.0, -1.0)
        block, h = divmod(r * LANE, HB)
        for c, (mask, line) in enumerate(zip(masks, halves)):
            value = jnp.where(mask == block, line[h // LANE] * sign, zero)
            table[c * LANE : (c + 1) * LANE, r * LANE : (r + 1) * LANE] = value.astype(bf16)

    local = lax.dot_general(table[...], design_ref[: LEVELS * LANE, :], NT, preferred_element_type=f32)
    local = (local * (1.0 / math.sqrt(HB))).astype(bf16)
    extra = packed_ref[packed_ref.shape[0] - SUB :, :]
    for m in range(2 * len(starts)):
        out_ref, start = (stay_ref, go_ref)[m % 2], starts[m // 2]
        if m < MATES:
            out_ref[start : start + samp, :] = local[m * samp : (m + 1) * samp]
            start += samp
        at = pl.multiple_of(jnp.bitwise_xor(index_ref[0], m) * share, share)
        put_sums(out_ref, start, packed_ref[pl.ds(at, share), :], extra)


def butterfly(pieces, place, index):
    bit = jnp.bitwise_and(jnp.right_shift(index, place), 1)
    sign = (1 - 2 * bit).astype(f32)
    return [
        ((sign * own + other) * half_root).astype(bf16).astype(f32) for own, other in zip(pieces[0::2], pieces[1::2])
    ]


def pair_kernel(samp, share, starts, index_ref, stay_ref, came_ref, *out_refs):
    for m, (start, out_ref) in enumerate(zip(starts, out_refs)):
        put = 0
        if 2 * m < MATES:
            here = slice(start, start + samp)
            pieces = [ref[here, :].astype(f32) for ref in (stay_ref, came_ref)]
            out_ref[:samp, :] = butterfly(pieces, 0, index_ref[0])[0].astype(bf16)
            put, start = samp, start + samp
        (own, own_extra), (other, other_extra) = [take_sums(ref, start, share) for ref in (stay_ref, came_ref)]
        put_sums(out_ref, put, own + other, own_extra + other_extra)


def mix_kernel(samp, share, index_ref, *refs):
    piece_refs, out_ref = refs[:-1], refs[-1]
    pieces = [ref[:samp, :].astype(f32) for ref in piece_refs[: MATES // 2]]
    for place in range(1, MIX_BITS):
        pieces = butterfly(pieces, place, index_ref[0])
    out_ref[:samp, :] = pieces[0].astype(bf16)
    sums = [take_sums(ref, samp if 2 * m < MATES else 0, share) for m, ref in enumerate(piece_refs)]
    put_sums(out_ref, samp, tree_sum([one for one, _ in sums]), tree_sum([one for _, one in sums]))


def stack_kernel(samp, share, index_ref, *refs):
    piece_refs, out_ref = refs[:-1], refs[-1]
    for m, ref in enumerate(piece_refs):
        at = pl.multiple_of(jnp.bitwise_xor(index_ref[1], m) * samp, samp)
        out_ref[pl.ds(at, samp), :] = ref[:samp, :]
    sums = [take_sums(ref, samp, share) for ref in piece_refs]
    put_sums(
        out_ref, samp * len(piece_refs), tree_sum([one for one, _ in sums]), tree_sum([one for _, one in sums])
    )


def spread(value):
    return jnp.broadcast_to(value, (SUB, LANE))


def reciprocal(value):
    return pltpu.reciprocal(value, approx=True)


def eliminate(tiles, aside, shelf):
    share = -(-len(aside) // len(tiles))
    lane = lax.broadcasted_iota(jnp.int32, (SUB, LANE), 1)
    sub = lax.broadcasted_iota(jnp.int32, (SUB, LANE), 0)
    tiles = list(tiles)
    scales = []
    for tile in range(len(tiles)):
        first = tile * SUB
        window = (lane >= first) & (lane < first + SUB)
        marks = [lane == first + k for k in range(SUB)]
        old = tiles[tile]
        columns = [spread(old[:, first + k : first + k + 1]) for k in range(SUB)]
        base = tile % 2 * (SUB + 1) * SUB
        shelf[base : base + SUB, :] = jnp.where(window, 0.0, old)
        for m in range(SUB):
            shelf[base + (m + 1) * SUB : base + (m + 2) * SUB, :] = columns[m]

        def take(m, k):
            at = base + m * SUB + k
            return spread(shelf[at : at + 1, :])

        pivot = [[take(m + 1, k) if m >= k else None for m in range(SUB)] for k in range(SUB)]
        rows = [jnp.where(marks[k], 1.0, take(0, k)) for k in range(SUB)]
        steps, near, far = [None] * SUB, {}, {}
        kept, roots = [None] * SUB, [None] * SUB

        def keep(k, low, ratio, values, others):
            last = others[k + 1]
            kept[k] = rows[k]
            for m in range(k, SUB):
                kept[k] = jnp.where(marks[m], values[m], kept[k])
            kept[k + 1] = rows[k + 1] - ratio * rows[k]
            for m in range(k + 1, SUB):
                kept[k + 1] = jnp.where(marks[m], others[m], kept[k + 1])
            roots[k], roots[k + 1] = lax.rsqrt(low), lax.rsqrt(last)

        for k in range(0, SUB, 4):
            low, cross, high = pivot[k][k], pivot[k][k + 1], pivot[k + 1][k + 1]
            area = low * high - cross * cross
            drop = {}
            for m in range(k + 2, SUB):
                near[k, m] = high * pivot[k][m] - cross * pivot[k + 1][m]
                far[k, m] = low * pivot[k + 1][m] - cross * pivot[k][m]
            for m in range(k + 2, SUB):
                for n in range(m, SUB):
                    drop[m, n] = pivot[k][m] * near[k, n] + pivot[k + 1][m] * far[k, n]
            c, d = k + 2, k + 3
            grown = {(m, n): area * pivot[m][n] - drop[m, n] for m in (c, d) for n in range(m, SUB)}
            low2, cross2, high2 = grown[c, c], grown[c, d], grown[d, d]
            area2 = low2 * high2 - cross2 * cross2
            over, over2 = reciprocal(area), reciprocal(area2)
            for m in range(k + 4, SUB):
                near[c, m] = high2 * grown[c, m] - cross2 * grown[d, m]
                far[c, m] = low2 * grown[d, m] - cross2 * grown[c, m]
            for m in range(k + 4, SUB):
                for n in range(m, SUB):
                    drop2 = grown[c, m] * near[c, n] + grown[d, m] * far[c, n]
                    pivot[m][n] = pivot[m][n] - over * (drop[m, n] + over2 * drop2)
            for m in range(k + 2, SUB):
                near[k, m], far[k, m] = over * near[k, m], over * far[k, m]
                rows[m] = rows[m] - (near[k, m] * rows[k] + far[k, m] * rows[k + 1])
            for m in range(k + 4, SUB):
                near[c, m], far[c, m] = over2 * near[c, m], over2 * far[c, m]
                rows[m] = rows[m] - (near[c, m] * rows[c] + far[c, m] * rows[d])
            steps[k] = over * (high * rows[k] - cross * rows[k + 1])
            steps[k + 1] = over * (low * rows[k + 1] - cross * rows[k])
            both = area * over2
            steps[c] = both * (high2 * rows[c] - cross2 * rows[d])
            steps[d] = both * (low2 * rows[d] - cross2 * rows[c])

            inner = reciprocal(low)
            ratio = cross * inner
            values = {m: pivot[k][m] for m in range(k, SUB)}
            others = {m: pivot[k + 1][m] - ratio * pivot[k][m] for m in range(k + 2, SUB)}
            others[k + 1] = area * inner
            keep(k, low, ratio, values, others)
            inner = reciprocal(low2)
            ratio = cross2 * inner
            values = {m: over * grown[c, m] for m in range(c, SUB)}
            others = {m: over * (grown[d, m] - ratio * grown[c, m]) for m in range(c + 2, SUB)}
            others[d] = over * (area2 * inner)
            keep(c, values[c], ratio, values, others)
        if tile + 1 < len(tiles):
            after = tiles[tile + 1]
            ahead = [spread(after[:, first + k : first + k + 1]) for k in range(SUB)]
            fresh = jnp.where(window, 0.0, after)
            for k in range(0, SUB, 2):
                for m in range(k + 2, SUB):
                    ahead[m] = ahead[m] - (near[k, m] * ahead[k] + far[k, m] * ahead[k + 1])
                fresh = fresh - (ahead[k] * steps[k] + ahead[k + 1] * steps[k + 1])
        for k in reversed(range(0, SUB, 2)):
            for m in reversed(range(k + 2, SUB)):
                steps[k] = steps[k] - near[k, m] * steps[m]
                steps[k + 1] = steps[k + 1] - far[k, m] * steps[m]
        for i in range(tile + 2, min(tile + 3, len(tiles))):
            change = [spread(tiles[i][:, first + k : first + k + 1]) * steps[k] for k in range(SUB)]
            tiles[i] = jnp.where(window, 0.0, tiles[i]) - tree_sum(change[::-1])
        if tile + 3 < len(tiles):
            stacked = steps[0]
            for k in range(1, SUB):
                stacked = jnp.where(sub >= k, steps[k], stacked)
            blank = jnp.zeros_like(stacked)
            stacked = jnp.concatenate([stacked, blank] if tile % 2 == 0 else [blank, stacked])
            none = jnp.zeros((PACK, LANE), bf16)
            before, after = tile // 2, len(tiles) // 2 - 1 - tile // 2
            parts = [jnp.concatenate([none] * before + [part] + [none] * after) for part in split(stacked)]
            change = jnp.dot(
                parts_of(jnp.concatenate(tiles[tile + 3 :]), LEFT, 1),
                jnp.concatenate([parts[k] for k in RIGHT]),
                preferred_element_type=f32,
            )
            for i in range(tile + 3, len(tiles)):
                at = (i - tile - 3) * SUB
                tiles[i] = jnp.where(window, 0.0, tiles[i]) - change[at : at + SUB]
        if tile + 1 < len(tiles):
            tiles[tile + 1] = fresh
        new, scale = kept[0], roots[0]
        for k in range(1, SUB):
            new = jnp.where(sub >= k, kept[k], new)
            scale = jnp.where(sub >= k, roots[k], scale)
        tiles[tile] = new
        scales.append(scale)
        for work in aside[tile * share : (tile + 1) * share]:
            work()
    return tiles, scales


LEFT, RIGHT = (0, 1, 0, 1, 2, 0), (0, 0, 1, 1, 0, 2)


def parts_of(value, order, axis):
    parts = split(value)
    return jnp.concatenate([parts[k] for k in order], axis=axis)


def put_pieces(rows_in, index_ref, piece_refs, sketch):
    for m, ref in enumerate(piece_refs):
        at = jnp.bitwise_xor(jnp.right_shift(index_ref[0], 1), m) * rows_in
        sketch[pl.ds(pl.multiple_of(at, rows_in), rows_in), :] = ref[:rows_in, :]


def gram_rows(sketch, here):
    return lax.dot_general(sketch[:, here], sketch[...], (((0,), (0,)), ((), ())), preferred_element_type=f32)


def gram_kernel(rows_in, index_ref, *refs):
    piece_refs, (gram_ref, sketch) = refs[:-2], refs[-2:]
    put_pieces(rows_in, index_ref, piece_refs, sketch)
    for at in range(0, gram_ref.shape[0], LANE):
        gram_ref[at : at + LANE, :] = gram_rows(sketch, slice(at, at + LANE))


def solve_kernel(
    ratio, apart, rows_in, share, index_ref, gram_ref, effects_ref, cov_ref, marks_ref, noise_ref, *refs
):
    piece_refs, (factor_hbm, solved_ref, resid_ref), scratch = refs[:-11], refs[-11:-8], refs[-8:]
    sketch, work, shelf, factor_ref, inverse_ref, packed, normal, sent = scratch
    count = work.shape[0] // LANE
    spans = [slice(at, at + LANE) for at in range(0, work.shape[0], LANE)]
    row_in, lane_in, same = eye()
    diagonals, units = [None] * count, [None] * count
    put_pieces(rows_in, index_ref, piece_refs[len(piece_refs) // 2 :], sketch)

    def take_rows(i):
        work[spans[i], :] = gram_ref[spans[i], :] + gram_rows(sketch, spans[i])

    def take_unit(i):
        diagonals[i] = jnp.sum(jnp.where(same, work[spans[i], spans[i]], 0.0), axis=0, keepdims=True)
        units[i] = lax.rsqrt(diagonals[i])

    def scale_rows(i):
        work[spans[i], :] = work[spans[i], :] * to_column(units[i], same) * jnp.concatenate(units, axis=1)

    extras, gradient = [], [None] * LEVELS

    def take_share(mask, ref):
        at = pl.multiple_of(jnp.bitwise_xor(index_ref[0], mask) * share, share)
        packed[pl.ds(at, share), :], extra = take_sums(ref, rows_in, share)
        extras.append(extra)

    def unpack(pair):
        both = packed[spans[pair], :]
        turned = both.T
        normal[spans[2 * pair], :] = jnp.where(row_in >= lane_in, both, turned)
        diagonal = jnp.where(same, extras[0][LEVELS + pair : LEVELS + pair + 1], turned)
        normal[spans[2 * pair + 1], :] = jnp.where(row_in < lane_in, both, diagonal)

    def take_gradient(level):
        column = to_column(effects_ref[level : level + 1, :], same)
        image = jnp.sum(normal[spans[level], :] * column, axis=0, keepdims=True)
        gradient[level] = image + extras[0][level : level + 1]

    def send_factor(i):
        return pltpu.make_async_copy(factor_ref.at[spans[i], :], factor_hbm.at[spans[i], :], sent.at[i])

    take_rows(0)
    take_unit(0)
    fresh = work[spans[0], spans[0]] * to_column(units[0], same) * units[0]
    aside = [functools.partial(take_rows, i) for i in range(1, count)]
    aside += [functools.partial(take_unit, i) for i in range(1, count)]
    aside += [functools.partial(scale_rows, i) for i in range(count)]
    later = [functools.partial(take_share, mask, ref) for mask, ref in zip(apart, piece_refs)]
    later += [functools.partial(unpack, pair) for pair in range(LEVELS // 2)]
    later += [functools.partial(take_gradient, level) for level in range(LEVELS)]
    for b, here in enumerate(spans):
        tiles, scales = eliminate([fresh[at : at + SUB] for at in range(0, LANE, SUB)], aside, shelf)
        scale = jnp.concatenate(scales)
        inner = jnp.concatenate(tiles) * scale
        lower = jnp.where(lane_in < row_in, inner, jnp.where(lane_in == row_in, scale, 0.0))
        lower_left, lower_right = parts_of(lower, LEFT, 1), parts_of(lower, RIGHT, 1)
        panels, steps = {}, {}

        def take_line(j, b=b, here=here, lower_left=lower_left, steps=steps):
            line = jnp.dot(lower_left, parts_of(work[here, spans[j]], RIGHT, 0), preferred_element_type=f32)
            steps[j] = parts_of(line, RIGHT, 0)
            if j > b:
                factor_ref[here, spans[j]] = line * (diagonals[j] * units[j] * ratio)
            else:
                factor_ref[here, spans[j]] = jnp.zeros((LANE, LANE), f32)
                inverse_ref[here, spans[j]] = line * units[j]

        def take_panel(i, here=here, lower_right=lower_right, panels=panels):
            panel = parts_of(work[spans[i], here], LEFT, 1)
            panels[i] = parts_of(lax.dot_general(panel, lower_right, NT, preferred_element_type=f32), LEFT, 1)

        def take_change(i, j, b=b, panels=panels, steps=steps):
            change = jnp.dot(panels[i], steps[j], preferred_element_type=f32)
            work[spans[i], spans[j]] = -change if j == b else work[spans[i], spans[j]] - change

        def put_own(here=here, inner=inner, lower=lower, b=b, steps=steps):
            steps[b] = parts_of(lower, RIGHT, 0)
            factor_ref[here, here] = jnp.where(lane_in >= row_in, inner, 0.0) * (diagonals[b] * units[b] * ratio)
            inverse_ref[here, here] = lower * units[b]

        if b + 1 < count:
            take_line(b + 1)
            take_panel(b + 1)
            fresh = work[spans[b + 1], spans[b + 1]]
            fresh = fresh - jnp.dot(panels[b + 1], steps[b + 1], preferred_element_type=f32)
        others = [j for j in range(count) if j not in (b, b + 1)]
        aside = [put_own] + [functools.partial(take_line, j) for j in others]
        aside += [functools.partial(take_panel, i) for i in range(b + 2, count)]
        aside += [
            functools.partial(take_change, i, j)
            for i in range(b + 1, count)
            for j in range(count)
            if (i, j) != (b + 1, b + 1)
        ]
        aside.append(lambda b=b: send_factor(b).start())
        if b == 1:
            aside += later
    for call_it in aside:
        call_it()

    def forward(row):
        sums = []
        for span in spans:
            sums.append(jnp.sum(inverse_ref[span, : span.stop] * row[:, : span.stop], axis=1, keepdims=True))
        return jnp.concatenate(sums)

    def backward(column):
        sums = []
        for span in spans:
            sums.append(jnp.sum(inverse_ref[span.start :, span] * column[span.start :], axis=0, keepdims=True))
        return jnp.concatenate(sums, axis=1)

    steer = forward(jnp.concatenate(gradient, axis=1))
    direction = steer
    gamma = jnp.sum(steer * steer, axis=0, keepdims=True)
    solved = jnp.zeros((1, cov_ref.shape[1] * LEVELS), f32)
    for step in range(ITERS):
        move = backward(direction)
        image = []
        for span in spans:
            image.append(jnp.sum(normal[span, :] * to_column(move[:, span], same), axis=0, keepdims=True))
        image = jnp.concatenate(image, axis=1)
        alpha = gamma / jnp.sum(move * image, axis=1, keepdims=True)
        solved = solved + alpha * move
        if step == ITERS - 1:
            break
        steer = steer - alpha * forward(image)
        gamma_new = jnp.sum(steer * steer, axis=0, keepdims=True)
        direction = steer + gamma_new / gamma * direction
        gamma = gamma_new
    solved = jnp.concatenate([solved[:, span] for span in spans])
    solved_ref[...] = solved

    left = [part.astype(f32) for part in split(effects_ref[...] - solved)]
    left = jnp.concatenate(left + [jnp.zeros((PACK - 3 * LEVELS, LANE), f32)]).astype(bf16)
    values = lax.dot_general(left, cov_ref[...], NT, preferred_element_type=f32)
    values = values[:LEVELS] + values[LEVELS : 2 * LEVELS] + values[2 * LEVELS : 3 * LEVELS]
    for r in range(marks_ref.shape[0]):
        code = jnp.bitwise_and(marks_ref[r : r + 1, :], LEVELS - 1)
        total = noise_ref[r : r + 1, :]
        for level in range(LEVELS):
            total = total + jnp.where(code == level, values[level : level + 1, r * LANE : (r + 1) * LANE], 0.0)
        resid_ref[r : r + 1, :] = total
    for i in range(count):
        send_factor(i).wait()


def call(kernel, name, outs, scratch, *operands):
    return pl.pallas_call(
        kernel,
        out_shape=[jax.ShapeDtypeStruct(shape, dtype) for shape, dtype in outs],
        in_specs=[SMEM if operand.ndim == 1 else VMEM for operand in operands],
        out_specs=[VMEM] * len(outs),
        scratch_shapes=[pltpu.VMEM(shape, dtype) for shape, dtype in scratch],
        compiler_params=pltpu.CompilerParams(vmem_limit_bytes=40 * 2**20),
        name=name,
    )(*operands)


def body(covariates, level_codes, sign_bits, sample_rows, effects, noise):
    wide, narrow = lax.axis_size("wide"), lax.axis_size("narrow")
    index = jnp.stack([lax.axis_index("wide"), lax.axis_index("narrow")]).astype(jnp.int32)
    rows_dev, cols = covariates.shape[0], LEVELS * COV
    samp = whole_up(sample_rows.shape[0], PACK)
    share = whole_up(max(2 * LANE // wide, 3 * SUB), PACK)
    sample_rows = jnp.pad(sample_rows, (0, samp - sample_rows.shape[0]), constant_values=-1)
    marks = (level_codes + LEVELS * sign_bits).reshape(-1, LANE)
    noise = noise.reshape(-1, LANE)
    effects = effects.reshape(LEVELS, COV)

    want = sample_rows[None, :]
    want = [want] + [partner(want, "wide", m) for m in range(2, MATES, 2)]
    want = [one for piece in want for one in (piece, partner(piece, "wide", 1))]
    want[0] = jnp.maximum(want[0], -1)

    design, packed = call(
        design_kernel,
        "design",
        [((cols + 3 * PACK, rows_dev), bf16), ((share * wide + SUB, LANE), f32)],
        [],
        covariates,
        marks,
        noise,
    )
    sizes = [samp * (2 * m < MATES) + share for m in range(wide // 2)]
    starts = [sum(sizes[:m]) for m in range(wide // 2)]
    stay, go = call(
        functools.partial(local_kernel, samp, share, starts),
        "local",
        [((sum(sizes), cols), bf16)] * 2,
        [((MATES * samp, rows_dev), bf16)],
        index,
        design,
        packed,
        marks,
        *want,
    )
    pieces = call(
        functools.partial(pair_kernel, samp, share, starts),
        "pair",
        [((size, cols), bf16) for size in sizes],
        [],
        index,
        stay,
        partner(go, "wide", 1),
    )
    pieces = [pieces[0]] + [partner(pieces[m], "wide", 2 * m) for m in range(1, wide // 2)]
    (piece,) = call(
        functools.partial(mix_kernel, samp, share), "mix", [((samp + share, cols), bf16)], [], index, *pieces
    )
    pieces = [piece] + [partner(piece, "narrow", m) for m in range(1, narrow)]
    rows_in = samp * narrow
    (piece,) = call(
        functools.partial(stack_kernel, samp, share), "stack", [((rows_in + share, cols), bf16)], [], index, *pieces
    )
    pieces = [piece] + [partner(piece, "wide", m) for m in range(2, wide, 2)]
    theirs = [partner(piece, "wide", 1) for piece in pieces]
    sketch = [((rows_in * (wide // 2), cols), bf16)]
    square = ((cols, cols), f32)
    (gram,) = call(functools.partial(gram_kernel, rows_in), "gram", [square], sketch, index, *pieces)
    apart = [2 * m + core for core in range(2) for m in range(wide // 2)]
    operands = (gram, effects, covariates, marks, noise, *pieces, *theirs)
    scratch = sketch + [
        square,
        ((2 * (SUB + 1) * SUB, LANE), f32),
        square,
        square,
        ((share * wide, LANE), f32),
        ((cols, LANE), f32),
    ]
    factor, solved, resid = pl.pallas_call(
        functools.partial(solve_kernel, math.sqrt(LEVELS / SKETCH), apart, rows_in, share),
        out_shape=[jax.ShapeDtypeStruct(shape, f32) for shape in ((cols, cols), (LEVELS, COV), noise.shape)],
        in_specs=[SMEM] + [VMEM] * len(operands),
        out_specs=[pl.BlockSpec(memory_space=pl.ANY), VMEM, VMEM],
        scratch_shapes=[pltpu.VMEM(shape, dtype) for shape, dtype in scratch]
        + [pltpu.SemaphoreType.DMA((cols // LANE,))],
        compiler_params=pltpu.CompilerParams(vmem_limit_bytes=40 * 2**20),
        name="solve",
    )(index, *operands)
    return solved.reshape(-1), resid.reshape(-1), factor


def solution(mesh):
    return jax.shard_map(
        body,
        mesh=mesh,
        in_specs=(
            P(("wide", "narrow"), None),
            P(("wide", "narrow")),
            P(("wide", "narrow")),
            P(("wide", "narrow")),
            P(),
            P(("wide", "narrow")),
        ),
        out_specs=(P(), P(("wide", "narrow")), P()),
        check_vma=False,
    )
```
